32 devices in a mesh: fsdp: 4 (over x, core), ctx: 2 (over y), tp: 4 (over z).
Axes of the slice: x: 2, y: 2, z: 4, core: 2. Of those that a mesh axis runs over, the one named last changes fastest.
Arguments:
- tokens: bfloat16 [8, 1024, 768], P('fsdp', 'ctx'), may hold values from -6 to 6
- teacher: bfloat16 [8, 1024, 768], P('fsdp', 'ctx'), may hold values from -6 to 6
- lengths: int32 [8], P('fsdp'), may hold values from 256 to 1024, as said below
- valid_mask: int32 [8, 1024], P('fsdp', 'ctx'), may hold values 0 or 1
- random_blocks: int32 [8, 16, 3], P('fsdp', 'ctx'), may hold values from 2 to 15
- step_count: int32 [1], replicated, may hold values from 2 to 20
- qkv_weight: float32 [3, 768, 768], P(None, 'fsdp', 'tp'), may hold values from -0.21875 to 0.21875
- out_weight: float32 [768, 768], P('tp', 'fsdp'), may hold values from -2.5 to 2.5
- up_weight: float32 [768, 3072], P('fsdp', 'tp'), may hold values from -0.21875 to 0.21875
- down_weight: float32 [3072, 768], P('tp', 'fsdp'), may hold values from -0.109375 to 0.109375
- norm_params: float32 [4, 768], P(None, 'fsdp'), may hold values from -1 to 1.5, as said below
- qkv_moment: float32 [3, 768, 768], P(None, 'fsdp', 'tp'), may hold values from -5.9604645e-07 to 5.9604645e-07
- qkv_square: float32 [3, 768, 768], P(None, 'fsdp', 'tp'), may hold values from 1.4122379e-16 to 5.6489517e-16
- out_moment: float32 [768, 768], P('tp', 'fsdp'), may hold values from -5.2154064e-08 to 5.2154064e-08
- out_square: float32 [768, 768], P('tp', 'fsdp'), may hold values from 1.1033109e-18 to 4.4132435e-18
- up_moment: float32 [768, 3072], P('fsdp', 'tp'), may hold values from -5.9604645e-07 to 5.9604645e-07
- up_square: float32 [768, 3072], P('fsdp', 'tp'), may hold values from 1.4122379e-16 to 5.6489517e-16
- down_moment: float32 [3072, 768], P('tp', 'fsdp'), may hold values from -5.9604645e-07 to 5.9604645e-07
- down_square: float32 [3072, 768], P('tp', 'fsdp'), may hold values from 1.4122379e-16 to 5.6489517e-16
- norm_moment: float32 [4, 768], P(None, 'fsdp'), may hold values from -2.3841858e-06 to 2.3841858e-06
- norm_square: float32 [4, 768], P(None, 'fsdp'), may hold values from 2.2595807e-15 to 9.038323e-15
Outputs:
- layer_out: bfloat16 [8, 1024, 768], P('fsdp', 'ctx')
- loss_value: float32 [], replicated
- input_grad: float32 [8, 1024, 768], P('fsdp', 'ctx')
- grad_norm: float32 [], replicated
- qkv_updated: float32 [3, 768, 768], P(None, 'fsdp', 'tp')
- qkv_moment_new: float32 [3, 768, 768], P(None, 'fsdp', 'tp')
- qkv_square_new: float32 [3, 768, 768], P(None, 'fsdp', 'tp')
- out_updated: float32 [768, 768], P('tp', 'fsdp')
- out_moment_new: float32 [768, 768], P('tp', 'fsdp')
- out_square_new: float32 [768, 768], P('tp', 'fsdp')
- up_updated: float32 [768, 3072], P('fsdp', 'tp')
- up_moment_new: float32 [768, 3072], P('fsdp', 'tp')
- up_square_new: float32 [768, 3072], P('fsdp', 'tp')
- down_updated: float32 [3072, 768], P('tp', 'fsdp')
- down_moment_new: float32 [3072, 768], P('tp', 'fsdp')
- down_square_new: float32 [3072, 768], P('tp', 'fsdp')
- norm_updated: float32 [4, 768], P(None, 'fsdp')
- norm_moment_new: float32 [4, 768], P(None, 'fsdp')
- norm_square_new: float32 [4, 768], P(None, 'fsdp')
The draws below stay inside these ranges and needn't reach their ends.
Inputs may be any that keep to these rules, and one draw needn't show every extreme that they name: `lengths`: one slot has exactly 1024 tokens and another exactly 256. `norm_params`: rows 0 and 2 are gains, rows 1 and 3 biases.
All inputs are finite; a program needn't handle non-finite values. No bound on the sum of `valid_mask` on one device may be relied on, other than what follows from the above.
Results may differ from the reference program's by a relative error of at most 0.019.
Values may be sent and summed in bfloat16 or wider, within the bound.
A program may use at most 256 MiB of HBM per device.

```python
import math
import jax
import jax.numpy as jnp
from jax import lax

D = 768
H = 12
HD = 64
FF = 3072
BLK = 64
SEQ = 1024
NBLK = 16
SLOTS = 8
PARAMS = 7080960


def draw_lengths(key, part):
    first_key, second_key = jax.random.split(key)
    order = jax.random.permutation(first_key, SLOTS)
    chosen = jax.random.randint(second_key, (SLOTS,), SEQ // 4, SEQ + 1)
    chosen = jnp.where(order == 0, SEQ, chosen)
    chosen = jnp.where(order == 1, SEQ // 4, chosen)
    return chosen.astype(jnp.int32)


def draw_norm_params(key, part):
    first_key, second_key = jax.random.split(key)
    gains = jax.random.uniform(first_key, (2, D), jnp.float32, 0.5, 1.5)
    shifts = jnp.clip(0.3 * jax.random.normal(second_key, (2, D), jnp.float32), -1.0, 1.0)
    return jnp.stack([gains[0], shifts[0], gains[1], shifts[1]], 0)


def with_ends(result, own_key, smallest, high):
    extent = result.shape
    index_at = [jax.random.randint(jax.random.fold_in(own_key, axis), (), 0, extent[axis]) for axis in range(len(extent))]
    result = result.at[tuple(index_at)].set(smallest)
    longest = extent.index(max(extent))
    index_at[longest] = (index_at[longest] + 1) % extent[longest]
    return result.at[tuple(index_at)].set(high)


def block_levels(own_key, shape, cuts, least, high):
    def one(dim, shards_of):
        steps = jax.random.uniform(jax.random.fold_in(jax.random.fold_in(own_key, 6), dim), (shards_of,), jnp.float32, least / len(cuts), high / len(cuts))
        return jnp.repeat(jnp.exp(steps), shape[dim] // shards_of).reshape((-1,) + (1,) * (len(shape) - dim - 1))

    loudness = one(*cuts[0])
    for cut in cuts[1:]:
        loudness = loudness * one(*cut)
    return loudness


def scatter_about(rng, dims, scale, bound, cuts=(), kind=jnp.bfloat16):
    result = scale * jax.random.normal(rng, dims, jnp.float32)
    if cuts:
        result = result * block_levels(rng, dims, cuts, -0.22, 0.18)
    return jnp.clip(result, -bound, bound).astype(kind)


def setup_inputs(seed: int = 0) -> dict:
    streams_of = jax.random.split(jax.random.key(seed), 22)
    return {
        "tokens": scatter_about(streams_of[0], (SLOTS, SEQ, D), 1.0, 6.0, ((0, 4), (1, 2))),
        "teacher": scatter_about(streams_of[1], (SLOTS, SEQ, D), 1.0, 6.0, ((0, 4), (1, 2))),
        "lengths": draw_lengths(jax.random.fold_in(streams_of[21], 71), 0),
        "valid_mask": with_ends((jax.random.randint(streams_of[3], (SLOTS, SEQ), 0, 4) < 3).astype(jnp.int32), jax.random.fold_in(streams_of[3], 1), 0, 1),
        "random_blocks": with_ends(jax.random.randint(streams_of[4], (SLOTS, NBLK, 3), 2, NBLK), jax.random.fold_in(streams_of[4], 1), 2, NBLK - 1).astype(jnp.int32),
        "step_count": jax.random.randint(streams_of[5], (1,), 2, 21).astype(jnp.int32),
        "qkv_weight": scatter_about(streams_of[6], (3, D, D), D ** -0.5, 0.21875, ((1, 4), (2, 4)), jnp.float32),
        "out_weight": scatter_about(streams_of[7], (D, D), (max(D // 128, 1)) ** -0.5, 2.5, ((0, 4), (1, 4)), jnp.float32),
        "up_weight": scatter_about(streams_of[8], (D, FF), D ** -0.5, 0.21875, ((0, 4), (1, 4)), jnp.float32),
        "down_weight": scatter_about(streams_of[9], (FF, D), FF ** -0.5, 0.109375, ((0, 4), (1, 4)), jnp.float32),
        "norm_params": draw_norm_params(jax.random.fold_in(streams_of[21], 71), 0),
        "qkv_moment": scatter_about(streams_of[11], (3, D, D), (0.00011 / PARAMS ** 0.5), 5.960464477539062e-07, ((1, 4), (2, 4)), jnp.float32),
        "qkv_square": jnp.clip(jnp.exp(math.log(5.648951663698391e-16) - 1.3862944 * jax.random.uniform(streams_of[12], (3, D, D), jnp.float32) ** block_levels(streams_of[12], (3, D, D), ((1, 4), (2, 4)), -0.2, 0.2)), 1.4122379159245977e-16, 5.648951663698391e-16),
        "out_moment": scatter_about(streams_of[13], (D, D), (0.00011 * (max(D // 128, 1) / D) ** 0.5 / PARAMS ** 0.5), 5.21540641784668e-08, ((0, 4), (1, 4)), jnp.float32),
        "out_square": jnp.clip(jnp.exp(math.log(4.413243487264368e-18) - 1.3862944 * jax.random.uniform(streams_of[14], (D, D), jnp.float32) ** block_levels(streams_of[14], (D, D), ((0, 4), (1, 4)), -0.2, 0.2)), 1.103310871816092e-18, 4.413243487264368e-18),
        "up_moment": scatter_about(streams_of[15], (D, FF), (0.00011 / PARAMS ** 0.5), 5.960464477539062e-07, ((0, 4), (1, 4)), jnp.float32),
        "up_square": jnp.clip(jnp.exp(math.log(5.648951663698391e-16) - 1.3862944 * jax.random.uniform(streams_of[16], (D, FF), jnp.float32) ** block_levels(streams_of[16], (D, FF), ((0, 4), (1, 4)), -0.2, 0.2)), 1.4122379159245977e-16, 5.648951663698391e-16),
        "down_moment": scatter_about(streams_of[17], (FF, D), (0.00011 / PARAMS ** 0.5), 5.960464477539062e-07, ((0, 4), (1, 4)), jnp.float32),
        "down_square": jnp.clip(jnp.exp(math.log(5.648951663698391e-16) - 1.3862944 * jax.random.uniform(streams_of[18], (FF, D), jnp.float32) ** block_levels(streams_of[18], (FF, D), ((0, 4), (1, 4)), -0.2, 0.2)), 1.4122379159245977e-16, 5.648951663698391e-16),
        "norm_moment": scatter_about(streams_of[19], (4, D), (0.00044 / PARAMS ** 0.5), 2.384185791015625e-06, ((1, 4),), jnp.float32),
        "norm_square": jnp.clip(jnp.exp(math.log(9.038322661917425e-15) - 1.3862944 * jax.random.uniform(streams_of[20], (4, D), jnp.float32) ** block_levels(streams_of[20], (4, D), ((1, 4),), -0.2, 0.2)), 2.2595806654793563e-15, 9.038322661917425e-15),
    }


@jax.custom_vjp
def low(v):
    return lax.optimization_barrier(v.astype(jnp.bfloat16)).astype(jnp.float32)

@jax.custom_vjp
def low_back(v):
    return v

def low_keep(v):
    return (low(v), None)

def low_pass(kept, grad):
    return (grad,)

def back_keep(v):
    return (v, None)

def back_low(kept, grad):
    return (low(grad),)
low.defvjp(low_keep, low_pass)
low_back.defvjp(back_keep, back_low)
highest = lax.Precision.HIGHEST
norm_eps = 1e-06
beta_one = 0.9
beta_two = 0.999
adam_eps = 1e-08
decay_rate = 0.01
clip_level = 0.001
rate_list = (0.04, 0.4, 0.04, 0.02, 0.2)
negative = -1e+30

def layer_norm(values, gain, shift):
    center = values - lax.optimization_barrier(jnp.mean(values, -1, keepdims=True))
    spread = lax.optimization_barrier(jnp.mean(center * center, -1, keepdims=True))
    return center * lax.rsqrt(spread + norm_eps) * gain + shift

def softmax_rows(scores):
    top_value = lax.optimization_barrier(jnp.max(scores, -1, keepdims=True))
    expo = jnp.exp(scores - top_value)
    return expo / lax.optimization_barrier(jnp.sum(expo, -1, keepdims=True))

def sequence_forward(inputs, weights, length, picks):
    qkv_w, out_w, up_w, down_w, norm_w = weights
    projected = low(low_back(jnp.einsum('td,cde->cte', inputs, qkv_w, precision=highest)))
    queries = projected[0].reshape(SEQ, H, HD)
    keys_all = projected[1].reshape(SEQ, H, HD)
    values_all = projected[2].reshape(SEQ, H, HD)
    scale = HD ** (-0.5)
    blocks = jnp.arange(NBLK, dtype=jnp.int32)
    window = jnp.stack([blocks * 0, blocks * 0 + 1, blocks - 1, blocks, blocks + 1], -1)
    listed = jnp.concatenate([window, picks.astype(jnp.int32)], -1)
    inside = (listed >= 0) & (listed < NBLK)
    safe = jnp.clip(listed, 0, NBLK - 1).astype(jnp.int32)
    key_pos = safe[:, :, None] * BLK + jnp.arange(BLK, dtype=jnp.int32)[None, None, :]
    counted = (inside[:, :, None] & (key_pos < length)).reshape(NBLK, 8 * BLK)
    key_blocks = keys_all.reshape(NBLK, BLK, H, HD)[safe].reshape(NBLK, 8 * BLK, H, HD)
    value_blocks = values_all.reshape(NBLK, BLK, H, HD)[safe].reshape(NBLK, 8 * BLK, H, HD)
    query_blocks = queries.reshape(NBLK, BLK, H, HD)
    scores = low_back(scale * jnp.einsum('nqhd,nkhd->nhqk', query_blocks, key_blocks, precision=highest))
    scores = jnp.where(counted[:, None, None, :], scores, negative)
    probs = low(softmax_rows(scores))
    sparse_out = jnp.einsum('nhqk,nkhd->nqhd', probs, value_blocks, precision=highest).reshape(SEQ, H, HD)
    head_rows = queries[:2 * BLK]
    global_scores = low_back(scale * jnp.einsum('qhd,khd->hqk', head_rows, keys_all, precision=highest))
    seen = jnp.arange(SEQ, dtype=jnp.int32) < length
    global_scores = jnp.where(seen[None, None, :], global_scores, negative)
    global_probs = low(softmax_rows(global_scores))
    global_out = jnp.einsum('hqk,khd->qhd', global_probs, values_all, precision=highest)
    attended = jnp.concatenate([global_out, sparse_out[2 * BLK:]], 0).reshape(SEQ, D)
    attended = low(low_back(attended))
    attn = low_back(jnp.dot(attended, out_w, precision=highest))
    hidden = layer_norm(inputs + attn, norm_w[0], norm_w[1])
    upper = low_back(jnp.dot(low(hidden), up_w, precision=highest))
    active = low(jax.nn.gelu(upper, approximate=True))
    mixed = low_back(jnp.dot(active, down_w, precision=highest))
    return layer_norm(hidden + mixed, norm_w[2], norm_w[3])

def adam_update(weight, gradient, moment, square, factor, steps_done, rate):
    clipped = gradient * factor
    new_moment = beta_one * moment + (1.0 - beta_one) * clipped
    new_square = beta_two * square + (1.0 - beta_two) * clipped * clipped
    corrected = new_moment / (1.0 - beta_one ** steps_done)
    scaled = new_square / (1.0 - beta_two ** steps_done)
    new_weight = weight - rate * (corrected / (jnp.sqrt(scaled) + adam_eps) + decay_rate * weight)
    return (new_weight, new_moment, new_square)

def reference(tokens, teacher, lengths, valid_mask, random_blocks, step_count, qkv_weight, out_weight, up_weight, down_weight, norm_params, qkv_moment, qkv_square, out_moment, out_square, up_moment, up_square, down_moment, down_square, norm_moment, norm_square):
    inputs = tokens.astype(jnp.float32)
    targets = teacher.astype(jnp.float32)
    positions = jnp.arange(SEQ, dtype=jnp.int32)
    live_rows = ((valid_mask == 1) & (positions[None, :] < lengths[:, None])).astype(jnp.float32)
    live_count = jnp.sum(live_rows)
    params = (qkv_weight, out_weight, up_weight, down_weight, norm_params)
    checked = jax.checkpoint(sequence_forward)

    def total_loss(inputs, params):
        rounded = tuple((low(member) for member in params))

        def one_slot(carry, items):
            slot_in, slot_target, length, slot_live, picks = items
            slot_out = checked(slot_in, rounded, length, picks)
            differ = slot_out - slot_target
            return (carry + jnp.sum(slot_live[:, None] * differ * differ), slot_out)
        summed, outputs = lax.scan(one_slot, jnp.zeros((), jnp.float32), (inputs, targets, lengths, live_rows, random_blocks))
        return (summed / (live_count * D), outputs)
    loss_value, pullback, outputs = jax.vjp(total_loss, inputs, params, has_aux=True)
    input_grad, grads = pullback(jnp.ones_like(loss_value))
    squares = sum((jnp.sum(gradient * gradient) for gradient in grads))
    grad_norm = jnp.sqrt(squares)
    factor = jnp.minimum(1.0, clip_level / (grad_norm + 1e-06))
    steps_done = step_count[0].astype(jnp.float32)
    qkv_new = adam_update(qkv_weight, grads[0], qkv_moment, qkv_square, factor, steps_done, rate_list[0])
    out_new = adam_update(out_weight, grads[1], out_moment, out_square, factor, steps_done, rate_list[1])
    up_new = adam_update(up_weight, grads[2], up_moment, up_square, factor, steps_done, rate_list[2])
    down_new = adam_update(down_weight, grads[3], down_moment, down_square, factor, steps_done, rate_list[3])
    norm_new = adam_update(norm_params, grads[4], norm_moment, norm_square, factor, steps_done, rate_list[4])
    return (outputs.astype(jnp.bfloat16), loss_value, input_grad, grad_norm, qkv_new[0], qkv_new[1], qkv_new[2], out_new[0], out_new[1], out_new[2], up_new[0], up_new[1], up_new[2], down_new[0], down_new[1], down_new[2], norm_new[0], norm_new[1], norm_new[2])
```

```python
import functools
from functools import partial

import jax
import jax.numpy as jnp
from jax import lax
from jax.experimental import pallas as pl
from jax.experimental.pallas import tpu as pltpu
from jax.sharding import PartitionSpec as P

HD = 64
BLK = 64
MESH = pl.DeviceIdType.MESH
f32 = jnp.float32
bf16 = jnp.bfloat16

norm_eps = 1e-06
beta_one = 0.9
beta_two = 0.999
adam_eps = 1e-08
decay_rate = 0.01
clip_level = 0.001
rate_list = (0.04, 0.4, 0.04, 0.02, 0.2)
negative = -1e30
VMEM_LIMIT = 58 * 2**20


def layer_norm(values, gain, shift):
    center = values - jnp.mean(values, -1, keepdims=True)
    inverse = lax.rsqrt(jnp.mean(center * center, -1, keepdims=True) + norm_eps)
    normed = center * inverse
    return (normed * gain + shift, normed, inverse)


def norm_backward(upstream, normed, inverse, gain):
    scaled = upstream * gain
    return inverse * (
        scaled
        - jnp.mean(scaled, -1, keepdims=True)
        - normed * jnp.mean(scaled * normed, -1, keepdims=True)
    )


def adam_update(weight, gradient, moment, square, factor, steps_done, rate):
    clipped = gradient * factor
    new_moment = beta_one * moment + (1.0 - beta_one) * clipped
    new_square = beta_two * square + (1.0 - beta_two) * clipped * clipped
    corrected = new_moment / (1.0 - beta_one**steps_done)
    scaled = new_square / (1.0 - beta_two**steps_done)
    new_weight = weight - rate * (corrected / (jnp.sqrt(scaled) + adam_eps) + decay_rate * weight)
    return (new_weight, new_moment, new_square)


def body_general(
    tokens,
    teacher,
    lengths,
    valid_mask,
    random_blocks,
    step_count,
    qkv_weight,
    out_weight,
    up_weight,
    down_weight,
    norm_params,
    qkv_moment,
    qkv_square,
    out_moment,
    out_square,
    up_moment,
    up_square,
    down_moment,
    down_square,
    norm_moment,
    norm_square,
):
    ctx_index = lax.axis_index("ctx")
    ctx_count = lax.axis_size("ctx")
    tp_index = lax.axis_index("tp")
    seqs_here, tok_count, width = tokens.shape
    local_blocks = tok_count // BLK
    block_count = local_blocks * ctx_count
    seq_len = tok_count * ctx_count
    width_local = qkv_weight.shape[2]
    heads_local = width_local // HD
    scale = HD ** (-0.5)
    full_qkv, full_out, full_up, full_down, full_norms = (
        lax.all_gather(qkv_weight.astype(bf16), "fsdp", axis=1, tiled=True),
        lax.all_gather(out_weight.astype(bf16), "fsdp", axis=1, tiled=True),
        lax.all_gather(up_weight.astype(bf16), "fsdp", axis=0, tiled=True),
        lax.all_gather(down_weight.astype(bf16), "fsdp", axis=1, tiled=True),
        lax.all_gather(norm_params.astype(bf16), "fsdp", axis=1, tiled=True),
    )
    gains = full_norms.astype(f32)
    projected = jnp.einsum("std,cde->stce", tokens, full_qkv, preferred_element_type=f32).astype(
        bf16
    )
    queries = projected[:, :, 0, :]
    kv_local = projected[:, :, 1:, :]
    gathered = lax.all_gather(kv_local, "ctx", axis=1, tiled=True)
    own_blocks = ctx_index * local_blocks + jnp.arange(local_blocks, dtype=jnp.int32)
    zero_row = own_blocks * 0
    window = jnp.stack([zero_row, zero_row + 1, own_blocks - 1, own_blocks, own_blocks + 1], -1)
    listed = jnp.concatenate(
        [jnp.broadcast_to(window[None], (seqs_here, local_blocks, 5)), random_blocks], -1
    )
    inside = (listed >= 0) & (listed < block_count)
    safe = jnp.clip(listed, 0, block_count - 1)
    key_pos = safe[..., None] * BLK + jnp.arange(BLK, dtype=jnp.int32)
    counted = (inside[..., None] & (key_pos < lengths[:, None, None, None])).reshape(
        seqs_here, local_blocks, 8 * BLK
    )
    key_live = jnp.arange(seq_len, dtype=jnp.int32)[None, :] < lengths[:, None]
    q_blocks = queries.reshape(seqs_here, local_blocks, BLK, heads_local, HD)
    head_rows = queries[:, : 2 * BLK].reshape(seqs_here, 2 * BLK, heads_local, HD)
    blocked = gathered.reshape(seqs_here, block_count, BLK, 2, width_local)
    flat = blocked.reshape(seqs_here * block_count, BLK, 2, width_local)
    offset = jnp.arange(seqs_here, dtype=jnp.int32)[:, None, None] * block_count
    picked = lax.map(
        lambda at: lax.dynamic_index_in_dim(flat, at, 0, keepdims=False), (safe + offset).reshape(-1)
    ).reshape(seqs_here, local_blocks, 8, BLK, 2, width_local)
    key_rows = picked[..., 0, :].reshape(seqs_here, local_blocks, 8 * BLK, heads_local, HD)
    value_rows = picked[..., 1, :].reshape(seqs_here, local_blocks, 8 * BLK, heads_local, HD)
    scores = (
        jnp.einsum("sbqhd,sbkhd->sbhqk", q_blocks, key_rows, preferred_element_type=f32) * scale
    )
    scores = jnp.where(counted[:, :, None, None, :], scores, negative)
    all_keys = gathered[:, :, 0, :].reshape(seqs_here, seq_len, heads_local, HD)
    all_values = gathered[:, :, 1, :].reshape(seqs_here, seq_len, heads_local, HD)
    wide_scores = (
        jnp.einsum("sqhd,skhd->shqk", head_rows, all_keys, preferred_element_type=f32) * scale
    )
    wide_scores = jnp.where(key_live[:, None, None, :], wide_scores, negative)
    top_value = jnp.max(scores, -1, keepdims=True)
    expo = jnp.exp(scores - top_value)
    summed = jnp.sum(expo, -1, keepdims=True)
    sparse_lse = top_value + jnp.log(summed)
    probs_b = (expo / summed).astype(bf16)
    sparse_out = jnp.einsum(
        "sbhqk,sbkhd->sbqhd", probs_b, value_rows, preferred_element_type=f32
    ).reshape(seqs_here, tok_count, width_local)
    wide_top = jnp.max(wide_scores, -1, keepdims=True)
    wide_expo = jnp.exp(wide_scores - wide_top)
    wide_sum = jnp.sum(wide_expo, -1, keepdims=True)
    wide_lse = wide_top + jnp.log(wide_sum)
    wide_probs = (wide_expo / wide_sum).astype(bf16)
    wide_out = jnp.einsum(
        "shqk,skhd->sqhd", wide_probs, all_values, preferred_element_type=f32
    ).reshape(seqs_here, 2 * BLK, width_local)
    is_first = ctx_index == 0
    row_ids = jnp.arange(tok_count, dtype=jnp.int32)
    global_row = (row_ids < 2 * BLK) & is_first
    rest_zeros = jnp.zeros((seqs_here, tok_count - 2 * BLK, width_local), f32)
    padded_wide = jnp.concatenate([wide_out, rest_zeros], 1)
    attended = jnp.where(global_row[None, :, None], padded_wide, sparse_out).astype(bf16)
    attn_part = jnp.einsum("ste,ed->std", attended, full_out, preferred_element_type=f32)
    positions = ctx_index * tok_count + row_ids
    live_rows = ((valid_mask == 1) & (positions[None, :] < lengths[:, None])).astype(f32)
    count_local = jnp.sum(live_rows)
    gelu_fn = partial(jax.nn.gelu, approximate=True)
    attn = lax.psum(attn_part.astype(jnp.bfloat16), "tp").astype(jnp.float32)
    hidden, normed_one, inverse_one = layer_norm(tokens.astype(f32) + attn, gains[0], gains[1])
    hidden_b = hidden.astype(bf16)
    upper = jnp.einsum("std,df->stf", hidden_b, full_up, preferred_element_type=f32)
    active_f, gelu_back = jax.vjp(gelu_fn, upper)
    active = active_f.astype(bf16)
    mixed = lax.psum(
        jnp.einsum("stf,fd->std", active, full_down, preferred_element_type=f32).astype(
            jnp.bfloat16
        ),
        "tp",
    ).astype(jnp.float32)
    result, normed_two, inverse_two = layer_norm(hidden + mixed, gains[2], gains[3])
    differ = result - teacher.astype(f32)
    error_local = jnp.sum(live_rows[..., None] * differ * differ)
    error_total, live_count = lax.psum((error_local, count_local), ("fsdp", "ctx"))
    loss_value = error_total / (live_count * width)
    grad_y = 2.0 * differ * live_rows[..., None] / (live_count * width)
    gain_two_grad = jnp.sum(grad_y * normed_two, (0, 1))
    bias_two_grad = jnp.sum(grad_y, (0, 1))
    grad_two = norm_backward(grad_y, normed_two, inverse_two, gains[2])
    grad_mixed = grad_two.astype(bf16)
    grad_active = jnp.einsum("std,fd->stf", grad_mixed, full_down, preferred_element_type=f32)
    grad_upper = gelu_back(grad_active)[0].astype(bf16)
    down_grad = jnp.einsum("stf,std->fd", active, grad_mixed, preferred_element_type=f32)
    up_grad = jnp.einsum("std,stf->df", hidden_b, grad_upper, preferred_element_type=f32)
    grad_hidden = grad_two + lax.psum(
        jnp.einsum("stf,df->std", grad_upper, full_up, preferred_element_type=f32).astype(
            jnp.bfloat16
        ),
        "tp",
    ).astype(jnp.float32)
    gain_one_grad = jnp.sum(grad_hidden * normed_one, (0, 1))
    bias_one_grad = jnp.sum(grad_hidden, (0, 1))
    grad_one = norm_backward(grad_hidden, normed_one, inverse_one, gains[0])
    norm_grad = jnp.stack([gain_one_grad, bias_one_grad, gain_two_grad, bias_two_grad], 0)
    grad_attn = grad_one.astype(bf16)
    out_grad = jnp.einsum("ste,std->ed", attended, grad_attn, preferred_element_type=f32)
    grad_attended = jnp.einsum(
        "std,ed->ste", grad_attn, full_out, preferred_element_type=f32
    ).astype(bf16)
    sparse_grad = jnp.where(global_row[None, :, None], jnp.zeros_like(grad_attended), grad_attended)
    sparse_grad = sparse_grad.reshape(seqs_here, local_blocks, BLK, heads_local, HD)
    probs = jnp.exp(scores - sparse_lse)
    grad_probs = jnp.einsum(
        "sbqhd,sbkhd->sbhqk", sparse_grad, value_rows, preferred_element_type=f32
    )
    row_dot = jnp.sum(probs * grad_probs, -1, keepdims=True)
    grad_scores = (probs * (grad_probs - row_dot)).astype(bf16)
    dq_sparse = (
        jnp.einsum("sbhqk,sbkhd->sbqhd", grad_scores, key_rows, preferred_element_type=f32) * scale
    )
    dk_rows = (
        jnp.einsum("sbhqk,sbqhd->sbkhd", grad_scores, q_blocks, preferred_element_type=f32) * scale
    )
    dv_rows = jnp.einsum(
        "sbhqk,sbqhd->sbkhd", probs.astype(bf16), sparse_grad, preferred_element_type=f32
    )
    list_grads = jnp.stack(
        [
            dk_rows.reshape(seqs_here, local_blocks, 8, BLK, width_local),
            dv_rows.reshape(seqs_here, local_blocks, 8, BLK, width_local),
        ],
        4,
    )
    seq_ids = jnp.broadcast_to(jnp.arange(seqs_here, dtype=jnp.int32)[:, None, None], safe.shape)
    kv_term = (
        jnp.zeros((block_count, seqs_here, BLK, 2, width_local), f32)
        .at[safe, seq_ids]
        .add(list_grads)
    )
    head_grad = jnp.where(
        is_first, grad_attended[:, : 2 * BLK], jnp.zeros_like(grad_attended[:, : 2 * BLK])
    )
    head_grad = head_grad.reshape(seqs_here, 2 * BLK, heads_local, HD)
    wide_probs_f = jnp.exp(wide_scores - wide_lse)
    wide_dprobs = jnp.einsum("sqhd,skhd->shqk", head_grad, all_values, preferred_element_type=f32)
    wide_dot = jnp.sum(wide_probs_f * wide_dprobs, -1, keepdims=True)
    wide_dscores = (wide_probs_f * (wide_dprobs - wide_dot)).astype(bf16)
    dq_wide = (
        jnp.einsum("shqk,skhd->sqhd", wide_dscores, all_keys, preferred_element_type=f32) * scale
    )
    split_scores = wide_dscores.reshape(seqs_here, heads_local, 2 * BLK, block_count, BLK)
    split_probs = wide_probs_f.astype(bf16).reshape(
        seqs_here, heads_local, 2 * BLK, block_count, BLK
    )
    dk_wide = (
        jnp.einsum("shqnb,sqhd->nsbhd", split_scores, head_rows, preferred_element_type=f32) * scale
    )
    dv_wide = jnp.einsum("shqnb,sqhd->nsbhd", split_probs, head_grad, preferred_element_type=f32)
    kv_term = kv_term + jnp.stack(
        [
            dk_wide.reshape(block_count, seqs_here, BLK, width_local),
            dv_wide.reshape(block_count, seqs_here, BLK, width_local),
        ],
        3,
    )
    kv_grads = lax.psum_scatter(
        kv_term.astype(jnp.bfloat16), "ctx", scatter_dimension=0, tiled=True
    ).astype(jnp.float32)
    kv_grads = jnp.transpose(kv_grads, (1, 0, 2, 3, 4)).reshape(
        seqs_here, tok_count, 2, width_local
    )
    dq_total = dq_sparse.reshape(seqs_here, tok_count, width_local) + jnp.concatenate(
        [dq_wide.reshape(seqs_here, 2 * BLK, width_local), rest_zeros], 1
    )
    grad_projected = jnp.concatenate([dq_total[:, :, None, :], kv_grads], 2).astype(bf16)
    qkv_grad = jnp.einsum("std,stce->cde", tokens, grad_projected, preferred_element_type=f32)
    input_part = jnp.einsum("stce,cde->std", grad_projected, full_qkv, preferred_element_type=f32)
    input_grad = grad_one + lax.psum(input_part.astype(jnp.bfloat16), "tp").astype(jnp.float32)
    local_grads = (qkv_grad, out_grad, up_grad, down_grad, norm_grad)
    owned = (
        lax.psum_scatter(
            local_grads[0].astype(jnp.bfloat16), "fsdp", scatter_dimension=1, tiled=True
        ).astype(jnp.float32),
        lax.psum_scatter(
            local_grads[1].astype(jnp.bfloat16), "fsdp", scatter_dimension=1, tiled=True
        ).astype(jnp.float32),
        lax.psum_scatter(
            local_grads[2].astype(jnp.bfloat16), "fsdp", scatter_dimension=0, tiled=True
        ).astype(jnp.float32),
        lax.psum_scatter(
            local_grads[3].astype(jnp.bfloat16), "fsdp", scatter_dimension=1, tiled=True
        ).astype(jnp.float32),
        lax.psum_scatter(
            local_grads[4].astype(jnp.bfloat16), "fsdp", scatter_dimension=1, tiled=True
        ).astype(jnp.float32),
    )
    shards = (
        lax.psum(owned[0].astype(jnp.bfloat16), "ctx").astype(jnp.float32),
        lax.psum(owned[1].astype(jnp.bfloat16), "ctx").astype(jnp.float32),
        lax.psum(owned[2].astype(jnp.bfloat16), "ctx").astype(jnp.float32),
        lax.psum(owned[3].astype(jnp.bfloat16), "ctx").astype(jnp.float32),
        lax.psum(owned[4].astype(jnp.bfloat16), "ctx").astype(jnp.float32),
    )
    matrix_squares = sum((jnp.sum(member * member) for member in shards[:4]))
    norm_squares = jnp.where(tp_index == 0, jnp.sum(shards[4] * shards[4]), 0.0)
    squares_total = lax.psum(matrix_squares + norm_squares, ("fsdp", "tp"))
    grad_norm = jnp.sqrt(squares_total)
    factor = jnp.minimum(1.0, clip_level / (grad_norm + 1e-06))
    steps_done = step_count[0].astype(f32)
    qkv_new = adam_update(
        qkv_weight, shards[0], qkv_moment, qkv_square, factor, steps_done, rate_list[0]
    )
    out_new = adam_update(
        out_weight, shards[1], out_moment, out_square, factor, steps_done, rate_list[1]
    )
    up_new = adam_update(
        up_weight, shards[2], up_moment, up_square, factor, steps_done, rate_list[2]
    )
    down_new = adam_update(
        down_weight, shards[3], down_moment, down_square, factor, steps_done, rate_list[3]
    )
    norm_new = adam_update(
        norm_params, shards[4], norm_moment, norm_square, factor, steps_done, rate_list[4]
    )
    return (
        result.astype(bf16),
        loss_value,
        input_grad,
        grad_norm,
        qkv_new[0],
        qkv_new[1],
        qkv_new[2],
        out_new[0],
        out_new[1],
        out_new[2],
        up_new[0],
        up_new[1],
        up_new[2],
        down_new[0],
        down_new[1],
        down_new[2],
        norm_new[0],
        norm_new[1],
        norm_new[2],
    )


def remote(src, dst, send, recv, dev):
    return pltpu.make_async_remote_copy(
        src_ref=src, dst_ref=dst, send_sem=send, recv_sem=recv, device_id=dev, device_id_type=MESH
    )


def dot_nn(a, b):
    return lax.dot_general(a, b, (((1,), (0,)), ((), ())), preferred_element_type=f32)


def dot_nt(a, b):
    return lax.dot_general(a, b, (((1,), (1,)), ((), ())), preferred_element_type=f32)


def dot_tn(a, b):
    return lax.dot_general(a, b, (((0,), (0,)), ((), ())), preferred_element_type=f32)


UW = 1792


class Peers:
    def __init__(self):
        f, c, t = lax.axis_index("fsdp"), lax.axis_index("ctx"), lax.axis_index("tp")
        x, k = f // 2, f % 2
        self.f, self.c, self.t = f, c, t
        self.f_core = x * 2 + (1 - k)
        self.f_x = (1 - x) * 2 + k
        self.f_xc = (1 - x) * 2 + (1 - k)
        self.core = (self.f_core, c, t)
        self.xdev = (self.f_x, c, t)
        self.ydev = (f, 1 - c, t)

    def z(self, t):
        return (self.f, self.c, t)

    def barrier(self):
        sem = pltpu.get_barrier_semaphore()
        for dev in (self.core, self.xdev, self.ydev, *(self.z((self.t + d) % 4) for d in (1, 2, 3))):
            pl.semaphore_signal(sem, inc=1, device_id=dev, device_id_type=MESH)
        pl.semaphore_wait(sem, 6)


def forward_attention_kernel(
    lengths_ref,
    tokens_ref,
    teacher_ref,
    qkvb_ref,
    upack_ref,
    rbt_ref,
    mask_ref,
    att_ref,
    u_ref,
    t_ref,
    w_ref,
    q_ref,
    k_ref,
    v_ref,
    kt_ref,
    pt_ref,
    tok_ref,
    teach_ref,
    live_ref,
    vt,
    bias,
    rb,
    att_out,
    att_tok,
    loc_sem,
    w_sem,
    y_sem,
    z_send,
    z_recv,
    x_send,
    x_recv,
    yw_send,
    yw_recv,
    c_send,
    c_recv,
    h_send,
    h_recv,
    a_send,
    a_recv,
):
    me = Peers()
    f, c, t = me.f, me.c, me.t
    seq = t_ref.shape[0]
    half = seq // 2
    rows_f = qkvb_ref.shape[1]
    me.barrier()
    sends = []

    def go(copy, pred=None):
        if pred is None:
            copy.start()
        else:
            pl.when(pred)(copy.start)
        sends.append((copy, pred))

    own_rows = pl.ds(pl.multiple_of(c * half, half), half)
    go(remote(tokens_ref.at[1 - c], t_ref.at[own_rows], y_sem.at[0], y_sem.at[1], me.ydev))
    go(remote(rbt_ref.at[1 - c], rb.at[c], y_sem.at[2], y_sem.at[3], me.ydev))
    go(remote(mask_ref.at[1 - c, t], live_ref.at[c], y_sem.at[4], y_sem.at[5], me.ydev))
    part = pl.ds(pl.multiple_of(t * 128, 128), 128)
    go(remote(teacher_ref.at[1 - c, part], teach_ref.at[c], y_sem.at[6], y_sem.at[7], me.ydev))

    def wblock(ff):
        return w_ref.at[:, pl.ds(pl.multiple_of(ff * rows_f, rows_f), rows_f), :]

    go(remote(qkvb_ref, wblock(f), w_sem.at[0], w_sem.at[1], me.xdev))
    go(remote(qkvb_ref, wblock(f), w_sem.at[2], w_sem.at[3], me.core))

    def shard(tt, ff):
        return u_ref.at[tt, pl.ds(pl.multiple_of(ff * rows_f, rows_f), rows_f), :]

    hrows = rows_f // 2

    def slab(tt, ff, h):
        return u_ref.at[tt, pl.ds(pl.multiple_of(ff * rows_f + h * hrows, hrows), hrows), :]

    def own_half(h):
        return upack_ref.at[pl.ds(pl.multiple_of(h * hrows, hrows), hrows), :]

    hs = (c, 1 - c)
    go(remote(own_half(c), slab(t, f, c), x_send.at[t], x_recv.at[t], me.xdev))
    for i in (0, 1):
        go(remote(own_half(hs[i]), slab(t, f, hs[i]), z_send.at[0, t, i], z_recv.at[t, i], me.z(t + 1)), t < 3)
        go(remote(own_half(hs[i]), slab(t, f, hs[i]), z_send.at[1, t, i], z_recv.at[t, i], me.z(t - 1)), t > 0)
    go(remote(upack_ref, shard(t, f), c_send.at[t], c_recv.at[t], me.core))

    local = [
        pltpu.make_async_copy(tokens_ref.at[c], t_ref.at[own_rows], loc_sem.at[0]),
        pltpu.make_async_copy(qkvb_ref, wblock(f), loc_sem.at[1]),
        pltpu.make_async_copy(upack_ref, shard(t, f), loc_sem.at[2]),
        pltpu.make_async_copy(teacher_ref.at[c, part], teach_ref.at[c], loc_sem.at[3]),
    ]
    for copy in local:
        copy.start()
    rb[c] = rbt_ref[c]
    live_ref[c] = mask_ref[c, t]

    def z_step(d):
        for tt, ok, on, nxt, way in ((t - d, t - d >= 0, t < 3, t + 1, 0), (t + d, t + d <= 3, t > 0, t - 1, 1)):
            go_on = ok & on
            for i in (0, 1):
                piece = slab(tt, f, hs[i])
                arrived = remote(piece, piece, z_send.at[way, tt, i], z_recv.at[tt, i], me.z(t))
                pl.when(ok)(arrived.wait_recv)
                go(remote(piece, piece, z_send.at[way, tt, i], z_recv.at[tt, i], me.z(nxt)), go_on)
                if i == 0:
                    go(remote(piece, piece, x_send.at[tt], x_recv.at[tt], me.xdev), ok)
            go(remote(shard(tt, f), shard(tt, f), c_send.at[tt], c_recv.at[tt], me.core), ok)

    def around(d):
        return ((t, None),) if d == 0 else ((t - d, t - d >= 0), (t + d, t + d <= 3))

    def when(ok, fn):
        if ok is None:
            fn()
        else:
            pl.when(ok)(fn)

    def x_step(d):
        for tt, ok in around(d):
            piece = slab(tt, me.f_x, c)
            when(ok, remote(piece, piece, x_send.at[tt], x_recv.at[tt], me.xdev).wait_recv)
            go(remote(piece, piece, yw_send.at[tt], yw_recv.at[tt], me.ydev), ok)
            go(remote(piece, piece, h_send.at[tt, 0], h_recv.at[tt, 0], me.core), ok)

    def y_step(d):
        for tt, ok in around(d):
            piece = slab(tt, me.f_x, 1 - c)
            when(ok, remote(piece, piece, yw_send.at[tt], yw_recv.at[tt], me.ydev).wait_recv)
            go(remote(piece, piece, h_send.at[tt, 1], h_recv.at[tt, 1], me.core), ok)

    remote(wblock(me.f_x), wblock(me.f_x), w_sem.at[0], w_sem.at[1], me.xdev).wait_recv()
    go(remote(wblock(me.f_x), wblock(me.f_x), w_sem.at[4], w_sem.at[5], me.core))
    remote(wblock(me.f_core), wblock(me.f_core), w_sem.at[2], w_sem.at[3], me.core).wait_recv()
    for copy in local[:2]:
        copy.wait()
    remote(wblock(me.f_xc), wblock(me.f_xc), w_sem.at[4], w_sem.at[5], me.core).wait_recv()

    width = q_ref.shape[0] * HD
    heads = q_ref.shape[0]

    def project(base, count):
        def step(i, carry):
            rows = pl.ds(pl.multiple_of(base + i * 256, 256), 256)
            piece = t_ref[rows, :]
            for j, ref in enumerate((q_ref, k_ref, v_ref)):
                made = dot_nn(piece, w_ref[j])
                for h in range(heads):
                    ref[h, rows, :] = made[:, h * HD : (h + 1) * HD].astype(bf16)
                if j:
                    (kt_ref if j == 1 else vt)[:, rows] = made.T.astype(bf16)
            return carry

        lax.fori_loop(0, count, step, 0)

    project(c * half, half // 256)
    x_step(0)
    other_rows = pl.ds(pl.multiple_of((1 - c) * half, half), half)
    remote(t_ref.at[other_rows], t_ref.at[other_rows], y_sem.at[0], y_sem.at[1], me.ydev).wait_recv()
    project((1 - c) * half, half // 256)
    remote(rb.at[1 - c], rb.at[1 - c], y_sem.at[2], y_sem.at[3], me.ydev).wait_recv()

    length = lengths_ref[c]
    nblk = seq // BLK
    pos_block = lax.broadcasted_iota(jnp.int32, (128, seq), 1) // BLK
    row = lax.broadcasted_iota(jnp.int32, (128, seq), 0)
    picks = dot_nn(rb[0].astype(bf16), (pos_block == row).astype(bf16)) + dot_nn(
        rb[1].astype(bf16), (pos_block == row + nblk // 2).astype(bf16)
    )
    key_block = lax.broadcasted_iota(jnp.int32, (nblk, seq), 0)
    query = lax.broadcasted_iota(jnp.int32, (nblk, seq), 1)
    own = query // BLK

    def same(a, b):
        return (a == b).astype(f32)

    times = same(key_block, 0) + same(key_block, 1) + same(key_block, own - 1)
    times += same(key_block, own) + same(key_block, own + 1)
    for j in range(3):
        times += same(key_block.astype(f32), picks[j : j + 1, :])
    times = jnp.where(query < 2 * BLK, 1.0, times)
    level = jnp.where(times > 0, jnp.log2(jnp.maximum(times, 1.0)), negative)
    for b in range(nblk):
        place = b * BLK + lax.broadcasted_iota(jnp.int32, (BLK, seq), 0)
        bias[b * BLK : (b + 1) * BLK, :] = jnp.where(
            place < length, jnp.broadcast_to(level[b : b + 1, :], (BLK, seq)), negative
        )

    factor = HD ** (-0.5) * 1.4426950408889634
    wide = 256

    def attend(h):
        def step(i, carry):
            cols = pl.ds(pl.multiple_of(i * wide, wide), wide)
            scores = dot_nt(k_ref[h], q_ref[h, cols, :]) * factor + bias[:, cols]
            top = jnp.max(scores, 0, keepdims=True)
            expo = jnp.exp2(scores - top)
            probs = (expo * (1.0 / jnp.sum(expo, 0, keepdims=True))).astype(bf16)
            pt_ref[h, :, cols] = probs
            att_out[h * HD : (h + 1) * HD, cols] = dot_nn(vt[h * HD : (h + 1) * HD, :], probs)
            return carry

        lax.fori_loop(0, seq // wide, step, 0)

    attend(0)
    z_step(1)
    x_step(1)
    attend(1)
    y_step(0)
    attend(2)
    for s in range(2):
        for tt in range(4):
            at = s * half + tt * 128
            tok_at = att_out[:, at : at + 128].T.astype(bf16)
            att_tok[s, tt] = tok_at
    for d in (1, 2, 3):
        to = (t + d) % 4
        go(remote(att_tok.at[:, to], att_ref.at[t], a_send.at[d], a_recv.at[d], me.z(to)))
    own_copy = pltpu.make_async_copy(att_tok.at[:, t], att_ref.at[t], loc_sem.at[4])
    own_copy.start()
    z_step(2)
    x_step(2)
    y_step(1)
    z_step(3)
    x_step(3)
    y_step(2)
    y_step(3)
    for s in range(2):
        tok_ref[s] = t_ref[pl.ds(pl.multiple_of(s * half + t * 128, 128), 128), :]
    for d in (1, 2, 3):
        src = (t + 4 - d) % 4
        remote(att_ref.at[src], att_ref.at[src], a_send.at[d], a_recv.at[d], me.z(src)).wait_recv()
    for tt in range(4):
        whole = shard(tt, me.f_core)
        remote(whole, whole, c_send.at[tt], c_recv.at[tt], me.core).wait_recv()
        for i in (0, 1):
            piece = slab(tt, me.f_xc, hs[i])
            remote(piece, piece, h_send.at[tt, i], h_recv.at[tt, i], me.core).wait_recv()
    there = live_ref.at[1 - c]
    remote(there, there, y_sem.at[4], y_sem.at[5], me.ydev).wait_recv()
    there = teach_ref.at[1 - c]
    remote(there, there, y_sem.at[6], y_sem.at[7], me.ydev).wait_recv()
    for copy in local[2:]:
        copy.wait()
    own_copy.wait()
    for copy, pred in sends:
        when(pred, copy.wait_send)


def forward_attention(lengths, tokens, teacher, qkvb, upack, rbt, mask, seq):
    heads = qkvb.shape[2] // HD
    width = heads * HD
    rows_f = qkvb.shape[1]
    depth = rows_f * 4
    vm = pl.BlockSpec(memory_space=pltpu.VMEM)
    hbm = pl.BlockSpec(memory_space=pl.ANY)
    dma = pltpu.SemaphoreType.DMA
    outs = [
        ((4, 2, 128, width), bf16, vm),
        ((4, depth, UW), bf16, hbm),
        ((seq, depth), bf16, vm),
        ((3, depth, width), bf16, vm),
        ((heads, seq, HD), bf16, vm),
        ((heads, seq, HD), bf16, vm),
        ((heads, seq, HD), bf16, vm),
        ((width, seq), bf16, vm),
        ((heads, seq, seq), bf16, vm),
        ((2, 128, depth), bf16, vm),
        ((2, 128, depth), bf16, vm),
        ((2, 8, 128), f32, vm),
    ]
    return pl.pallas_call(
        forward_attention_kernel,
        name="forward_attention",
        out_shape=[jax.ShapeDtypeStruct(s, d) for s, d, _ in outs],
        in_specs=[pl.BlockSpec(memory_space=pltpu.SMEM), hbm, hbm, vm, vm, vm, vm],
        out_specs=[m for _, _, m in outs],
        scratch_shapes=[
            pltpu.VMEM((width, seq), bf16),
            pltpu.VMEM((seq, seq), f32),
            pltpu.VMEM((2, 8, 128), f32),
            pltpu.VMEM((width, seq), f32),
            pltpu.VMEM((2, 4, 128, width), bf16),
            dma((5,)),
            dma((6,)),
            dma((8,)),
            dma((2, 4, 2)),
            dma((4, 2)),
            dma((4,)),
            dma((4,)),
            dma((4,)),
            dma((4,)),
            dma((4,)),
            dma((4,)),
            dma((4, 2)),
            dma((4, 2)),
            dma((4,)),
            dma((4,)),
        ],
        compiler_params=pltpu.CompilerParams(
            collective_id=0, has_side_effects=True, vmem_limit_bytes=VMEM_LIMIT
        ),
    )(lengths, tokens, teacher, qkvb, upack, rbt, mask)


def column(row):
    return row.T[:, 0:1]


def layer_kernel(
    lengths_ref,
    count_ref,
    att_ref,
    u_ref,
    tok_ref,
    teach_ref,
    live_ref,
    out_ref,
    err_ref,
    g_ref,
    gatt_ref,
    gone_ref,
    act,
    slope,
):
    c, t = lax.axis_index("ctx"), lax.axis_index("tp")
    depth = tok_ref.shape[2]
    rows = 2 * 128
    length = lengths_ref[c]
    inv_width = 1.0 / depth
    norms = u_ref[0, :, 1728:1736].astype(f32).T
    gains = [norms[i : i + 1, :] for i in range(4)]

    def both(ref):
        return ref[...].reshape(rows, depth).astype(f32)

    def mean(v):
        return jnp.sum(v, -1, keepdims=True) * inv_width

    def normalize(v):
        center = v - mean(v)
        inverse = lax.rsqrt(mean(center * center) + norm_eps)
        return center * inverse, inverse

    def back(up, normed, inverse, gain):
        scaled = up * gain
        return inverse * (scaled - mean(scaled) - normed * mean(scaled * normed))

    att = [att_ref[tt].reshape(rows, att_ref.shape[3]) for tt in range(4)]
    attn = dot_nt(att[0], u_ref[0, :, 1536:1728])
    for tt in range(1, 4):
        attn += dot_nt(att[tt], u_ref[tt, :, 1536:1728])
    normed_one, inverse_one = normalize(both(tok_ref) + attn)
    hidden = normed_one * gains[0] + gains[1]
    hidden_b = hidden.astype(bf16)
    cube = 0.044715
    root = 0.7978845608028654

    def up_step(tt, mixed):
        upper = dot_nn(hidden_b, u_ref[tt, :, 0:768])
        square = upper * upper
        th = jnp.tanh(root * upper * (1.0 + cube * square))
        act_t = (0.5 * upper * (1.0 + th)).astype(bf16)
        act[tt] = act_t
        slope[tt] = 0.5 * (1.0 + th) + 0.5 * upper * (1.0 - th * th) * root * (1.0 + 3.0 * cube * square)
        return mixed + dot_nt(act_t, u_ref[tt, :, 768:1536])

    mixed = lax.fori_loop(0, 4, up_step, jnp.zeros((rows, depth), f32))
    normed_two, inverse_two = normalize(hidden + mixed)
    result = normed_two * gains[2] + gains[3]
    out_ref[...] = result.astype(bf16).reshape(2, 128, depth)
    alive = jnp.concatenate([column(live_ref[0]), column(live_ref[1])], 0)
    row = lax.broadcasted_iota(jnp.int32, (rows, 1), 0)
    place = jnp.where(row < 128, row, row - 128 + 512) + t * 128
    live = jnp.where((alive == 1.0) & (place < length), 1.0, 0.0)
    differ = result - both(teach_ref)
    weighed = differ * live
    err_ref[0, 0] = jnp.sum(weighed * differ)
    grad_y = weighed * (2.0 / (count_ref[0, 0] * depth))
    sums = [None] * 4
    sums[2] = jnp.sum(grad_y * normed_two, 0, keepdims=True)
    sums[3] = jnp.sum(grad_y, 0, keepdims=True)
    grad_two = back(grad_y, normed_two, inverse_two, gains[2])
    gm = grad_two.astype(bf16)
    gm_t = grad_two.T.astype(bf16)
    hidden_t = hidden.T.astype(bf16)

    def down_step(tt, total):
        ga = dot_nn(gm, u_ref[tt, :, 768:1536])
        gu = (ga * slope[tt]).astype(bf16)
        g_ref[tt, :, 768:1536] = dot_nn(gm_t, act[tt]).astype(bf16)
        g_ref[tt, :, 0:768] = dot_nn(hidden_t, gu).astype(bf16)
        return total + dot_nt(gu, u_ref[tt, :, 0:768])

    grad_hidden = lax.fori_loop(0, 4, down_step, grad_two)
    sums[0] = jnp.sum(grad_hidden * normed_one, 0, keepdims=True)
    sums[1] = jnp.sum(grad_hidden, 0, keepdims=True)
    grad_one = back(grad_hidden, normed_one, inverse_one, gains[0])
    gone_ref[...] = grad_one.reshape(2, 128, depth)
    ga = grad_one.astype(bf16)
    ga_t = grad_one.T.astype(bf16)
    norm_rows = jnp.concatenate(sums + [jnp.zeros((4, depth), f32)], 0)
    norm_cols = jnp.concatenate([norm_rows.T, jnp.zeros((depth, UW - 1736), f32)], 1).astype(bf16)
    for tt in range(4):
        back_t = dot_nn(ga, u_ref[tt, :, 1536:1728]).astype(bf16)
        gatt_ref[tt] = back_t.reshape(2, 128, back_t.shape[1])
        g_ref[tt, :, 1536:1728] = dot_nn(ga_t, att[tt]).astype(bf16)
        g_ref[tt, :, 1728:1792] = norm_cols


def layer(lengths, count, att, u, tok, teach, live):
    depth = tok.shape[2]
    vm = pl.BlockSpec(memory_space=pltpu.VMEM)
    smem = pl.BlockSpec(memory_space=pltpu.SMEM)
    return pl.pallas_call(
        layer_kernel,
        name="layer",
        out_shape=[
            jax.ShapeDtypeStruct((2, 128, depth), bf16),
            jax.ShapeDtypeStruct((1, 1), f32),
            jax.ShapeDtypeStruct((4, depth, UW), bf16),
            jax.ShapeDtypeStruct(att.shape, bf16),
            jax.ShapeDtypeStruct((2, 128, depth), f32),
        ],
        in_specs=[smem, smem, vm, vm, vm, vm, vm],
        out_specs=[vm, smem, vm, vm, vm],
        scratch_shapes=[
            pltpu.VMEM((4, 256, 768), bf16),
            pltpu.VMEM((4, 256, 768), f32),
        ],
        compiler_params=pltpu.CompilerParams(vmem_limit_bytes=VMEM_LIMIT),
    )(lengths, count, att, u, tok, teach, live)


def attention_back_kernel(
    do_ref, q_ref, k_ref, v_ref, kt_ref, pt_ref, t_ref, w_ref, part_ref, grad_ref, do, dqt, dk, dv, proj
):
    heads, seq = q_ref.shape[0], q_ref.shape[1]
    width = heads * HD
    scale = HD ** (-0.5)
    wide = 256
    for h in range(heads):
        do[h] = do_ref[:, h * HD : (h + 1) * HD]
    for h in range(heads):
        dk[...] = jnp.zeros_like(dk)
        dv[...] = jnp.zeros_like(dv)

        def step(i, carry):
            cols = pl.ds(pl.multiple_of(i * wide, wide), wide)
            mine = do[h, cols, :]
            probs = pt_ref[h, :, cols]
            gp = dot_nt(v_ref[h], mine)
            pf = probs.astype(f32)
            mix = jnp.sum(pf * gp, 0, keepdims=True)
            gs = (pf * (gp - mix)).astype(bf16)
            dk[...] += dot_nn(gs, q_ref[h, cols, :])
            dv[...] += dot_nn(probs, mine)
            dqt[h * HD : (h + 1) * HD, cols] = dot_nn(kt_ref[h * HD : (h + 1) * HD, :], gs)
            return carry

        lax.fori_loop(0, seq // wide, step, 0)
        proj[1, :, h * HD : (h + 1) * HD] = (dk[...] * scale).astype(bf16)
        proj[2, :, h * HD : (h + 1) * HD] = dv[...].astype(bf16)
    proj[0] = (dqt[...].T * scale).astype(bf16)

    def rows_step(i, carry):
        rows = pl.ds(pl.multiple_of(i * 256, 256), 256)
        total = dot_nt(proj[0, rows, :], w_ref[0])
        for j in (1, 2):
            total += dot_nt(proj[j, rows, :], w_ref[j])
        part_ref[rows, :] = total.astype(bf16)
        return carry

    lax.fori_loop(0, seq // 256, rows_step, 0)
    for j in range(3):
        grad_ref[j] = dot_tn(t_ref[...], proj[j]).astype(bf16)


def attention_back(do, q, k, v, kt, pt, tokens, w):
    heads, seq = q.shape[:2]
    width = heads * HD
    vm = pl.BlockSpec(memory_space=pltpu.VMEM)
    return pl.pallas_call(
        attention_back_kernel,
        name="attention_back",
        out_shape=[
            jax.ShapeDtypeStruct(tokens.shape, bf16),
            jax.ShapeDtypeStruct(w.shape, bf16),
        ],
        in_specs=[vm] * 8,
        out_specs=[vm] * 2,
        scratch_shapes=[
            pltpu.VMEM((heads, seq, HD), bf16),
            pltpu.VMEM((width, seq), f32),
            pltpu.VMEM((seq, HD), f32),
            pltpu.VMEM((seq, HD), f32),
            pltpu.VMEM((3, seq, width), bf16),
        ],
        compiler_params=pltpu.CompilerParams(vmem_limit_bytes=VMEM_LIMIT),
    )(do, q, k, v, kt, pt, tokens, w)


def body_swapped(
    tokens,
    teacher,
    lengths,
    valid_mask,
    random_blocks,
    step_count,
    qkv_weight,
    out_weight,
    up_weight,
    down_weight,
    norm_params,
    qkv_moment,
    qkv_square,
    out_moment,
    out_square,
    up_moment,
    up_square,
    down_moment,
    down_square,
    norm_moment,
    norm_square,
):
    c, t = lax.axis_index("ctx"), lax.axis_index("tp")
    seqs, tok_count, width = tokens.shape
    seq = tok_count * 2
    upack = jnp.concatenate(
        [
            up_weight,
            down_weight.T,
            out_weight.T,
            norm_params.T,
            jnp.zeros((192, 60), f32),
        ],
        1,
    ).astype(bf16)
    qkvb = qkv_weight.astype(bf16)
    rbt = jnp.pad(
        jnp.swapaxes(random_blocks, 1, 2).astype(f32), ((0, 0), (0, 5), (0, 120))
    )
    mask = jnp.broadcast_to(valid_mask.reshape(seqs, 4, 1, 128).astype(f32), (seqs, 4, 8, 128))
    positions = c * tok_count + jnp.arange(tok_count, dtype=jnp.int32)
    live_rows = ((valid_mask == 1) & (positions[None, :] < lengths[:, None])).astype(f32)
    live_count = lax.psum(jnp.sum(live_rows), ("fsdp", "ctx"))
    att, u, tk, w, q, k, v, kt, pt, tok, teach, live = forward_attention(
        lengths, tokens, teacher, qkvb, upack, rbt, mask, seq
    )
    out_part, err, g, gatt, gone = layer(lengths, live_count.reshape(1, 1), att, u, tok, teach, live)
    do = lax.all_to_all(gatt, "tp", 0, 0)
    do = jnp.swapaxes(do, 0, 1).reshape(seq, att.shape[3])
    part, qkv_part = attention_back(do, q, k, v, kt, pt, tk, w)
    error_total = lax.psum(err[0, 0], ("fsdp", "ctx", "tp"))
    loss_value = error_total / (live_count * width)

    def spread(piece):
        swapped = lax.all_to_all(piece, "ctx", 0, 0)
        return lax.all_gather(swapped, "tp", axis=1, tiled=True)

    layer_out = spread(out_part)
    summed = lax.psum_scatter(part.reshape(2, 4, 128, width), "tp", scatter_dimension=1, tiled=False)
    input_grad = spread((summed.astype(f32) + gone).astype(bf16)).astype(f32)
    g = lax.psum_scatter(g, "tp", scatter_dimension=0, tiled=False)
    g = lax.psum_scatter(g, "fsdp", scatter_dimension=0, tiled=True)
    g = lax.psum(g, "ctx").astype(f32)
    qkv_grad = lax.psum_scatter(qkv_part, "fsdp", scatter_dimension=1, tiled=True)
    qkv_grad = lax.psum(qkv_grad, "ctx").astype(f32)
    up_grad, down_grad, out_grad, norm_grad = g[:, :768], g[:, 768:1536].T, g[:, 1536:1728].T, g[:, 1728:1732].T
    shards = (qkv_grad, out_grad, up_grad, down_grad, norm_grad)
    squares = sum(jnp.sum(m * m) for m in shards[:4]) + jnp.where(t == 0, jnp.sum(norm_grad * norm_grad), 0.0)
    grad_norm = jnp.sqrt(lax.psum(squares, ("fsdp", "tp")))
    factor = jnp.minimum(1.0, clip_level / (grad_norm + 1e-06))
    steps_done = step_count[0].astype(f32)
    state = (
        (qkv_weight, qkv_moment, qkv_square),
        (out_weight, out_moment, out_square),
        (up_weight, up_moment, up_square),
        (down_weight, down_moment, down_square),
        (norm_params, norm_moment, norm_square),
    )
    new = [
        adam_update(weight, grad, moment, square, factor, steps_done, rate)
        for (weight, moment, square), grad, rate in zip(state, shards, rate_list)
    ]
    return (layer_out, loss_value, input_grad, grad_norm, *(v for group in new for v in group))


def solution(mesh):
    in_specs = (
        P("fsdp", "ctx", None),
        P("fsdp", "ctx", None),
        P("fsdp"),
        P("fsdp", "ctx"),
        P("fsdp", "ctx", None),
        P(),
        P(None, "fsdp", "tp"),
        P("tp", "fsdp"),
        P("fsdp", "tp"),
        P("tp", "fsdp"),
        P(None, "fsdp"),
        P(None, "fsdp", "tp"),
        P(None, "fsdp", "tp"),
        P("tp", "fsdp"),
        P("tp", "fsdp"),
        P("fsdp", "tp"),
        P("fsdp", "tp"),
        P("tp", "fsdp"),
        P("tp", "fsdp"),
        P(None, "fsdp"),
        P(None, "fsdp"),
    )
    out_specs = (
        P("fsdp", "ctx", None),
        P(),
        P("fsdp", "ctx", None),
        P(),
        P(None, "fsdp", "tp"),
        P(None, "fsdp", "tp"),
        P(None, "fsdp", "tp"),
        P("tp", "fsdp"),
        P("tp", "fsdp"),
        P("tp", "fsdp"),
        P("fsdp", "tp"),
        P("fsdp", "tp"),
        P("fsdp", "tp"),
        P("tp", "fsdp"),
        P("tp", "fsdp"),
        P("tp", "fsdp"),
        P(None, "fsdp"),
        P(None, "fsdp"),
        P(None, "fsdp"),
    )
    sizes = dict(mesh.shape)
    small = sizes == {"fsdp": 4, "ctx": 2, "tp": 4}
    body = body_swapped if small else body_general
    return jax.shard_map(body, mesh=mesh, in_specs=in_specs, out_specs=out_specs, check_vma=False)
```

```python
import functools
from functools import partial

import jax
import jax.numpy as jnp
from jax import lax
from jax.experimental import pallas as pl
from jax.experimental.pallas import tpu as pltpu
from jax.sharding import PartitionSpec as P

HD = 64
BLK = 64
MESH = pl.DeviceIdType.MESH
f32 = jnp.float32
bf16 = jnp.bfloat16

norm_eps = 1e-06
beta_one = 0.9
beta_two = 0.999
adam_eps = 1e-08
decay_rate = 0.01
clip_level = 0.001
rate_list = (0.04, 0.4, 0.04, 0.02, 0.2)
negative = -1e30
VMEM_LIMIT = 58 * 2**20


def layer_norm(values, gain, shift):
    center = values - jnp.mean(values, -1, keepdims=True)
    inverse = lax.rsqrt(jnp.mean(center * center, -1, keepdims=True) + norm_eps)
    normed = center * inverse
    return (normed * gain + shift, normed, inverse)


def norm_backward(upstream, normed, inverse, gain):
    scaled = upstream * gain
    return inverse * (
        scaled
        - jnp.mean(scaled, -1, keepdims=True)
        - normed * jnp.mean(scaled * normed, -1, keepdims=True)
    )


def adam_update(weight, gradient, moment, square, factor, steps_done, rate):
    clipped = gradient * factor
    new_moment = beta_one * moment + (1.0 - beta_one) * clipped
    new_square = beta_two * square + (1.0 - beta_two) * clipped * clipped
    corrected = new_moment / (1.0 - beta_one**steps_done)
    scaled = new_square / (1.0 - beta_two**steps_done)
    new_weight = weight - rate * (corrected / (jnp.sqrt(scaled) + adam_eps) + decay_rate * weight)
    return (new_weight, new_moment, new_square)


def body_general(
    tokens,
    teacher,
    lengths,
    valid_mask,
    random_blocks,
    step_count,
    qkv_weight,
    out_weight,
    up_weight,
    down_weight,
    norm_params,
    qkv_moment,
    qkv_square,
    out_moment,
    out_square,
    up_moment,
    up_square,
    down_moment,
    down_square,
    norm_moment,
    norm_square,
):
    ctx_index = lax.axis_index("ctx")
    ctx_count = lax.axis_size("ctx")
    tp_index = lax.axis_index("tp")
    seqs_here, tok_count, width = tokens.shape
    local_blocks = tok_count // BLK
    block_count = local_blocks * ctx_count
    seq_len = tok_count * ctx_count
    width_local = qkv_weight.shape[2]
    heads_local = width_local // HD
    scale = HD ** (-0.5)
    full_qkv, full_out, full_up, full_down, full_norms = (
        lax.all_gather(qkv_weight.astype(bf16), "fsdp", axis=1, tiled=True),
        lax.all_gather(out_weight.astype(bf16), "fsdp", axis=1, tiled=True),
        lax.all_gather(up_weight.astype(bf16), "fsdp", axis=0, tiled=True),
        lax.all_gather(down_weight.astype(bf16), "fsdp", axis=1, tiled=True),
        lax.all_gather(norm_params.astype(bf16), "fsdp", axis=1, tiled=True),
    )
    gains = full_norms.astype(f32)
    projected = jnp.einsum("std,cde->stce", tokens, full_qkv, preferred_element_type=f32).astype(
        bf16
    )
    queries = projected[:, :, 0, :]
    kv_local = projected[:, :, 1:, :]
    gathered = lax.all_gather(kv_local, "ctx", axis=1, tiled=True)
    own_blocks = ctx_index * local_blocks + jnp.arange(local_blocks, dtype=jnp.int32)
    zero_row = own_blocks * 0
    window = jnp.stack([zero_row, zero_row + 1, own_blocks - 1, own_blocks, own_blocks + 1], -1)
    listed = jnp.concatenate(
        [jnp.broadcast_to(window[None], (seqs_here, local_blocks, 5)), random_blocks], -1
    )
    inside = (listed >= 0) & (listed < block_count)
    safe = jnp.clip(listed, 0, block_count - 1)
    key_pos = safe[..., None] * BLK + jnp.arange(BLK, dtype=jnp.int32)
    counted = (inside[..., None] & (key_pos < lengths[:, None, None, None])).reshape(
        seqs_here, local_blocks, 8 * BLK
    )
    key_live = jnp.arange(seq_len, dtype=jnp.int32)[None, :] < lengths[:, None]
    q_blocks = queries.reshape(seqs_here, local_blocks, BLK, heads_local, HD)
    head_rows = queries[:, : 2 * BLK].reshape(seqs_here, 2 * BLK, heads_local, HD)
    blocked = gathered.reshape(seqs_here, block_count, BLK, 2, width_local)
    flat = blocked.reshape(seqs_here * block_count, BLK, 2, width_local)
    offset = jnp.arange(seqs_here, dtype=jnp.int32)[:, None, None] * block_count
    picked = lax.map(
        lambda at: lax.dynamic_index_in_dim(flat, at, 0, keepdims=False), (safe + offset).reshape(-1)
    ).reshape(seqs_here, local_blocks, 8, BLK, 2, width_local)
    key_rows = picked[..., 0, :].reshape(seqs_here, local_blocks, 8 * BLK, heads_local, HD)
    value_rows = picked[..., 1, :].reshape(seqs_here, local_blocks, 8 * BLK, heads_local, HD)
    scores = (
        jnp.einsum("sbqhd,sbkhd->sbhqk", q_blocks, key_rows, preferred_element_type=f32) * scale
    )
    scores = jnp.where(counted[:, :, None, None, :], scores, negative)
    all_keys = gathered[:, :, 0, :].reshape(seqs_here, seq_len, heads_local, HD)
    all_values = gathered[:, :, 1, :].reshape(seqs_here, seq_len, heads_local, HD)
    wide_scores = (
        jnp.einsum("sqhd,skhd->shqk", head_rows, all_keys, preferred_element_type=f32) * scale
    )
    wide_scores = jnp.where(key_live[:, None, None, :], wide_scores, negative)
    top_value = jnp.max(scores, -1, keepdims=True)
    expo = jnp.exp(scores - top_value)
    summed = jnp.sum(expo, -1, keepdims=True)
    sparse_lse = top_value + jnp.log(summed)
    probs_b = (expo / summed).astype(bf16)
    sparse_out = jnp.einsum(
        "sbhqk,sbkhd->sbqhd", probs_b, value_rows, preferred_element_type=f32
    ).reshape(seqs_here, tok_count, width_local)
    wide_top = jnp.max(wide_scores, -1, keepdims=True)
    wide_expo = jnp.exp(wide_scores - wide_top)
    wide_sum = jnp.sum(wide_expo, -1, keepdims=True)
    wide_lse = wide_top + jnp.log(wide_sum)
    wide_probs = (wide_expo / wide_sum).astype(bf16)
    wide_out = jnp.einsum(
        "shqk,skhd->sqhd", wide_probs, all_values, preferred_element_type=f32
    ).reshape(seqs_here, 2 * BLK, width_local)
    is_first = ctx_index == 0
    row_ids = jnp.arange(tok_count, dtype=jnp.int32)
    global_row = (row_ids < 2 * BLK) & is_first
    rest_zeros = jnp.zeros((seqs_here, tok_count - 2 * BLK, width_local), f32)
    padded_wide = jnp.concatenate([wide_out, rest_zeros], 1)
    attended = jnp.where(global_row[None, :, None], padded_wide, sparse_out).astype(bf16)
    attn_part = jnp.einsum("ste,ed->std", attended, full_out, preferred_element_type=f32)
    positions = ctx_index * tok_count + row_ids
    live_rows = ((valid_mask == 1) & (positions[None, :] < lengths[:, None])).astype(f32)
    count_local = jnp.sum(live_rows)
    gelu_fn = partial(jax.nn.gelu, approximate=True)
    attn = lax.psum(attn_part.astype(jnp.bfloat16), "tp").astype(jnp.float32)
    hidden, normed_one, inverse_one = layer_norm(tokens.astype(f32) + attn, gains[0], gains[1])
    hidden_b = hidden.astype(bf16)
    upper = jnp.einsum("std,df->stf", hidden_b, full_up, preferred_element_type=f32)
    active_f, gelu_back = jax.vjp(gelu_fn, upper)
    active = active_f.astype(bf16)
    mixed = lax.psum(
        jnp.einsum("stf,fd->std", active, full_down, preferred_element_type=f32).astype(
            jnp.bfloat16
        ),
        "tp",
    ).astype(jnp.float32)
    result, normed_two, inverse_two = layer_norm(hidden + mixed, gains[2], gains[3])
    differ = result - teacher.astype(f32)
    error_local = jnp.sum(live_rows[..., None] * differ * differ)
    error_total, live_count = lax.psum((error_local, count_local), ("fsdp", "ctx"))
    loss_value = error_total / (live_count * width)
    grad_y = 2.0 * differ * live_rows[..., None] / (live_count * width)
    gain_two_grad = jnp.sum(grad_y * normed_two, (0, 1))
    bias_two_grad = jnp.sum(grad_y, (0, 1))
    grad_two = norm_backward(grad_y, normed_two, inverse_two, gains[2])
    grad_mixed = grad_two.astype(bf16)
    grad_active = jnp.einsum("std,fd->stf", grad_mixed, full_down, preferred_element_type=f32)
    grad_upper = gelu_back(grad_active)[0].astype(bf16)
    down_grad = jnp.einsum("stf,std->fd", active, grad_mixed, preferred_element_type=f32)
    up_grad = jnp.einsum("std,stf->df", hidden_b, grad_upper, preferred_element_type=f32)
    grad_hidden = grad_two + lax.psum(
        jnp.einsum("stf,df->std", grad_upper, full_up, preferred_element_type=f32).astype(
            jnp.bfloat16
        ),
        "tp",
    ).astype(jnp.float32)
    gain_one_grad = jnp.sum(grad_hidden * normed_one, (0, 1))
    bias_one_grad = jnp.sum(grad_hidden, (0, 1))
    grad_one = norm_backward(grad_hidden, normed_one, inverse_one, gains[0])
    norm_grad = jnp.stack([gain_one_grad, bias_one_grad, gain_two_grad, bias_two_grad], 0)
    grad_attn = grad_one.astype(bf16)
    out_grad = jnp.einsum("ste,std->ed", attended, grad_attn, preferred_element_type=f32)
    grad_attended = jnp.einsum(
        "std,ed->ste", grad_attn, full_out, preferred_element_type=f32
    ).astype(bf16)
    sparse_grad = jnp.where(global_row[None, :, None], jnp.zeros_like(grad_attended), grad_attended)
    sparse_grad = sparse_grad.reshape(seqs_here, local_blocks, BLK, heads_local, HD)
    probs = jnp.exp(scores - sparse_lse)
    grad_probs = jnp.einsum(
        "sbqhd,sbkhd->sbhqk", sparse_grad, value_rows, preferred_element_type=f32
    )
    row_dot = jnp.sum(probs * grad_probs, -1, keepdims=True)
    grad_scores = (probs * (grad_probs - row_dot)).astype(bf16)
    dq_sparse = (
        jnp.einsum("sbhqk,sbkhd->sbqhd", grad_scores, key_rows, preferred_element_type=f32) * scale
    )
    dk_rows = (
        jnp.einsum("sbhqk,sbqhd->sbkhd", grad_scores, q_blocks, preferred_element_type=f32) * scale
    )
    dv_rows = jnp.einsum(
        "sbhqk,sbqhd->sbkhd", probs.astype(bf16), sparse_grad, preferred_element_type=f32
    )
    list_grads = jnp.stack(
        [
            dk_rows.reshape(seqs_here, local_blocks, 8, BLK, width_local),
            dv_rows.reshape(seqs_here, local_blocks, 8, BLK, width_local),
        ],
        4,
    )
    seq_ids = jnp.broadcast_to(jnp.arange(seqs_here, dtype=jnp.int32)[:, None, None], safe.shape)
    kv_term = (
        jnp.zeros((block_count, seqs_here, BLK, 2, width_local), f32)
        .at[safe, seq_ids]
        .add(list_grads)
    )
    head_grad = jnp.where(
        is_first, grad_attended[:, : 2 * BLK], jnp.zeros_like(grad_attended[:, : 2 * BLK])
    )
    head_grad = head_grad.reshape(seqs_here, 2 * BLK, heads_local, HD)
    wide_probs_f = jnp.exp(wide_scores - wide_lse)
    wide_dprobs = jnp.einsum("sqhd,skhd->shqk", head_grad, all_values, preferred_element_type=f32)
    wide_dot = jnp.sum(wide_probs_f * wide_dprobs, -1, keepdims=True)
    wide_dscores = (wide_probs_f * (wide_dprobs - wide_dot)).astype(bf16)
    dq_wide = (
        jnp.einsum("shqk,skhd->sqhd", wide_dscores, all_keys, preferred_element_type=f32) * scale
    )
    split_scores = wide_dscores.reshape(seqs_here, heads_local, 2 * BLK, block_count, BLK)
    split_probs = wide_probs_f.astype(bf16).reshape(
        seqs_here, heads_local, 2 * BLK, block_count, BLK
    )
    dk_wide = (
        jnp.einsum("shqnb,sqhd->nsbhd", split_scores, head_rows, preferred_element_type=f32) * scale
    )
    dv_wide = jnp.einsum("shqnb,sqhd->nsbhd", split_probs, head_grad, preferred_element_type=f32)
    kv_term = kv_term + jnp.stack(
        [
            dk_wide.reshape(block_count, seqs_here, BLK, width_local),
            dv_wide.reshape(block_count, seqs_here, BLK, width_local),
        ],
        3,
    )
    kv_grads = lax.psum_scatter(
        kv_term.astype(jnp.bfloat16), "ctx", scatter_dimension=0, tiled=True
    ).astype(jnp.float32)
    kv_grads = jnp.transpose(kv_grads, (1, 0, 2, 3, 4)).reshape(
        seqs_here, tok_count, 2, width_local
    )
    dq_total = dq_sparse.reshape(seqs_here, tok_count, width_local) + jnp.concatenate(
        [dq_wide.reshape(seqs_here, 2 * BLK, width_local), rest_zeros], 1
    )
    grad_projected = jnp.concatenate([dq_total[:, :, None, :], kv_grads], 2).astype(bf16)
    qkv_grad = jnp.einsum("std,stce->cde", tokens, grad_projected, preferred_element_type=f32)
    input_part = jnp.einsum("stce,cde->std", grad_projected, full_qkv, preferred_element_type=f32)
    input_grad = grad_one + lax.psum(input_part.astype(jnp.bfloat16), "tp").astype(jnp.float32)
    local_grads = (qkv_grad, out_grad, up_grad, down_grad, norm_grad)
    owned = (
        lax.psum_scatter(
            local_grads[0].astype(jnp.bfloat16), "fsdp", scatter_dimension=1, tiled=True
        ).astype(jnp.float32),
        lax.psum_scatter(
            local_grads[1].astype(jnp.bfloat16), "fsdp", scatter_dimension=1, tiled=True
        ).astype(jnp.float32),
        lax.psum_scatter(
            local_grads[2].astype(jnp.bfloat16), "fsdp", scatter_dimension=0, tiled=True
        ).astype(jnp.float32),
        lax.psum_scatter(
            local_grads[3].astype(jnp.bfloat16), "fsdp", scatter_dimension=1, tiled=True
        ).astype(jnp.float32),
        lax.psum_scatter(
            local_grads[4].astype(jnp.bfloat16), "fsdp", scatter_dimension=1, tiled=True
        ).astype(jnp.float32),
    )
    shards = (
        lax.psum(owned[0].astype(jnp.bfloat16), "ctx").astype(jnp.float32),
        lax.psum(owned[1].astype(jnp.bfloat16), "ctx").astype(jnp.float32),
        lax.psum(owned[2].astype(jnp.bfloat16), "ctx").astype(jnp.float32),
        lax.psum(owned[3].astype(jnp.bfloat16), "ctx").astype(jnp.float32),
        lax.psum(owned[4].astype(jnp.bfloat16), "ctx").astype(jnp.float32),
    )
    matrix_squares = sum((jnp.sum(member * member) for member in shards[:4]))
    norm_squares = jnp.where(tp_index == 0, jnp.sum(shards[4] * shards[4]), 0.0)
    squares_total = lax.psum(matrix_squares + norm_squares, ("fsdp", "tp"))
    grad_norm = jnp.sqrt(squares_total)
    factor = jnp.minimum(1.0, clip_level / (grad_norm + 1e-06))
    steps_done = step_count[0].astype(f32)
    qkv_new = adam_update(
        qkv_weight, shards[0], qkv_moment, qkv_square, factor, steps_done, rate_list[0]
    )
    out_new = adam_update(
        out_weight, shards[1], out_moment, out_square, factor, steps_done, rate_list[1]
    )
    up_new = adam_update(
        up_weight, shards[2], up_moment, up_square, factor, steps_done, rate_list[2]
    )
    down_new = adam_update(
        down_weight, shards[3], down_moment, down_square, factor, steps_done, rate_list[3]
    )
    norm_new = adam_update(
        norm_params, shards[4], norm_moment, norm_square, factor, steps_done, rate_list[4]
    )
    return (
        result.astype(bf16),
        loss_value,
        input_grad,
        grad_norm,
        qkv_new[0],
        qkv_new[1],
        qkv_new[2],
        out_new[0],
        out_new[1],
        out_new[2],
        up_new[0],
        up_new[1],
        up_new[2],
        down_new[0],
        down_new[1],
        down_new[2],
        norm_new[0],
        norm_new[1],
        norm_new[2],
    )


def remote(src, dst, send, recv, dev):
    return pltpu.make_async_remote_copy(
        src_ref=src, dst_ref=dst, send_sem=send, recv_sem=recv, device_id=dev, device_id_type=MESH
    )


def dot_nn(a, b):
    return lax.dot_general(a, b, (((1,), (0,)), ((), ())), preferred_element_type=f32)


def dot_nt(a, b):
    return lax.dot_general(a, b, (((1,), (1,)), ((), ())), preferred_element_type=f32)


def dot_tn(a, b):
    return lax.dot_general(a, b, (((0,), (0,)), ((), ())), preferred_element_type=f32)


UW = 1792


class Peers:
    def __init__(self):
        f, c, t = lax.axis_index("fsdp"), lax.axis_index("ctx"), lax.axis_index("tp")
        x, k = f // 2, f % 2
        self.f, self.c, self.t = f, c, t
        self.f_core = x * 2 + (1 - k)
        self.f_x = (1 - x) * 2 + k
        self.f_xc = (1 - x) * 2 + (1 - k)
        self.core = (self.f_core, c, t)
        self.xdev = (self.f_x, c, t)
        self.ydev = (f, 1 - c, t)

    def z(self, t):
        return (self.f, self.c, t)

    def barrier(self):
        sem = pltpu.get_barrier_semaphore()
        for dev in (self.core, self.xdev, self.ydev, *(self.z((self.t + d) % 4) for d in (1, 2, 3))):
            pl.semaphore_signal(sem, inc=1, device_id=dev, device_id_type=MESH)
        pl.semaphore_wait(sem, 6)


def forward_attention_kernel(
    lengths_ref,
    tokens_ref,
    teacher_ref,
    qkvb_ref,
    upack_ref,
    rbt_ref,
    mask_ref,
    att_ref,
    u_ref,
    t_ref,
    w_ref,
    q_ref,
    k_ref,
    v_ref,
    kt_ref,
    pt_ref,
    tok_ref,
    teach_ref,
    live_ref,
    vt,
    bias,
    rb,
    att_out,
    att_tok,
    loc_sem,
    w_sem,
    y_sem,
    z_send,
    z_recv,
    x_send,
    x_recv,
    yw_send,
    yw_recv,
    c_send,
    c_recv,
    h_send,
    h_recv,
    a_send,
    a_recv,
):
    me = Peers()
    f, c, t = me.f, me.c, me.t
    seq = t_ref.shape[0]
    half = seq // 2
    rows_f = qkvb_ref.shape[1]
    me.barrier()
    sends = []

    def go(copy, pred=None):
        if pred is None:
            copy.start()
        else:
            pl.when(pred)(copy.start)
        sends.append((copy, pred))

    own_rows = pl.ds(pl.multiple_of(c * half, half), half)
    go(remote(tokens_ref.at[1 - c], t_ref.at[own_rows], y_sem.at[0], y_sem.at[1], me.ydev))
    go(remote(rbt_ref.at[1 - c], rb.at[c], y_sem.at[2], y_sem.at[3], me.ydev))
    go(remote(mask_ref.at[1 - c, t], live_ref.at[c], y_sem.at[4], y_sem.at[5], me.ydev))
    part = pl.ds(pl.multiple_of(t * 128, 128), 128)
    go(remote(teacher_ref.at[1 - c, part], teach_ref.at[c], y_sem.at[6], y_sem.at[7], me.ydev))

    def wblock(ff):
        return w_ref.at[:, pl.ds(pl.multiple_of(ff * rows_f, rows_f), rows_f), :]

    go(remote(qkvb_ref, wblock(f), w_sem.at[0], w_sem.at[1], me.xdev))
    go(remote(qkvb_ref, wblock(f), w_sem.at[2], w_sem.at[3], me.core))

    def shard(tt, ff):
        return u_ref.at[tt, pl.ds(pl.multiple_of(ff * rows_f, rows_f), rows_f), :]

    hrows = rows_f // 2

    def slab(tt, ff, h):
        return u_ref.at[tt, pl.ds(pl.multiple_of(ff * rows_f + h * hrows, hrows), hrows), :]

    def own_half(h):
        return upack_ref.at[pl.ds(pl.multiple_of(h * hrows, hrows), hrows), :]

    hs = (c, 1 - c)
    go(remote(own_half(c), slab(t, f, c), x_send.at[t], x_recv.at[t], me.xdev))
    for i in (0, 1):
        go(remote(own_half(hs[i]), slab(t, f, hs[i]), z_send.at[0, t, i], z_recv.at[t, i], me.z(t + 1)), t < 3)
        go(remote(own_half(hs[i]), slab(t, f, hs[i]), z_send.at[1, t, i], z_recv.at[t, i], me.z(t - 1)), t > 0)
    go(remote(upack_ref, shard(t, f), c_send.at[t], c_recv.at[t], me.core))

    local = [
        pltpu.make_async_copy(tokens_ref.at[c], t_ref.at[own_rows], loc_sem.at[0]),
        pltpu.make_async_copy(qkvb_ref, wblock(f), loc_sem.at[1]),
        pltpu.make_async_copy(upack_ref, shard(t, f), loc_sem.at[2]),
        pltpu.make_async_copy(teacher_ref.at[c, part], teach_ref.at[c], loc_sem.at[3]),
    ]
    for copy in local:
        copy.start()
    rb[c] = rbt_ref[c]
    live_ref[c] = mask_ref[c, t]

    def z_step(d):
        for tt, ok, on, nxt, way in ((t - d, t - d >= 0, t < 3, t + 1, 0), (t + d, t + d <= 3, t > 0, t - 1, 1)):
            go_on = ok & on
            for i in (0, 1):
                piece = slab(tt, f, hs[i])
                arrived = remote(piece, piece, z_send.at[way, tt, i], z_recv.at[tt, i], me.z(t))
                pl.when(ok)(arrived.wait_recv)
                go(remote(piece, piece, z_send.at[way, tt, i], z_recv.at[tt, i], me.z(nxt)), go_on)
                if i == 0:
                    go(remote(piece, piece, x_send.at[tt], x_recv.at[tt], me.xdev), ok)
            go(remote(shard(tt, f), shard(tt, f), c_send.at[tt], c_recv.at[tt], me.core), ok)

    def around(d):
        return ((t, None),) if d == 0 else ((t - d, t - d >= 0), (t + d, t + d <= 3))

    def when(ok, fn):
        if ok is None:
            fn()
        else:
            pl.when(ok)(fn)

    def x_step(d):
        for tt, ok in around(d):
            piece = slab(tt, me.f_x, c)
            when(ok, remote(piece, piece, x_send.at[tt], x_recv.at[tt], me.xdev).wait_recv)
            go(remote(piece, piece, yw_send.at[tt], yw_recv.at[tt], me.ydev), ok)
            go(remote(piece, piece, h_send.at[tt, 0], h_recv.at[tt, 0], me.core), ok)

    def y_step(d):
        for tt, ok in around(d):
            piece = slab(tt, me.f_x, 1 - c)
            when(ok, remote(piece, piece, yw_send.at[tt], yw_recv.at[tt], me.ydev).wait_recv)
            go(remote(piece, piece, h_send.at[tt, 1], h_recv.at[tt, 1], me.core), ok)

    remote(wblock(me.f_x), wblock(me.f_x), w_sem.at[0], w_sem.at[1], me.xdev).wait_recv()
    go(remote(wblock(me.f_x), wblock(me.f_x), w_sem.at[4], w_sem.at[5], me.core))
    remote(wblock(me.f_core), wblock(me.f_core), w_sem.at[2], w_sem.at[3], me.core).wait_recv()
    for copy in local[:2]:
        copy.wait()
    remote(wblock(me.f_xc), wblock(me.f_xc), w_sem.at[4], w_sem.at[5], me.core).wait_recv()

    width = q_ref.shape[0] * HD
    heads = q_ref.shape[0]

    def project(base, count):
        def step(i, carry):
            rows = pl.ds(pl.multiple_of(base + i * 256, 256), 256)
            piece = t_ref[rows, :]
            for j, ref in enumerate((q_ref, k_ref, v_ref)):
                made = dot_nn(piece, w_ref[j])
                for h in range(heads):
                    ref[h, rows, :] = made[:, h * HD : (h + 1) * HD].astype(bf16)
                if j:
                    (kt_ref if j == 1 else vt)[:, rows] = made.T.astype(bf16)
            return carry

        lax.fori_loop(0, count, step, 0)

    project(c * half, half // 256)
    x_step(0)
    other_rows = pl.ds(pl.multiple_of((1 - c) * half, half), half)
    remote(t_ref.at[other_rows], t_ref.at[other_rows], y_sem.at[0], y_sem.at[1], me.ydev).wait_recv()
    project((1 - c) * half, half // 256)
    remote(rb.at[1 - c], rb.at[1 - c], y_sem.at[2], y_sem.at[3], me.ydev).wait_recv()

    length = lengths_ref[c]
    nblk = seq // BLK
    pos_block = lax.broadcasted_iota(jnp.int32, (128, seq), 1) // BLK
    row = lax.broadcasted_iota(jnp.int32, (128, seq), 0)
    picks = dot_nn(rb[0].astype(bf16), (pos_block == row).astype(bf16)) + dot_nn(
        rb[1].astype(bf16), (pos_block == row + nblk // 2).astype(bf16)
    )
    key_block = lax.broadcasted_iota(jnp.int32, (nblk, seq), 0)
    query = lax.broadcasted_iota(jnp.int32, (nblk, seq), 1)
    own = query // BLK

    def same(a, b):
        return (a == b).astype(f32)

    times = same(key_block, 0) + same(key_block, 1) + same(key_block, own - 1)
    times += same(key_block, own) + same(key_block, own + 1)
    for j in range(3):
        times += same(key_block.astype(f32), picks[j : j + 1, :])
    times = jnp.where(query < 2 * BLK, 1.0, times)
    level = jnp.where(times > 0, jnp.log2(jnp.maximum(times, 1.0)), negative)
    for b in range(nblk):
        place = b * BLK + lax.broadcasted_iota(jnp.int32, (BLK, seq), 0)
        bias[b * BLK : (b + 1) * BLK, :] = jnp.where(
            place < length, jnp.broadcast_to(level[b : b + 1, :], (BLK, seq)), negative
        )

    factor = HD ** (-0.5) * 1.4426950408889634
    wide = 256

    def attend(h):
        def step(i, carry):
            cols = pl.ds(pl.multiple_of(i * wide, wide), wide)
            scores = dot_nt(k_ref[h], q_ref[h, cols, :]) * factor + bias[:, cols]
            top = jnp.max(scores, 0, keepdims=True)
            expo = jnp.exp2(scores - top)
            probs = (expo * (1.0 / jnp.sum(expo, 0, keepdims=True))).astype(bf16)
            pt_ref[h, :, cols] = probs
            att_out[h * HD : (h + 1) * HD, cols] = dot_nn(vt[h * HD : (h + 1) * HD, :], probs)
            return carry

        lax.fori_loop(0, seq // wide, step, 0)

    attend(0)
    z_step(1)
    x_step(1)
    attend(1)
    y_step(0)
    attend(2)
    for s in range(2):
        for tt in range(4):
            at = s * half + tt * 128
            tok_at = att_out[:, at : at + 128].T.astype(bf16)
            att_tok[s, tt] = tok_at
    for d in (1, 2, 3):
        to = (t + d) % 4
        go(remote(att_tok.at[:, to], att_ref.at[t], a_send.at[d], a_recv.at[d], me.z(to)))
    own_copy = pltpu.make_async_copy(att_tok.at[:, t], att_ref.at[t], loc_sem.at[4])
    own_copy.start()
    z_step(2)
    x_step(2)
    y_step(1)
    z_step(3)
    x_step(3)
    y_step(2)
    y_step(3)
    for s in range(2):
        tok_ref[s] = t_ref[pl.ds(pl.multiple_of(s * half + t * 128, 128), 128), :]
    for d in (1, 2, 3):
        src = (t + 4 - d) % 4
        remote(att_ref.at[src], att_ref.at[src], a_send.at[d], a_recv.at[d], me.z(src)).wait_recv()
    for tt in range(4):
        whole = shard(tt, me.f_core)
        remote(whole, whole, c_send.at[tt], c_recv.at[tt], me.core).wait_recv()
        for i in (0, 1):
            piece = slab(tt, me.f_xc, hs[i])
            remote(piece, piece, h_send.at[tt, i], h_recv.at[tt, i], me.core).wait_recv()
    there = live_ref.at[1 - c]
    remote(there, there, y_sem.at[4], y_sem.at[5], me.ydev).wait_recv()
    there = teach_ref.at[1 - c]
    remote(there, there, y_sem.at[6], y_sem.at[7], me.ydev).wait_recv()
    for copy in local[2:]:
        copy.wait()
    own_copy.wait()
    for copy, pred in sends:
        when(pred, copy.wait_send)


def forward_attention(lengths, tokens, teacher, qkvb, upack, rbt, mask, seq):
    heads = qkvb.shape[2] // HD
    width = heads * HD
    rows_f = qkvb.shape[1]
    depth = rows_f * 4
    vm = pl.BlockSpec(memory_space=pltpu.VMEM)
    hbm = pl.BlockSpec(memory_space=pl.ANY)
    dma = pltpu.SemaphoreType.DMA
    outs = [
        ((4, 2, 128, width), bf16, vm),
        ((4, depth, UW), bf16, hbm),
        ((seq, depth), bf16, vm),
        ((3, depth, width), bf16, vm),
        ((heads, seq, HD), bf16, vm),
        ((heads, seq, HD), bf16, vm),
        ((heads, seq, HD), bf16, vm),
        ((width, seq), bf16, vm),
        ((heads, seq, seq), bf16, vm),
        ((2, 128, depth), bf16, vm),
        ((2, 128, depth), bf16, vm),
        ((2, 8, 128), f32, vm),
    ]
    return pl.pallas_call(
        forward_attention_kernel,
        name="forward_attention",
        out_shape=[jax.ShapeDtypeStruct(s, d) for s, d, _ in outs],
        in_specs=[pl.BlockSpec(memory_space=pltpu.SMEM), hbm, hbm, vm, vm, vm, vm],
        out_specs=[m for _, _, m in outs],
        scratch_shapes=[
            pltpu.VMEM((width, seq), bf16),
            pltpu.VMEM((seq, seq), f32),
            pltpu.VMEM((2, 8, 128), f32),
            pltpu.VMEM((width, seq), f32),
            pltpu.VMEM((2, 4, 128, width), bf16),
            dma((5,)),
            dma((6,)),
            dma((8,)),
            dma((2, 4, 2)),
            dma((4, 2)),
            dma((4,)),
            dma((4,)),
            dma((4,)),
            dma((4,)),
            dma((4,)),
            dma((4,)),
            dma((4, 2)),
            dma((4, 2)),
            dma((4,)),
            dma((4,)),
        ],
        compiler_params=pltpu.CompilerParams(
            collective_id=0, has_side_effects=True, vmem_limit_bytes=VMEM_LIMIT
        ),
    )(lengths, tokens, teacher, qkvb, upack, rbt, mask)


def column(row):
    return row.T[:, 0:1]


def add_rows(dst, a, b, step=16):
    def one(i, carry):
        rows = pl.ds(pl.multiple_of(i * step, step), step)
        dst[rows, :] = a[rows, :] + b[rows, :]
        return carry

    lax.fori_loop(0, dst.shape[0] // step, one, 0)


class Line:
    def __init__(self, me, go, block, send, recv):
        self.me, self.go, self.block, self.send, self.recv = me, go, block, send, recv

    def start(self):
        t = self.me.t
        mine = self.block(t)
        self.go(remote(mine, mine, self.send.at[0, t], self.recv.at[t], self.me.z(t + 1)), t < 3)
        self.go(remote(mine, mine, self.send.at[1, t], self.recv.at[t], self.me.z(t - 1)), t > 0)

    def step(self, d):
        t = self.me.t
        for tt, ok, on, nxt, way in ((t - d, t - d >= 0, t < 3, t + 1, 0), (t + d, t + d <= 3, t > 0, t - 1, 1)):
            piece = self.block(tt)
            pl.when(ok)(remote(piece, piece, self.send.at[way, tt], self.recv.at[tt], self.me.z(t)).wait_recv)
            if d < 3:
                self.go(remote(piece, piece, self.send.at[way, tt], self.recv.at[tt], self.me.z(nxt)), ok & on)


class Chain:
    def __init__(self, me, go, own, left, right, send, recv_l, recv_r):
        self.me, self.go, self.own, self.left, self.right = me, go, own, left, right
        self.send, self.recv_l, self.recv_r = send, recv_l, recv_r

    def arrived(self, tt, way):
        buf, recv = (self.left, self.recv_l) if way == 0 else (self.right, self.recv_r)
        remote(buf(tt), buf(tt), self.send.at[tt], recv.at[tt], self.me.z(self.me.t)).wait_recv()

    def pass_on(self, tt, way):
        t = self.me.t
        inner = (t > 0) if way == 0 else (t < 3)
        ahead = (tt > t) if way == 0 else (tt < t)
        buf, recv = (self.left, self.recv_l) if way == 0 else (self.right, self.recv_r)

        @pl.when(ahead & inner)
        def _():
            self.arrived(tt, way)
            add_rows(self.own(tt), self.own(tt), buf(tt))

        to = self.me.z(t + 1 if way == 0 else t - 1)
        self.go(remote(self.own(tt), buf(tt), self.send.at[tt], recv.at[tt], to), ahead)

    def end(self):
        t = self.me.t
        mine = self.own(t)

        @pl.when(t > 0)
        def _():
            self.arrived(t, 0)
            add_rows(mine, mine, self.left(t))

        @pl.when(t < 3)
        def _():
            self.arrived(t, 1)
            add_rows(mine, mine, self.right(t))


CHAIN_ORDER = ((3, 0), (0, 1), (2, 0), (1, 1), (1, 0), (2, 1))


def backward_kernel(names, *refs):
    r = dict(zip(names, refs, strict=True))
    me = Peers()
    f, c, t = me.f, me.c, me.t
    x = f // 2
    k = f % 2
    depth = r["u"].shape[1]
    rows_f = depth // 4
    hrows = rows_f // 2
    qrows = rows_f // 4
    seq = r["t"].shape[0]
    half = seq // 2
    heads = r["q"].shape[0]
    width = heads * HD
    sends = []

    def when(ok, fn):
        if ok is None:
            fn()
        else:
            pl.when(ok)(fn)

    def go(copy, pred=None):
        when(pred, copy.start)
        sends.append((copy, pred))

    loads = {}
    order = ["att", "u0", "u1", "u2", "u3", "pt", "q", "k", "v", "kt", "w", "t"]
    for i, name in enumerate(order):
        if name[0] == "u":
            j = int(name[1])
            loads[name] = pltpu.make_async_copy(r["u"].at[j], r["u_v"].at[j], r["load_sem"].at[i])
        else:
            loads[name] = pltpu.make_async_copy(r[name], r[name + "_v"], r["load_sem"].at[i])
        loads[name].start()
    me.barrier()

    att_v, u_v, g_v, act, slope = r["att_v"], r["u_v"], r["g_v"], r["act"], r["slope"]
    rows = 2 * 128
    length = r["lengths"][c]
    inv_width = 1.0 / depth

    def both(ref):
        return ref[...].reshape(rows, depth).astype(f32)

    def mean(v):
        return jnp.sum(v, -1, keepdims=True) * inv_width

    def normalize(v):
        center = v - mean(v)
        inverse = lax.rsqrt(mean(center * center) + norm_eps)
        return center * inverse, inverse

    def back(up, normed, inverse, gain):
        scaled = up * gain
        return inverse * (scaled - mean(scaled) - normed * mean(scaled * normed))

    for name in ("att", "u0", "u1", "u2", "u3"):
        loads[name].wait()
    norms = u_v[0, :, 1728:1736].astype(f32).T
    gains = [norms[i : i + 1, :] for i in range(4)]
    att = [att_v[tt].reshape(rows, width) for tt in range(4)]
    attn = dot_nt(att[0], u_v[0, :, 1536:1728])
    for tt in range(1, 4):
        attn += dot_nt(att[tt], u_v[tt, :, 1536:1728])
    normed_one, inverse_one = normalize(both(r["tok"]) + attn)
    hidden = normed_one * gains[0] + gains[1]
    hidden_b = hidden.astype(bf16)
    cube = 0.044715
    root = 0.7978845608028654

    def up_step(tt, mixed):
        upper = dot_nn(hidden_b, u_v[tt, :, 0:768])
        square = upper * upper
        th = jnp.tanh(root * upper * (1.0 + cube * square))
        act_t = (0.5 * upper * (1.0 + th)).astype(bf16)
        act[tt] = act_t
        bend = 0.5 * (1.0 + th) + 0.5 * upper * (1.0 - th * th) * root * (1.0 + 3.0 * cube * square)
        slope[tt] = bend.astype(bf16)
        return mixed + dot_nt(act_t, u_v[tt, :, 768:1536])

    mixed = lax.fori_loop(0, 4, up_step, jnp.zeros((rows, depth), f32))
    normed_two, inverse_two = normalize(hidden + mixed)
    result = normed_two * gains[2] + gains[3]

    r["piece"][...] = result.astype(bf16).reshape(2, 128, depth)
    part = pl.ds(pl.multiple_of(t * 128, 128), 128)
    lo = r["lo"]
    go(remote(r["piece"].at[1 - c], lo.at[c, part], r["s_sem"].at[0], r["s_sem"].at[1], me.ydev))
    own_lo = pltpu.make_async_copy(r["piece"].at[c], lo.at[c, part], r["load_sem"].at[12])
    own_lo.start()

    def lo_block(tt):
        return lo.at[:, pl.ds(pl.multiple_of(tt * 128, 128), 128), :]

    lo_line = Line(me, go, lo_block, r["lo_send"], r["lo_recv"])

    alive = jnp.concatenate([column(r["live"][0]), column(r["live"][1])], 0)
    row = lax.broadcasted_iota(jnp.int32, (rows, 1), 0)
    place = jnp.where(row < 128, row, row - 128 + half) + t * 128
    live = jnp.where((alive == 1.0) & (place < length), 1.0, 0.0)
    differ = result - both(r["teach"])
    weighed = differ * live
    r["err"][0, 0] = jnp.sum(weighed * differ)
    grad_y = weighed * (2.0 / (r["count"][0, 0] * depth))
    sums = [None] * 4
    sums[2] = jnp.sum(grad_y * normed_two, 0, keepdims=True)
    sums[3] = jnp.sum(grad_y, 0, keepdims=True)
    grad_two = back(grad_y, normed_two, inverse_two, gains[2])
    gm = grad_two.astype(bf16)
    gm_t = grad_two.T.astype(bf16)
    hidden_t = hidden.T.astype(bf16)

    there = lo.at[1 - c, part]
    remote(there, there, r["s_sem"].at[0], r["s_sem"].at[1], me.ydev).wait_recv()
    own_lo.wait()
    lo_line.start()

    def down_step(tt, total):
        ga = dot_nn(gm, u_v[tt, :, 768:1536])
        gu = (ga * slope[tt].astype(f32)).astype(bf16)
        g_v[tt, :, 768:1536] = dot_nn(gm_t, act[tt]).astype(bf16)
        g_v[tt, :, 0:768] = dot_nn(hidden_t, gu).astype(bf16)
        return total + dot_nt(gu, u_v[tt, :, 0:768])

    grad_hidden = lax.fori_loop(0, 4, down_step, grad_two)
    sums[0] = jnp.sum(grad_hidden * normed_one, 0, keepdims=True)
    sums[1] = jnp.sum(grad_hidden, 0, keepdims=True)
    grad_one = back(grad_hidden, normed_one, inverse_one, gains[0])
    r["gone"][...] = grad_one.reshape(2, 128, depth)
    ga = grad_one.astype(bf16)
    gatt, do_in = r["gatt"], r["do_in"]
    for tt in range(4):
        back_t = dot_nn(ga, u_v[tt, :, 1536:1728]).astype(bf16)
        gatt[tt] = back_t.reshape(2, 128, width)
    for d in (1, 2, 3):
        to = (t + d) % 4
        go(remote(gatt.at[to], do_in.at[t], r["a_send"].at[d], r["a_recv"].at[d], me.z(to)))
    do_in[t] = gatt[t]
    for i, dev in enumerate((me.core, me.xdev, me.ydev)):
        pl.semaphore_signal(r["free"].at[i], inc=1, device_id=dev, device_id_type=MESH)
    ga_t = grad_one.T.astype(bf16)
    norm_rows = jnp.concatenate(sums + [jnp.zeros((4, depth), f32)], 0)
    norm_cols = jnp.concatenate([norm_rows.T, jnp.zeros((depth, UW - 1736), f32)], 1).astype(bf16)
    for tt in range(4):
        g_v[tt, :, 1536:1728] = dot_nn(ga_t, att[tt]).astype(bf16)
        g_v[tt, :, 1728:1792] = norm_cols

    far = 1 - x
    for i in range(3):
        pl.semaphore_wait(r["free"].at[i], 1)

    def g_rows(tt, ff):
        return g_v.at[tt, pl.ds(pl.multiple_of(ff * rows_f, rows_f), rows_f), :]

    def rc_all(xx, tt):
        return u_v.at[tt, pl.ds(pl.multiple_of(xx * rows_f, rows_f), rows_f), :]

    def room(n):
        return lambda tt, i=0, size=hrows: u_v.at[tt, pl.ds((4 + n) * hrows + i * qrows, size), :]

    xg_at, yg_at, zl_at, zr_at = (room(n) for n in range(4))

    for xx in (far, x):
        for tt in range(4):
            ff = xx * 2 + (1 - k)
            go(remote(g_rows(tt, ff), rc_all(xx, tt), r["rc_send"].at[xx, tt], r["rc_recv"].at[xx, tt], me.core))

    lo_line.step(1)

    def rc_rows(xx, tt, h, q0, n):
        return u_v.at[tt, pl.ds(pl.multiple_of(xx * rows_f + h * hrows + q0, qrows), n), :]

    def core_step(xx, tt):
        view = rc_all(xx, tt)
        remote(view, view, r["rc_send"].at[xx, tt], r["rc_recv"].at[xx, tt], me.core).wait_recv()
        add_rows(view, view, g_rows(tt, xx * 2 + k))

    def far_step(tt):
        core_step(far, tt)
        dx, dy = r["dx"], r["dy"]
        go(remote(rc_rows(far, tt, 1 - c, 0, qrows), dx.at[tt], r["dx_send"].at[tt], r["dx_recv"].at[tt], me.xdev))
        go(remote(rc_rows(far, tt, 1 - c, qrows, qrows), dy.at[tt], r["dy_send"].at[tt], r["dy_recv"].at[tt], me.ydev))
        go(remote(rc_rows(far, tt, c, 0, qrows), xg_at(tt, 0, qrows), r["xg_send"].at[tt, 0], r["xg_recv"].at[tt, 0], me.xdev))

    def near_step(tt):
        core_step(x, tt)
        go(remote(rc_rows(x, tt, 1 - c, qrows, qrows), yg_at(tt, 1, qrows), r["yg_send"].at[tt, 1], r["yg_recv"].at[tt, 1], me.ydev))

    def diag_step(tt):
        dx, dy = r["dx"], r["dy"]
        remote(dx.at[tt], dx.at[tt], r["dx_send"].at[tt], r["dx_recv"].at[tt], me.xdev).wait_recv()
        mine = rc_rows(x, tt, 1 - c, 0, qrows)
        add_rows(mine, mine, dx.at[tt])
        go(remote(mine, yg_at(tt, 0, qrows), r["yg_send"].at[tt, 0], r["yg_recv"].at[tt, 0], me.ydev))
        remote(dy.at[tt], dy.at[tt], r["dy_send"].at[tt], r["dy_recv"].at[tt], me.ydev).wait_recv()
        mine = rc_rows(far, tt, c, qrows, qrows)
        add_rows(mine, mine, dy.at[tt])
        go(remote(mine, xg_at(tt, 1, qrows), r["xg_send"].at[tt, 1], r["xg_recv"].at[tt, 1], me.xdev))

    def sum_step(tt):
        for i in (0, 1):
            xg, yg = xg_at(tt, i, qrows), yg_at(tt, i, qrows)
            mine = rc_rows(x, tt, c, i * qrows, qrows)
            remote(xg, xg, r["xg_send"].at[tt, i], r["xg_recv"].at[tt, i], me.xdev).wait_recv()
            add_rows(mine, mine, xg)
            remote(yg, yg, r["yg_send"].at[tt, i], r["yg_recv"].at[tt, i], me.ydev).wait_recv()
            add_rows(mine, mine, yg)

    ORDER = (3, 0, 2, 1)
    w_chain = Chain(
        me, go, lambda tt: rc_rows(x, tt, c, 0, hrows), zl_at, zr_at,
        r["zw_send"], r["zw_recv_l"], r["zw_recv_r"],
    )

    for tt in ORDER:
        far_step(tt)
    lo_line.step(2)

    for name in ("pt", "q", "k", "v", "kt", "w", "t"):
        loads[name].wait()
    do, proj, dqt, dk, dv = r["do"], r["proj"], r["dqt"], r["dk"], r["dv"]
    for d in (1, 2, 3):
        src = (t + 4 - d) % 4
        remote(do_in.at[src], do_in.at[src], r["a_send"].at[d], r["a_recv"].at[d], me.z(src)).wait_recv()
    for s in range(2):
        for tt in range(4):
            at = s * half + tt * 128
            for h in range(heads):
                do[h, at : at + 128, :] = do_in[tt, s, :, h * HD : (h + 1) * HD]
    q_v, k_v, v_v, kt_v, pt_v, t_v, w_v = (r[n + "_v"] for n in ("q", "k", "v", "kt", "pt", "t", "w"))
    scale = HD ** (-0.5)
    wide = 256

    def attend_back(h):
        dk[...] = jnp.zeros_like(dk)
        dv[...] = jnp.zeros_like(dv)

        def step(i, carry):
            cols = pl.ds(pl.multiple_of(i * wide, wide), wide)
            mine = do[h, cols, :]
            probs = pt_v[h, :, cols]
            gp = dot_nt(v_v[h], mine)
            pf = probs.astype(f32)
            mix = jnp.sum(pf * gp, 0, keepdims=True)
            gs = (pf * (gp - mix)).astype(bf16)
            dk[...] += dot_nn(gs, q_v[h, cols, :])
            dv[...] += dot_nn(probs, mine)
            dqt[h * HD : (h + 1) * HD, cols] = dot_nn(kt_v[h * HD : (h + 1) * HD, :], gs)
            return carry

        lax.fori_loop(0, seq // wide, step, 0)
        proj[1, :, h * HD : (h + 1) * HD] = (dk[...] * scale).astype(bf16)
        proj[2, :, h * HD : (h + 1) * HD] = dv[...].astype(bf16)

    attend_back(0)
    for tt in ORDER:
        near_step(tt)
    attend_back(1)
    for tt in ORDER:
        diag_step(tt)
    lo_line.step(3)
    attend_back(2)
    proj[0] = (dqt[...].T * scale).astype(bf16)
    ip = r["ip"]

    def rows_step(i, carry):
        at = pl.ds(pl.multiple_of(i * 128, 128), 128)
        total = dot_nt(proj[0, at, :], w_v[0])
        for j in (1, 2):
            total += dot_nt(proj[j, at, :], w_v[j])
        ip[i // 4, i % 4] = total.astype(bf16)
        return carry

    lax.fori_loop(0, seq // 128, rows_step, 0)

    def ip_chain(j, s):
        return Chain(
            me, go, lambda tt: ip.at[s, tt], lambda tt: act.at[tt, pl.ds(j * 128, 128), :], lambda tt: slope.at[tt, pl.ds(j * 128, 128), :],
            r["i_send"].at[j], r["i_recv_l"].at[j], r["i_recv_r"].at[j],
        )

    chains = [ip_chain(0, 1 - c), ip_chain(1, c)]
    for tt, way in CHAIN_ORDER[:2]:
        chains[0].pass_on(tt, way)
    qg = r["qg"]
    for j in range(3):
        qg[j] = dot_tn(t_v[...], proj[j]).astype(bf16)

    def q_rows(ff):
        return qg.at[:, pl.ds(pl.multiple_of(ff * rows_f, rows_f), rows_f), :]

    qc, qs = r["qc"], r["q_sem"]
    go(remote(q_rows(far * 2 + 1 - k), qc.at[0], qs.at[0], qs.at[1], me.core))
    go(remote(q_rows(x * 2 + 1 - k), qc.at[1], qs.at[2], qs.at[3], me.core))
    for tt, way in CHAIN_ORDER[2:]:
        chains[0].pass_on(tt, way)
    remote(qc.at[0], qc.at[0], qs.at[0], qs.at[1], me.core).wait_recv()
    qc[0] = qc[0] + qg[:, pl.ds(pl.multiple_of((far * 2 + k) * rows_f, rows_f), rows_f), :]
    go(remote(qc.at[0], qc.at[2], qs.at[4], qs.at[5], me.xdev))
    for tt, way in CHAIN_ORDER:
        chains[1].pass_on(tt, way)
    remote(qc.at[1], qc.at[1], qs.at[2], qs.at[3], me.core).wait_recv()
    qc[1] = qc[1] + qg[:, pl.ds(pl.multiple_of((x * 2 + k) * rows_f, rows_f), rows_f), :]
    for tt in ORDER:
        sum_step(tt)
    remote(qc.at[2], qc.at[2], qs.at[4], qs.at[5], me.xdev).wait_recv()
    qc[1] = qc[1] + qc[2]
    go(remote(qc.at[1], qc.at[3], qs.at[6], qs.at[7], me.ydev))

    ig = r["ig"]
    igp = r["igp"]

    def finish(j, s):
        chains[j].end()
        igp[j] = (ip[s, t].astype(f32) + r["gone"][s]).astype(bf16)

    finish(0, 1 - c)
    go(remote(igp.at[0], ig.at[c, part], r["s_sem"].at[2], r["s_sem"].at[3], me.ydev))
    finish(1, c)
    own_ig = pltpu.make_async_copy(igp.at[1], ig.at[c, part], r["load_sem"].at[13])
    own_ig.start()

    def ig_line(j, s):
        def block(tt):
            return ig.at[s, pl.ds(pl.multiple_of(tt * 128, 128), 128), :]

        return Line(me, go, block, r["ig_send"].at[j], r["ig_recv"].at[j])

    lines = [ig_line(0, c), ig_line(1, 1 - c)]
    own_ig.wait()
    lines[0].start()
    there = ig.at[1 - c, part]
    remote(there, there, r["s_sem"].at[2], r["s_sem"].at[3], me.ydev).wait_recv()
    lines[1].start()
    for tt, way in CHAIN_ORDER[:2]:
        w_chain.pass_on(tt, way)
    lines[0].step(1)
    lines[1].step(1)
    for tt, way in CHAIN_ORDER[2:]:
        w_chain.pass_on(tt, way)
    lines[0].step(2)
    lines[1].step(2)
    w_chain.end()
    fin = r["fin"]
    fin[c] = rc_rows(x, t, c, 0, hrows)[...]
    go(remote(fin.at[c], fin.at[c], r["s_sem"].at[4], r["s_sem"].at[5], me.ydev))
    lines[0].step(3)
    lines[1].step(3)
    remote(qc.at[3], qc.at[3], qs.at[6], qs.at[7], me.ydev).wait_recv()
    r["qsum"][...] = qc[1].astype(f32) + qc[3].astype(f32)
    remote(fin.at[1 - c], fin.at[1 - c], r["s_sem"].at[4], r["s_sem"].at[5], me.ydev).wait_recv()
    r["gsum"][...] = fin[...].reshape(rows_f, UW).astype(f32)
    for copy, pred in sends:
        when(pred, copy.wait_send)


def backward(lengths, count, att, u, tok, teach, live, q, k, v, kt, pt, tokens, w):
    depth = tok.shape[2]
    heads, seq = q.shape[:2]
    width = heads * HD
    rows_f = depth // 4
    vm = pl.BlockSpec(memory_space=pltpu.VMEM)
    smem = pl.BlockSpec(memory_space=pltpu.SMEM)
    hbm = pl.BlockSpec(memory_space=pl.ANY)
    dma = pltpu.SemaphoreType.DMA

    def vb(*shape):
        return pltpu.VMEM(shape, bf16)

    def vf(*shape):
        return pltpu.VMEM(shape, f32)

    ins = dict(
        lengths=(lengths, smem), count=(count, smem), att=(att, hbm), u=(u, hbm), tok=(tok, vm), teach=(teach, vm),
        live=(live, vm), q=(q, hbm), k=(k, hbm), v=(v, hbm), kt=(kt, hbm), pt=(pt, hbm), t=(tokens, hbm), w=(w, hbm),
    )
    outs = dict(
        lo=((2, seq // 2, depth), bf16, hbm),
        ig=((2, seq // 2, depth), bf16, hbm),
        gsum=((rows_f, UW), f32, vm),
        qsum=((3, rows_f, width), f32, vm),
        err=((1, 1), f32, smem),
    )
    h, qr = rows_f // 2, rows_f // 4
    scratch = dict(
        att_v=vb(*att.shape), u_v=vb(*u.shape), pt_v=vb(*pt.shape), q_v=vb(*q.shape), k_v=vb(*k.shape), v_v=vb(*v.shape),
        kt_v=vb(*kt.shape), w_v=vb(*w.shape), t_v=vb(*tokens.shape), g_v=vb(*u.shape), act=vb(4, 256, 768),
        slope=vb(4, 256, 768), piece=vb(2, 128, depth), gone=vf(2, 128, depth), gatt=vb(*att.shape), do_in=vb(*att.shape),
        dx=vb(4, qr, UW), dy=vb(4, qr, UW),
        do=vb(heads, seq, HD), proj=vb(3, seq, width), dqt=vf(width, seq),
        dk=vf(seq, HD), dv=vf(seq, HD), ip=vb(2, 4, 128, depth),
        igp=vb(2, 128, depth), qg=vb(3, depth, width), qc=vb(4, 3, rows_f, width), fin=vb(2, h, UW),
        load_sem=dma((14,)), s_sem=dma((6,)), lo_send=dma((2, 4)), lo_recv=dma((4,)), a_send=dma((4,)), a_recv=dma((4,)),
        rc_send=dma((2, 4)), rc_recv=dma((2, 4)), dx_send=dma((4,)), dx_recv=dma((4,)), dy_send=dma((4,)),
        dy_recv=dma((4,)), xg_send=dma((4, 2)), xg_recv=dma((4, 2)), yg_send=dma((4, 2)), yg_recv=dma((4, 2)),
        zw_send=dma((4,)), zw_recv_l=dma((4,)), zw_recv_r=dma((4,)), i_send=dma((2, 4)), i_recv_l=dma((2, 4)),
        i_recv_r=dma((2, 4)), ig_send=dma((2, 2, 4)), ig_recv=dma((2, 4)), q_sem=dma((8,)), free=pltpu.SemaphoreType.REGULAR((3,)),
    )
    return pl.pallas_call(
        functools.partial(backward_kernel, (*ins, *outs, *scratch)),
        name="backward",
        out_shape=[jax.ShapeDtypeStruct(s, d) for s, d, _ in outs.values()],
        in_specs=[m for _, m in ins.values()],
        out_specs=[m for _, _, m in outs.values()],
        scratch_shapes=list(scratch.values()),
        compiler_params=pltpu.CompilerParams(
            collective_id=1, has_side_effects=True, vmem_limit_bytes=60 * 2**20
        ),
    )(*(a for a, _ in ins.values()))


def body_swapped(
    tokens,
    teacher,
    lengths,
    valid_mask,
    random_blocks,
    step_count,
    qkv_weight,
    out_weight,
    up_weight,
    down_weight,
    norm_params,
    qkv_moment,
    qkv_square,
    out_moment,
    out_square,
    up_moment,
    up_square,
    down_moment,
    down_square,
    norm_moment,
    norm_square,
):
    c, t = lax.axis_index("ctx"), lax.axis_index("tp")
    seqs, tok_count, width = tokens.shape
    seq = tok_count * 2
    upack = jnp.concatenate(
        [
            up_weight,
            down_weight.T,
            out_weight.T,
            norm_params.T,
            jnp.zeros((192, 60), f32),
        ],
        1,
    ).astype(bf16)
    qkvb = qkv_weight.astype(bf16)
    rbt = jnp.pad(
        jnp.swapaxes(random_blocks, 1, 2).astype(f32), ((0, 0), (0, 5), (0, 120))
    )
    mask = jnp.broadcast_to(valid_mask.reshape(seqs, 4, 1, 128).astype(f32), (seqs, 4, 8, 128))
    positions = c * tok_count + jnp.arange(tok_count, dtype=jnp.int32)
    live_rows = ((valid_mask == 1) & (positions[None, :] < lengths[:, None])).astype(f32)
    live_count = lax.psum(jnp.sum(live_rows), ("fsdp", "ctx"))
    att, u, tk, w, q, k, v, kt, pt, tok, teach, live = forward_attention(
        lengths, tokens, teacher, qkvb, upack, rbt, mask, seq
    )
    layer_out, ig, g, qkv_grad, err = backward(
        lengths, live_count.reshape(1, 1), att, u, tok, teach, live, q, k, v, kt, pt, tk, w
    )
    error_total = lax.psum(err[0, 0], ("fsdp", "ctx", "tp"))
    loss_value = error_total / (live_count * width)
    input_grad = ig.astype(f32)
    up_grad, down_grad, out_grad, norm_grad = g[:, :768], g[:, 768:1536].T, g[:, 1536:1728].T, g[:, 1728:1732].T
    shards = (qkv_grad, out_grad, up_grad, down_grad, norm_grad)
    squares = sum(jnp.sum(m * m) for m in shards[:4]) + jnp.where(t == 0, jnp.sum(norm_grad * norm_grad), 0.0)
    grad_norm = jnp.sqrt(lax.psum(squares, ("fsdp", "tp")))
    factor = jnp.minimum(1.0, clip_level / (grad_norm + 1e-06))
    steps_done = step_count[0].astype(f32)
    state = (
        (qkv_weight, qkv_moment, qkv_square),
        (out_weight, out_moment, out_square),
        (up_weight, up_moment, up_square),
        (down_weight, down_moment, down_square),
        (norm_params, norm_moment, norm_square),
    )
    new = [
        adam_update(weight, grad, moment, square, factor, steps_done, rate)
        for (weight, moment, square), grad, rate in zip(state, shards, rate_list)
    ]
    return (layer_out, loss_value, input_grad, grad_norm, *(v for group in new for v in group))


def solution(mesh):
    in_specs = (
        P("fsdp", "ctx", None),
        P("fsdp", "ctx", None),
        P("fsdp"),
        P("fsdp", "ctx"),
        P("fsdp", "ctx", None),
        P(),
        P(None, "fsdp", "tp"),
        P("tp", "fsdp"),
        P("fsdp", "tp"),
        P("tp", "fsdp"),
        P(None, "fsdp"),
        P(None, "fsdp", "tp"),
        P(None, "fsdp", "tp"),
        P("tp", "fsdp"),
        P("tp", "fsdp"),
        P("fsdp", "tp"),
        P("fsdp", "tp"),
        P("tp", "fsdp"),
        P("tp", "fsdp"),
        P(None, "fsdp"),
        P(None, "fsdp"),
    )
    out_specs = (
        P("fsdp", "ctx", None),
        P(),
        P("fsdp", "ctx", None),
        P(),
        P(None, "fsdp", "tp"),
        P(None, "fsdp", "tp"),
        P(None, "fsdp", "tp"),
        P("tp", "fsdp"),
        P("tp", "fsdp"),
        P("tp", "fsdp"),
        P("fsdp", "tp"),
        P("fsdp", "tp"),
        P("fsdp", "tp"),
        P("tp", "fsdp"),
        P("tp", "fsdp"),
        P("tp", "fsdp"),
        P(None, "fsdp"),
        P(None, "fsdp"),
        P(None, "fsdp"),
    )
    sizes = dict(mesh.shape)
    small = sizes == {"fsdp": 4, "ctx": 2, "tp": 4}
    body = body_swapped if small else body_general
    return jax.shard_map(body, mesh=mesh, in_specs=in_specs, out_specs=out_specs, check_vma=False)
```

```python
import functools
import types
from functools import partial

import jax
import jax.numpy as jnp
from jax import lax
from jax.experimental import pallas as pl
from jax.experimental.pallas import tpu as pltpu
from jax.sharding import PartitionSpec as P

HD = 64
BLK = 64
MESH = pl.DeviceIdType.MESH
f32 = jnp.float32
bf16 = jnp.bfloat16

norm_eps = 1e-06
beta_one = 0.9
beta_two = 0.999
adam_eps = 1e-08
decay_rate = 0.01
clip_level = 0.001
rate_list = (0.04, 0.4, 0.04, 0.02, 0.2)
negative = -1e30
VMEM_LIMIT = 58 * 2**20


def layer_norm(values, gain, shift):
    center = values - jnp.mean(values, -1, keepdims=True)
    inverse = lax.rsqrt(jnp.mean(center * center, -1, keepdims=True) + norm_eps)
    normed = center * inverse
    return (normed * gain + shift, normed, inverse)


def norm_backward(upstream, normed, inverse, gain):
    scaled = upstream * gain
    return inverse * (
        scaled
        - jnp.mean(scaled, -1, keepdims=True)
        - normed * jnp.mean(scaled * normed, -1, keepdims=True)
    )


def adam_update(weight, gradient, moment, square, factor, steps_done, rate):
    clipped = gradient * factor
    new_moment = beta_one * moment + (1.0 - beta_one) * clipped
    new_square = beta_two * square + (1.0 - beta_two) * clipped * clipped
    corrected = new_moment / (1.0 - beta_one**steps_done)
    scaled = new_square / (1.0 - beta_two**steps_done)
    new_weight = weight - rate * (corrected / (jnp.sqrt(scaled) + adam_eps) + decay_rate * weight)
    return (new_weight, new_moment, new_square)


def body_general(
    tokens,
    teacher,
    lengths,
    valid_mask,
    random_blocks,
    step_count,
    qkv_weight,
    out_weight,
    up_weight,
    down_weight,
    norm_params,
    qkv_moment,
    qkv_square,
    out_moment,
    out_square,
    up_moment,
    up_square,
    down_moment,
    down_square,
    norm_moment,
    norm_square,
):
    ctx_index = lax.axis_index("ctx")
    ctx_count = lax.axis_size("ctx")
    tp_index = lax.axis_index("tp")
    seqs_here, tok_count, width = tokens.shape
    local_blocks = tok_count // BLK
    block_count = local_blocks * ctx_count
    seq_len = tok_count * ctx_count
    width_local = qkv_weight.shape[2]
    heads_local = width_local // HD
    scale = HD ** (-0.5)
    full_qkv, full_out, full_up, full_down, full_norms = (
        lax.all_gather(qkv_weight.astype(bf16), "fsdp", axis=1, tiled=True),
        lax.all_gather(out_weight.astype(bf16), "fsdp", axis=1, tiled=True),
        lax.all_gather(up_weight.astype(bf16), "fsdp", axis=0, tiled=True),
        lax.all_gather(down_weight.astype(bf16), "fsdp", axis=1, tiled=True),
        lax.all_gather(norm_params.astype(bf16), "fsdp", axis=1, tiled=True),
    )
    gains = full_norms.astype(f32)
    projected = jnp.einsum("std,cde->stce", tokens, full_qkv, preferred_element_type=f32).astype(
        bf16
    )
    queries = projected[:, :, 0, :]
    kv_local = projected[:, :, 1:, :]
    gathered = lax.all_gather(kv_local, "ctx", axis=1, tiled=True)
    own_blocks = ctx_index * local_blocks + jnp.arange(local_blocks, dtype=jnp.int32)
    zero_row = own_blocks * 0
    window = jnp.stack([zero_row, zero_row + 1, own_blocks - 1, own_blocks, own_blocks + 1], -1)
    listed = jnp.concatenate(
        [jnp.broadcast_to(window[None], (seqs_here, local_blocks, 5)), random_blocks], -1
    )
    inside = (listed >= 0) & (listed < block_count)
    safe = jnp.clip(listed, 0, block_count - 1)
    key_pos = safe[..., None] * BLK + jnp.arange(BLK, dtype=jnp.int32)
    counted = (inside[..., None] & (key_pos < lengths[:, None, None, None])).reshape(
        seqs_here, local_blocks, 8 * BLK
    )
    key_live = jnp.arange(seq_len, dtype=jnp.int32)[None, :] < lengths[:, None]
    q_blocks = queries.reshape(seqs_here, local_blocks, BLK, heads_local, HD)
    head_rows = queries[:, : 2 * BLK].reshape(seqs_here, 2 * BLK, heads_local, HD)
    blocked = gathered.reshape(seqs_here, block_count, BLK, 2, width_local)
    flat = blocked.reshape(seqs_here * block_count, BLK, 2, width_local)
    offset = jnp.arange(seqs_here, dtype=jnp.int32)[:, None, None] * block_count
    picked = lax.map(
        lambda at: lax.dynamic_index_in_dim(flat, at, 0, keepdims=False), (safe + offset).reshape(-1)
    ).reshape(seqs_here, local_blocks, 8, BLK, 2, width_local)
    key_rows = picked[..., 0, :].reshape(seqs_here, local_blocks, 8 * BLK, heads_local, HD)
    value_rows = picked[..., 1, :].reshape(seqs_here, local_blocks, 8 * BLK, heads_local, HD)
    scores = (
        jnp.einsum("sbqhd,sbkhd->sbhqk", q_blocks, key_rows, preferred_element_type=f32) * scale
    )
    scores = jnp.where(counted[:, :, None, None, :], scores, negative)
    all_keys = gathered[:, :, 0, :].reshape(seqs_here, seq_len, heads_local, HD)
    all_values = gathered[:, :, 1, :].reshape(seqs_here, seq_len, heads_local, HD)
    wide_scores = (
        jnp.einsum("sqhd,skhd->shqk", head_rows, all_keys, preferred_element_type=f32) * scale
    )
    wide_scores = jnp.where(key_live[:, None, None, :], wide_scores, negative)
    top_value = jnp.max(scores, -1, keepdims=True)
    expo = jnp.exp(scores - top_value)
    summed = jnp.sum(expo, -1, keepdims=True)
    sparse_lse = top_value + jnp.log(summed)
    probs_b = (expo / summed).astype(bf16)
    sparse_out = jnp.einsum(
        "sbhqk,sbkhd->sbqhd", probs_b, value_rows, preferred_element_type=f32
    ).reshape(seqs_here, tok_count, width_local)
    wide_top = jnp.max(wide_scores, -1, keepdims=True)
    wide_expo = jnp.exp(wide_scores - wide_top)
    wide_sum = jnp.sum(wide_expo, -1, keepdims=True)
    wide_lse = wide_top + jnp.log(wide_sum)
    wide_probs = (wide_expo / wide_sum).astype(bf16)
    wide_out = jnp.einsum(
        "shqk,skhd->sqhd", wide_probs, all_values, preferred_element_type=f32
    ).reshape(seqs_here, 2 * BLK, width_local)
    is_first = ctx_index == 0
    row_ids = jnp.arange(tok_count, dtype=jnp.int32)
    global_row = (row_ids < 2 * BLK) & is_first
    rest_zeros = jnp.zeros((seqs_here, tok_count - 2 * BLK, width_local), f32)
    padded_wide = jnp.concatenate([wide_out, rest_zeros], 1)
    attended = jnp.where(global_row[None, :, None], padded_wide, sparse_out).astype(bf16)
    attn_part = jnp.einsum("ste,ed->std", attended, full_out, preferred_element_type=f32)
    positions = ctx_index * tok_count + row_ids
    live_rows = ((valid_mask == 1) & (positions[None, :] < lengths[:, None])).astype(f32)
    count_local = jnp.sum(live_rows)
    gelu_fn = partial(jax.nn.gelu, approximate=True)
    attn = lax.psum(attn_part.astype(jnp.bfloat16), "tp").astype(jnp.float32)
    hidden, normed_one, inverse_one = layer_norm(tokens.astype(f32) + attn, gains[0], gains[1])
    hidden_b = hidden.astype(bf16)
    upper = jnp.einsum("std,df->stf", hidden_b, full_up, preferred_element_type=f32)
    active_f, gelu_back = jax.vjp(gelu_fn, upper)
    active = active_f.astype(bf16)
    mixed = lax.psum(
        jnp.einsum("stf,fd->std", active, full_down, preferred_element_type=f32).astype(
            jnp.bfloat16
        ),
        "tp",
    ).astype(jnp.float32)
    result, normed_two, inverse_two = layer_norm(hidden + mixed, gains[2], gains[3])
    differ = result - teacher.astype(f32)
    error_local = jnp.sum(live_rows[..., None] * differ * differ)
    error_total, live_count = lax.psum((error_local, count_local), ("fsdp", "ctx"))
    loss_value = error_total / (live_count * width)
    grad_y = 2.0 * differ * live_rows[..., None] / (live_count * width)
    gain_two_grad = jnp.sum(grad_y * normed_two, (0, 1))
    bias_two_grad = jnp.sum(grad_y, (0, 1))
    grad_two = norm_backward(grad_y, normed_two, inverse_two, gains[2])
    grad_mixed = grad_two.astype(bf16)
    grad_active = jnp.einsum("std,fd->stf", grad_mixed, full_down, preferred_element_type=f32)
    grad_upper = gelu_back(grad_active)[0].astype(bf16)
    down_grad = jnp.einsum("stf,std->fd", active, grad_mixed, preferred_element_type=f32)
    up_grad = jnp.einsum("std,stf->df", hidden_b, grad_upper, preferred_element_type=f32)
    grad_hidden = grad_two + lax.psum(
        jnp.einsum("stf,df->std", grad_upper, full_up, preferred_element_type=f32).astype(
            jnp.bfloat16
        ),
        "tp",
    ).astype(jnp.float32)
    gain_one_grad = jnp.sum(grad_hidden * normed_one, (0, 1))
    bias_one_grad = jnp.sum(grad_hidden, (0, 1))
    grad_one = norm_backward(grad_hidden, normed_one, inverse_one, gains[0])
    norm_grad = jnp.stack([gain_one_grad, bias_one_grad, gain_two_grad, bias_two_grad], 0)
    grad_attn = grad_one.astype(bf16)
    out_grad = jnp.einsum("ste,std->ed", attended, grad_attn, preferred_element_type=f32)
    grad_attended = jnp.einsum(
        "std,ed->ste", grad_attn, full_out, preferred_element_type=f32
    ).astype(bf16)
    sparse_grad = jnp.where(global_row[None, :, None], jnp.zeros_like(grad_attended), grad_attended)
    sparse_grad = sparse_grad.reshape(seqs_here, local_blocks, BLK, heads_local, HD)
    probs = jnp.exp(scores - sparse_lse)
    grad_probs = jnp.einsum(
        "sbqhd,sbkhd->sbhqk", sparse_grad, value_rows, preferred_element_type=f32
    )
    row_dot = jnp.sum(probs * grad_probs, -1, keepdims=True)
    grad_scores = (probs * (grad_probs - row_dot)).astype(bf16)
    dq_sparse = (
        jnp.einsum("sbhqk,sbkhd->sbqhd", grad_scores, key_rows, preferred_element_type=f32) * scale
    )
    dk_rows = (
        jnp.einsum("sbhqk,sbqhd->sbkhd", grad_scores, q_blocks, preferred_element_type=f32) * scale
    )
    dv_rows = jnp.einsum(
        "sbhqk,sbqhd->sbkhd", probs.astype(bf16), sparse_grad, preferred_element_type=f32
    )
    list_grads = jnp.stack(
        [
            dk_rows.reshape(seqs_here, local_blocks, 8, BLK, width_local),
            dv_rows.reshape(seqs_here, local_blocks, 8, BLK, width_local),
        ],
        4,
    )
    seq_ids = jnp.broadcast_to(jnp.arange(seqs_here, dtype=jnp.int32)[:, None, None], safe.shape)
    kv_term = (
        jnp.zeros((block_count, seqs_here, BLK, 2, width_local), f32)
        .at[safe, seq_ids]
        .add(list_grads)
    )
    head_grad = jnp.where(
        is_first, grad_attended[:, : 2 * BLK], jnp.zeros_like(grad_attended[:, : 2 * BLK])
    )
    head_grad = head_grad.reshape(seqs_here, 2 * BLK, heads_local, HD)
    wide_probs_f = jnp.exp(wide_scores - wide_lse)
    wide_dprobs = jnp.einsum("sqhd,skhd->shqk", head_grad, all_values, preferred_element_type=f32)
    wide_dot = jnp.sum(wide_probs_f * wide_dprobs, -1, keepdims=True)
    wide_dscores = (wide_probs_f * (wide_dprobs - wide_dot)).astype(bf16)
    dq_wide = (
        jnp.einsum("shqk,skhd->sqhd", wide_dscores, all_keys, preferred_element_type=f32) * scale
    )
    split_scores = wide_dscores.reshape(seqs_here, heads_local, 2 * BLK, block_count, BLK)
    split_probs = wide_probs_f.astype(bf16).reshape(
        seqs_here, heads_local, 2 * BLK, block_count, BLK
    )
    dk_wide = (
        jnp.einsum("shqnb,sqhd->nsbhd", split_scores, head_rows, preferred_element_type=f32) * scale
    )
    dv_wide = jnp.einsum("shqnb,sqhd->nsbhd", split_probs, head_grad, preferred_element_type=f32)
    kv_term = kv_term + jnp.stack(
        [
            dk_wide.reshape(block_count, seqs_here, BLK, width_local),
            dv_wide.reshape(block_count, seqs_here, BLK, width_local),
        ],
        3,
    )
    kv_grads = lax.psum_scatter(
        kv_term.astype(jnp.bfloat16), "ctx", scatter_dimension=0, tiled=True
    ).astype(jnp.float32)
    kv_grads = jnp.transpose(kv_grads, (1, 0, 2, 3, 4)).reshape(
        seqs_here, tok_count, 2, width_local
    )
    dq_total = dq_sparse.reshape(seqs_here, tok_count, width_local) + jnp.concatenate(
        [dq_wide.reshape(seqs_here, 2 * BLK, width_local), rest_zeros], 1
    )
    grad_projected = jnp.concatenate([dq_total[:, :, None, :], kv_grads], 2).astype(bf16)
    qkv_grad = jnp.einsum("std,stce->cde", tokens, grad_projected, preferred_element_type=f32)
    input_part = jnp.einsum("stce,cde->std", grad_projected, full_qkv, preferred_element_type=f32)
    input_grad = grad_one + lax.psum(input_part.astype(jnp.bfloat16), "tp").astype(jnp.float32)
    local_grads = (qkv_grad, out_grad, up_grad, down_grad, norm_grad)
    owned = (
        lax.psum_scatter(
            local_grads[0].astype(jnp.bfloat16), "fsdp", scatter_dimension=1, tiled=True
        ).astype(jnp.float32),
        lax.psum_scatter(
            local_grads[1].astype(jnp.bfloat16), "fsdp", scatter_dimension=1, tiled=True
        ).astype(jnp.float32),
        lax.psum_scatter(
            local_grads[2].astype(jnp.bfloat16), "fsdp", scatter_dimension=0, tiled=True
        ).astype(jnp.float32),
        lax.psum_scatter(
            local_grads[3].astype(jnp.bfloat16), "fsdp", scatter_dimension=1, tiled=True
        ).astype(jnp.float32),
        lax.psum_scatter(
            local_grads[4].astype(jnp.bfloat16), "fsdp", scatter_dimension=1, tiled=True
        ).astype(jnp.float32),
    )
    shards = (
        lax.psum(owned[0].astype(jnp.bfloat16), "ctx").astype(jnp.float32),
        lax.psum(owned[1].astype(jnp.bfloat16), "ctx").astype(jnp.float32),
        lax.psum(owned[2].astype(jnp.bfloat16), "ctx").astype(jnp.float32),
        lax.psum(owned[3].astype(jnp.bfloat16), "ctx").astype(jnp.float32),
        lax.psum(owned[4].astype(jnp.bfloat16), "ctx").astype(jnp.float32),
    )
    matrix_squares = sum((jnp.sum(member * member) for member in shards[:4]))
    norm_squares = jnp.where(tp_index == 0, jnp.sum(shards[4] * shards[4]), 0.0)
    squares_total = lax.psum(matrix_squares + norm_squares, ("fsdp", "tp"))
    grad_norm = jnp.sqrt(squares_total)
    factor = jnp.minimum(1.0, clip_level / (grad_norm + 1e-06))
    steps_done = step_count[0].astype(f32)
    qkv_new = adam_update(
        qkv_weight, shards[0], qkv_moment, qkv_square, factor, steps_done, rate_list[0]
    )
    out_new = adam_update(
        out_weight, shards[1], out_moment, out_square, factor, steps_done, rate_list[1]
    )
    up_new = adam_update(
        up_weight, shards[2], up_moment, up_square, factor, steps_done, rate_list[2]
    )
    down_new = adam_update(
        down_weight, shards[3], down_moment, down_square, factor, steps_done, rate_list[3]
    )
    norm_new = adam_update(
        norm_params, shards[4], norm_moment, norm_square, factor, steps_done, rate_list[4]
    )
    return (
        result.astype(bf16),
        loss_value,
        input_grad,
        grad_norm,
        qkv_new[0],
        qkv_new[1],
        qkv_new[2],
        out_new[0],
        out_new[1],
        out_new[2],
        up_new[0],
        up_new[1],
        up_new[2],
        down_new[0],
        down_new[1],
        down_new[2],
        norm_new[0],
        norm_new[1],
        norm_new[2],
    )


def remote(src, dst, send, recv, dev):
    return pltpu.make_async_remote_copy(
        src_ref=src, dst_ref=dst, send_sem=send, recv_sem=recv, device_id=dev, device_id_type=MESH
    )


def dot_nn(a, b):
    return lax.dot_general(a, b, (((1,), (0,)), ((), ())), preferred_element_type=f32)


def dot_nt(a, b):
    return lax.dot_general(a, b, (((1,), (1,)), ((), ())), preferred_element_type=f32)


def dot_tn(a, b):
    return lax.dot_general(a, b, (((0,), (0,)), ((), ())), preferred_element_type=f32)


UW = 1792


class Peers:
    def __init__(self):
        f, c, t = lax.axis_index("fsdp"), lax.axis_index("ctx"), lax.axis_index("tp")
        x, k = f // 2, f % 2
        self.f, self.c, self.t = f, c, t
        self.f_core = x * 2 + (1 - k)
        self.f_x = (1 - x) * 2 + k
        self.f_xc = (1 - x) * 2 + (1 - k)
        self.core = (self.f_core, c, t)
        self.xdev = (self.f_x, c, t)
        self.ydev = (f, 1 - c, t)

    def z(self, t):
        return (self.f, self.c, t)

    def flipped(self, d):
        x, k = self.f // 2, self.f % 2
        x = 1 - x if d // 4 else x
        k = 1 - k if d % 2 else k
        return x * 2 + k, 1 - self.c if d // 2 % 2 else self.c

    def owners(self):
        return [(d, (*self.flipped(d), self.t)) for d in range(1, 8)]

    def barrier(self, whole=False):
        sem = pltpu.get_barrier_semaphore()
        devs = [dev for _, dev in self.owners()] if whole else [self.core, self.xdev, self.ydev]
        devs += [self.z((self.t + d) % 4) for d in (1, 2, 3)]
        for dev in devs:
            pl.semaphore_signal(sem, inc=1, device_id=dev, device_id_type=MESH)
        pl.semaphore_wait(sem, len(devs))


def forward_attention_kernel(
    lengths_ref,
    tokens_ref,
    teacher_ref,
    qkv_ref,
    up_ref,
    down_ref,
    out_ref,
    norm_ref,
    blocks_ref,
    valid_ref,
    att_ref,
    u_ref,
    t_ref,
    w_ref,
    q_ref,
    k_ref,
    v_ref,
    kt_ref,
    pt_ref,
    tok_ref,
    teach_ref,
    live_ref,
    count_ref,
    upack_ref,
    qkvb_ref,
    rbt_ref,
    mask_ref,
    tally,
    vt,
    bias,
    rb,
    att_out,
    att_tok,
    loc_sem,
    w_sem,
    y_sem,
    z_send,
    z_recv,
    x_send,
    x_recv,
    yw_send,
    yw_recv,
    c_send,
    c_recv,
    h_send,
    h_recv,
    a_send,
    a_recv,
    n_sem,
):
    me = Peers()
    f, c, t = me.f, me.c, me.t
    seq = t_ref.shape[0]
    half = seq // 2
    rows_f = qkvb_ref.shape[1]
    sends = []
    qkvb_ref[...] = qkv_ref[...].astype(bf16)
    upack_ref[:, 0:768] = up_ref[...].astype(bf16)
    upack_ref[:, 768:1536] = down_ref[...].astype(bf16)
    tail = jnp.concatenate(
        [out_ref[...].T, jnp.concatenate([norm_ref[...], jnp.zeros((60, rows_f), f32)], 0).T], 1
    )
    upack_ref[:, 1536:1792] = tail.astype(bf16)
    for s in range(2):
        rbt_ref[s] = jnp.zeros((8, 128), f32)
        rbt_ref[s, 0:3, 0 : blocks_ref.shape[2]] = blocks_ref[:, s, :].astype(f32)
        mask_ref[s] = jnp.broadcast_to(valid_ref[s : s + 1, :].astype(f32), (8, half))
    spot = c * half + lax.broadcasted_iota(jnp.int32, (1, half), 1)
    found = jnp.zeros((1, half), f32)
    for s in range(2):
        found += jnp.where((valid_ref[s : s + 1, :] == 1) & (spot < lengths_ref[s]), 1.0, 0.0)
    count_ref[...] = jnp.broadcast_to(jnp.sum(found, 1, keepdims=True), (8, 128))
    me.barrier()

    def go(copy, pred=None):
        if pred is None:
            copy.start()
        else:
            pl.when(pred)(copy.start)
        sends.append((copy, pred))
    own_rows = pl.ds(pl.multiple_of(c * half, half), half)
    go(remote(tokens_ref.at[1 - c], t_ref.at[own_rows], y_sem.at[0], y_sem.at[1], me.ydev))
    go(remote(rbt_ref.at[1 - c], rb.at[c], y_sem.at[2], y_sem.at[3], me.ydev))
    go(remote(mask_ref.at[1 - c], live_ref.at[c], y_sem.at[4], y_sem.at[5], me.ydev))
    part = pl.ds(pl.multiple_of(t * 128, 128), 128)
    go(remote(teacher_ref.at[1 - c, part], teach_ref.at[c], y_sem.at[6], y_sem.at[7], me.ydev))

    def wblock(ff):
        return w_ref.at[:, pl.ds(pl.multiple_of(ff * rows_f, rows_f), rows_f), :]

    go(remote(qkvb_ref, wblock(f), w_sem.at[0], w_sem.at[1], me.xdev))
    go(remote(qkvb_ref, wblock(f), w_sem.at[2], w_sem.at[3], me.core))

    def shard(tt, ff):
        return u_ref.at[tt, pl.ds(pl.multiple_of(ff * rows_f, rows_f), rows_f), :]

    hrows = rows_f // 2

    def slab(tt, ff, h):
        return u_ref.at[tt, pl.ds(pl.multiple_of(ff * rows_f + h * hrows, hrows), hrows), :]

    def own_half(h):
        return upack_ref.at[pl.ds(pl.multiple_of(h * hrows, hrows), hrows), :]

    hs = (c, 1 - c)
    go(remote(own_half(c), slab(t, f, c), x_send.at[t], x_recv.at[t], me.xdev))
    for i in (0, 1):
        go(remote(own_half(hs[i]), slab(t, f, hs[i]), z_send.at[0, t, i], z_recv.at[t, i], me.z(t + 1)), t < 3)
        go(remote(own_half(hs[i]), slab(t, f, hs[i]), z_send.at[1, t, i], z_recv.at[t, i], me.z(t - 1)), t > 0)
    go(remote(upack_ref, shard(t, f), c_send.at[t], c_recv.at[t], me.core))

    local = [
        pltpu.make_async_copy(tokens_ref.at[c], t_ref.at[own_rows], loc_sem.at[0]),
        pltpu.make_async_copy(qkvb_ref, wblock(f), loc_sem.at[1]),
        pltpu.make_async_copy(upack_ref, shard(t, f), loc_sem.at[2]),
        pltpu.make_async_copy(teacher_ref.at[c, part], teach_ref.at[c], loc_sem.at[3]),
    ]
    for copy in local:
        copy.start()
    rb[c] = rbt_ref[c]
    live_ref[c] = mask_ref[c]

    peers = (me.core, me.xdev, me.ydev)

    def tally_send(i):
        go(remote(count_ref if i == 0 else tally.at[i + 2], tally.at[i], n_sem.at[0, i], n_sem.at[1, i], peers[i]))

    def tally_take(i):
        remote(tally.at[i], tally.at[i], n_sem.at[0, i], n_sem.at[1, i], peers[i]).wait_recv()
        tally[3 + i] = (count_ref[...] if i == 0 else tally[i + 2]) + tally[i]

    tally_send(0)

    def z_step(d):
        for tt, ok, on, nxt, way in ((t - d, t - d >= 0, t < 3, t + 1, 0), (t + d, t + d <= 3, t > 0, t - 1, 1)):
            go_on = ok & on
            for i in (0, 1):
                piece = slab(tt, f, hs[i])
                arrived = remote(piece, piece, z_send.at[way, tt, i], z_recv.at[tt, i], me.z(t))
                pl.when(ok)(arrived.wait_recv)
                go(remote(piece, piece, z_send.at[way, tt, i], z_recv.at[tt, i], me.z(nxt)), go_on)
                if i == 0:
                    go(remote(piece, piece, x_send.at[tt], x_recv.at[tt], me.xdev), ok)
            go(remote(shard(tt, f), shard(tt, f), c_send.at[tt], c_recv.at[tt], me.core), ok)

    def around(d):
        return ((t, None),) if d == 0 else ((t - d, t - d >= 0), (t + d, t + d <= 3))

    def when(ok, fn):
        if ok is None:
            fn()
        else:
            pl.when(ok)(fn)

    def x_step(d):
        for tt, ok in around(d):
            piece = slab(tt, me.f_x, c)
            when(ok, remote(piece, piece, x_send.at[tt], x_recv.at[tt], me.xdev).wait_recv)
            go(remote(piece, piece, yw_send.at[tt], yw_recv.at[tt], me.ydev), ok)
            go(remote(piece, piece, h_send.at[tt, 0], h_recv.at[tt, 0], me.core), ok)

    def y_step(d):
        for tt, ok in around(d):
            piece = slab(tt, me.f_x, 1 - c)
            when(ok, remote(piece, piece, yw_send.at[tt], yw_recv.at[tt], me.ydev).wait_recv)
            go(remote(piece, piece, h_send.at[tt, 1], h_recv.at[tt, 1], me.core), ok)
    remote(wblock(me.f_x), wblock(me.f_x), w_sem.at[0], w_sem.at[1], me.xdev).wait_recv()
    go(remote(wblock(me.f_x), wblock(me.f_x), w_sem.at[4], w_sem.at[5], me.core))
    remote(wblock(me.f_core), wblock(me.f_core), w_sem.at[2], w_sem.at[3], me.core).wait_recv()
    for copy in local[:2]:
        copy.wait()
    remote(wblock(me.f_xc), wblock(me.f_xc), w_sem.at[4], w_sem.at[5], me.core).wait_recv()

    width = q_ref.shape[0] * HD
    heads = q_ref.shape[0]

    def project(base, count):
        def step(i, carry):
            rows = pl.ds(pl.multiple_of(base + i * 256, 256), 256)
            piece = t_ref[rows, :]
            for j, ref in enumerate((q_ref, k_ref, v_ref)):
                made = dot_nn(piece, w_ref[j])
                for h in range(heads):
                    ref[h, rows, :] = made[:, h * HD : (h + 1) * HD].astype(bf16)
                if j:
                    (kt_ref if j == 1 else vt)[:, rows] = made.T.astype(bf16)
            return carry

        lax.fori_loop(0, count, step, 0)
    tally_take(0)
    tally_send(1)
    project(c * half, half // 256)
    tally_take(1)
    tally_send(2)
    x_step(0)
    z_step(1)
    other_rows = pl.ds(pl.multiple_of((1 - c) * half, half), half)
    remote(t_ref.at[other_rows], t_ref.at[other_rows], y_sem.at[0], y_sem.at[1], me.ydev).wait_recv()
    project((1 - c) * half, half // 256)
    remote(rb.at[1 - c], rb.at[1 - c], y_sem.at[2], y_sem.at[3], me.ydev).wait_recv()
    length = lengths_ref[c]
    nblk = seq // BLK
    pos_block = lax.broadcasted_iota(jnp.int32, (128, seq), 1) // BLK
    row = lax.broadcasted_iota(jnp.int32, (128, seq), 0)
    picks = dot_nn(rb[0].astype(bf16), (pos_block == row).astype(bf16)) + dot_nn(
        rb[1].astype(bf16), (pos_block == row + nblk // 2).astype(bf16)
    )
    key_block = lax.broadcasted_iota(jnp.int32, (nblk, seq), 0)
    query = lax.broadcasted_iota(jnp.int32, (nblk, seq), 1)
    own = query // BLK

    def same(a, b):
        return (a == b).astype(f32)

    times = same(key_block, 0) + same(key_block, 1) + same(key_block, own - 1)
    times += same(key_block, own) + same(key_block, own + 1)
    for j in range(3):
        times += same(key_block.astype(f32), picks[j : j + 1, :])
    times = jnp.where(query < 2 * BLK, 1.0, times)
    level = jnp.where(times > 0, jnp.log2(jnp.maximum(times, 1.0)), negative)
    for b in range(nblk):
        place = b * BLK + lax.broadcasted_iota(jnp.int32, (BLK, seq), 0)
        bias[b * BLK : (b + 1) * BLK, :] = jnp.where(
            place < length, jnp.broadcast_to(level[b : b + 1, :], (BLK, seq)), negative
        )

    factor = HD ** (-0.5) * 1.4426950408889634
    wide = 256

    def attend(h):
        def step(i, carry):
            cols = pl.ds(pl.multiple_of(i * wide, wide), wide)
            scores = dot_nt(k_ref[h], q_ref[h, cols, :]) * factor + bias[:, cols]
            top = jnp.max(scores, 0, keepdims=True)
            expo = jnp.exp2(scores - top)
            probs = (expo * (1.0 / jnp.sum(expo, 0, keepdims=True))).astype(bf16)
            pt_ref[h, :, cols] = probs
            att_out[h * HD : (h + 1) * HD, cols] = dot_nn(vt[h * HD : (h + 1) * HD, :], probs)
            return carry

        lax.fori_loop(0, seq // wide, step, 0)
    attend(0)
    x_step(1)
    z_step(2)
    attend(1)
    y_step(0)
    attend(2)
    for s in range(2):
        for tt in range(4):
            at = s * half + tt * 128
            tok_at = att_out[:, at : at + 128].T.astype(bf16)
            att_tok[s, tt] = tok_at
    for d in (1, 2, 3):
        to = (t + d) % 4
        go(remote(att_tok.at[:, to], att_ref.at[t], a_send.at[d], a_recv.at[d], me.z(to)))
    own_copy = pltpu.make_async_copy(att_tok.at[:, t], att_ref.at[t], loc_sem.at[4])
    own_copy.start()
    y_step(1)
    x_step(2)
    z_step(3)
    y_step(2)
    x_step(3)
    y_step(3)
    for s in range(2):
        tok_ref[s] = t_ref[pl.ds(pl.multiple_of(s * half + t * 128, 128), 128), :]
    for d in (1, 2, 3):
        src = (t + 4 - d) % 4
        remote(att_ref.at[src], att_ref.at[src], a_send.at[d], a_recv.at[d], me.z(src)).wait_recv()
    for tt in range(4):
        whole = shard(tt, me.f_core)
        remote(whole, whole, c_send.at[tt], c_recv.at[tt], me.core).wait_recv()
        for i in (0, 1):
            piece = slab(tt, me.f_xc, hs[i])
            remote(piece, piece, h_send.at[tt, i], h_recv.at[tt, i], me.core).wait_recv()
    there = live_ref.at[1 - c]
    remote(there, there, y_sem.at[4], y_sem.at[5], me.ydev).wait_recv()
    there = teach_ref.at[1 - c]
    remote(there, there, y_sem.at[6], y_sem.at[7], me.ydev).wait_recv()
    for copy in local[2:]:
        copy.wait()
    own_copy.wait()
    tally_take(2)
    for copy, pred in sends:
        when(pred, copy.wait_send)
    count_ref[...] = tally[5]


def forward_attention(lengths, tokens, teacher, qkv, up, down, out, norm, blocks, valid):
    seq = tokens.shape[1] * 2
    heads = qkv.shape[2] // HD
    width = heads * HD
    rows_f = qkv.shape[1]
    depth = rows_f * 4
    vm = pl.BlockSpec(memory_space=pltpu.VMEM)
    hbm = pl.BlockSpec(memory_space=pl.ANY)
    dma = pltpu.SemaphoreType.DMA
    outs = [
        ((4, 2, 128, width), bf16, vm),
        ((4, depth, UW), bf16, hbm),
        ((seq, depth), bf16, vm),
        ((3, depth, width), bf16, vm),
        ((heads, seq, HD), bf16, vm),
        ((heads, seq, HD), bf16, vm),
        ((heads, seq, HD), bf16, vm),
        ((width, seq), bf16, vm),
        ((heads, seq, seq), bf16, vm),
        ((2, 128, depth), bf16, vm),
        ((2, 128, depth), bf16, vm),
        ((2, 8, seq // 2), f32, vm),
        ((8, 128), f32, vm),
    ]
    return pl.pallas_call(
        forward_attention_kernel,
        name="forward_attention",
        out_shape=[jax.ShapeDtypeStruct(s, d) for s, d, _ in outs],
        in_specs=[pl.BlockSpec(memory_space=pltpu.SMEM), hbm, hbm, *[vm] * 7],
        out_specs=[m for _, _, m in outs],
        scratch_shapes=[
            pltpu.VMEM((rows_f, UW), bf16),
            pltpu.VMEM(qkv.shape, bf16),
            pltpu.VMEM((2, 8, 128), f32),
            pltpu.VMEM((2, 8, seq // 2), f32),
            pltpu.VMEM((6, 8, 128), f32),
            pltpu.VMEM((width, seq), bf16),
            pltpu.VMEM((seq, seq), f32),
            pltpu.VMEM((2, 8, 128), f32),
            pltpu.VMEM((width, seq), f32),
            pltpu.VMEM((2, 4, 128, width), bf16),
            dma((5,)),
            dma((6,)),
            dma((8,)),
            dma((2, 4, 2)),
            dma((4, 2)),
            dma((4,)),
            dma((4,)),
            dma((4,)),
            dma((4,)),
            dma((4,)),
            dma((4,)),
            dma((4, 2)),
            dma((4, 2)),
            dma((4,)),
            dma((4,)),
            dma((2, 3)),
        ],
        compiler_params=pltpu.CompilerParams(
            collective_id=0, has_side_effects=True, vmem_limit_bytes=VMEM_LIMIT
        ),
    )(lengths, tokens, teacher, qkv, up, down, out, norm, blocks, valid)


def column(row):
    return row.T[:, 0:1]


def add_rows(dst, a, b, step=16):
    if len(dst.shape) == 3:
        for i in range(dst.shape[0]):
            add_rows(dst.at[i], a.at[i], b.at[i], step)
        return

    def one(i, carry):
        rows = pl.ds(pl.multiple_of(i * step, step), step)
        dst[rows, :] = a[rows, :] + b[rows, :]
        return carry

    lax.fori_loop(0, dst.shape[0] // step, one, 0)


class Line:
    def __init__(self, me, go, block, send, recv):
        self.me, self.go, self.block, self.send, self.recv = me, go, block, send, recv

    def start(self):
        t = self.me.t
        mine = self.block(t)
        self.go(remote(mine, mine, self.send.at[0, t], self.recv.at[t], self.me.z(t + 1)), t < 3)
        self.go(remote(mine, mine, self.send.at[1, t], self.recv.at[t], self.me.z(t - 1)), t > 0)

    def step(self, d):
        t = self.me.t
        for tt, ok, on, nxt, way in ((t - d, t - d >= 0, t < 3, t + 1, 0), (t + d, t + d <= 3, t > 0, t - 1, 1)):
            piece = self.block(tt)
            pl.when(ok)(remote(piece, piece, self.send.at[way, tt], self.recv.at[tt], self.me.z(t)).wait_recv)
            if d < 3:
                self.go(remote(piece, piece, self.send.at[way, tt], self.recv.at[tt], self.me.z(nxt)), ok & on)


class Chain:
    def __init__(self, me, go, own, left, right, send, recv_l, recv_r):
        self.me, self.go, self.own, self.left, self.right = me, go, own, left, right
        self.send, self.recv_l, self.recv_r = send, recv_l, recv_r

    def arrived(self, tt, way):
        buf, recv = (self.left, self.recv_l) if way == 0 else (self.right, self.recv_r)
        remote(buf(tt), buf(tt), self.send.at[tt], recv.at[tt], self.me.z(self.me.t)).wait_recv()

    def pass_on(self, tt, way):
        t = self.me.t
        inner = (t > 0) if way == 0 else (t < 3)
        ahead = (tt > t) if way == 0 else (tt < t)
        buf, recv = (self.left, self.recv_l) if way == 0 else (self.right, self.recv_r)

        @pl.when(ahead & inner)
        def _():
            self.arrived(tt, way)
            add_rows(self.own(tt), self.own(tt), buf(tt))

        to = self.me.z(t + 1 if way == 0 else t - 1)
        self.go(remote(self.own(tt), buf(tt), self.send.at[tt], recv.at[tt], to), ahead)

    def end(self):
        t = self.me.t
        mine = self.own(t)

        @pl.when(t > 0)
        def _():
            self.arrived(t, 0)
            add_rows(mine, mine, self.left(t))

        @pl.when(t < 3)
        def _():
            self.arrived(t, 1)
            add_rows(mine, mine, self.right(t))


CHAIN_ORDER = ((3, 0), (0, 1), (2, 0), (1, 1), (1, 0), (2, 1))


TAIL = None
FF_COLS = 1536


def backward_kernel(names, *refs):
    r = types.SimpleNamespace(**dict(zip(names, refs, strict=True)))
    me = Peers()
    f, c, t = me.f, me.c, me.t
    x = f // 2
    k = f % 2
    depth = r.u.shape[1]
    rows_f = depth // 4
    hrows = rows_f // 2
    qrows = rows_f // 4
    seq = r.t.shape[0]
    half = seq // 2
    heads = r.q.shape[0]
    width = heads * HD
    sends = []

    def when(ok, fn):
        if ok is None:
            fn()
        else:
            pl.when(ok)(fn)

    def go(copy, pred=None):
        when(pred, copy.start)
        sends.append((copy, pred))

    def load(i, src, dst):
        copy = pltpu.make_async_copy(src, dst, r.load_sem.at[i])
        copy.start()
        return copy

    first = [load(0, r.att, r.att_v), *(load(1 + j, r.u.at[j], r.u_v.at[j]) for j in range(4))]
    me.barrier(True)

    att_v, u_v, g_v, act, slope = r.att_v, r.u_v, r.g_v, r.act, r.slope
    rows = 2 * 128
    length = r.lengths[c]
    inv_width = 1.0 / depth

    def both(ref):
        return ref[...].reshape(rows, depth).astype(f32)

    def mean(v):
        return jnp.sum(v, -1, keepdims=True) * inv_width

    def normalize(v):
        center = v - mean(v)
        inverse = lax.rsqrt(mean(center * center) + norm_eps)
        return center * inverse, inverse

    def back(up, normed, inverse, gain):
        scaled = up * gain
        return inverse * (scaled - mean(scaled) - normed * mean(scaled * normed))
    for copy in first:
        copy.wait()
    pairs = ((r.pt, r.pt_v), (r.q, r.q_v), (r.k, r.k_v), (r.v, r.v_v), (r.kt, r.kt_v), (r.w, r.w_v), (r.t, r.t_v))
    later = [load(5 + i, src, dst) for i, (src, dst) in enumerate(pairs)]
    norms = u_v[0, :, 1728:1736].astype(f32).T
    gains = [norms[i : i + 1, :] for i in range(4)]
    att = [att_v[tt].reshape(rows, width) for tt in range(4)]
    attn = dot_nt(att[0], u_v[0, :, 1536:1728])
    for tt in range(1, 4):
        attn += dot_nt(att[tt], u_v[tt, :, 1536:1728])
    normed_one, inverse_one = normalize(both(r.tok) + attn)
    hidden = normed_one * gains[0] + gains[1]
    hidden_b = hidden.astype(bf16)
    cube = 0.044715
    root = 0.7978845608028654

    def up_step(tt, mixed):
        upper = dot_nn(hidden_b, u_v[tt, :, 0:768])
        square = upper * upper
        th = jnp.tanh(root * upper * (1.0 + cube * square))
        act_t = (0.5 * upper * (1.0 + th)).astype(bf16)
        act[tt] = act_t
        bend = 0.5 * (1.0 + th) + 0.5 * upper * (1.0 - th * th) * root * (1.0 + 3.0 * cube * square)
        slope[tt] = bend.astype(bf16)
        return mixed + dot_nt(act_t, u_v[tt, :, 768:1536])
    mixed = lax.fori_loop(0, 4, up_step, jnp.zeros((rows, depth), f32))
    normed_two, inverse_two = normalize(hidden + mixed)
    result = normed_two * gains[2] + gains[3]

    r.piece[...] = result.astype(bf16).reshape(2, 128, depth)
    part = pl.ds(pl.multiple_of(t * 128, 128), 128)
    lo = r.lo
    go(remote(r.piece.at[1 - c], lo.at[c, part], r.s_sem.at[0], r.s_sem.at[1], me.ydev))
    own_lo = pltpu.make_async_copy(r.piece.at[c], lo.at[c, part], r.load_sem.at[12])
    own_lo.start()

    def lo_block(tt):
        return lo.at[:, pl.ds(pl.multiple_of(tt * 128, 128), 128), :]

    lo_line = Line(me, go, lo_block, r.lo_send, r.lo_recv)

    alive = jnp.concatenate([column(r.live[s, :, part]) for s in range(2)], 0)
    row = lax.broadcasted_iota(jnp.int32, (rows, 1), 0)
    place = jnp.where(row < 128, row, row - 128 + half) + t * 128
    live = jnp.where((alive == 1.0) & (place < length), 1.0, 0.0)
    differ = result - both(r.teach)
    weighed = differ * live
    missed = jnp.sum(jnp.sum(weighed * differ, 1, keepdims=True), 0, keepdims=True)
    grad_y = weighed * (2.0 / (r.count[0:1, 0:1] * depth))
    sums = [None] * 4
    sums[2] = jnp.sum(grad_y * normed_two, 0, keepdims=True)
    sums[3] = jnp.sum(grad_y, 0, keepdims=True)
    grad_two = back(grad_y, normed_two, inverse_two, gains[2])
    gm = grad_two.astype(bf16)
    gm_t = grad_two.T.astype(bf16)
    hidden_t = hidden.T.astype(bf16)
    there = lo.at[1 - c, part]
    remote(there, there, r.s_sem.at[0], r.s_sem.at[1], me.ydev).wait_recv()
    own_lo.wait()
    lo_line.start()

    far = 1 - x
    trio = (me.core, me.xdev, me.ydev)

    def region(ref, unit, at, n):
        rows_at = pl.ds(pl.multiple_of(at, qrows), n)
        return ref.at[:, rows_at, FF_COLS:UW] if unit is TAIL else ref.at[unit, rows_at, 0:FF_COLS]

    def g_rows(unit, ff):
        return region(g_v, unit, ff * rows_f, rows_f)

    def rc_rows(xx, unit, at=0, n=rows_f):
        return region(u_v, unit, xx * rows_f + at, n)

    def room(n):
        return lambda unit, i: region(u_v, unit, (4 + n) * hrows + i * qrows, qrows)

    xg_at, yg_at = room(0), room(1)

    def d_at(ref, unit):
        return ref.at[:, :, FF_COLS:UW] if unit is TAIL else ref.at[unit, :, 0:FF_COLS]

    def slot(unit):
        return 4 if unit is TAIL else unit

    def credit(unit):
        for j, dev in enumerate(trio):
            pl.semaphore_signal(r.free.at[j, slot(unit)], inc=1, device_id=dev, device_id_type=MESH)

    def rc_copies(unit):
        return [
            remote(g_rows(unit, xx * 2 + 1 - k), rc_rows(xx, unit), r.rc_send.at[xx, slot(unit)],
                   r.rc_recv.at[xx, slot(unit)], me.core)
            for xx in (far, x)
        ]

    def far_copies(unit):
        i = slot(unit)
        h, other = c * hrows, (1 - c) * hrows
        return [
            remote(rc_rows(far, unit, other, qrows), d_at(r.dx, unit), r.dx_send.at[i], r.dx_recv.at[i], me.xdev),
            remote(rc_rows(far, unit, other + qrows, qrows), d_at(r.dy, unit), r.dy_send.at[i], r.dy_recv.at[i], me.ydev),
            remote(rc_rows(far, unit, h, qrows), xg_at(unit, 0), r.xg_send.at[i, 0], r.xg_recv.at[i, 0], me.xdev),
        ]

    def rc_step(unit):
        pl.semaphore_wait(r.free.at[0, slot(unit)], 1)
        for copy in rc_copies(unit):
            copy.start()

    def core_step(xx, unit):
        view = rc_rows(xx, unit)
        i = slot(unit)
        remote(view, view, r.rc_send.at[xx, i], r.rc_recv.at[xx, i], me.core).wait_recv()
        add_rows(view, view, g_rows(unit, xx * 2 + k))

    def far_step(unit):
        core_step(far, unit)
        for j in (1, 2):
            pl.semaphore_wait(r.free.at[j, slot(unit)], 1)
        for copy in far_copies(unit):
            copy.start()

    def near_step(unit):
        core_step(x, unit)
        i = slot(unit)
        mine = rc_rows(x, unit, (1 - c) * hrows + qrows, qrows)
        go(remote(mine, yg_at(unit, 1), r.yg_send.at[i, 1], r.yg_recv.at[i, 1], me.ydev))

    def diag_step(unit):
        i = slot(unit)
        dx, dy = d_at(r.dx, unit), d_at(r.dy, unit)
        remote(dx, dx, r.dx_send.at[i], r.dx_recv.at[i], me.xdev).wait_recv()
        mine = rc_rows(x, unit, (1 - c) * hrows, qrows)
        add_rows(mine, mine, dx)
        go(remote(mine, yg_at(unit, 0), r.yg_send.at[i, 0], r.yg_recv.at[i, 0], me.ydev))
        remote(dy, dy, r.dy_send.at[i], r.dy_recv.at[i], me.ydev).wait_recv()
        mine = rc_rows(far, unit, c * hrows + qrows, qrows)
        add_rows(mine, mine, dy)
        go(remote(mine, xg_at(unit, 1), r.xg_send.at[i, 1], r.xg_recv.at[i, 1], me.xdev))

    def sum_step(unit):
        at = slot(unit)
        for i in (0, 1):
            xg, yg = xg_at(unit, i), yg_at(unit, i)
            mine = rc_rows(x, unit, c * hrows + i * qrows, qrows)
            remote(xg, xg, r.xg_send.at[at, i], r.xg_recv.at[at, i], me.xdev).wait_recv()
            add_rows(mine, mine, xg)
            remote(yg, yg, r.yg_send.at[at, i], r.yg_recv.at[at, i], me.ydev).wait_recv()
            add_rows(mine, mine, yg)

    def own_rows(tt):
        return u_v.at[tt, pl.ds(pl.multiple_of(x * rows_f + c * hrows, hrows), hrows), :]

    w_chain = Chain(
        me, go, own_rows, lambda tt: u_v.at[tt, pl.ds(6 * hrows, hrows), :],
        lambda tt: u_v.at[tt, pl.ds(7 * hrows, hrows), :], r.zw_send, r.zw_recv_l, r.zw_recv_r,
    )

    def turn(i):
        return ((i + 1) % 2) * (3 - i // 2) + (i % 2) * (i // 2)

    ORDER = (3, 0, 2, 1)

    def down_step(i, total):
        tt = turn(i)
        ga = dot_nn(gm, u_v[tt, :, 768:1536])
        gu = (ga * slope[tt].astype(f32)).astype(bf16)
        g_v[tt, :, 768:1536] = dot_nn(gm_t, act[tt]).astype(bf16)
        g_v[tt, :, 0:768] = dot_nn(hidden_t, gu).astype(bf16)
        total = total + dot_nt(gu, u_v[tt, :, 0:768])
        credit(tt)

        @pl.when(i >= 1)
        def _():
            rc_step(turn(i - 1))

        @pl.when(i >= 2)
        def _():
            far_step(turn(i - 2))

        return total

    grad_hidden = lax.fori_loop(0, 4, down_step, grad_two)
    rc_step(ORDER[3])
    sums[0] = jnp.sum(grad_hidden * normed_one, 0, keepdims=True)
    sums[1] = jnp.sum(grad_hidden, 0, keepdims=True)
    grad_one = back(grad_hidden, normed_one, inverse_one, gains[0])
    r.gone[...] = grad_one.reshape(2, 128, depth)
    ga = grad_one.astype(bf16)
    gatt, do_in = r.gatt, r.do_in
    for tt in range(4):
        back_t = dot_nn(ga, u_v[tt, :, 1536:1728]).astype(bf16)
        gatt[tt] = back_t.reshape(2, 128, width)
    for d in (1, 2, 3):
        to = (t + d) % 4
        go(remote(gatt.at[to], do_in.at[t], r.a_send.at[d], r.a_recv.at[d], me.z(to)))
    do_in[t] = gatt[t]
    credit(TAIL)
    far_step(ORDER[2])
    ga_t = grad_one.T.astype(bf16)
    ez, ef = r.ez, r.ef
    mine_at = f * 2 + c
    ez[t] = jnp.concatenate(sums + [jnp.broadcast_to(missed, (4, depth))], 0)
    for d in (1, 2, 3):
        go(remote(ez.at[t], ez.at[t], r.e_sem.at[0, d], r.e_sem.at[1, d], me.z((t + d) % 4)))

    def sums_on():
        for d in (1, 2, 3):
            src = ez.at[(t + 4 - d) % 4]
            remote(src, src, r.e_sem.at[0, d], r.e_sem.at[1, d], me.z(t)).wait_recv()
        ef[mine_at] = (ez[0] + ez[1]) + (ez[2] + ez[3])
        for d, dev in me.owners():
            go(remote(ef.at[mine_at], ef.at[mine_at], r.e_sem.at[0, 3 + d], r.e_sem.at[1, 3 + d], dev))

    def sums_end():
        for d, dev in me.owners():
            ff, cc = me.flipped(d)
            src = ef.at[ff * 2 + cc]
            remote(src, src, r.e_sem.at[0, 3 + d], r.e_sem.at[1, 3 + d], dev).wait_recv()
        total = ef[0]
        for i in range(1, 8):
            total += ef[i]
        r.sums[...] = total

    for tt in range(4):
        g_v[tt, :, 1536:1728] = dot_nn(ga_t, att[tt]).astype(bf16)
        g_v[tt, :, 1728:1792] = jnp.zeros((depth, UW - 1728), bf16)
    rc_step(TAIL)
    near_step(ORDER[0])
    far_step(ORDER[3])
    near_step(ORDER[1])
    lo_line.step(1)
    diag_step(ORDER[0])
    far_step(TAIL)
    near_step(ORDER[2])
    near_step(ORDER[3])
    near_step(TAIL)
    for unit in (*ORDER, TAIL):
        sends.extend((copy, None) for copy in rc_copies(unit) + far_copies(unit))
    lo_line.step(2)

    for copy in later:
        copy.wait()
    do, proj, dqt, dk, dv = r.do, r.proj, r.dqt, r.dk, r.dv
    for d in (1, 2, 3):
        src = (t + 4 - d) % 4
        remote(do_in.at[src], do_in.at[src], r.a_send.at[d], r.a_recv.at[d], me.z(src)).wait_recv()
    for s in range(2):
        for tt in range(4):
            at = s * half + tt * 128
            for h in range(heads):
                do[h, at : at + 128, :] = do_in[tt, s, :, h * HD : (h + 1) * HD]
    q_v, k_v, v_v, kt_v, pt_v, t_v, w_v = (r.q_v, r.k_v, r.v_v, r.kt_v, r.pt_v, r.t_v, r.w_v)
    scale = HD ** (-0.5)
    wide = 256

    def attend_back(h):
        dk[...] = jnp.zeros_like(dk)
        dv[...] = jnp.zeros_like(dv)

        def step(i, carry):
            cols = pl.ds(pl.multiple_of(i * wide, wide), wide)
            mine = do[h, cols, :]
            probs = pt_v[h, :, cols]
            gp = dot_nt(v_v[h], mine)
            pf = probs.astype(f32)
            mix = jnp.sum(pf * gp, 0, keepdims=True)
            gs = (pf * (gp - mix)).astype(bf16)
            dk[...] += dot_nn(gs, q_v[h, cols, :])
            dv[...] += dot_nn(probs, mine)
            dqt[h * HD : (h + 1) * HD, cols] = dot_nn(kt_v[h * HD : (h + 1) * HD, :], gs)
            return carry

        lax.fori_loop(0, seq // wide, step, 0)
        proj[1, :, h * HD : (h + 1) * HD] = (dk[...] * scale).astype(bf16)
        proj[2, :, h * HD : (h + 1) * HD] = dv[...].astype(bf16)
    attend_back(0)
    diag_step(ORDER[1])
    attend_back(1)
    diag_step(ORDER[2])
    attend_back(2)
    proj[0] = (dqt[...].T * scale).astype(bf16)
    ip = r.ip

    def rows_step(i, carry):
        at = pl.ds(pl.multiple_of(i * 128, 128), 128)
        total = dot_nt(proj[0, at, :], w_v[0])
        for j in (1, 2):
            total += dot_nt(proj[j, at, :], w_v[j])
        ip[i // 4, i % 4] = total.astype(bf16)
        return carry

    lax.fori_loop(0, seq // 128, rows_step, 0)
    def ip_chain(j, s):
        return Chain(
            me, go, lambda tt: ip.at[s, tt], lambda tt: act.at[tt, pl.ds(j * 128, 128), :], lambda tt: slope.at[tt, pl.ds(j * 128, 128), :],
            r.i_send.at[j], r.i_recv_l.at[j], r.i_recv_r.at[j],
        )

    chains = [ip_chain(0, 1 - c), ip_chain(1, c)]
    ig, igp, qg, qc, qs, fin = r.ig, r.igp, r.qg, r.qc, r.q_sem, r.fin

    def q_rows(ff):
        return qg.at[:, pl.ds(pl.multiple_of(ff * rows_f, rows_f), rows_f), :]

    def finish(j, s):
        chains[j].end()
        igp[j] = (ip[s, t].astype(f32) + r.gone[s]).astype(bf16)

    def ig_line(j, s):
        def block(tt):
            return ig.at[s, pl.ds(pl.multiple_of(tt * 128, 128), 128), :]

        return Line(me, go, block, r.ig_send.at[j], r.ig_recv.at[j])

    lines = [ig_line(0, c), ig_line(1, 1 - c)]

    def sum_pass(tt, passes):
        sum_step(tt)
        for at, way in passes:
            w_chain.pass_on(at, way)

    def q_take(i, j, dev):
        remote(qc.at[i], qc.at[i], qs.at[j], qs.at[j + 1], dev).wait_recv()

    def q_add(i, ff):
        qc[i] = qc[i] + qg[:, pl.ds(pl.multiple_of(ff * rows_f, rows_f), rows_f), :]

    for tt, way in CHAIN_ORDER[:2]:
        chains[0].pass_on(tt, way)
    diag_step(ORDER[3])
    diag_step(TAIL)
    sums_on()
    for tt, way in CHAIN_ORDER[2:]:
        chains[0].pass_on(tt, way)
    for j in range(3):
        qg[j] = dot_tn(t_v[...], proj[j]).astype(bf16)
    go(remote(q_rows(far * 2 + 1 - k), qc.at[0], qs.at[0], qs.at[1], me.core))
    go(remote(q_rows(x * 2 + 1 - k), qc.at[1], qs.at[2], qs.at[3], me.core))
    for tt, way in CHAIN_ORDER:
        chains[1].pass_on(tt, way)
    q_take(0, 0, me.core)
    q_add(0, far * 2 + k)
    go(remote(qc.at[0], qc.at[2], qs.at[4], qs.at[5], me.xdev))
    q_take(1, 2, me.core)
    q_add(1, x * 2 + k)
    finish(0, 1 - c)
    go(remote(igp.at[0], ig.at[c, part], r.s_sem.at[2], r.s_sem.at[3], me.ydev))
    lo_line.step(3)
    sum_step(TAIL)
    sum_pass(3, CHAIN_ORDER[:1])
    sum_pass(0, CHAIN_ORDER[1:2])
    finish(1, c)
    own_ig = pltpu.make_async_copy(igp.at[1], ig.at[c, part], r.load_sem.at[13])
    own_ig.start()
    own_ig.wait()
    lines[0].start()
    there = ig.at[1 - c, part]
    remote(there, there, r.s_sem.at[2], r.s_sem.at[3], me.ydev).wait_recv()
    lines[1].start()
    q_take(2, 4, me.xdev)
    qc[1] = qc[1] + qc[2]
    go(remote(qc.at[1], qc.at[3], qs.at[6], qs.at[7], me.ydev))
    sum_pass(2, ((2, 0),))
    sum_pass(1, ((1, 1), (1, 0), (2, 1)))
    lines[0].step(1)
    lines[1].step(1)
    w_chain.end()
    fin[c] = own_rows(t)[...]
    go(remote(fin.at[c], fin.at[c], r.s_sem.at[4], r.s_sem.at[5], me.ydev))
    q_take(3, 6, me.ydev)
    qsum = r.qsum
    total = jnp.zeros((1, width), f32)
    for j in range(3):
        qsum[j] = qc[1, j].astype(f32) + qc[3, j].astype(f32)
        total += jnp.sum(qsum[j] * qsum[j], 0, keepdims=True)
    total = 0.5 * jnp.sum(total, 1, keepdims=True)

    def square_step(i, carry):
        row = fin[c, pl.ds(pl.multiple_of(i * 16, 16), 16), :].astype(f32)
        return carry + jnp.sum(row * row, 0, keepdims=True)

    wide_total = lax.fori_loop(0, hrows // 16, square_step, jnp.zeros((1, UW), f32))
    total += jnp.sum(wide_total, 1, keepdims=True)
    sz, sf = r.sz, r.sf
    sz[t] = jnp.broadcast_to(total, (8, 128))
    for d in (1, 2, 3):
        go(remote(sz.at[t], sz.at[t], r.f_sem.at[0, d], r.f_sem.at[1, d], me.z((t + d) % 4)))
    lines[0].step(2)
    lines[1].step(2)
    for d in (1, 2, 3):
        src = sz.at[(t + 4 - d) % 4]
        remote(src, src, r.f_sem.at[0, d], r.f_sem.at[1, d], me.z(t)).wait_recv()
    mine = f * 2 + c
    sf[mine] = (sz[0] + sz[1]) + (sz[2] + sz[3])
    for d, dev in me.owners():
        go(remote(sf.at[mine], sf.at[mine], r.f_sem.at[0, 3 + d], r.f_sem.at[1, 3 + d], dev))
    lines[0].step(3)
    lines[1].step(3)
    remote(fin.at[1 - c], fin.at[1 - c], r.s_sem.at[4], r.s_sem.at[5], me.ydev).wait_recv()
    r.gsum[...] = fin[...].reshape(rows_f, UW)
    sums_end()
    for d, dev in me.owners():
        ff, cc = me.flipped(d)
        src = sf.at[ff * 2 + cc]
        remote(src, src, r.f_sem.at[0, 3 + d], r.f_sem.at[1, 3 + d], dev).wait_recv()
    all_sq = sf[0]
    for i in range(1, 8):
        all_sq += sf[i]
    r.squares[...] = all_sq
    for copy, pred in sends:
        when(pred, copy.wait_send)


def backward(lengths, count, att, u, tok, teach, live, q, k, v, kt, pt, tokens, w):
    depth = tok.shape[2]
    heads, seq = q.shape[:2]
    width = heads * HD
    rows_f = depth // 4
    vm = pl.BlockSpec(memory_space=pltpu.VMEM)
    smem = pl.BlockSpec(memory_space=pltpu.SMEM)
    hbm = pl.BlockSpec(memory_space=pl.ANY)
    dma = pltpu.SemaphoreType.DMA

    def vb(*shape):
        return pltpu.VMEM(shape, bf16)

    def vf(*shape):
        return pltpu.VMEM(shape, f32)

    ins = dict(
        lengths=(lengths, smem), count=(count, vm), att=(att, hbm), u=(u, hbm), tok=(tok, vm), teach=(teach, vm),
        live=(live, vm), q=(q, hbm), k=(k, hbm), v=(v, hbm), kt=(kt, hbm), pt=(pt, hbm), t=(tokens, hbm), w=(w, hbm),
    )
    outs = dict(
        lo=((2, seq // 2, depth), bf16, hbm),
        ig=((2, seq // 2, depth), bf16, hbm),
        gsum=((rows_f, UW), bf16, vm),
        qsum=((3, rows_f, width), f32, vm),
        sums=((8, depth), f32, vm),
        squares=((8, 128), f32, vm),
    )
    h, qr = rows_f // 2, rows_f // 4
    scratch = dict(
        att_v=vb(*att.shape), u_v=vb(*u.shape), pt_v=vb(*pt.shape), q_v=vb(*q.shape), k_v=vb(*k.shape), v_v=vb(*v.shape),
        kt_v=vb(*kt.shape), w_v=vb(*w.shape), t_v=vb(*tokens.shape), g_v=vb(*u.shape), act=vb(4, 256, 768),
        slope=vb(4, 256, 768), piece=vb(2, 128, depth), gone=vf(2, 128, depth), gatt=vb(*att.shape), do_in=vb(*att.shape),
        dx=vb(4, qr, UW), dy=vb(4, qr, UW),
        do=vb(heads, seq, HD), proj=vb(3, seq, width), dqt=vf(width, seq),
        dk=vf(seq, HD), dv=vf(seq, HD), ip=vb(2, 4, 128, depth),
        igp=vb(2, 128, depth), qg=vb(3, depth, width), qc=vb(4, 3, rows_f, width), fin=vb(2, h, UW),
        load_sem=dma((14,)), s_sem=dma((6,)), lo_send=dma((2, 4)), lo_recv=dma((4,)), a_send=dma((4,)), a_recv=dma((4,)),
        rc_send=dma((2, 5)), rc_recv=dma((2, 5)), dx_send=dma((5,)), dx_recv=dma((5,)), dy_send=dma((5,)),
        dy_recv=dma((5,)), xg_send=dma((5, 2)), xg_recv=dma((5, 2)), yg_send=dma((5, 2)), yg_recv=dma((5, 2)),
        zw_send=dma((4,)), zw_recv_l=dma((4,)), zw_recv_r=dma((4,)), i_send=dma((2, 4)), i_recv_l=dma((2, 4)),
        i_recv_r=dma((2, 4)), ig_send=dma((2, 2, 4)), ig_recv=dma((2, 4)), q_sem=dma((8,)), ez=vf(4, 8, depth), ef=vf(8, 8, depth),
        sz=vf(4, 8, 128), sf=vf(8, 8, 128), e_sem=dma((2, 11)), f_sem=dma((2, 11)),
        free=pltpu.SemaphoreType.REGULAR((3, 5)),
    )
    return pl.pallas_call(
        functools.partial(backward_kernel, (*ins, *outs, *scratch)),
        name="backward",
        out_shape=[jax.ShapeDtypeStruct(s, d) for s, d, _ in outs.values()],
        in_specs=[m for _, m in ins.values()],
        out_specs=[m for _, _, m in outs.values()],
        scratch_shapes=list(scratch.values()),
        compiler_params=pltpu.CompilerParams(
            collective_id=1, has_side_effects=True, vmem_limit_bytes=60 * 2**20
        ),
    )(*(a for a, _ in ins.values()))


def update_kernel(names, *refs):
    r = types.SimpleNamespace(**dict(zip(names, refs, strict=True)))
    f = lax.axis_index("fsdp")
    copy = pltpu.make_async_copy(r.lo, r.held, r.sem.at[0])
    copy.start()
    depth = r.sums.shape[1]
    rows_f = depth // 4
    sums = r.sums[0:4, :]
    total = r.squares[0:1, 0:1] + jnp.sum(jnp.sum(sums * sums, 1, keepdims=True), 0, keepdims=True)
    norm = jnp.sqrt(total)
    factor = jnp.minimum(1.0, clip_level / (norm + 1e-06))
    r.norm[...] = norm
    r.loss[...] = r.sums[4:5, 0:1] / (r.count[0:1, 0:1] * depth)
    steps = jnp.full((1, 1), r.steps[0]).astype(f32)
    one = 1.0 / (1.0 - jnp.exp(steps * -0.10536051565782628))
    two = 1.0 / (1.0 - jnp.exp(steps * -0.0010005003335835335))

    def move(name, grad, at, rate):
        clipped = grad * factor
        new_moment = beta_one * getattr(r, name + "_m")[at] + (1.0 - beta_one) * clipped
        new_square = beta_two * getattr(r, name + "_s")[at] + (1.0 - beta_two) * clipped * clipped
        weight = getattr(r, name + "_w")[at]
        step = new_moment * one / (jnp.sqrt(new_square * two) + adam_eps) + decay_rate * weight
        getattr(r, name + "_w_new")[at] = weight - rate * step
        getattr(r, name + "_m_new")[at] = new_moment
        getattr(r, name + "_s_new")[at] = new_square

    gsum = r.gsum

    def rows_step(i, carry):
        rows = pl.ds(pl.multiple_of(i * 16, 16), 16)
        move("up", gsum[rows, 0:768].astype(f32), (rows, slice(None)), rate_list[2])
        move("down", gsum[rows, 768:1536].astype(f32), (rows, slice(None)), rate_list[3])
        for j in range(3):
            move("qkv", r.qsum[j, rows, :], (j, rows, slice(None)), rate_list[0])
        return carry

    lax.fori_loop(0, rows_f // 16, rows_step, 0)
    move("out", gsum[:, 1536:1728].astype(f32).T, (slice(None), slice(None)), rate_list[1])
    mine = sums[:, 0:rows_f]
    for i in range(1, 4):
        mine = jnp.where(f == i, sums[:, i * rows_f : (i + 1) * rows_f], mine)
    move("norm", mine, (slice(None), slice(None)), rate_list[4])

    def cast_step(i, carry):
        rows = pl.ds(pl.multiple_of(i * 64, 64), 64)
        for s in range(2):
            r.input_grad[s, rows, :] = r.ig[s, rows, :].astype(f32)
        return carry

    copy.wait()
    copy = pltpu.make_async_copy(r.held, r.layer_out, r.sem.at[1])
    copy.start()
    lax.fori_loop(0, r.ig.shape[1] // 64, cast_step, 0)
    copy.wait()


def update(steps, lo, ig, gsum, qsum, sums, squares, count, state):
    vm = pl.BlockSpec(memory_space=pltpu.VMEM)
    smem = pl.BlockSpec(memory_space=pltpu.SMEM)
    hbm = pl.BlockSpec(memory_space=pl.ANY)
    ins = dict(
        steps=(steps, smem), lo=(lo, hbm), ig=(ig, vm), gsum=(gsum, vm), qsum=(qsum, vm), sums=(sums, vm),
        squares=(squares, vm), count=(count, vm),
    )
    outs = dict(
        layer_out=(jax.ShapeDtypeStruct(lo.shape, bf16), hbm),
        loss=(jax.ShapeDtypeStruct((1, 1), f32), vm),
        input_grad=(jax.ShapeDtypeStruct(ig.shape, f32), vm),
        norm=(jax.ShapeDtypeStruct((1, 1), f32), vm),
    )
    for name, group in state.items():
        for kind, array in zip("wms", group):
            ins[f"{name}_{kind}"] = (array, vm)
            outs[f"{name}_{kind}_new"] = (jax.ShapeDtypeStruct(array.shape, f32), vm)
    return pl.pallas_call(
        functools.partial(update_kernel, (*ins, *outs, "held", "sem")),
        name="update",
        out_shape=[shape for shape, _ in outs.values()],
        in_specs=[m for _, m in ins.values()],
        out_specs=[m for _, m in outs.values()],
        scratch_shapes=[pltpu.VMEM(lo.shape, bf16), pltpu.SemaphoreType.DMA((2,))],
        compiler_params=pltpu.CompilerParams(vmem_limit_bytes=50 * 2**20),
    )(*(a for a, _ in ins.values()))


def body_swapped(
    tokens,
    teacher,
    lengths,
    valid_mask,
    random_blocks,
    step_count,
    qkv_weight,
    out_weight,
    up_weight,
    down_weight,
    norm_params,
    qkv_moment,
    qkv_square,
    out_moment,
    out_square,
    up_moment,
    up_square,
    down_moment,
    down_square,
    norm_moment,
    norm_square,
):
    blocks = jnp.transpose(random_blocks, (2, 0, 1))
    att, u, tk, w, q, k, v, kt, pt, tok, teach, live, count = forward_attention(
        lengths, tokens, teacher, qkv_weight, up_weight, down_weight.T, out_weight, norm_params, blocks, valid_mask
    )
    lo, ig, gsum, qsum, sums, squares = backward(lengths, count, att, u, tok, teach, live, q, k, v, kt, pt, tk, w)
    state = dict(
        qkv=(qkv_weight, qkv_moment, qkv_square),
        out=(out_weight, out_moment, out_square),
        up=(up_weight, up_moment, up_square),
        down=(down_weight.T, down_moment.T, down_square.T),
        norm=(norm_params, norm_moment, norm_square),
    )
    layer_out, loss, input_grad, grad_norm, *new = update(
        step_count, lo, ig, gsum, qsum, sums, squares, count, state
    )
    new[9:12] = [v.T for v in new[9:12]]
    return (layer_out, loss.reshape(()), input_grad, grad_norm.reshape(()), *new)


def solution(mesh):
    in_specs = (
        P("fsdp", "ctx", None),
        P("fsdp", "ctx", None),
        P("fsdp"),
        P("fsdp", "ctx"),
        P("fsdp", "ctx", None),
        P(),
        P(None, "fsdp", "tp"),
        P("tp", "fsdp"),
        P("fsdp", "tp"),
        P("tp", "fsdp"),
        P(None, "fsdp"),
        P(None, "fsdp", "tp"),
        P(None, "fsdp", "tp"),
        P("tp", "fsdp"),
        P("tp", "fsdp"),
        P("fsdp", "tp"),
        P("fsdp", "tp"),
        P("tp", "fsdp"),
        P("tp", "fsdp"),
        P(None, "fsdp"),
        P(None, "fsdp"),
    )
    out_specs = (
        P("fsdp", "ctx", None),
        P(),
        P("fsdp", "ctx", None),
        P(),
        P(None, "fsdp", "tp"),
        P(None, "fsdp", "tp"),
        P(None, "fsdp", "tp"),
        P("tp", "fsdp"),
        P("tp", "fsdp"),
        P("tp", "fsdp"),
        P("fsdp", "tp"),
        P("fsdp", "tp"),
        P("fsdp", "tp"),
        P("tp", "fsdp"),
        P("tp", "fsdp"),
        P("tp", "fsdp"),
        P(None, "fsdp"),
        P(None, "fsdp"),
        P(None, "fsdp"),
    )
    sizes = dict(mesh.shape)
    small = sizes == {"fsdp": 4, "ctx": 2, "tp": 4}
    body = body_swapped if small else body_general
    return jax.shard_map(body, mesh=mesh, in_specs=in_specs, out_specs=out_specs, check_vma=False)
```

```python
import functools
import types
from functools import partial

import jax
import jax.numpy as jnp
from jax import lax
from jax.experimental import pallas as pl
from jax.experimental.pallas import tpu as pltpu
from jax.sharding import PartitionSpec as P

HD = 64
BLK = 64
MESH = pl.DeviceIdType.MESH
f32 = jnp.float32
bf16 = jnp.bfloat16

norm_eps = 1e-06
beta_one = 0.9
beta_two = 0.999
adam_eps = 1e-08
decay_rate = 0.01
clip_level = 0.001
rate_list = (0.04, 0.4, 0.04, 0.02, 0.2)
negative = -1e30
VMEM_LIMIT = 58 * 2**20


def layer_norm(values, gain, shift):
    center = values - jnp.mean(values, -1, keepdims=True)
    inverse = lax.rsqrt(jnp.mean(center * center, -1, keepdims=True) + norm_eps)
    normed = center * inverse
    return (normed * gain + shift, normed, inverse)


def norm_backward(upstream, normed, inverse, gain):
    scaled = upstream * gain
    return inverse * (
        scaled
        - jnp.mean(scaled, -1, keepdims=True)
        - normed * jnp.mean(scaled * normed, -1, keepdims=True)
    )


def adam_update(weight, gradient, moment, square, factor, steps_done, rate):
    clipped = gradient * factor
    new_moment = beta_one * moment + (1.0 - beta_one) * clipped
    new_square = beta_two * square + (1.0 - beta_two) * clipped * clipped
    corrected = new_moment / (1.0 - beta_one**steps_done)
    scaled = new_square / (1.0 - beta_two**steps_done)
    new_weight = weight - rate * (corrected / (jnp.sqrt(scaled) + adam_eps) + decay_rate * weight)
    return (new_weight, new_moment, new_square)


def body_general(
    tokens,
    teacher,
    lengths,
    valid_mask,
    random_blocks,
    step_count,
    qkv_weight,
    out_weight,
    up_weight,
    down_weight,
    norm_params,
    qkv_moment,
    qkv_square,
    out_moment,
    out_square,
    up_moment,
    up_square,
    down_moment,
    down_square,
    norm_moment,
    norm_square,
):
    ctx_index = lax.axis_index("ctx")
    ctx_count = lax.axis_size("ctx")
    tp_index = lax.axis_index("tp")
    seqs_here, tok_count, width = tokens.shape
    local_blocks = tok_count // BLK
    block_count = local_blocks * ctx_count
    seq_len = tok_count * ctx_count
    width_local = qkv_weight.shape[2]
    heads_local = width_local // HD
    scale = HD ** (-0.5)
    full_qkv, full_out, full_up, full_down, full_norms = (
        lax.all_gather(qkv_weight.astype(bf16), "fsdp", axis=1, tiled=True),
        lax.all_gather(out_weight.astype(bf16), "fsdp", axis=1, tiled=True),
        lax.all_gather(up_weight.astype(bf16), "fsdp", axis=0, tiled=True),
        lax.all_gather(down_weight.astype(bf16), "fsdp", axis=1, tiled=True),
        lax.all_gather(norm_params.astype(bf16), "fsdp", axis=1, tiled=True),
    )
    gains = full_norms.astype(f32)
    projected = jnp.einsum("std,cde->stce", tokens, full_qkv, preferred_element_type=f32).astype(
        bf16
    )
    queries = projected[:, :, 0, :]
    kv_local = projected[:, :, 1:, :]
    gathered = lax.all_gather(kv_local, "ctx", axis=1, tiled=True)
    own_blocks = ctx_index * local_blocks + jnp.arange(local_blocks, dtype=jnp.int32)
    zero_row = own_blocks * 0
    window = jnp.stack([zero_row, zero_row + 1, own_blocks - 1, own_blocks, own_blocks + 1], -1)
    listed = jnp.concatenate(
        [jnp.broadcast_to(window[None], (seqs_here, local_blocks, 5)), random_blocks], -1
    )
    inside = (listed >= 0) & (listed < block_count)
    safe = jnp.clip(listed, 0, block_count - 1)
    key_pos = safe[..., None] * BLK + jnp.arange(BLK, dtype=jnp.int32)
    counted = (inside[..., None] & (key_pos < lengths[:, None, None, None])).reshape(
        seqs_here, local_blocks, 8 * BLK
    )
    key_live = jnp.arange(seq_len, dtype=jnp.int32)[None, :] < lengths[:, None]
    q_blocks = queries.reshape(seqs_here, local_blocks, BLK, heads_local, HD)
    head_rows = queries[:, : 2 * BLK].reshape(seqs_here, 2 * BLK, heads_local, HD)
    blocked = gathered.reshape(seqs_here, block_count, BLK, 2, width_local)
    flat = blocked.reshape(seqs_here * block_count, BLK, 2, width_local)
    offset = jnp.arange(seqs_here, dtype=jnp.int32)[:, None, None] * block_count
    picked = lax.map(
        lambda at: lax.dynamic_index_in_dim(flat, at, 0, keepdims=False), (safe + offset).reshape(-1)
    ).reshape(seqs_here, local_blocks, 8, BLK, 2, width_local)
    key_rows = picked[..., 0, :].reshape(seqs_here, local_blocks, 8 * BLK, heads_local, HD)
    value_rows = picked[..., 1, :].reshape(seqs_here, local_blocks, 8 * BLK, heads_local, HD)
    scores = (
        jnp.einsum("sbqhd,sbkhd->sbhqk", q_blocks, key_rows, preferred_element_type=f32) * scale
    )
    scores = jnp.where(counted[:, :, None, None, :], scores, negative)
    all_keys = gathered[:, :, 0, :].reshape(seqs_here, seq_len, heads_local, HD)
    all_values = gathered[:, :, 1, :].reshape(seqs_here, seq_len, heads_local, HD)
    wide_scores = (
        jnp.einsum("sqhd,skhd->shqk", head_rows, all_keys, preferred_element_type=f32) * scale
    )
    wide_scores = jnp.where(key_live[:, None, None, :], wide_scores, negative)
    top_value = jnp.max(scores, -1, keepdims=True)
    expo = jnp.exp(scores - top_value)
    summed = jnp.sum(expo, -1, keepdims=True)
    sparse_lse = top_value + jnp.log(summed)
    probs_b = (expo / summed).astype(bf16)
    sparse_out = jnp.einsum(
        "sbhqk,sbkhd->sbqhd", probs_b, value_rows, preferred_element_type=f32
    ).reshape(seqs_here, tok_count, width_local)
    wide_top = jnp.max(wide_scores, -1, keepdims=True)
    wide_expo = jnp.exp(wide_scores - wide_top)
    wide_sum = jnp.sum(wide_expo, -1, keepdims=True)
    wide_lse = wide_top + jnp.log(wide_sum)
    wide_probs = (wide_expo / wide_sum).astype(bf16)
    wide_out = jnp.einsum(
        "shqk,skhd->sqhd", wide_probs, all_values, preferred_element_type=f32
    ).reshape(seqs_here, 2 * BLK, width_local)
    is_first = ctx_index == 0
    row_ids = jnp.arange(tok_count, dtype=jnp.int32)
    global_row = (row_ids < 2 * BLK) & is_first
    rest_zeros = jnp.zeros((seqs_here, tok_count - 2 * BLK, width_local), f32)
    padded_wide = jnp.concatenate([wide_out, rest_zeros], 1)
    attended = jnp.where(global_row[None, :, None], padded_wide, sparse_out).astype(bf16)
    attn_part = jnp.einsum("ste,ed->std", attended, full_out, preferred_element_type=f32)
    positions = ctx_index * tok_count + row_ids
    live_rows = ((valid_mask == 1) & (positions[None, :] < lengths[:, None])).astype(f32)
    count_local = jnp.sum(live_rows)
    gelu_fn = partial(jax.nn.gelu, approximate=True)
    attn = lax.psum(attn_part.astype(jnp.bfloat16), "tp").astype(jnp.float32)
    hidden, normed_one, inverse_one = layer_norm(tokens.astype(f32) + attn, gains[0], gains[1])
    hidden_b = hidden.astype(bf16)
    upper = jnp.einsum("std,df->stf", hidden_b, full_up, preferred_element_type=f32)
    active_f, gelu_back = jax.vjp(gelu_fn, upper)
    active = active_f.astype(bf16)
    mixed = lax.psum(
        jnp.einsum("stf,fd->std", active, full_down, preferred_element_type=f32).astype(
            jnp.bfloat16
        ),
        "tp",
    ).astype(jnp.float32)
    result, normed_two, inverse_two = layer_norm(hidden + mixed, gains[2], gains[3])
    differ = result - teacher.astype(f32)
    error_local = jnp.sum(live_rows[..., None] * differ * differ)
    error_total, live_count = lax.psum((error_local, count_local), ("fsdp", "ctx"))
    loss_value = error_total / (live_count * width)
    grad_y = 2.0 * differ * live_rows[..., None] / (live_count * width)
    gain_two_grad = jnp.sum(grad_y * normed_two, (0, 1))
    bias_two_grad = jnp.sum(grad_y, (0, 1))
    grad_two = norm_backward(grad_y, normed_two, inverse_two, gains[2])
    grad_mixed = grad_two.astype(bf16)
    grad_active = jnp.einsum("std,fd->stf", grad_mixed, full_down, preferred_element_type=f32)
    grad_upper = gelu_back(grad_active)[0].astype(bf16)
    down_grad = jnp.einsum("stf,std->fd", active, grad_mixed, preferred_element_type=f32)
    up_grad = jnp.einsum("std,stf->df", hidden_b, grad_upper, preferred_element_type=f32)
    grad_hidden = grad_two + lax.psum(
        jnp.einsum("stf,df->std", grad_upper, full_up, preferred_element_type=f32).astype(
            jnp.bfloat16
        ),
        "tp",
    ).astype(jnp.float32)
    gain_one_grad = jnp.sum(grad_hidden * normed_one, (0, 1))
    bias_one_grad = jnp.sum(grad_hidden, (0, 1))
    grad_one = norm_backward(grad_hidden, normed_one, inverse_one, gains[0])
    norm_grad = jnp.stack([gain_one_grad, bias_one_grad, gain_two_grad, bias_two_grad], 0)
    grad_attn = grad_one.astype(bf16)
    out_grad = jnp.einsum("ste,std->ed", attended, grad_attn, preferred_element_type=f32)
    grad_attended = jnp.einsum(
        "std,ed->ste", grad_attn, full_out, preferred_element_type=f32
    ).astype(bf16)
    sparse_grad = jnp.where(global_row[None, :, None], jnp.zeros_like(grad_attended), grad_attended)
    sparse_grad = sparse_grad.reshape(seqs_here, local_blocks, BLK, heads_local, HD)
    probs = jnp.exp(scores - sparse_lse)
    grad_probs = jnp.einsum(
        "sbqhd,sbkhd->sbhqk", sparse_grad, value_rows, preferred_element_type=f32
    )
    row_dot = jnp.sum(probs * grad_probs, -1, keepdims=True)
    grad_scores = (probs * (grad_probs - row_dot)).astype(bf16)
    dq_sparse = (
        jnp.einsum("sbhqk,sbkhd->sbqhd", grad_scores, key_rows, preferred_element_type=f32) * scale
    )
    dk_rows = (
        jnp.einsum("sbhqk,sbqhd->sbkhd", grad_scores, q_blocks, preferred_element_type=f32) * scale
    )
    dv_rows = jnp.einsum(
        "sbhqk,sbqhd->sbkhd", probs.astype(bf16), sparse_grad, preferred_element_type=f32
    )
    list_grads = jnp.stack(
        [
            dk_rows.reshape(seqs_here, local_blocks, 8, BLK, width_local),
            dv_rows.reshape(seqs_here, local_blocks, 8, BLK, width_local),
        ],
        4,
    )
    seq_ids = jnp.broadcast_to(jnp.arange(seqs_here, dtype=jnp.int32)[:, None, None], safe.shape)
    kv_term = (
        jnp.zeros((block_count, seqs_here, BLK, 2, width_local), f32)
        .at[safe, seq_ids]
        .add(list_grads)
    )
    head_grad = jnp.where(
        is_first, grad_attended[:, : 2 * BLK], jnp.zeros_like(grad_attended[:, : 2 * BLK])
    )
    head_grad = head_grad.reshape(seqs_here, 2 * BLK, heads_local, HD)
    wide_probs_f = jnp.exp(wide_scores - wide_lse)
    wide_dprobs = jnp.einsum("sqhd,skhd->shqk", head_grad, all_values, preferred_element_type=f32)
    wide_dot = jnp.sum(wide_probs_f * wide_dprobs, -1, keepdims=True)
    wide_dscores = (wide_probs_f * (wide_dprobs - wide_dot)).astype(bf16)
    dq_wide = (
        jnp.einsum("shqk,skhd->sqhd", wide_dscores, all_keys, preferred_element_type=f32) * scale
    )
    split_scores = wide_dscores.reshape(seqs_here, heads_local, 2 * BLK, block_count, BLK)
    split_probs = wide_probs_f.astype(bf16).reshape(
        seqs_here, heads_local, 2 * BLK, block_count, BLK
    )
    dk_wide = (
        jnp.einsum("shqnb,sqhd->nsbhd", split_scores, head_rows, preferred_element_type=f32) * scale
    )
    dv_wide = jnp.einsum("shqnb,sqhd->nsbhd", split_probs, head_grad, preferred_element_type=f32)
    kv_term = kv_term + jnp.stack(
        [
            dk_wide.reshape(block_count, seqs_here, BLK, width_local),
            dv_wide.reshape(block_count, seqs_here, BLK, width_local),
        ],
        3,
    )
    kv_grads = lax.psum_scatter(
        kv_term.astype(jnp.bfloat16), "ctx", scatter_dimension=0, tiled=True
    ).astype(jnp.float32)
    kv_grads = jnp.transpose(kv_grads, (1, 0, 2, 3, 4)).reshape(
        seqs_here, tok_count, 2, width_local
    )
    dq_total = dq_sparse.reshape(seqs_here, tok_count, width_local) + jnp.concatenate(
        [dq_wide.reshape(seqs_here, 2 * BLK, width_local), rest_zeros], 1
    )
    grad_projected = jnp.concatenate([dq_total[:, :, None, :], kv_grads], 2).astype(bf16)
    qkv_grad = jnp.einsum("std,stce->cde", tokens, grad_projected, preferred_element_type=f32)
    input_part = jnp.einsum("stce,cde->std", grad_projected, full_qkv, preferred_element_type=f32)
    input_grad = grad_one + lax.psum(input_part.astype(jnp.bfloat16), "tp").astype(jnp.float32)
    local_grads = (qkv_grad, out_grad, up_grad, down_grad, norm_grad)
    owned = (
        lax.psum_scatter(
            local_grads[0].astype(jnp.bfloat16), "fsdp", scatter_dimension=1, tiled=True
        ).astype(jnp.float32),
        lax.psum_scatter(
            local_grads[1].astype(jnp.bfloat16), "fsdp", scatter_dimension=1, tiled=True
        ).astype(jnp.float32),
        lax.psum_scatter(
            local_grads[2].astype(jnp.bfloat16), "fsdp", scatter_dimension=0, tiled=True
        ).astype(jnp.float32),
        lax.psum_scatter(
            local_grads[3].astype(jnp.bfloat16), "fsdp", scatter_dimension=1, tiled=True
        ).astype(jnp.float32),
        lax.psum_scatter(
            local_grads[4].astype(jnp.bfloat16), "fsdp", scatter_dimension=1, tiled=True
        ).astype(jnp.float32),
    )
    shards = (
        lax.psum(owned[0].astype(jnp.bfloat16), "ctx").astype(jnp.float32),
        lax.psum(owned[1].astype(jnp.bfloat16), "ctx").astype(jnp.float32),
        lax.psum(owned[2].astype(jnp.bfloat16), "ctx").astype(jnp.float32),
        lax.psum(owned[3].astype(jnp.bfloat16), "ctx").astype(jnp.float32),
        lax.psum(owned[4].astype(jnp.bfloat16), "ctx").astype(jnp.float32),
    )
    matrix_squares = sum((jnp.sum(member * member) for member in shards[:4]))
    norm_squares = jnp.where(tp_index == 0, jnp.sum(shards[4] * shards[4]), 0.0)
    squares_total = lax.psum(matrix_squares + norm_squares, ("fsdp", "tp"))
    grad_norm = jnp.sqrt(squares_total)
    factor = jnp.minimum(1.0, clip_level / (grad_norm + 1e-06))
    steps_done = step_count[0].astype(f32)
    qkv_new = adam_update(
        qkv_weight, shards[0], qkv_moment, qkv_square, factor, steps_done, rate_list[0]
    )
    out_new = adam_update(
        out_weight, shards[1], out_moment, out_square, factor, steps_done, rate_list[1]
    )
    up_new = adam_update(
        up_weight, shards[2], up_moment, up_square, factor, steps_done, rate_list[2]
    )
    down_new = adam_update(
        down_weight, shards[3], down_moment, down_square, factor, steps_done, rate_list[3]
    )
    norm_new = adam_update(
        norm_params, shards[4], norm_moment, norm_square, factor, steps_done, rate_list[4]
    )
    return (
        result.astype(bf16),
        loss_value,
        input_grad,
        grad_norm,
        qkv_new[0],
        qkv_new[1],
        qkv_new[2],
        out_new[0],
        out_new[1],
        out_new[2],
        up_new[0],
        up_new[1],
        up_new[2],
        down_new[0],
        down_new[1],
        down_new[2],
        norm_new[0],
        norm_new[1],
        norm_new[2],
    )


def remote(src, dst, send, recv, dev):
    return pltpu.make_async_remote_copy(
        src_ref=src, dst_ref=dst, send_sem=send, recv_sem=recv, device_id=dev, device_id_type=MESH
    )


def dot_nn(a, b):
    return lax.dot_general(a, b, (((1,), (0,)), ((), ())), preferred_element_type=f32)


def dot_nt(a, b):
    return lax.dot_general(a, b, (((1,), (1,)), ((), ())), preferred_element_type=f32)


def dot_tn(a, b):
    return lax.dot_general(a, b, (((0,), (0,)), ((), ())), preferred_element_type=f32)


UW = 1792


class Peers:
    def __init__(self):
        f, c, t = lax.axis_index("fsdp"), lax.axis_index("ctx"), lax.axis_index("tp")
        x, k = f // 2, f % 2
        self.f, self.c, self.t = f, c, t
        self.f_core = x * 2 + (1 - k)
        self.f_x = (1 - x) * 2 + k
        self.f_xc = (1 - x) * 2 + (1 - k)
        self.core = (self.f_core, c, t)
        self.xdev = (self.f_x, c, t)
        self.ydev = (f, 1 - c, t)

    def z(self, t):
        return (self.f, self.c, t)

    def flipped(self, d):
        x, k = self.f // 2, self.f % 2
        x = 1 - x if d // 4 else x
        k = 1 - k if d % 2 else k
        return x * 2 + k, 1 - self.c if d // 2 % 2 else self.c

    def owners(self):
        return [(d, (*self.flipped(d), self.t)) for d in range(1, 8)]

    def barrier(self, whole=False):
        sem = pltpu.get_barrier_semaphore()
        devs = [dev for _, dev in self.owners()] if whole else [self.core, self.xdev, self.ydev]
        devs += [self.z((self.t + d) % 4) for d in (1, 2, 3)]
        for dev in devs:
            pl.semaphore_signal(sem, inc=1, device_id=dev, device_id_type=MESH)
        pl.semaphore_wait(sem, len(devs))


def column(row):
    return row.T[:, 0:1]


def add_rows(dst, a, b, step=16):
    if len(dst.shape) == 3:
        for i in range(dst.shape[0]):
            add_rows(dst.at[i], a.at[i], b.at[i], step)
        return

    def one(i, carry):
        rows = pl.ds(pl.multiple_of(i * step, step), step)
        dst[rows, :] = a[rows, :] + b[rows, :]
        return carry

    lax.fori_loop(0, dst.shape[0] // step, one, 0)


class Line:
    def __init__(self, me, go, block, send, recv):
        self.me, self.go, self.block, self.send, self.recv = me, go, block, send, recv

    def first(self, src=None):
        t = self.me.t
        mine = self.block(t)
        src = mine if src is None else src
        return [
            (remote(src, mine, self.send.at[0, t], self.recv.at[t], self.me.z(t + 1)), t < 3),
            (remote(src, mine, self.send.at[1, t], self.recv.at[t], self.me.z(t - 1)), t > 0),
        ]

    def start(self, src=None):
        for copy, pred in self.first(src):
            self.go(copy, pred)

    def step(self, d):
        t = self.me.t
        for tt, ok, on, nxt, way in ((t - d, t - d >= 0, t < 3, t + 1, 0), (t + d, t + d <= 3, t > 0, t - 1, 1)):
            piece = self.block(tt)
            pl.when(ok)(remote(piece, piece, self.send.at[way, tt], self.recv.at[tt], self.me.z(t)).wait_recv)
            if d < 3:
                self.go(remote(piece, piece, self.send.at[way, tt], self.recv.at[tt], self.me.z(nxt)), ok & on)


class Chain:
    def __init__(self, me, go, own, left, right, send, recv_l, recv_r):
        self.me, self.go, self.own, self.left, self.right = me, go, own, left, right
        self.send, self.recv_l, self.recv_r = send, recv_l, recv_r

    def arrived(self, tt, way):
        buf, recv = (self.left, self.recv_l) if way == 0 else (self.right, self.recv_r)
        remote(buf(tt), buf(tt), self.send.at[tt], recv.at[tt], self.me.z(self.me.t)).wait_recv()

    def pass_on(self, tt, way):
        t = self.me.t
        inner = (t > 0) if way == 0 else (t < 3)
        ahead = (tt > t) if way == 0 else (tt < t)
        buf, recv = (self.left, self.recv_l) if way == 0 else (self.right, self.recv_r)

        @pl.when(ahead & inner)
        def _():
            self.arrived(tt, way)
            add_rows(self.own(tt), self.own(tt), buf(tt))

        to = self.me.z(t + 1 if way == 0 else t - 1)
        self.go(remote(self.own(tt), buf(tt), self.send.at[tt], recv.at[tt], to), ahead)

    def end(self):
        t = self.me.t
        mine = self.own(t)

        @pl.when(t > 0)
        def _():
            self.arrived(t, 0)
            add_rows(mine, mine, self.left(t))

        @pl.when(t < 3)
        def _():
            self.arrived(t, 1)
            add_rows(mine, mine, self.right(t))


CHAIN_ORDER = ((3, 0), (0, 1), (2, 0), (1, 1), (1, 0), (2, 1))


TAIL = None
FF_COLS = 1536


def train_kernel(names, *refs):
    r = types.SimpleNamespace(**dict(zip(names, refs, strict=True)))
    me = Peers()
    f, c, t = me.f, me.c, me.t
    seq = r.t_v.shape[0]
    half = seq // 2
    rows_f = r.qkvb.shape[1]
    sends = []
    heads = r.q_v.shape[0]
    width = heads * HD
    depth = rows_f * 4
    hrows = rows_f // 2
    qrows = rows_f // 4
    r.qkvb[...] = r.qkv[...].astype(bf16)
    r.upack[:, 0:768] = r.up[...].astype(bf16)
    r.upack[:, 768:1536] = r.down[...].astype(bf16)
    tail = jnp.concatenate(
        [r.out[...].T, jnp.concatenate([r.norm[...], jnp.zeros((60, rows_f), f32)], 0).T], 1
    )
    r.upack[:, 1536:1792] = tail.astype(bf16)
    for s in range(2):
        r.rbt[s] = jnp.zeros((8, 128), f32)
        r.rbt[s, 0:3, 0 : r.blocks.shape[2]] = r.blocks[:, s, :].astype(f32)
        r.mask[s] = jnp.broadcast_to(r.valid[s : s + 1, :].astype(f32), (8, half))
    spot = c * half + lax.broadcasted_iota(jnp.int32, (1, half), 1)
    found = jnp.zeros((1, half), f32)
    for s in range(2):
        found += jnp.where((r.valid[s : s + 1, :] == 1) & (spot < r.lengths[s]), 1.0, 0.0)
    r.count[...] = jnp.broadcast_to(jnp.sum(found, 1, keepdims=True), (8, 128))
    me.barrier(True)

    def go(copy, pred=None):
        if pred is None:
            copy.start()
        else:
            pl.when(pred)(copy.start)
        sends.append((copy, pred))
    own_rows = pl.ds(pl.multiple_of(c * half, half), half)
    go(remote(r.tokens.at[1 - c], r.t_v.at[own_rows], r.y_sem.at[0], r.y_sem.at[1], me.ydev))
    go(remote(r.rbt.at[1 - c], r.rb.at[c], r.y_sem.at[2], r.y_sem.at[3], me.ydev))
    go(remote(r.mask.at[1 - c], r.live.at[c], r.y_sem.at[4], r.y_sem.at[5], me.ydev))
    part = pl.ds(pl.multiple_of(t * 128, 128), 128)
    go(remote(r.teacher.at[1 - c, part], r.teach.at[c], r.y_sem.at[6], r.y_sem.at[7], me.ydev))

    def wblock(ff):
        return r.w_v.at[:, pl.ds(pl.multiple_of(ff * rows_f, rows_f), rows_f), :]

    go(remote(r.qkvb, wblock(f), r.w_sem.at[0], r.w_sem.at[1], me.xdev))
    go(remote(r.qkvb, wblock(f), r.w_sem.at[2], r.w_sem.at[3], me.core))

    def cols(u):
        return slice(FF_COLS, UW) if u == 0 else slice(0, FF_COLS)

    def shard(tt, ff, u):
        return r.u_v.at[tt, pl.ds(pl.multiple_of(ff * rows_f, rows_f), rows_f), cols(u)]

    def slab(tt, ff, h, u):
        return r.u_v.at[tt, pl.ds(pl.multiple_of(ff * rows_f + h * hrows, hrows), hrows), cols(u)]

    def own_half(h, u):
        return r.upack.at[pl.ds(pl.multiple_of(h * hrows, hrows), hrows), cols(u)]

    hs = (c, 1 - c)
    for u in (0, 1):
        go(remote(own_half(c, u), slab(t, f, c, u), r.x_send.at[u, t], r.x_recv.at[u, t], me.xdev))
        for i in (0, 1):
            mine, there = own_half(hs[i], u), slab(t, f, hs[i], u)
            go(remote(mine, there, r.z_send.at[u, 0, t, i], r.z_recv.at[u, t, i], me.z(t + 1)), t < 3)
            go(remote(mine, there, r.z_send.at[u, 1, t, i], r.z_recv.at[u, t, i], me.z(t - 1)), t > 0)
        go(remote(r.upack.at[:, cols(u)], shard(t, f, u), r.c_send.at[u, t], r.c_recv.at[u, t], me.core))

    local = [
        pltpu.make_async_copy(r.tokens.at[c], r.t_v.at[own_rows], r.loc_sem.at[0]),
        pltpu.make_async_copy(r.qkvb, wblock(f), r.loc_sem.at[1]),
        pltpu.make_async_copy(r.upack, r.u_v.at[t, pl.ds(pl.multiple_of(f * rows_f, rows_f), rows_f), :], r.loc_sem.at[2]),
        pltpu.make_async_copy(r.teacher.at[c, part], r.teach.at[c], r.loc_sem.at[3]),
    ]
    for copy in local:
        copy.start()
    r.rb[c] = r.rbt[c]
    r.live[c] = r.mask[c]

    peers = (me.core, me.xdev, me.ydev)

    def tally_send(i):
        go(remote(r.count if i == 0 else r.tally.at[i + 2], r.tally.at[i], r.n_sem.at[0, i], r.n_sem.at[1, i], peers[i]))

    def tally_take(i):
        remote(r.tally.at[i], r.tally.at[i], r.n_sem.at[0, i], r.n_sem.at[1, i], peers[i]).wait_recv()
        r.tally[3 + i] = (r.count[...] if i == 0 else r.tally[i + 2]) + r.tally[i]

    tally_send(0)

    def z_step(d, u):
        for tt, ok, on, nxt, way in ((t - d, t - d >= 0, t < 3, t + 1, 0), (t + d, t + d <= 3, t > 0, t - 1, 1)):
            go_on = ok & on
            for i in (0, 1):
                piece = slab(tt, f, hs[i], u)
                send, recv = r.z_send.at[u, way, tt, i], r.z_recv.at[u, tt, i]
                pl.when(ok)(remote(piece, piece, send, recv, me.z(t)).wait_recv)
                go(remote(piece, piece, send, recv, me.z(nxt)), go_on)
                if i == 0:
                    go(remote(piece, piece, r.x_send.at[u, tt], r.x_recv.at[u, tt], me.xdev), ok)
            whole = shard(tt, f, u)
            go(remote(whole, whole, r.c_send.at[u, tt], r.c_recv.at[u, tt], me.core), ok)

    def around(d):
        return ((t, None),) if d == 0 else ((t - d, t - d >= 0), (t + d, t + d <= 3))

    def when(ok, fn):
        if ok is None:
            fn()
        else:
            pl.when(ok)(fn)

    def x_step(d, u):
        for tt, ok in around(d):
            piece = slab(tt, me.f_x, c, u)
            when(ok, remote(piece, piece, r.x_send.at[u, tt], r.x_recv.at[u, tt], me.xdev).wait_recv)
            go(remote(piece, piece, r.yw_send.at[u, tt], r.yw_recv.at[u, tt], me.ydev), ok)
            go(remote(piece, piece, r.h_send.at[u, tt, 0], r.h_recv.at[u, tt, 0], me.core), ok)

    def y_step(d, u):
        for tt, ok in around(d):
            piece = slab(tt, me.f_x, 1 - c, u)
            when(ok, remote(piece, piece, r.yw_send.at[u, tt], r.yw_recv.at[u, tt], me.ydev).wait_recv)
            go(remote(piece, piece, r.h_send.at[u, tt, 1], r.h_recv.at[u, tt, 1], me.core), ok)

    def core_wait(tt, u):
        whole = shard(tt, me.f_core, u)
        remote(whole, whole, r.c_send.at[u, tt], r.c_recv.at[u, tt], me.core).wait_recv()
        for i in (0, 1):
            piece = slab(tt, me.f_xc, hs[i], u)
            remote(piece, piece, r.h_send.at[u, tt, i], r.h_recv.at[u, tt, i], me.core).wait_recv()

    remote(wblock(me.f_x), wblock(me.f_x), r.w_sem.at[0], r.w_sem.at[1], me.xdev).wait_recv()
    go(remote(wblock(me.f_x), wblock(me.f_x), r.w_sem.at[4], r.w_sem.at[5], me.core))
    remote(wblock(me.f_core), wblock(me.f_core), r.w_sem.at[2], r.w_sem.at[3], me.core).wait_recv()
    for copy in local[:2]:
        copy.wait()
    remote(wblock(me.f_xc), wblock(me.f_xc), r.w_sem.at[4], r.w_sem.at[5], me.core).wait_recv()


    def project(base, count):
        def step(i, carry):
            rows = pl.ds(pl.multiple_of(base + i * 256, 256), 256)
            piece = r.t_v[rows, :]
            for j, ref in enumerate((r.q_v, r.k_v, r.v_v)):
                made = dot_nn(piece, r.w_v[j])
                for h in range(heads):
                    ref[h, rows, :] = made[:, h * HD : (h + 1) * HD].astype(bf16)
                if j:
                    (r.kt_v if j == 1 else r.vt)[:, rows] = made.T.astype(bf16)
            return carry

        lax.fori_loop(0, count, step, 0)
    tally_take(0)
    tally_send(1)
    project(c * half, half // 256)
    x_step(0, 0)
    z_step(1, 0)
    x_step(0, 1)
    z_step(1, 1)
    x_step(1, 0)
    z_step(2, 0)
    y_step(0, 0)
    tally_take(1)
    tally_send(2)
    other_rows = pl.ds(pl.multiple_of((1 - c) * half, half), half)
    remote(r.t_v.at[other_rows], r.t_v.at[other_rows], r.y_sem.at[0], r.y_sem.at[1], me.ydev).wait_recv()
    project((1 - c) * half, half // 256)
    remote(r.rb.at[1 - c], r.rb.at[1 - c], r.y_sem.at[2], r.y_sem.at[3], me.ydev).wait_recv()
    length = r.lengths[c]
    nblk = seq // BLK
    pos_block = lax.broadcasted_iota(jnp.int32, (128, seq), 1) // BLK
    row = lax.broadcasted_iota(jnp.int32, (128, seq), 0)
    picks = dot_nn(r.rb[0].astype(bf16), (pos_block == row).astype(bf16)) + dot_nn(
        r.rb[1].astype(bf16), (pos_block == row + nblk // 2).astype(bf16)
    )
    key_block = lax.broadcasted_iota(jnp.int32, (nblk, seq), 0)
    query = lax.broadcasted_iota(jnp.int32, (nblk, seq), 1)
    own = query // BLK

    def same(a, b):
        return (a == b).astype(f32)

    times = same(key_block, 0) + same(key_block, 1) + same(key_block, own - 1)
    times += same(key_block, own) + same(key_block, own + 1)
    for j in range(3):
        times += same(key_block.astype(f32), picks[j : j + 1, :])
    times = jnp.where(query < 2 * BLK, 1.0, times)
    level = jnp.where(times > 0, jnp.log2(jnp.maximum(times, 1.0)), negative)
    r.level[...] = level
    factor = HD ** (-0.5) * 1.4426950408889634
    wide = 256

    def attend(i):
        cols = slice(i * wide, (i + 1) * wide)
        for b in range(nblk):
            place = b * BLK + lax.broadcasted_iota(jnp.int32, (BLK, wide), 0)
            row = jnp.broadcast_to(r.level[b : b + 1, cols], (BLK, wide))
            r.bias[b * BLK : (b + 1) * BLK, :] = jnp.where(place < length, row, negative)

        def step(h, carry):
            scores = dot_nt(r.k_v[h], r.q_v[h, cols, :]) * factor + r.bias[...]
            top = jnp.max(scores, 0, keepdims=True)
            expo = jnp.exp2(scores - top)
            probs = (expo * (1.0 / jnp.sum(expo, 0, keepdims=True))).astype(bf16)
            r.pt_v[h, :, cols] = probs
            rows = pl.ds(pl.multiple_of(h * HD, HD), HD)
            r.dqt[rows, cols] = dot_nn(r.vt[rows, :], probs)
            return carry

        lax.fori_loop(0, heads, step, 0)
        s = i * wide // half
        for tt in range(i * wide % half // 128, i * wide % half // 128 + 2):
            at = s * half + tt * 128
            made = r.dqt[:, at : at + 128].T.astype(bf16)
            r.gatt[tt, s] = made

            @pl.when(t == tt)
            def _():
                r.att_v[tt, s] = made

            go(remote(r.gatt.at[tt, s], r.att_v.at[t, s], r.o_send.at[s, tt], r.o_recv.at[s, t], me.z(tt)), t != tt)

    attend(0)
    x_step(1, 1)
    z_step(2, 1)
    z_step(3, 0)
    x_step(2, 0)
    y_step(1, 0)
    attend(1)
    y_step(0, 1)
    x_step(3, 0)
    y_step(2, 0)
    attend(2)
    y_step(3, 0)
    attend(3)
    y_step(1, 1)
    x_step(2, 1)
    z_step(3, 1)
    for s in range(2):
        r.tok[s] = r.t_v[pl.ds(pl.multiple_of(s * half + t * 128, 128), 128), :]
    for s in range(2):
        for d in (1, 2, 3):
            src = (t + d) % 4
            piece = r.att_v.at[src, s]
            remote(piece, piece, r.o_send.at[s, t], r.o_recv.at[s, src], me.z(t)).wait_recv()
    for copy in local[2:]:
        copy.wait()
    for tt in range(4):
        core_wait(tt, 0)

    x = f // 2
    k = f % 2
    att_v, u_v, g_v, act, slope = r.att_v, r.u_v, r.g_v, r.act, r.slope
    rows = 2 * 128
    inv_width = 1.0 / depth

    def both(ref):
        return ref[...].reshape(rows, depth).astype(f32)

    def mean(v):
        return jnp.sum(v, -1, keepdims=True) * inv_width

    def normalize(v):
        center = v - mean(v)
        inverse = lax.rsqrt(mean(center * center) + norm_eps)
        return center * inverse, inverse

    def back(up, normed, inverse, gain):
        scaled = up * gain
        return inverse * (scaled - mean(scaled) - normed * mean(scaled * normed))
    norms = u_v[0, :, 1728:1736].astype(f32).T
    gains = [norms[i : i + 1, :] for i in range(4)]
    att = [att_v[tt].reshape(rows, width) for tt in range(4)]
    attn = dot_nt(att[0], u_v[0, :, 1536:1728])
    for tt in range(1, 4):
        attn += dot_nt(att[tt], u_v[tt, :, 1536:1728])
    normed_one, inverse_one = normalize(both(r.tok) + attn)
    hidden = normed_one * gains[0] + gains[1]
    hidden_b = hidden.astype(bf16)
    cube = 0.044715
    root = 0.7978845608028654

    def up_step(tt, mixed):
        upper = dot_nn(hidden_b, u_v[tt, :, 0:768])
        square = upper * upper
        th = jnp.tanh(root * upper * (1.0 + cube * square))
        act_t = (0.5 * upper * (1.0 + th)).astype(bf16)
        act[tt] = act_t
        bend = 0.5 * (1.0 + th) + 0.5 * upper * (1.0 - th * th) * root * (1.0 + 3.0 * cube * square)
        slope[tt] = bend.astype(bf16)
        return mixed + dot_nt(act_t, u_v[tt, :, 768:1536])
    second = t - 1 + 2 * ((3 - t) // 3)
    fourth = 3 * (1 - t // 2)
    x_step(3, 1)
    core_wait(t, 1)
    mixed = up_step(t, jnp.zeros((rows, depth), f32))
    y_step(2, 1)
    core_wait(second, 1)
    mixed = up_step(second, mixed)
    core_wait(6 - t - second - fourth, 1)
    mixed = up_step(6 - t - second - fourth, mixed)
    y_step(3, 1)
    core_wait(fourth, 1)
    mixed = up_step(fourth, mixed)
    there = r.live.at[1 - c]
    remote(there, there, r.y_sem.at[4], r.y_sem.at[5], me.ydev).wait_recv()
    there = r.teach.at[1 - c]
    remote(there, there, r.y_sem.at[6], r.y_sem.at[7], me.ydev).wait_recv()
    tally_take(2)
    for copy, pred in sends:
        when(pred, copy.wait_send)
    r.count[...] = r.tally[5]
    sends.clear()
    normed_two, inverse_two = normalize(hidden + mixed)
    result = normed_two * gains[2] + gains[3]

    r.piece[...] = result.astype(bf16).reshape(2, 128, depth)
    lo = r.lo
    lo_send = remote(r.piece.at[1 - c], lo.at[c, part], r.s_sem.at[0], r.s_sem.at[1], me.ydev)
    lo_send.start()
    own_lo = pltpu.make_async_copy(r.piece.at[c], lo.at[c, part], r.load_sem.at[1])
    own_lo.start()

    def lo_block(tt):
        return lo.at[:, pl.ds(pl.multiple_of(tt * 128, 128), 128), :]

    lo_line = Line(me, go, lo_block, r.lo_send, r.lo_recv)

    alive = jnp.concatenate([column(r.live[s, :, part]) for s in range(2)], 0)
    row = lax.broadcasted_iota(jnp.int32, (rows, 1), 0)
    place = jnp.where(row < 128, row, row - 128 + half) + t * 128
    live = jnp.where((alive == 1.0) & (place < length), 1.0, 0.0)
    differ = result - both(r.teach)
    weighed = differ * live
    missed = jnp.sum(jnp.sum(weighed * differ, 1, keepdims=True), 0, keepdims=True)
    grad_y = weighed * (2.0 / (r.count[0:1, 0:1] * depth))
    sums = [None] * 4
    sums[2] = jnp.sum(grad_y * normed_two, 0, keepdims=True)
    sums[3] = jnp.sum(grad_y, 0, keepdims=True)
    grad_two = back(grad_y, normed_two, inverse_two, gains[2])
    gm = grad_two.astype(bf16)
    gm_t = grad_two.T.astype(bf16)
    hidden_t = hidden.T.astype(bf16)
    there = lo.at[1 - c, part]
    lo_there = remote(there, there, r.s_sem.at[0], r.s_sem.at[1], me.ydev)
    lo_first = lo_line.first()
    sends.extend(lo_first)

    far = 1 - x
    trio = (me.core, me.xdev, me.ydev)

    def region(ref, unit, at, n, whole=None):
        rows_at = pl.ds(pl.multiple_of(at, qrows), n)
        if whole is not None:
            return ref.at[unit, rows_at, :]
        return ref.at[:, rows_at, FF_COLS:UW] if unit is TAIL else ref.at[unit, rows_at, 0:FF_COLS]

    def g_rows(unit, ff):
        return region(g_v, unit, ff * rows_f, rows_f)

    def rc_rows(xx, unit, at=0, n=rows_f):
        return region(u_v, unit, xx * rows_f + at, n)

    def room(n):
        return lambda unit, i: region(u_v, unit, (4 + n) * hrows + i * qrows, qrows)

    xg_at, yg_at = room(0), room(1)

    def d_at(ref, unit):
        return ref.at[:, :, FF_COLS:UW] if unit is TAIL else ref.at[unit, :, 0:FF_COLS]

    def slot(unit):
        return 4 if unit is TAIL else unit

    def credit(unit):
        for j, dev in enumerate(trio):
            pl.semaphore_signal(r.free.at[j, slot(unit)], inc=1, device_id=dev, device_id_type=MESH)

    def rc_copies(unit):
        return [
            remote(g_rows(unit, xx * 2 + 1 - k), rc_rows(xx, unit), r.rc_send.at[xx, slot(unit)],
                   r.rc_recv.at[xx, slot(unit)], me.core)
            for xx in (far, x)
        ]

    def far_copies(unit):
        i = slot(unit)
        h, other = c * hrows, (1 - c) * hrows
        return [
            remote(rc_rows(far, unit, other, qrows), d_at(r.dx, unit), r.dx_send.at[i], r.dx_recv.at[i], me.xdev),
            remote(rc_rows(far, unit, other + qrows, qrows), d_at(r.dy, unit), r.dy_send.at[i], r.dy_recv.at[i], me.ydev),
            remote(rc_rows(far, unit, h, qrows), xg_at(unit, 0), r.xg_send.at[i, 0], r.xg_recv.at[i, 0], me.xdev),
        ]

    def rc_step(unit):
        pl.semaphore_wait(r.free.at[0, slot(unit)], 1)
        for copy in rc_copies(unit):
            copy.start()

    def core_step(xx, unit):
        view = rc_rows(xx, unit)
        i = slot(unit)
        remote(view, view, r.rc_send.at[xx, i], r.rc_recv.at[xx, i], me.core).wait_recv()
        add_rows(view, view, g_rows(unit, xx * 2 + k))

    def far_step(unit):
        core_step(far, unit)
        for j in (1, 2):
            pl.semaphore_wait(r.free.at[j, slot(unit)], 1)
        for copy in far_copies(unit):
            copy.start()

    def near_step(unit):
        core_step(x, unit)
        i = slot(unit)
        mine = rc_rows(x, unit, (1 - c) * hrows + qrows, qrows)
        go(remote(mine, yg_at(unit, 1), r.yg_send.at[i, 1], r.yg_recv.at[i, 1], me.ydev))

    def diag_step(unit):
        i = slot(unit)
        dx, dy = d_at(r.dx, unit), d_at(r.dy, unit)
        remote(dx, dx, r.dx_send.at[i], r.dx_recv.at[i], me.xdev).wait_recv()
        mine = rc_rows(x, unit, (1 - c) * hrows, qrows)
        add_rows(mine, mine, dx)
        go(remote(mine, yg_at(unit, 0), r.yg_send.at[i, 0], r.yg_recv.at[i, 0], me.ydev))
        remote(dy, dy, r.dy_send.at[i], r.dy_recv.at[i], me.ydev).wait_recv()
        mine = rc_rows(far, unit, c * hrows + qrows, qrows)
        add_rows(mine, mine, dy)
        go(remote(mine, xg_at(unit, 1), r.xg_send.at[i, 1], r.xg_recv.at[i, 1], me.xdev))

    def sum_step(unit):
        at = slot(unit)
        for i in (0, 1):
            xg, yg = xg_at(unit, i), yg_at(unit, i)
            mine = rc_rows(x, unit, c * hrows + i * qrows, qrows)
            remote(xg, xg, r.xg_send.at[at, i], r.xg_recv.at[at, i], me.xdev).wait_recv()
            add_rows(mine, mine, xg)
            remote(yg, yg, r.yg_send.at[at, i], r.yg_recv.at[at, i], me.ydev).wait_recv()
            add_rows(mine, mine, yg)

    def sum_rows(tt):
        return u_v.at[tt, pl.ds(pl.multiple_of(x * rows_f + c * hrows, hrows), hrows), :]

    w_chain = Chain(
        me, go, sum_rows, lambda tt: u_v.at[tt, pl.ds(6 * hrows, hrows), :],
        lambda tt: u_v.at[tt, pl.ds(7 * hrows, hrows), :], r.zw_send, r.zw_recv_l, r.zw_recv_r,
    )

    def turn(i):
        return ((i + 1) % 2) * (3 - i // 2) + (i % 2) * (i // 2)

    ORDER = (3, 0, 2, 1)

    def down_step(i, total):
        tt = turn(i)
        ga = dot_nn(gm, u_v[tt, :, 768:1536])
        gu = (ga * slope[tt].astype(f32)).astype(bf16)
        g_v[tt, :, 768:1536] = dot_nn(gm_t, act[tt]).astype(bf16)
        g_v[tt, :, 0:768] = dot_nn(hidden_t, gu).astype(bf16)
        total = total + dot_nt(gu, u_v[tt, :, 0:768])
        credit(tt)

        @pl.when(i == 1)
        def _():
            lo_there.wait_recv()
            own_lo.wait()
            for copy, pred in lo_first:
                when(pred, copy.start)

        @pl.when(i >= 1)
        def _():
            rc_step(turn(i - 1))

        @pl.when(i >= 2)
        def _():
            far_step(turn(i - 2))

        return total

    grad_hidden = lax.fori_loop(0, 4, down_step, grad_two)
    rc_step(ORDER[3])
    sums[0] = jnp.sum(grad_hidden * normed_one, 0, keepdims=True)
    sums[1] = jnp.sum(grad_hidden, 0, keepdims=True)
    grad_one = back(grad_hidden, normed_one, inverse_one, gains[0])
    r.gone[...] = grad_one.reshape(2, 128, depth)
    ga = grad_one.astype(bf16)
    gatt, do_in = r.gatt, r.do_in
    for tt in range(4):
        back_t = dot_nn(ga, u_v[tt, :, 1536:1728]).astype(bf16)
        gatt[tt] = back_t.reshape(2, 128, width)
    for d in (1, 2, 3):
        to = (t + d) % 4
        go(remote(gatt.at[to], do_in.at[t], r.a_send.at[d], r.a_recv.at[d], me.z(to)))
    do_in[t] = gatt[t]
    credit(TAIL)
    far_step(ORDER[2])
    ga_t = grad_one.T.astype(bf16)
    ez, ef = r.ez, r.ef
    mine_at = f * 2 + c
    ez[t] = jnp.concatenate(sums + [jnp.broadcast_to(missed, (4, depth))], 0)
    for d in (1, 2, 3):
        go(remote(ez.at[t], ez.at[t], r.e_sem.at[0, d], r.e_sem.at[1, d], me.z((t + d) % 4)))

    def sums_on():
        for d in (1, 2, 3):
            src = ez.at[(t + 4 - d) % 4]
            remote(src, src, r.e_sem.at[0, d], r.e_sem.at[1, d], me.z(t)).wait_recv()
        ef[mine_at] = (ez[0] + ez[1]) + (ez[2] + ez[3])
        for d, dev in me.owners():
            go(remote(ef.at[mine_at], ef.at[mine_at], r.e_sem.at[0, 3 + d], r.e_sem.at[1, 3 + d], dev))

    def sums_end():
        for d, dev in me.owners():
            ff, cc = me.flipped(d)
            src = ef.at[ff * 2 + cc]
            remote(src, src, r.e_sem.at[0, 3 + d], r.e_sem.at[1, 3 + d], dev).wait_recv()
        total = ef[0]
        for i in range(1, 8):
            total += ef[i]
        r.sums[...] = total

    for tt in range(4):
        g_v[tt, :, 1536:1728] = dot_nn(ga_t, att[tt]).astype(bf16)
        g_v[tt, :, 1728:1792] = jnp.zeros((depth, UW - 1728), bf16)
    rc_step(TAIL)
    near_step(ORDER[0])
    far_step(ORDER[3])
    near_step(ORDER[1])
    lo_line.step(1)
    far_step(TAIL)
    near_step(ORDER[2])
    near_step(ORDER[3])
    near_step(TAIL)
    for unit in (*ORDER, TAIL):
        sends.extend((copy, None) for copy in rc_copies(unit) + far_copies(unit))

    do, proj, dqt = r.do, r.proj, r.dqt
    dk, dv = r.bias.at[:, 0:HD], r.bias.at[:, 128 : 128 + HD]
    for d in (1, 2, 3):
        src = (t + 4 - d) % 4
        remote(do_in.at[src], do_in.at[src], r.a_send.at[d], r.a_recv.at[d], me.z(src)).wait_recv()
    for s in range(2):
        for tt in range(4):
            at = s * half + tt * 128
            for h in range(heads):
                do[h, at : at + 128, :] = do_in[tt, s, :, h * HD : (h + 1) * HD]
    q_v, k_v, v_v, kt_v, pt_v, t_v, w_v = (r.q_v, r.k_v, r.v_v, r.kt_v, r.pt_v, r.t_v, r.w_v)
    scale = HD ** (-0.5)

    def attend_back(h):
        dk[...] = jnp.zeros((seq, HD), f32)
        dv[...] = jnp.zeros((seq, HD), f32)

        def step(i, carry):
            cols = pl.ds(pl.multiple_of(i * wide, wide), wide)
            mine = do[h, cols, :]
            probs = pt_v[h, :, cols]
            gp = dot_nt(v_v[h], mine)
            pf = probs.astype(f32)
            mix = jnp.sum(pf * gp, 0, keepdims=True)
            gs = (pf * (gp - mix)).astype(bf16)
            dk[...] += dot_nn(gs, q_v[h, cols, :])
            dv[...] += dot_nn(probs, mine)
            dqt[h * HD : (h + 1) * HD, cols] = dot_nn(kt_v[h * HD : (h + 1) * HD, :], gs)
            return carry

        lax.fori_loop(0, seq // wide, step, 0)
        proj[1, :, h * HD : (h + 1) * HD] = (dk[...] * scale).astype(bf16)
        proj[2, :, h * HD : (h + 1) * HD] = dv[...].astype(bf16)
    attend_back(0)
    diag_step(ORDER[0])
    lo_line.step(2)
    diag_step(ORDER[1])
    attend_back(1)
    diag_step(TAIL)
    diag_step(ORDER[2])
    attend_back(2)
    lo_send.wait_send()
    proj[0] = (dqt[...].T * scale).astype(bf16)
    ip = r.ip

    def input_part(s):
        def rows_step(i, carry):
            at = pl.ds(pl.multiple_of(s * half + i * 128, 128), 128)
            total = dot_nt(proj[0, at, :], w_v[0])
            for j in (1, 2):
                total += dot_nt(proj[j, at, :], w_v[j])
            ip[s, i] = total.astype(bf16)
            return carry

        lax.fori_loop(0, half // 128, rows_step, 0)

    def ip_chain(j, s):
        return Chain(
            me, go, lambda tt: ip.at[s, tt], lambda tt: act.at[tt, pl.ds(j * 128, 128), :], lambda tt: slope.at[tt, pl.ds(j * 128, 128), :],
            r.i_send.at[j], r.i_recv_l.at[j], r.i_recv_r.at[j],
        )

    chains = [ip_chain(0, 1 - c), ip_chain(1, c)]
    ig, igp, qg, qc, qs = r.ig, r.piece, r.qg, r.qc, r.q_sem

    def q_rows(ff):
        return qg.at[:, pl.ds(pl.multiple_of(ff * rows_f, rows_f), rows_f), :]

    def finish(j, s):
        chains[j].end()
        igp[j] = (ip[s, t].astype(f32) + r.gone[s]).astype(bf16)

    def ig_line(j, s):
        def block(tt):
            return ig.at[s, pl.ds(pl.multiple_of(tt * 128, 128), 128), :]

        return Line(me, go, block, r.ig_send.at[j], r.ig_recv.at[j])

    lines = [ig_line(0, c), ig_line(1, 1 - c)]

    def sum_pass(tt, passes):
        sum_step(tt)
        for at, way in passes:
            w_chain.pass_on(at, way)

    def q_take(i, j, dev):
        remote(qc.at[i], qc.at[i], qs.at[j], qs.at[j + 1], dev).wait_recv()

    def q_add(i, ff):
        qc[i] = qc[i] + qg[:, pl.ds(pl.multiple_of(ff * rows_f, rows_f), rows_f), :]

    def chain_pass(j, lo_at, hi_at):
        for tt, way in CHAIN_ORDER[lo_at:hi_at]:
            chains[j].pass_on(tt, way)

    input_part(1 - c)
    chain_pass(0, 0, 2)
    input_part(c)
    chain_pass(0, 2, 4)
    chain_pass(1, 0, 2)
    sum_step(TAIL)
    sum_pass(3, CHAIN_ORDER[:1])
    sum_pass(0, CHAIN_ORDER[1:2])
    chain_pass(0, 4, 6)
    finish(0, 1 - c)
    go(remote(igp.at[0], ig.at[c, part], r.s_sem.at[2], r.s_sem.at[3], me.ydev))
    diag_step(ORDER[3])
    sums_on()
    chain_pass(1, 2, 4)
    for j in range(3):
        qg[j] = dot_tn(t_v[...], proj[j]).astype(bf16)
    go(remote(q_rows(far * 2 + 1 - k), qc.at[0], qs.at[0], qs.at[1], me.core))
    go(remote(q_rows(x * 2 + 1 - k), qc.at[1], qs.at[2], qs.at[3], me.core))
    chain_pass(1, 4, 6)
    there = ig.at[1 - c, part]
    remote(there, there, r.s_sem.at[2], r.s_sem.at[3], me.ydev).wait_recv()
    lines[1].start()
    finish(1, c)
    own_ig = pltpu.make_async_copy(igp.at[1], ig.at[c, part], r.load_sem.at[2])
    own_ig.start()
    lines[0].start(igp.at[1])
    q_take(0, 0, me.core)
    q_add(0, far * 2 + k)
    go(remote(qc.at[0], qc.at[2], qs.at[4], qs.at[5], me.xdev))
    q_take(1, 2, me.core)
    q_add(1, x * 2 + k)
    lo_line.step(3)
    sum_pass(2, ((2, 0),))
    sum_pass(1, ((1, 1), (1, 0), (2, 1)))
    lines[1].step(1)
    q_take(2, 4, me.xdev)
    qc[1] = qc[1] + qc[2]
    go(remote(qc.at[1], qc.at[3], qs.at[6], qs.at[7], me.ydev))
    lines[0].step(1)
    w_chain.end()
    fin = r.dx

    def fin_half(h):
        return fin.at[pl.ds(h * 2, 2)]

    for i in (0, 1):
        fin[c * 2 + i] = region(u_v, t, x * rows_f + c * hrows + i * qrows, qrows, 0)[...]
    go(remote(fin_half(c), fin_half(c), r.s_sem.at[4], r.s_sem.at[5], me.ydev))
    q_take(3, 6, me.ydev)
    qsum = r.qsum
    total = jnp.zeros((1, width), f32)
    for j in range(3):
        qsum[j] = qc[1, j].astype(f32) + qc[3, j].astype(f32)
        total += jnp.sum(qsum[j] * qsum[j], 0, keepdims=True)
    total = 0.5 * jnp.sum(total, 1, keepdims=True)

    def square_step(i, carry):
        for j in (0, 1):
            row = fin[c * 2 + j, pl.ds(pl.multiple_of(i * 16, 16), 16), :].astype(f32)
            carry += jnp.sum(row * row, 0, keepdims=True)
        return carry

    wide_total = lax.fori_loop(0, qrows // 16, square_step, jnp.zeros((1, UW), f32))
    total += jnp.sum(wide_total, 1, keepdims=True)
    sz, sf = r.sz, r.sf
    sz[t] = jnp.broadcast_to(total, (8, 128))
    for d in (1, 2, 3):
        go(remote(sz.at[t], sz.at[t], r.f_sem.at[0, d], r.f_sem.at[1, d], me.z((t + d) % 4)))
    lines[0].step(2)
    lines[1].step(2)
    for d in (1, 2, 3):
        src = sz.at[(t + 4 - d) % 4]
        remote(src, src, r.f_sem.at[0, d], r.f_sem.at[1, d], me.z(t)).wait_recv()
    mine = f * 2 + c
    sf[mine] = (sz[0] + sz[1]) + (sz[2] + sz[3])
    for d, dev in me.owners():
        go(remote(sf.at[mine], sf.at[mine], r.f_sem.at[0, 3 + d], r.f_sem.at[1, 3 + d], dev))
    lines[0].step(3)
    lines[1].step(3)
    remote(fin_half(1 - c), fin_half(1 - c), r.s_sem.at[4], r.s_sem.at[5], me.ydev).wait_recv()
    out_copy = pltpu.make_async_copy(fin, r.gsum, r.load_sem.at[0])
    out_copy.start()
    sums_end()
    for d, dev in me.owners():
        ff, cc = me.flipped(d)
        src = sf.at[ff * 2 + cc]
        remote(src, src, r.f_sem.at[0, 3 + d], r.f_sem.at[1, 3 + d], dev).wait_recv()
    all_sq = sf[0]
    for i in range(1, 8):
        all_sq += sf[i]
    r.squares[...] = all_sq
    for copy, pred in sends:
        when(pred, copy.wait_send)
    out_copy.wait()
    own_ig.wait()


def train(lengths, tokens, teacher, qkv, up, down, out, norm, blocks, valid):
    seq = tokens.shape[1] * 2
    width = qkv.shape[2]
    heads = width // HD
    rows_f = qkv.shape[1]
    depth = rows_f * 4
    vm = pl.BlockSpec(memory_space=pltpu.VMEM)
    smem = pl.BlockSpec(memory_space=pltpu.SMEM)
    hbm = pl.BlockSpec(memory_space=pl.ANY)
    dma = pltpu.SemaphoreType.DMA

    def vb(*shape):
        return pltpu.VMEM(shape, bf16)

    def vf(*shape):
        return pltpu.VMEM(shape, f32)

    ins = dict(
        lengths=(lengths, smem), tokens=(tokens, hbm), teacher=(teacher, hbm), qkv=(qkv, vm), up=(up, vm), down=(down, vm),
        out=(out, vm), norm=(norm, vm), blocks=(blocks, vm), valid=(valid, vm),
    )
    qr = rows_f // 4
    outs = dict(
        lo=((2, seq // 2, depth), bf16, hbm),
        ig=((2, seq // 2, depth), bf16, hbm),
        gsum=((4, qr, UW), bf16, hbm),
        qsum=((3, rows_f, width), f32, vm),
        sums=((8, depth), f32, vm),
        squares=((8, 128), f32, vm),
        count=((8, 128), f32, vm),
    )
    scratch = dict(
        att_v=vb(4, 2, 128, width), u_v=vb(4, depth, UW), pt_v=vb(heads, seq, seq), q_v=vb(heads, seq, HD),
        k_v=vb(heads, seq, HD), v_v=vb(heads, seq, HD), kt_v=vb(width, seq), w_v=vb(3, depth, width), t_v=vb(seq, depth),
        tok=vb(2, 128, depth), teach=vb(2, 128, depth), live=vf(2, 8, seq // 2), upack=vb(rows_f, UW),
        qkvb=vb(3, rows_f, width), rbt=vf(2, 8, 128), mask=vf(2, 8, seq // 2), tally=vf(6, 8, 128), vt=vb(width, seq),
        rb=vf(2, 8, 128), level=vf(seq // BLK, seq), bias=vf(seq, 256), loc_sem=dma((5,)), w_sem=dma((6,)), y_sem=dma((8,)),
        z_send=dma((2, 2, 4, 2)), z_recv=dma((2, 4, 2)), x_send=dma((2, 4)), x_recv=dma((2, 4)), yw_send=dma((2, 4)),
        yw_recv=dma((2, 4)),
        c_send=dma((2, 4)), c_recv=dma((2, 4)), h_send=dma((2, 4, 2)), h_recv=dma((2, 4, 2)), o_send=dma((2, 4)), o_recv=dma((2, 4)),
        n_sem=dma((2, 3)),
        g_v=vb(4, depth, UW), act=vb(4, 256, 768),
        slope=vb(4, 256, 768), piece=vb(2, 128, depth), gone=vf(2, 128, depth), gatt=vb(4, 2, 128, width),
        do_in=vb(4, 2, 128, width), dx=vb(4, qr, UW), dy=vb(4, qr, UW), do=vb(heads, seq, HD), proj=vb(3, seq, width),
        dqt=vf(width, seq), ip=vb(2, 4, 128, depth),
        qg=vb(3, depth, width), qc=vb(4, 3, rows_f, width),
        load_sem=dma((15,)), s_sem=dma((6,)), lo_send=dma((2, 4)), lo_recv=dma((4,)), a_send=dma((4,)), a_recv=dma((4,)),
        rc_send=dma((2, 5)), rc_recv=dma((2, 5)), dx_send=dma((5,)), dx_recv=dma((5,)), dy_send=dma((5,)),
        dy_recv=dma((5,)), xg_send=dma((5, 2)), xg_recv=dma((5, 2)), yg_send=dma((5, 2)), yg_recv=dma((5, 2)),
        zw_send=dma((4,)), zw_recv_l=dma((4,)), zw_recv_r=dma((4,)), i_send=dma((2, 4)), i_recv_l=dma((2, 4)),
        i_recv_r=dma((2, 4)), ig_send=dma((2, 2, 4)), ig_recv=dma((2, 4)), q_sem=dma((8,)), ez=vf(4, 8, depth), ef=vf(8, 8, depth),
        sz=vf(4, 8, 128), sf=vf(8, 8, 128), e_sem=dma((2, 11)), f_sem=dma((2, 11)),
        free=pltpu.SemaphoreType.REGULAR((3, 5)),
    )
    return pl.pallas_call(
        functools.partial(train_kernel, (*ins, *outs, *scratch)),
        name="train",
        out_shape=[jax.ShapeDtypeStruct(s, d) for s, d, _ in outs.values()],
        in_specs=[m for _, m in ins.values()],
        out_specs=[m for _, _, m in outs.values()],
        scratch_shapes=list(scratch.values()),
        compiler_params=pltpu.CompilerParams(
            collective_id=0, has_side_effects=True, vmem_limit_bytes=62 * 2**20
        ),
    )(*(a for a, _ in ins.values()))


def update_kernel(names, *refs):
    r = types.SimpleNamespace(**dict(zip(names, refs, strict=True)))
    f = lax.axis_index("fsdp")
    copy = pltpu.make_async_copy(r.lo, r.held, r.sem.at[0])
    copy.start()
    depth = r.sums.shape[1]
    rows_f = depth // 4
    sums = r.sums[0:4, :]
    total = r.squares[0:1, 0:1] + jnp.sum(jnp.sum(sums * sums, 1, keepdims=True), 0, keepdims=True)
    norm = jnp.sqrt(total)
    factor = jnp.minimum(1.0, clip_level / (norm + 1e-06))
    r.norm[...] = norm
    r.loss[...] = r.sums[4:5, 0:1] / (r.count[0:1, 0:1] * depth)
    steps = jnp.full((1, 1), r.steps[0]).astype(f32)
    one = 1.0 / (1.0 - jnp.exp(steps * -0.10536051565782628))
    two = 1.0 / (1.0 - jnp.exp(steps * -0.0010005003335835335))

    def move(name, grad, at, rate):
        clipped = grad * factor
        new_moment = beta_one * getattr(r, name + "_m")[at] + (1.0 - beta_one) * clipped
        new_square = beta_two * getattr(r, name + "_s")[at] + (1.0 - beta_two) * clipped * clipped
        weight = getattr(r, name + "_w")[at]
        step = new_moment * one / (jnp.sqrt(new_square * two) + adam_eps) + decay_rate * weight
        getattr(r, name + "_w_new")[at] = weight - rate * step
        getattr(r, name + "_m_new")[at] = new_moment
        getattr(r, name + "_s_new")[at] = new_square

    gsum = r.gsum

    def rows_step(i, carry):
        rows = pl.ds(pl.multiple_of(i * 16, 16), 16)
        move("up", gsum[rows, 0:768].astype(f32), (rows, slice(None)), rate_list[2])
        move("down", gsum[rows, 768:1536].astype(f32), (rows, slice(None)), rate_list[3])
        for j in range(3):
            move("qkv", r.qsum[j, rows, :], (j, rows, slice(None)), rate_list[0])
        return carry

    lax.fori_loop(0, rows_f // 16, rows_step, 0)
    move("out", gsum[:, 1536:1728].astype(f32).T, (slice(None), slice(None)), rate_list[1])
    mine = sums[:, 0:rows_f]
    for i in range(1, 4):
        mine = jnp.where(f == i, sums[:, i * rows_f : (i + 1) * rows_f], mine)
    move("norm", mine, (slice(None), slice(None)), rate_list[4])

    def cast_step(i, carry):
        rows = pl.ds(pl.multiple_of(i * 64, 64), 64)
        for s in range(2):
            r.input_grad[s, rows, :] = r.ig[s, rows, :].astype(f32)
        return carry

    copy.wait()
    copy = pltpu.make_async_copy(r.held, r.layer_out, r.sem.at[1])
    copy.start()
    lax.fori_loop(0, r.ig.shape[1] // 64, cast_step, 0)
    copy.wait()


def update(steps, lo, ig, gsum, qsum, sums, squares, count, state):
    vm = pl.BlockSpec(memory_space=pltpu.VMEM)
    smem = pl.BlockSpec(memory_space=pltpu.SMEM)
    hbm = pl.BlockSpec(memory_space=pl.ANY)
    ins = dict(
        steps=(steps, smem), lo=(lo, hbm), ig=(ig, vm), gsum=(gsum, vm), qsum=(qsum, vm), sums=(sums, vm),
        squares=(squares, vm), count=(count, vm),
    )
    outs = dict(
        layer_out=(jax.ShapeDtypeStruct(lo.shape, bf16), hbm),
        loss=(jax.ShapeDtypeStruct((1, 1), f32), vm),
        input_grad=(jax.ShapeDtypeStruct(ig.shape, f32), vm),
        norm=(jax.ShapeDtypeStruct((1, 1), f32), vm),
    )
    for name, group in state.items():
        for kind, array in zip("wms", group):
            ins[f"{name}_{kind}"] = (array, vm)
            outs[f"{name}_{kind}_new"] = (jax.ShapeDtypeStruct(array.shape, f32), vm)
    return pl.pallas_call(
        functools.partial(update_kernel, (*ins, *outs, "held", "sem")),
        name="update",
        out_shape=[shape for shape, _ in outs.values()],
        in_specs=[m for _, m in ins.values()],
        out_specs=[m for _, m in outs.values()],
        scratch_shapes=[pltpu.VMEM(lo.shape, bf16), pltpu.SemaphoreType.DMA((2,))],
        compiler_params=pltpu.CompilerParams(vmem_limit_bytes=50 * 2**20),
    )(*(a for a, _ in ins.values()))


def body_swapped(
    tokens,
    teacher,
    lengths,
    valid_mask,
    random_blocks,
    step_count,
    qkv_weight,
    out_weight,
    up_weight,
    down_weight,
    norm_params,
    qkv_moment,
    qkv_square,
    out_moment,
    out_square,
    up_moment,
    up_square,
    down_moment,
    down_square,
    norm_moment,
    norm_square,
):
    blocks = jnp.transpose(random_blocks, (2, 0, 1))
    lo, ig, gsum, qsum, sums, squares, count = train(
        lengths, tokens, teacher, qkv_weight, up_weight, down_weight.T, out_weight, norm_params, blocks, valid_mask
    )
    gsum = gsum.reshape(-1, UW)
    state = dict(
        qkv=(qkv_weight, qkv_moment, qkv_square),
        out=(out_weight, out_moment, out_square),
        up=(up_weight, up_moment, up_square),
        down=(down_weight.T, down_moment.T, down_square.T),
        norm=(norm_params, norm_moment, norm_square),
    )
    layer_out, loss, input_grad, grad_norm, *new = update(
        step_count, lo, ig, gsum, qsum, sums, squares, count, state
    )
    new[9:12] = [v.T for v in new[9:12]]
    return (layer_out, loss.reshape(()), input_grad, grad_norm.reshape(()), *new)


def solution(mesh):
    in_specs = (
        P("fsdp", "ctx", None),
        P("fsdp", "ctx", None),
        P("fsdp"),
        P("fsdp", "ctx"),
        P("fsdp", "ctx", None),
        P(),
        P(None, "fsdp", "tp"),
        P("tp", "fsdp"),
        P("fsdp", "tp"),
        P("tp", "fsdp"),
        P(None, "fsdp"),
        P(None, "fsdp", "tp"),
        P(None, "fsdp", "tp"),
        P("tp", "fsdp"),
        P("tp", "fsdp"),
        P("fsdp", "tp"),
        P("fsdp", "tp"),
        P("tp", "fsdp"),
        P("tp", "fsdp"),
        P(None, "fsdp"),
        P(None, "fsdp"),
    )
    out_specs = (
        P("fsdp", "ctx", None),
        P(),
        P("fsdp", "ctx", None),
        P(),
        P(None, "fsdp", "tp"),
        P(None, "fsdp", "tp"),
        P(None, "fsdp", "tp"),
        P("tp", "fsdp"),
        P("tp", "fsdp"),
        P("tp", "fsdp"),
        P("fsdp", "tp"),
        P("fsdp", "tp"),
        P("fsdp", "tp"),
        P("tp", "fsdp"),
        P("tp", "fsdp"),
        P("tp", "fsdp"),
        P(None, "fsdp"),
        P(None, "fsdp"),
        P(None, "fsdp"),
    )
    sizes = dict(mesh.shape)
    small = sizes == {"fsdp": 4, "ctx": 2, "tp": 4}
    body = body_swapped if small else body_general
    return jax.shard_map(body, mesh=mesh, in_specs=in_specs, out_specs=out_specs, check_vma=False)
```

```python
import functools
import types
from functools import partial

import jax
import jax.numpy as jnp
from jax import lax
from jax.experimental import pallas as pl
from jax.experimental.pallas import tpu as pltpu
from jax.sharding import PartitionSpec as P

HD = 64
BLK = 64
MESH = pl.DeviceIdType.MESH
f32 = jnp.float32
bf16 = jnp.bfloat16

norm_eps = 1e-06
beta_one = 0.9
beta_two = 0.999
adam_eps = 1e-08
decay_rate = 0.01
clip_level = 0.001
rate_list = (0.04, 0.4, 0.04, 0.02, 0.2)
negative = -1e30
VMEM_LIMIT = 58 * 2**20


def layer_norm(values, gain, shift):
    center = values - jnp.mean(values, -1, keepdims=True)
    inverse = lax.rsqrt(jnp.mean(center * center, -1, keepdims=True) + norm_eps)
    normed = center * inverse
    return (normed * gain + shift, normed, inverse)


def norm_backward(upstream, normed, inverse, gain):
    scaled = upstream * gain
    return inverse * (
        scaled
        - jnp.mean(scaled, -1, keepdims=True)
        - normed * jnp.mean(scaled * normed, -1, keepdims=True)
    )


def adam_update(weight, gradient, moment, square, factor, steps_done, rate):
    clipped = gradient * factor
    new_moment = beta_one * moment + (1.0 - beta_one) * clipped
    new_square = beta_two * square + (1.0 - beta_two) * clipped * clipped
    corrected = new_moment / (1.0 - beta_one**steps_done)
    scaled = new_square / (1.0 - beta_two**steps_done)
    new_weight = weight - rate * (corrected / (jnp.sqrt(scaled) + adam_eps) + decay_rate * weight)
    return (new_weight, new_moment, new_square)


def body_general(
    tokens,
    teacher,
    lengths,
    valid_mask,
    random_blocks,
    step_count,
    qkv_weight,
    out_weight,
    up_weight,
    down_weight,
    norm_params,
    qkv_moment,
    qkv_square,
    out_moment,
    out_square,
    up_moment,
    up_square,
    down_moment,
    down_square,
    norm_moment,
    norm_square,
):
    ctx_index = lax.axis_index("ctx")
    ctx_count = lax.axis_size("ctx")
    tp_index = lax.axis_index("tp")
    seqs_here, tok_count, width = tokens.shape
    local_blocks = tok_count // BLK
    block_count = local_blocks * ctx_count
    seq_len = tok_count * ctx_count
    width_local = qkv_weight.shape[2]
    heads_local = width_local // HD
    scale = HD ** (-0.5)
    full_qkv, full_out, full_up, full_down, full_norms = (
        lax.all_gather(qkv_weight.astype(bf16), "fsdp", axis=1, tiled=True),
        lax.all_gather(out_weight.astype(bf16), "fsdp", axis=1, tiled=True),
        lax.all_gather(up_weight.astype(bf16), "fsdp", axis=0, tiled=True),
        lax.all_gather(down_weight.astype(bf16), "fsdp", axis=1, tiled=True),
        lax.all_gather(norm_params.astype(bf16), "fsdp", axis=1, tiled=True),
    )
    gains = full_norms.astype(f32)
    projected = jnp.einsum("std,cde->stce", tokens, full_qkv, preferred_element_type=f32).astype(
        bf16
    )
    queries = projected[:, :, 0, :]
    kv_local = projected[:, :, 1:, :]
    gathered = lax.all_gather(kv_local, "ctx", axis=1, tiled=True)
    own_blocks = ctx_index * local_blocks + jnp.arange(local_blocks, dtype=jnp.int32)
    zero_row = own_blocks * 0
    window = jnp.stack([zero_row, zero_row + 1, own_blocks - 1, own_blocks, own_blocks + 1], -1)
    listed = jnp.concatenate(
        [jnp.broadcast_to(window[None], (seqs_here, local_blocks, 5)), random_blocks], -1
    )
    inside = (listed >= 0) & (listed < block_count)
    safe = jnp.clip(listed, 0, block_count - 1)
    key_pos = safe[..., None] * BLK + jnp.arange(BLK, dtype=jnp.int32)
    counted = (inside[..., None] & (key_pos < lengths[:, None, None, None])).reshape(
        seqs_here, local_blocks, 8 * BLK
    )
    key_live = jnp.arange(seq_len, dtype=jnp.int32)[None, :] < lengths[:, None]
    q_blocks = queries.reshape(seqs_here, local_blocks, BLK, heads_local, HD)
    head_rows = queries[:, : 2 * BLK].reshape(seqs_here, 2 * BLK, heads_local, HD)
    blocked = gathered.reshape(seqs_here, block_count, BLK, 2, width_local)
    flat = blocked.reshape(seqs_here * block_count, BLK, 2, width_local)
    offset = jnp.arange(seqs_here, dtype=jnp.int32)[:, None, None] * block_count
    picked = lax.map(
        lambda at: lax.dynamic_index_in_dim(flat, at, 0, keepdims=False), (safe + offset).reshape(-1)
    ).reshape(seqs_here, local_blocks, 8, BLK, 2, width_local)
    key_rows = picked[..., 0, :].reshape(seqs_here, local_blocks, 8 * BLK, heads_local, HD)
    value_rows = picked[..., 1, :].reshape(seqs_here, local_blocks, 8 * BLK, heads_local, HD)
    scores = (
        jnp.einsum("sbqhd,sbkhd->sbhqk", q_blocks, key_rows, preferred_element_type=f32) * scale
    )
    scores = jnp.where(counted[:, :, None, None, :], scores, negative)
    all_keys = gathered[:, :, 0, :].reshape(seqs_here, seq_len, heads_local, HD)
    all_values = gathered[:, :, 1, :].reshape(seqs_here, seq_len, heads_local, HD)
    wide_scores = (
        jnp.einsum("sqhd,skhd->shqk", head_rows, all_keys, preferred_element_type=f32) * scale
    )
    wide_scores = jnp.where(key_live[:, None, None, :], wide_scores, negative)
    top_value = jnp.max(scores, -1, keepdims=True)
    expo = jnp.exp(scores - top_value)
    summed = jnp.sum(expo, -1, keepdims=True)
    sparse_lse = top_value + jnp.log(summed)
    probs_b = (expo / summed).astype(bf16)
    sparse_out = jnp.einsum(
        "sbhqk,sbkhd->sbqhd", probs_b, value_rows, preferred_element_type=f32
    ).reshape(seqs_here, tok_count, width_local)
    wide_top = jnp.max(wide_scores, -1, keepdims=True)
    wide_expo = jnp.exp(wide_scores - wide_top)
    wide_sum = jnp.sum(wide_expo, -1, keepdims=True)
    wide_lse = wide_top + jnp.log(wide_sum)
    wide_probs = (wide_expo / wide_sum).astype(bf16)
    wide_out = jnp.einsum(
        "shqk,skhd->sqhd", wide_probs, all_values, preferred_element_type=f32
    ).reshape(seqs_here, 2 * BLK, width_local)
    is_first = ctx_index == 0
    row_ids = jnp.arange(tok_count, dtype=jnp.int32)
    global_row = (row_ids < 2 * BLK) & is_first
    rest_zeros = jnp.zeros((seqs_here, tok_count - 2 * BLK, width_local), f32)
    padded_wide = jnp.concatenate([wide_out, rest_zeros], 1)
    attended = jnp.where(global_row[None, :, None], padded_wide, sparse_out).astype(bf16)
    attn_part = jnp.einsum("ste,ed->std", attended, full_out, preferred_element_type=f32)
    positions = ctx_index * tok_count + row_ids
    live_rows = ((valid_mask == 1) & (positions[None, :] < lengths[:, None])).astype(f32)
    count_local = jnp.sum(live_rows)
    gelu_fn = partial(jax.nn.gelu, approximate=True)
    attn = lax.psum(attn_part.astype(jnp.bfloat16), "tp").astype(jnp.float32)
    hidden, normed_one, inverse_one = layer_norm(tokens.astype(f32) + attn, gains[0], gains[1])
    hidden_b = hidden.astype(bf16)
    upper = jnp.einsum("std,df->stf", hidden_b, full_up, preferred_element_type=f32)
    active_f, gelu_back = jax.vjp(gelu_fn, upper)
    active = active_f.astype(bf16)
    mixed = lax.psum(
        jnp.einsum("stf,fd->std", active, full_down, preferred_element_type=f32).astype(
            jnp.bfloat16
        ),
        "tp",
    ).astype(jnp.float32)
    result, normed_two, inverse_two = layer_norm(hidden + mixed, gains[2], gains[3])
    differ = result - teacher.astype(f32)
    error_local = jnp.sum(live_rows[..., None] * differ * differ)
    error_total, live_count = lax.psum((error_local, count_local), ("fsdp", "ctx"))
    loss_value = error_total / (live_count * width)
    grad_y = 2.0 * differ * live_rows[..., None] / (live_count * width)
    gain_two_grad = jnp.sum(grad_y * normed_two, (0, 1))
    bias_two_grad = jnp.sum(grad_y, (0, 1))
    grad_two = norm_backward(grad_y, normed_two, inverse_two, gains[2])
    grad_mixed = grad_two.astype(bf16)
    grad_active = jnp.einsum("std,fd->stf", grad_mixed, full_down, preferred_element_type=f32)
    grad_upper = gelu_back(grad_active)[0].astype(bf16)
    down_grad = jnp.einsum("stf,std->fd", active, grad_mixed, preferred_element_type=f32)
    up_grad = jnp.einsum("std,stf->df", hidden_b, grad_upper, preferred_element_type=f32)
    grad_hidden = grad_two + lax.psum(
        jnp.einsum("stf,df->std", grad_upper, full_up, preferred_element_type=f32).astype(
            jnp.bfloat16
        ),
        "tp",
    ).astype(jnp.float32)
    gain_one_grad = jnp.sum(grad_hidden * normed_one, (0, 1))
    bias_one_grad = jnp.sum(grad_hidden, (0, 1))
    grad_one = norm_backward(grad_hidden, normed_one, inverse_one, gains[0])
    norm_grad = jnp.stack([gain_one_grad, bias_one_grad, gain_two_grad, bias_two_grad], 0)
    grad_attn = grad_one.astype(bf16)
    out_grad = jnp.einsum("ste,std->ed", attended, grad_attn, preferred_element_type=f32)
    grad_attended = jnp.einsum(
        "std,ed->ste", grad_attn, full_out, preferred_element_type=f32
    ).astype(bf16)
    sparse_grad = jnp.where(global_row[None, :, None], jnp.zeros_like(grad_attended), grad_attended)
    sparse_grad = sparse_grad.reshape(seqs_here, local_blocks, BLK, heads_local, HD)
    probs = jnp.exp(scores - sparse_lse)
    grad_probs = jnp.einsum(
        "sbqhd,sbkhd->sbhqk", sparse_grad, value_rows, preferred_element_type=f32
    )
    row_dot = jnp.sum(probs * grad_probs, -1, keepdims=True)
    grad_scores = (probs * (grad_probs - row_dot)).astype(bf16)
    dq_sparse = (
        jnp.einsum("sbhqk,sbkhd->sbqhd", grad_scores, key_rows, preferred_element_type=f32) * scale
    )
    dk_rows = (
        jnp.einsum("sbhqk,sbqhd->sbkhd", grad_scores, q_blocks, preferred_element_type=f32) * scale
    )
    dv_rows = jnp.einsum(
        "sbhqk,sbqhd->sbkhd", probs.astype(bf16), sparse_grad, preferred_element_type=f32
    )
    list_grads = jnp.stack(
        [
            dk_rows.reshape(seqs_here, local_blocks, 8, BLK, width_local),
            dv_rows.reshape(seqs_here, local_blocks, 8, BLK, width_local),
        ],
        4,
    )
    seq_ids = jnp.broadcast_to(jnp.arange(seqs_here, dtype=jnp.int32)[:, None, None], safe.shape)
    kv_term = (
        jnp.zeros((block_count, seqs_here, BLK, 2, width_local), f32)
        .at[safe, seq_ids]
        .add(list_grads)
    )
    head_grad = jnp.where(
        is_first, grad_attended[:, : 2 * BLK], jnp.zeros_like(grad_attended[:, : 2 * BLK])
    )
    head_grad = head_grad.reshape(seqs_here, 2 * BLK, heads_local, HD)
    wide_probs_f = jnp.exp(wide_scores - wide_lse)
    wide_dprobs = jnp.einsum("sqhd,skhd->shqk", head_grad, all_values, preferred_element_type=f32)
    wide_dot = jnp.sum(wide_probs_f * wide_dprobs, -1, keepdims=True)
    wide_dscores = (wide_probs_f * (wide_dprobs - wide_dot)).astype(bf16)
    dq_wide = (
        jnp.einsum("shqk,skhd->sqhd", wide_dscores, all_keys, preferred_element_type=f32) * scale
    )
    split_scores = wide_dscores.reshape(seqs_here, heads_local, 2 * BLK, block_count, BLK)
    split_probs = wide_probs_f.astype(bf16).reshape(
        seqs_here, heads_local, 2 * BLK, block_count, BLK
    )
    dk_wide = (
        jnp.einsum("shqnb,sqhd->nsbhd", split_scores, head_rows, preferred_element_type=f32) * scale
    )
    dv_wide = jnp.einsum("shqnb,sqhd->nsbhd", split_probs, head_grad, preferred_element_type=f32)
    kv_term = kv_term + jnp.stack(
        [
            dk_wide.reshape(block_count, seqs_here, BLK, width_local),
            dv_wide.reshape(block_count, seqs_here, BLK, width_local),
        ],
        3,
    )
    kv_grads = lax.psum_scatter(
        kv_term.astype(jnp.bfloat16), "ctx", scatter_dimension=0, tiled=True
    ).astype(jnp.float32)
    kv_grads = jnp.transpose(kv_grads, (1, 0, 2, 3, 4)).reshape(
        seqs_here, tok_count, 2, width_local
    )
    dq_total = dq_sparse.reshape(seqs_here, tok_count, width_local) + jnp.concatenate(
        [dq_wide.reshape(seqs_here, 2 * BLK, width_local), rest_zeros], 1
    )
    grad_projected = jnp.concatenate([dq_total[:, :, None, :], kv_grads], 2).astype(bf16)
    qkv_grad = jnp.einsum("std,stce->cde", tokens, grad_projected, preferred_element_type=f32)
    input_part = jnp.einsum("stce,cde->std", grad_projected, full_qkv, preferred_element_type=f32)
    input_grad = grad_one + lax.psum(input_part.astype(jnp.bfloat16), "tp").astype(jnp.float32)
    local_grads = (qkv_grad, out_grad, up_grad, down_grad, norm_grad)
    owned = (
        lax.psum_scatter(
            local_grads[0].astype(jnp.bfloat16), "fsdp", scatter_dimension=1, tiled=True
        ).astype(jnp.float32),
        lax.psum_scatter(
            local_grads[1].astype(jnp.bfloat16), "fsdp", scatter_dimension=1, tiled=True
        ).astype(jnp.float32),
        lax.psum_scatter(
            local_grads[2].astype(jnp.bfloat16), "fsdp", scatter_dimension=0, tiled=True
        ).astype(jnp.float32),
        lax.psum_scatter(
            local_grads[3].astype(jnp.bfloat16), "fsdp", scatter_dimension=1, tiled=True
        ).astype(jnp.float32),
        lax.psum_scatter(
            local_grads[4].astype(jnp.bfloat16), "fsdp", scatter_dimension=1, tiled=True
        ).astype(jnp.float32),
    )
    shards = (
        lax.psum(owned[0].astype(jnp.bfloat16), "ctx").astype(jnp.float32),
        lax.psum(owned[1].astype(jnp.bfloat16), "ctx").astype(jnp.float32),
        lax.psum(owned[2].astype(jnp.bfloat16), "ctx").astype(jnp.float32),
        lax.psum(owned[3].astype(jnp.bfloat16), "ctx").astype(jnp.float32),
        lax.psum(owned[4].astype(jnp.bfloat16), "ctx").astype(jnp.float32),
    )
    matrix_squares = sum((jnp.sum(member * member) for member in shards[:4]))
    norm_squares = jnp.where(tp_index == 0, jnp.sum(shards[4] * shards[4]), 0.0)
    squares_total = lax.psum(matrix_squares + norm_squares, ("fsdp", "tp"))
    grad_norm = jnp.sqrt(squares_total)
    factor = jnp.minimum(1.0, clip_level / (grad_norm + 1e-06))
    steps_done = step_count[0].astype(f32)
    qkv_new = adam_update(
        qkv_weight, shards[0], qkv_moment, qkv_square, factor, steps_done, rate_list[0]
    )
    out_new = adam_update(
        out_weight, shards[1], out_moment, out_square, factor, steps_done, rate_list[1]
    )
    up_new = adam_update(
        up_weight, shards[2], up_moment, up_square, factor, steps_done, rate_list[2]
    )
    down_new = adam_update(
        down_weight, shards[3], down_moment, down_square, factor, steps_done, rate_list[3]
    )
    norm_new = adam_update(
        norm_params, shards[4], norm_moment, norm_square, factor, steps_done, rate_list[4]
    )
    return (
        result.astype(bf16),
        loss_value,
        input_grad,
        grad_norm,
        qkv_new[0],
        qkv_new[1],
        qkv_new[2],
        out_new[0],
        out_new[1],
        out_new[2],
        up_new[0],
        up_new[1],
        up_new[2],
        down_new[0],
        down_new[1],
        down_new[2],
        norm_new[0],
        norm_new[1],
        norm_new[2],
    )


def remote(src, dst, send, recv, dev):
    return pltpu.make_async_remote_copy(
        src_ref=src, dst_ref=dst, send_sem=send, recv_sem=recv, device_id=dev, device_id_type=MESH
    )


def dot_nn(a, b):
    return lax.dot_general(a, b, (((1,), (0,)), ((), ())), preferred_element_type=f32)


def dot_nt(a, b):
    return lax.dot_general(a, b, (((1,), (1,)), ((), ())), preferred_element_type=f32)


def dot_tn(a, b):
    return lax.dot_general(a, b, (((0,), (0,)), ((), ())), preferred_element_type=f32)


UW = 1792


class Peers:
    def __init__(self):
        f, c, t = lax.axis_index("fsdp"), lax.axis_index("ctx"), lax.axis_index("tp")
        x, k = f // 2, f % 2
        self.f, self.c, self.t = f, c, t
        self.f_core = x * 2 + (1 - k)
        self.f_x = (1 - x) * 2 + k
        self.f_xc = (1 - x) * 2 + (1 - k)
        self.core = (self.f_core, c, t)
        self.xdev = (self.f_x, c, t)
        self.ydev = (f, 1 - c, t)

    def z(self, t):
        return (self.f, self.c, t)

    def flipped(self, d):
        x, k = self.f // 2, self.f % 2
        x = 1 - x if d // 4 else x
        k = 1 - k if d % 2 else k
        return x * 2 + k, 1 - self.c if d // 2 % 2 else self.c

    def owners(self):
        return [(d, (*self.flipped(d), self.t)) for d in range(1, 8)]

    def barrier(self, whole=False):
        sem = pltpu.get_barrier_semaphore()
        devs = [dev for _, dev in self.owners()] if whole else [self.core, self.xdev, self.ydev]
        devs += [self.z((self.t + d) % 4) for d in (1, 2, 3)]
        for dev in devs:
            pl.semaphore_signal(sem, inc=1, device_id=dev, device_id_type=MESH)
        pl.semaphore_wait(sem, len(devs))


def column(row):
    return row.T[:, 0:1]


def add_rows(dst, a, b, step=16):
    if len(dst.shape) == 3:
        for i in range(dst.shape[0]):
            add_rows(dst.at[i], a.at[i], b.at[i], step)
        return

    def one(i, carry):
        rows = pl.ds(pl.multiple_of(i * step, step), step)
        dst[rows, :] = a[rows, :] + b[rows, :]
        return carry

    lax.fori_loop(0, dst.shape[0] // step, one, 0)


class Line:
    def __init__(self, me, go, block, send, recv):
        self.me, self.go, self.block, self.send, self.recv = me, go, block, send, recv

    def first(self, src=None):
        t = self.me.t
        mine = self.block(t)
        src = mine if src is None else src
        return [
            (remote(src, mine, self.send.at[0, t], self.recv.at[t], self.me.z(t + 1)), t < 3),
            (remote(src, mine, self.send.at[1, t], self.recv.at[t], self.me.z(t - 1)), t > 0),
        ]

    def start(self, src=None):
        for copy, pred in self.first(src):
            self.go(copy, pred)

    def step(self, d):
        t = self.me.t
        for tt, ok, on, nxt, way in ((t - d, t - d >= 0, t < 3, t + 1, 0), (t + d, t + d <= 3, t > 0, t - 1, 1)):
            piece = self.block(tt)
            pl.when(ok)(remote(piece, piece, self.send.at[way, tt], self.recv.at[tt], self.me.z(t)).wait_recv)
            if d < 3:
                self.go(remote(piece, piece, self.send.at[way, tt], self.recv.at[tt], self.me.z(nxt)), ok & on)


class Chain:
    def __init__(self, me, go, own, left, right, send, recv_l, recv_r):
        self.me, self.go, self.own, self.left, self.right = me, go, own, left, right
        self.send, self.recv_l, self.recv_r = send, recv_l, recv_r

    def arrived(self, tt, way):
        buf, recv = (self.left, self.recv_l) if way == 0 else (self.right, self.recv_r)
        remote(buf(tt), buf(tt), self.send.at[tt], recv.at[tt], self.me.z(self.me.t)).wait_recv()

    def pass_on(self, tt, way):
        t = self.me.t
        inner = (t > 0) if way == 0 else (t < 3)
        ahead = (tt > t) if way == 0 else (tt < t)
        buf, recv = (self.left, self.recv_l) if way == 0 else (self.right, self.recv_r)

        @pl.when(ahead & inner)
        def _():
            self.arrived(tt, way)
            add_rows(self.own(tt), self.own(tt), buf(tt))

        to = self.me.z(t + 1 if way == 0 else t - 1)
        self.go(remote(self.own(tt), buf(tt), self.send.at[tt], recv.at[tt], to), ahead)

    def end(self):
        t = self.me.t
        mine = self.own(t)

        @pl.when(t > 0)
        def _():
            self.arrived(t, 0)
            add_rows(mine, mine, self.left(t))

        @pl.when(t < 3)
        def _():
            self.arrived(t, 1)
            add_rows(mine, mine, self.right(t))


CHAIN_ORDER = ((3, 0), (0, 1), (2, 0), (1, 1), (1, 0), (2, 1))


TAIL = None
FF_COLS = 1536


def train_kernel(names, *refs):
    r = types.SimpleNamespace(**dict(zip(names, refs, strict=True)))
    me = Peers()
    f, c, t = me.f, me.c, me.t
    seq = r.t_v.shape[0]
    half = seq // 2
    rows_f = r.qkvb.shape[1]
    sends = []
    heads = r.q_v.shape[0]
    width = heads * HD
    depth = rows_f * 4
    hrows = rows_f // 2
    qrows = rows_f // 4
    r.qkvb[...] = r.qkv[...].astype(bf16)
    r.upack[:, 0:768] = r.up[...].astype(bf16)
    r.upack[:, 768:1536] = r.down[...].astype(bf16)
    tail = jnp.concatenate(
        [r.out[...].T, jnp.concatenate([r.norm[...], jnp.zeros((60, rows_f), f32)], 0).T], 1
    )
    r.upack[:, 1536:1792] = tail.astype(bf16)
    for s in range(2):
        r.rbt[s] = jnp.zeros((8, 128), f32)
        r.rbt[s, 0:3, 0 : r.blocks.shape[2]] = r.blocks[:, s, :].astype(f32)
        r.mask[s] = jnp.broadcast_to(r.valid[s : s + 1, :].astype(f32), (8, half))
    spot = c * half + lax.broadcasted_iota(jnp.int32, (1, half), 1)
    found = jnp.zeros((1, half), f32)
    for s in range(2):
        found += jnp.where((r.valid[s : s + 1, :] == 1) & (spot < r.lengths[s]), 1.0, 0.0)
    r.count[...] = jnp.broadcast_to(jnp.sum(found, 1, keepdims=True), (8, 128))
    me.barrier(True)

    def go(copy, pred=None):
        if pred is None:
            copy.start()
        else:
            pl.when(pred)(copy.start)
        sends.append((copy, pred))
    own_rows = pl.ds(pl.multiple_of(c * half, half), half)
    go(remote(r.tokens.at[1 - c], r.t_v.at[own_rows], r.y_sem.at[0], r.y_sem.at[1], me.ydev))
    go(remote(r.rbt.at[1 - c], r.rb.at[c], r.y_sem.at[2], r.y_sem.at[3], me.ydev))
    go(remote(r.mask.at[1 - c], r.live.at[c], r.y_sem.at[4], r.y_sem.at[5], me.ydev))
    part = pl.ds(pl.multiple_of(t * 128, 128), 128)

    def wblock(ff):
        return r.w_v.at[:, pl.ds(pl.multiple_of(ff * rows_f, rows_f), rows_f), :]

    go(remote(r.qkvb, wblock(f), r.w_sem.at[0], r.w_sem.at[1], me.xdev))
    go(remote(r.qkvb, wblock(f), r.w_sem.at[2], r.w_sem.at[3], me.core))

    def cols(u):
        return slice(FF_COLS, UW) if u == 0 else slice(0, FF_COLS)

    def shard(tt, ff, u):
        return r.u_v.at[tt, pl.ds(pl.multiple_of(ff * rows_f, rows_f), rows_f), cols(u)]

    def slab(tt, ff, h, u):
        return r.u_v.at[tt, pl.ds(pl.multiple_of(ff * rows_f + h * hrows, hrows), hrows), cols(u)]

    def own_half(h, u):
        return r.upack.at[pl.ds(pl.multiple_of(h * hrows, hrows), hrows), cols(u)]

    hs = (c, 1 - c)
    for u in (0, 1):
        go(remote(own_half(c, u), slab(t, f, c, u), r.x_send.at[u, t], r.x_recv.at[u, t], me.xdev))
        for i in (0, 1):
            mine, there = own_half(hs[i], u), slab(t, f, hs[i], u)
            go(remote(mine, there, r.z_send.at[u, 0, t, i], r.z_recv.at[u, t, i], me.z(t + 1)), t < 3)
            go(remote(mine, there, r.z_send.at[u, 1, t, i], r.z_recv.at[u, t, i], me.z(t - 1)), t > 0)
        go(remote(r.upack.at[:, cols(u)], shard(t, f, u), r.c_send.at[u, t], r.c_recv.at[u, t], me.core))

    local = [
        pltpu.make_async_copy(r.tokens.at[c], r.t_v.at[own_rows], r.loc_sem.at[0]),
        pltpu.make_async_copy(r.qkvb, wblock(f), r.loc_sem.at[1]),
        pltpu.make_async_copy(r.upack, r.u_v.at[t, pl.ds(pl.multiple_of(f * rows_f, rows_f), rows_f), :], r.loc_sem.at[2]),
        pltpu.make_async_copy(r.teacher.at[c, part], r.teach.at[c], r.loc_sem.at[3]),
    ]
    for copy in local:
        copy.start()
    r.rb[c] = r.rbt[c]
    r.live[c] = r.mask[c]

    peers = (me.core, me.xdev, me.ydev)

    def tally_send(i):
        go(remote(r.count if i == 0 else r.tally.at[i + 2], r.tally.at[i], r.n_sem.at[0, i], r.n_sem.at[1, i], peers[i]))

    def tally_take(i):
        remote(r.tally.at[i], r.tally.at[i], r.n_sem.at[0, i], r.n_sem.at[1, i], peers[i]).wait_recv()
        r.tally[3 + i] = (r.count[...] if i == 0 else r.tally[i + 2]) + r.tally[i]

    tally_send(0)

    def z_step(d, u):
        for tt, ok, on, nxt, way in ((t - d, t - d >= 0, t < 3, t + 1, 0), (t + d, t + d <= 3, t > 0, t - 1, 1)):
            go_on = ok & on
            for i in (0, 1):
                piece = slab(tt, f, hs[i], u)
                send, recv = r.z_send.at[u, way, tt, i], r.z_recv.at[u, tt, i]
                pl.when(ok)(remote(piece, piece, send, recv, me.z(t)).wait_recv)
                go(remote(piece, piece, send, recv, me.z(nxt)), go_on)
                if i == 0:
                    go(remote(piece, piece, r.x_send.at[u, tt], r.x_recv.at[u, tt], me.xdev), ok)
            whole = shard(tt, f, u)
            go(remote(whole, whole, r.c_send.at[u, tt], r.c_recv.at[u, tt], me.core), ok)

    def around(d):
        return ((t, None),) if d == 0 else ((t - d, t - d >= 0), (t + d, t + d <= 3))

    def when(ok, fn):
        if ok is None:
            fn()
        else:
            pl.when(ok)(fn)

    def x_step(d, u):
        for tt, ok in around(d):
            piece = slab(tt, me.f_x, c, u)
            when(ok, remote(piece, piece, r.x_send.at[u, tt], r.x_recv.at[u, tt], me.xdev).wait_recv)
            go(remote(piece, piece, r.yw_send.at[u, tt], r.yw_recv.at[u, tt], me.ydev), ok)
            go(remote(piece, piece, r.h_send.at[u, tt, 0], r.h_recv.at[u, tt, 0], me.core), ok)

    def y_step(d, u):
        for tt, ok in around(d):
            piece = slab(tt, me.f_x, 1 - c, u)
            when(ok, remote(piece, piece, r.yw_send.at[u, tt], r.yw_recv.at[u, tt], me.ydev).wait_recv)
            go(remote(piece, piece, r.h_send.at[u, tt, 1], r.h_recv.at[u, tt, 1], me.core), ok)

    def core_wait(tt, u):
        whole = shard(tt, me.f_core, u)
        remote(whole, whole, r.c_send.at[u, tt], r.c_recv.at[u, tt], me.core).wait_recv()
        for i in (0, 1):
            piece = slab(tt, me.f_xc, hs[i], u)
            remote(piece, piece, r.h_send.at[u, tt, i], r.h_recv.at[u, tt, i], me.core).wait_recv()

    remote(wblock(me.f_x), wblock(me.f_x), r.w_sem.at[0], r.w_sem.at[1], me.xdev).wait_recv()
    go(remote(wblock(me.f_x), wblock(me.f_x), r.w_sem.at[4], r.w_sem.at[5], me.core))
    remote(wblock(me.f_core), wblock(me.f_core), r.w_sem.at[2], r.w_sem.at[3], me.core).wait_recv()
    for copy in local[:2]:
        copy.wait()
    remote(wblock(me.f_xc), wblock(me.f_xc), r.w_sem.at[4], r.w_sem.at[5], me.core).wait_recv()


    def project(base, count):
        def step(i, carry):
            rows = pl.ds(pl.multiple_of(base + i * 256, 256), 256)
            piece = r.t_v[rows, :]
            for j, ref in enumerate((r.q_v, r.k_v, r.v_v)):
                made = dot_nn(piece, r.w_v[j])
                for h in range(heads):
                    ref[h, rows, :] = made[:, h * HD : (h + 1) * HD].astype(bf16)
                if j:
                    (r.kt_v if j == 1 else r.vt)[:, rows] = made.T.astype(bf16)
            return carry

        lax.fori_loop(0, count, step, 0)
    tally_take(0)
    tally_send(1)
    project(c * half, half // 256)
    x_step(0, 0)
    z_step(1, 0)
    x_step(0, 1)
    z_step(1, 1)
    x_step(1, 0)
    z_step(2, 0)
    y_step(0, 0)
    tally_take(1)
    tally_send(2)
    other_rows = pl.ds(pl.multiple_of((1 - c) * half, half), half)
    remote(r.t_v.at[other_rows], r.t_v.at[other_rows], r.y_sem.at[0], r.y_sem.at[1], me.ydev).wait_recv()
    project((1 - c) * half, half // 256)
    remote(r.rb.at[1 - c], r.rb.at[1 - c], r.y_sem.at[2], r.y_sem.at[3], me.ydev).wait_recv()
    length = r.lengths[c]
    nblk = seq // BLK
    pos_block = lax.broadcasted_iota(jnp.int32, (128, seq), 1) // BLK
    row = lax.broadcasted_iota(jnp.int32, (128, seq), 0)
    picks = dot_nn(r.rb[0].astype(bf16), (pos_block == row).astype(bf16)) + dot_nn(
        r.rb[1].astype(bf16), (pos_block == row + nblk // 2).astype(bf16)
    )
    key_block = lax.broadcasted_iota(jnp.int32, (nblk, seq), 0)
    query = lax.broadcasted_iota(jnp.int32, (nblk, seq), 1)
    own = query // BLK

    def same(a, b):
        return (a == b).astype(f32)

    times = same(key_block, 0) + same(key_block, 1) + same(key_block, own - 1)
    times += same(key_block, own) + same(key_block, own + 1)
    for j in range(3):
        times += same(key_block.astype(f32), picks[j : j + 1, :])
    times = jnp.where(query < 2 * BLK, 1.0, times)
    level = jnp.where(times > 0, jnp.log2(jnp.maximum(times, 1.0)), negative)
    r.level[...] = level
    factor = HD ** (-0.5) * 1.4426950408889634
    wide = 256

    def attend(i):
        cols = slice(i * wide, (i + 1) * wide)
        for b in range(nblk):
            place = b * BLK + lax.broadcasted_iota(jnp.int32, (BLK, wide), 0)
            row = jnp.broadcast_to(r.level[b : b + 1, cols], (BLK, wide))
            r.bias[b * BLK : (b + 1) * BLK, :] = jnp.where(place < length, row, negative)

        def step(h, carry):
            scores = dot_nt(r.k_v[h], r.q_v[h, cols, :]) * factor + r.bias[...]
            top = jnp.max(scores, 0, keepdims=True)
            expo = jnp.exp2(scores - top)
            probs = (expo * (1.0 / jnp.sum(expo, 0, keepdims=True))).astype(bf16)
            r.pt_v[h, :, cols] = probs
            rows = pl.ds(pl.multiple_of(h * HD, HD), HD)
            r.dqt[rows, cols] = dot_nn(r.vt[rows, :], probs)
            return carry

        lax.fori_loop(0, heads, step, 0)
        s = i * wide // half
        for tt in range(i * wide % half // 128, i * wide % half // 128 + 2):
            at = s * half + tt * 128
            made = r.dqt[:, at : at + 128].T.astype(bf16)
            r.gatt[tt, s] = made

            @pl.when(t == tt)
            def _():
                r.att_v[tt, s] = made

            go(remote(r.gatt.at[tt, s], r.att_v.at[t, s], r.o_send.at[s, tt], r.o_recv.at[s, t], me.z(tt)), t != tt)

    attend(0)
    x_step(1, 1)
    z_step(2, 1)
    z_step(3, 0)
    x_step(2, 0)
    y_step(1, 0)
    attend(1)
    y_step(0, 1)
    x_step(3, 0)
    y_step(2, 0)
    attend(2)
    y_step(3, 0)
    attend(3)
    go(remote(r.teacher.at[1 - c, part], r.teach.at[c], r.y_sem.at[6], r.y_sem.at[7], me.ydev))
    y_step(1, 1)
    x_step(2, 1)
    z_step(3, 1)
    for s in range(2):
        r.tok[s] = r.t_v[pl.ds(pl.multiple_of(s * half + t * 128, 128), 128), :]
    for s in range(2):
        for d in (1, 2, 3):
            src = (t + d) % 4
            piece = r.att_v.at[src, s]
            remote(piece, piece, r.o_send.at[s, t], r.o_recv.at[s, src], me.z(t)).wait_recv()
    for copy in local[2:]:
        copy.wait()
    for tt in range(4):
        core_wait(tt, 0)

    x = f // 2
    k = f % 2
    att_v, u_v, g_v, act, slope = r.att_v, r.u_v, r.g_v, r.act, r.slope
    rows = 2 * 128
    inv_width = 1.0 / depth

    def both(ref):
        return ref[...].reshape(rows, depth).astype(f32)

    def mean(v):
        return jnp.sum(v, -1, keepdims=True) * inv_width

    def normalize(v):
        center = v - mean(v)
        inverse = lax.rsqrt(mean(center * center) + norm_eps)
        return center * inverse, inverse

    def back(up, normed, inverse, gain):
        scaled = up * gain
        return inverse * (scaled - mean(scaled) - normed * mean(scaled * normed))
    norms = u_v[0, :, 1728:1736].astype(f32).T
    gains = [norms[i : i + 1, :] for i in range(4)]
    att = [att_v[tt].reshape(rows, width) for tt in range(4)]
    attn = dot_nt(att[0], u_v[0, :, 1536:1728])
    for tt in range(1, 4):
        attn += dot_nt(att[tt], u_v[tt, :, 1536:1728])
    normed_one, inverse_one = normalize(both(r.tok) + attn)
    hidden = normed_one * gains[0] + gains[1]
    hidden_b = hidden.astype(bf16)
    cube = 0.044715
    root = 0.7978845608028654

    def up_step(tt, mixed):
        upper = dot_nn(hidden_b, u_v[tt, :, 0:768])
        square = upper * upper
        th = jnp.tanh(root * upper * (1.0 + cube * square))
        act_t = (0.5 * upper * (1.0 + th)).astype(bf16)
        act[tt] = act_t
        bend = 0.5 * (1.0 + th) + 0.5 * upper * (1.0 - th * th) * root * (1.0 + 3.0 * cube * square)
        slope[tt] = bend.astype(bf16)
        return mixed + dot_nt(act_t, u_v[tt, :, 768:1536])
    second = t - 1 + 2 * ((3 - t) // 3)
    fourth = 3 * (1 - t // 2)
    x_step(3, 1)
    core_wait(t, 1)
    mixed = up_step(t, jnp.zeros((rows, depth), f32))
    y_step(2, 1)
    core_wait(second, 1)
    mixed = up_step(second, mixed)
    core_wait(6 - t - second - fourth, 1)
    mixed = up_step(6 - t - second - fourth, mixed)
    y_step(3, 1)
    core_wait(fourth, 1)
    mixed = up_step(fourth, mixed)
    there = r.live.at[1 - c]
    remote(there, there, r.y_sem.at[4], r.y_sem.at[5], me.ydev).wait_recv()
    there = r.teach.at[1 - c]
    remote(there, there, r.y_sem.at[6], r.y_sem.at[7], me.ydev).wait_recv()
    tally_take(2)
    for copy, pred in sends:
        when(pred, copy.wait_send)
    r.count[...] = r.tally[5]
    sends.clear()
    normed_two, inverse_two = normalize(hidden + mixed)
    result = normed_two * gains[2] + gains[3]

    r.piece[...] = result.astype(bf16).reshape(2, 128, depth)
    lo = r.lo
    lo_send = remote(r.piece.at[1 - c], lo.at[c, part], r.s_sem.at[0], r.s_sem.at[1], me.ydev)
    lo_send.start()
    own_lo = pltpu.make_async_copy(r.piece.at[c], lo.at[c, part], r.load_sem.at[1])
    own_lo.start()

    def lo_block(tt):
        return lo.at[:, pl.ds(pl.multiple_of(tt * 128, 128), 128), :]

    lo_line = Line(me, go, lo_block, r.lo_send, r.lo_recv)

    alive = jnp.concatenate([column(r.live[s, :, part]) for s in range(2)], 0)
    row = lax.broadcasted_iota(jnp.int32, (rows, 1), 0)
    place = jnp.where(row < 128, row, row - 128 + half) + t * 128
    live = jnp.where((alive == 1.0) & (place < length), 1.0, 0.0)
    differ = result - both(r.teach)
    weighed = differ * live
    missed = jnp.sum(jnp.sum(weighed * differ, 1, keepdims=True), 0, keepdims=True)
    grad_y = weighed * (2.0 / (r.count[0:1, 0:1] * depth))
    sums = [None] * 4
    sums[2] = jnp.sum(grad_y * normed_two, 0, keepdims=True)
    sums[3] = jnp.sum(grad_y, 0, keepdims=True)
    grad_two = back(grad_y, normed_two, inverse_two, gains[2])
    gm = grad_two.astype(bf16)
    gm_t = grad_two.T.astype(bf16)
    hidden_t = hidden.T.astype(bf16)
    there = lo.at[1 - c, part]
    lo_there = remote(there, there, r.s_sem.at[0], r.s_sem.at[1], me.ydev)
    lo_first = lo_line.first()
    sends.extend(lo_first)

    far = 1 - x
    trio = (me.core, me.xdev, me.ydev)

    def region(ref, unit, at, n, whole=None):
        rows_at = pl.ds(pl.multiple_of(at, qrows), n)
        if whole is not None:
            return ref.at[unit, rows_at, :]
        return ref.at[:, rows_at, FF_COLS:UW] if unit is TAIL else ref.at[unit, rows_at, 0:FF_COLS]

    def g_rows(unit, ff):
        return region(g_v, unit, ff * rows_f, rows_f)

    def rc_rows(xx, unit, at=0, n=rows_f):
        return region(u_v, unit, xx * rows_f + at, n)

    def room(n):
        return lambda unit, i: region(u_v, unit, (4 + n) * hrows + i * qrows, qrows)

    xg_at, yg_at = room(0), room(1)

    def d_at(ref, unit):
        return ref.at[:, :, FF_COLS:UW] if unit is TAIL else ref.at[unit, :, 0:FF_COLS]

    def slot(unit):
        return 4 if unit is TAIL else unit

    def credit(unit):
        for j, dev in enumerate(trio):
            pl.semaphore_signal(r.free.at[j, slot(unit)], inc=1, device_id=dev, device_id_type=MESH)

    def rc_copies(unit):
        return [
            remote(g_rows(unit, xx * 2 + 1 - k), rc_rows(xx, unit), r.rc_send.at[xx, slot(unit)],
                   r.rc_recv.at[xx, slot(unit)], me.core)
            for xx in (far, x)
        ]

    def far_copies(unit):
        i = slot(unit)
        h, other = c * hrows, (1 - c) * hrows
        return [
            remote(rc_rows(far, unit, other, qrows), d_at(r.dx, unit), r.dx_send.at[i], r.dx_recv.at[i], me.xdev),
            remote(rc_rows(far, unit, other + qrows, qrows), d_at(r.dy, unit), r.dy_send.at[i], r.dy_recv.at[i], me.ydev),
            remote(rc_rows(far, unit, h, qrows), xg_at(unit, 0), r.xg_send.at[i, 0], r.xg_recv.at[i, 0], me.xdev),
        ]

    def rc_step(unit):
        pl.semaphore_wait(r.free.at[0, slot(unit)], 1)
        for copy in rc_copies(unit):
            copy.start()

    def core_step(xx, unit):
        view = rc_rows(xx, unit)
        i = slot(unit)
        remote(view, view, r.rc_send.at[xx, i], r.rc_recv.at[xx, i], me.core).wait_recv()
        add_rows(view, view, g_rows(unit, xx * 2 + k))

    def far_step(unit):
        core_step(far, unit)
        for j in (1, 2):
            pl.semaphore_wait(r.free.at[j, slot(unit)], 1)
        for copy in far_copies(unit):
            copy.start()

    def near_step(unit):
        core_step(x, unit)
        i = slot(unit)
        mine = rc_rows(x, unit, (1 - c) * hrows + qrows, qrows)
        go(remote(mine, yg_at(unit, 1), r.yg_send.at[i, 1], r.yg_recv.at[i, 1], me.ydev))

    def diag_step(unit):
        i = slot(unit)
        dx, dy = d_at(r.dx, unit), d_at(r.dy, unit)
        remote(dx, dx, r.dx_send.at[i], r.dx_recv.at[i], me.xdev).wait_recv()
        mine = rc_rows(x, unit, (1 - c) * hrows, qrows)
        add_rows(mine, mine, dx)
        go(remote(mine, yg_at(unit, 0), r.yg_send.at[i, 0], r.yg_recv.at[i, 0], me.ydev))
        remote(dy, dy, r.dy_send.at[i], r.dy_recv.at[i], me.ydev).wait_recv()
        mine = rc_rows(far, unit, c * hrows + qrows, qrows)
        add_rows(mine, mine, dy)
        go(remote(mine, xg_at(unit, 1), r.xg_send.at[i, 1], r.xg_recv.at[i, 1], me.xdev))

    def sum_step(unit):
        at = slot(unit)
        for i in (0, 1):
            xg, yg = xg_at(unit, i), yg_at(unit, i)
            mine = rc_rows(x, unit, c * hrows + i * qrows, qrows)
            remote(xg, xg, r.xg_send.at[at, i], r.xg_recv.at[at, i], me.xdev).wait_recv()
            add_rows(mine, mine, xg)
            remote(yg, yg, r.yg_send.at[at, i], r.yg_recv.at[at, i], me.ydev).wait_recv()
            add_rows(mine, mine, yg)

    def sum_rows(tt):
        return u_v.at[tt, pl.ds(pl.multiple_of(x * rows_f + c * hrows, hrows), hrows), :]

    w_chain = Chain(
        me, go, sum_rows, lambda tt: u_v.at[tt, pl.ds(6 * hrows, hrows), :],
        lambda tt: u_v.at[tt, pl.ds(7 * hrows, hrows), :], r.zw_send, r.zw_recv_l, r.zw_recv_r,
    )

    def turn(i):
        return ((i + 1) % 2) * (3 - i // 2) + (i % 2) * (i // 2)

    ORDER = (3, 0, 2, 1)

    def down_step(i, total):
        tt = turn(i)
        ga = dot_nn(gm, u_v[tt, :, 768:1536])
        gu = (ga * slope[tt].astype(f32)).astype(bf16)
        g_v[tt, :, 768:1536] = dot_nn(gm_t, act[tt]).astype(bf16)
        g_v[tt, :, 0:768] = dot_nn(hidden_t, gu).astype(bf16)
        total = total + dot_nt(gu, u_v[tt, :, 0:768])
        credit(tt)

        @pl.when(i == 1)
        def _():
            lo_there.wait_recv()
            own_lo.wait()
            for copy, pred in lo_first:
                when(pred, copy.start)

        @pl.when(i >= 1)
        def _():
            rc_step(turn(i - 1))

        @pl.when(i >= 2)
        def _():
            far_step(turn(i - 2))

        return total

    grad_hidden = lax.fori_loop(0, 4, down_step, grad_two)
    rc_step(ORDER[3])
    sums[0] = jnp.sum(grad_hidden * normed_one, 0, keepdims=True)
    sums[1] = jnp.sum(grad_hidden, 0, keepdims=True)
    grad_one = back(grad_hidden, normed_one, inverse_one, gains[0])
    r.gone[...] = grad_one.reshape(2, 128, depth)
    ga = grad_one.astype(bf16)
    gatt, do_in = r.gatt, r.do_in
    for tt in range(4):
        back_t = dot_nn(ga, u_v[tt, :, 1536:1728]).astype(bf16)
        gatt[tt] = back_t.reshape(2, 128, width)
    for d in (1, 2, 3):
        to = (t + d) % 4
        go(remote(gatt.at[to], do_in.at[t], r.a_send.at[d], r.a_recv.at[d], me.z(to)))
    do_in[t] = gatt[t]
    credit(TAIL)
    far_step(ORDER[2])
    ga_t = grad_one.T.astype(bf16)
    ez, ef = r.ez, r.ef
    mine_at = f * 2 + c
    ez[t] = jnp.concatenate(sums + [jnp.broadcast_to(missed, (4, depth))], 0)
    for d in (1, 2, 3):
        go(remote(ez.at[t], ez.at[t], r.e_sem.at[0, d], r.e_sem.at[1, d], me.z((t + d) % 4)))

    def sums_on():
        for d in (1, 2, 3):
            src = ez.at[(t + 4 - d) % 4]
            remote(src, src, r.e_sem.at[0, d], r.e_sem.at[1, d], me.z(t)).wait_recv()
        ef[mine_at] = (ez[0] + ez[1]) + (ez[2] + ez[3])
        for d, dev in me.owners():
            go(remote(ef.at[mine_at], ef.at[mine_at], r.e_sem.at[0, 3 + d], r.e_sem.at[1, 3 + d], dev))

    def sums_end():
        for d, dev in me.owners():
            ff, cc = me.flipped(d)
            src = ef.at[ff * 2 + cc]
            remote(src, src, r.e_sem.at[0, 3 + d], r.e_sem.at[1, 3 + d], dev).wait_recv()
        total = ef[0]
        for i in range(1, 8):
            total += ef[i]
        r.sums[...] = total

    for tt in range(4):
        g_v[tt, :, 1536:1728] = dot_nn(ga_t, att[tt]).astype(bf16)
        g_v[tt, :, 1728:1792] = jnp.zeros((depth, UW - 1728), bf16)
    rc_step(TAIL)
    near_step(ORDER[0])
    far_step(ORDER[3])
    near_step(ORDER[1])
    lo_line.step(1)
    far_step(TAIL)
    near_step(ORDER[2])
    near_step(ORDER[3])
    near_step(TAIL)
    for unit in (*ORDER, TAIL):
        sends.extend((copy, None) for copy in rc_copies(unit) + far_copies(unit))

    do, proj, dqt = r.do, r.proj, r.dqt
    dk, dv = r.bias.at[:, 0:HD], r.bias.at[:, 128 : 128 + HD]
    for d in (1, 2, 3):
        src = (t + 4 - d) % 4
        remote(do_in.at[src], do_in.at[src], r.a_send.at[d], r.a_recv.at[d], me.z(src)).wait_recv()
    for s in range(2):
        for tt in range(4):
            at = s * half + tt * 128
            for h in range(heads):
                do[h, at : at + 128, :] = do_in[tt, s, :, h * HD : (h + 1) * HD]
    q_v, k_v, v_v, kt_v, pt_v, t_v, w_v = (r.q_v, r.k_v, r.v_v, r.kt_v, r.pt_v, r.t_v, r.w_v)
    scale = HD ** (-0.5)

    def attend_back(h):
        dk[...] = jnp.zeros((seq, HD), f32)
        dv[...] = jnp.zeros((seq, HD), f32)

        def step(i, carry):
            cols = pl.ds(pl.multiple_of(i * wide, wide), wide)
            mine = do[h, cols, :]
            probs = pt_v[h, :, cols]
            gp = dot_nt(v_v[h], mine)
            pf = probs.astype(f32)
            mix = jnp.sum(pf * gp, 0, keepdims=True)
            gs = (pf * (gp - mix)).astype(bf16)
            dk[...] += dot_nn(gs, q_v[h, cols, :])
            dv[...] += dot_nn(probs, mine)
            dqt[h * HD : (h + 1) * HD, cols] = dot_nn(kt_v[h * HD : (h + 1) * HD, :], gs)
            return carry

        lax.fori_loop(0, seq // wide, step, 0)
        proj[1, :, h * HD : (h + 1) * HD] = (dk[...] * scale).astype(bf16)
        proj[2, :, h * HD : (h + 1) * HD] = dv[...].astype(bf16)
    attend_back(0)
    diag_step(ORDER[0])
    lo_line.step(2)
    diag_step(ORDER[1])
    attend_back(1)
    diag_step(TAIL)
    diag_step(ORDER[2])
    attend_back(2)
    lo_send.wait_send()
    proj[0] = (dqt[...].T * scale).astype(bf16)
    ip = r.ip

    def input_part(s):
        def rows_step(i, carry):
            at = pl.ds(pl.multiple_of(s * half + i * 128, 128), 128)
            total = dot_nt(proj[0, at, :], w_v[0])
            for j in (1, 2):
                total += dot_nt(proj[j, at, :], w_v[j])
            ip[s, i] = total.astype(bf16)
            return carry

        lax.fori_loop(0, half // 128, rows_step, 0)

    def ip_chain(j, s):
        return Chain(
            me, go, lambda tt: ip.at[s, tt], lambda tt: act.at[tt, pl.ds(j * 128, 128), :], lambda tt: slope.at[tt, pl.ds(j * 128, 128), :],
            r.i_send.at[j], r.i_recv_l.at[j], r.i_recv_r.at[j],
        )

    chains = [ip_chain(0, 1 - c), ip_chain(1, c)]
    ig, igp, qg, qc, qs = r.ig, r.piece, r.qg, r.qc, r.q_sem

    def q_rows(ff):
        return qg.at[:, pl.ds(pl.multiple_of(ff * rows_f, rows_f), rows_f), :]

    def finish(j, s):
        chains[j].end()
        igp[j] = (ip[s, t].astype(f32) + r.gone[s]).astype(bf16)

    def ig_line(j, s):
        def block(tt):
            return ig.at[s, pl.ds(pl.multiple_of(tt * 128, 128), 128), :]

        return Line(me, go, block, r.ig_send.at[j], r.ig_recv.at[j])

    lines = [ig_line(0, c), ig_line(1, 1 - c)]

    def sum_pass(tt, passes):
        sum_step(tt)
        for at, way in passes:
            w_chain.pass_on(at, way)

    def q_take(i, j, dev):
        remote(qc.at[i], qc.at[i], qs.at[j], qs.at[j + 1], dev).wait_recv()

    def q_add(i, ff):
        qc[i] = qc[i] + qg[:, pl.ds(pl.multiple_of(ff * rows_f, rows_f), rows_f), :]

    def chain_pass(j, lo_at, hi_at):
        for tt, way in CHAIN_ORDER[lo_at:hi_at]:
            chains[j].pass_on(tt, way)

    input_part(1 - c)
    chain_pass(0, 0, 2)
    input_part(c)
    chain_pass(0, 2, 4)
    chain_pass(1, 0, 2)
    sum_step(TAIL)
    sum_pass(3, CHAIN_ORDER[:1])
    sum_pass(0, CHAIN_ORDER[1:2])
    chain_pass(0, 4, 6)
    finish(0, 1 - c)
    go(remote(igp.at[0], ig.at[c, part], r.s_sem.at[2], r.s_sem.at[3], me.ydev))
    diag_step(ORDER[3])
    sums_on()
    chain_pass(1, 2, 4)
    for j in range(3):
        qg[j] = dot_tn(t_v[...], proj[j]).astype(bf16)
    go(remote(q_rows(far * 2 + 1 - k), qc.at[0], qs.at[0], qs.at[1], me.core))
    go(remote(q_rows(x * 2 + 1 - k), qc.at[1], qs.at[2], qs.at[3], me.core))
    chain_pass(1, 4, 6)
    there = ig.at[1 - c, part]
    remote(there, there, r.s_sem.at[2], r.s_sem.at[3], me.ydev).wait_recv()
    lines[1].start()
    finish(1, c)
    own_ig = pltpu.make_async_copy(igp.at[1], ig.at[c, part], r.load_sem.at[2])
    own_ig.start()
    lines[0].start(igp.at[1])
    q_take(0, 0, me.core)
    q_add(0, far * 2 + k)
    go(remote(qc.at[0], qc.at[2], qs.at[4], qs.at[5], me.xdev))
    q_take(1, 2, me.core)
    q_add(1, x * 2 + k)
    lo_line.step(3)
    sum_pass(2, ((2, 0),))
    sum_pass(1, ((1, 1), (1, 0), (2, 1)))
    lines[1].step(1)
    q_take(2, 4, me.xdev)
    qc[1] = qc[1] + qc[2]
    go(remote(qc.at[1], qc.at[3], qs.at[6], qs.at[7], me.ydev))
    lines[0].step(1)
    w_chain.end()
    fin = r.dx

    def fin_half(h):
        return fin.at[pl.ds(h * 2, 2)]

    for i in (0, 1):
        fin[c * 2 + i] = region(u_v, t, x * rows_f + c * hrows + i * qrows, qrows, 0)[...]
    go(remote(fin_half(c), fin_half(c), r.s_sem.at[4], r.s_sem.at[5], me.ydev))
    q_take(3, 6, me.ydev)
    qsum = r.qsum
    total = jnp.zeros((1, width), f32)
    for j in range(3):
        qsum[j] = qc[1, j].astype(f32) + qc[3, j].astype(f32)
        total += jnp.sum(qsum[j] * qsum[j], 0, keepdims=True)
    total = 0.5 * jnp.sum(total, 1, keepdims=True)

    def square_step(i, carry):
        for j in (0, 1):
            row = fin[c * 2 + j, pl.ds(pl.multiple_of(i * 16, 16), 16), :].astype(f32)
            carry += jnp.sum(row * row, 0, keepdims=True)
        return carry

    wide_total = lax.fori_loop(0, qrows // 16, square_step, jnp.zeros((1, UW), f32))
    total += jnp.sum(wide_total, 1, keepdims=True)
    sz, sf = r.sz, r.sf
    sz[t] = jnp.broadcast_to(total, (8, 128))
    for d in (1, 2, 3):
        go(remote(sz.at[t], sz.at[t], r.f_sem.at[0, d], r.f_sem.at[1, d], me.z((t + d) % 4)))
    lines[0].step(2)
    lines[1].step(2)
    for d in (1, 2, 3):
        src = sz.at[(t + 4 - d) % 4]
        remote(src, src, r.f_sem.at[0, d], r.f_sem.at[1, d], me.z(t)).wait_recv()
    mine = f * 2 + c
    sf[mine] = (sz[0] + sz[1]) + (sz[2] + sz[3])
    for d, dev in me.owners():
        go(remote(sf.at[mine], sf.at[mine], r.f_sem.at[0, 3 + d], r.f_sem.at[1, 3 + d], dev))
    lines[0].step(3)
    lines[1].step(3)
    remote(fin_half(1 - c), fin_half(1 - c), r.s_sem.at[4], r.s_sem.at[5], me.ydev).wait_recv()
    out_copy = pltpu.make_async_copy(fin, r.gsum, r.load_sem.at[0])
    out_copy.start()
    sums_end()
    for d, dev in me.owners():
        ff, cc = me.flipped(d)
        src = sf.at[ff * 2 + cc]
        remote(src, src, r.f_sem.at[0, 3 + d], r.f_sem.at[1, 3 + d], dev).wait_recv()
    all_sq = sf[0]
    for i in range(1, 8):
        all_sq += sf[i]
    r.squares[...] = all_sq
    for copy, pred in sends:
        when(pred, copy.wait_send)
    out_copy.wait()
    own_ig.wait()


def train(lengths, tokens, teacher, qkv, up, down, out, norm, blocks, valid):
    seq = tokens.shape[1] * 2
    width = qkv.shape[2]
    heads = width // HD
    rows_f = qkv.shape[1]
    depth = rows_f * 4
    vm = pl.BlockSpec(memory_space=pltpu.VMEM)
    smem = pl.BlockSpec(memory_space=pltpu.SMEM)
    hbm = pl.BlockSpec(memory_space=pl.ANY)
    dma = pltpu.SemaphoreType.DMA

    def vb(*shape):
        return pltpu.VMEM(shape, bf16)

    def vf(*shape):
        return pltpu.VMEM(shape, f32)

    ins = dict(
        lengths=(lengths, smem), tokens=(tokens, hbm), teacher=(teacher, hbm), qkv=(qkv, vm), up=(up, vm), down=(down, vm),
        out=(out, vm), norm=(norm, vm), blocks=(blocks, vm), valid=(valid, vm),
    )
    qr = rows_f // 4
    outs = dict(
        lo=((2, seq // 2, depth), bf16, hbm),
        ig=((2, seq // 2, depth), bf16, hbm),
        gsum=((4, qr, UW), bf16, hbm),
        qsum=((3, rows_f, width), f32, vm),
        sums=((8, depth), f32, vm),
        squares=((8, 128), f32, vm),
        count=((8, 128), f32, vm),
    )
    scratch = dict(
        att_v=vb(4, 2, 128, width), u_v=vb(4, depth, UW), pt_v=vb(heads, seq, seq), q_v=vb(heads, seq, HD),
        k_v=vb(heads, seq, HD), v_v=vb(heads, seq, HD), kt_v=vb(width, seq), w_v=vb(3, depth, width), t_v=vb(seq, depth),
        tok=vb(2, 128, depth), teach=vb(2, 128, depth), live=vf(2, 8, seq // 2), upack=vb(rows_f, UW),
        qkvb=vb(3, rows_f, width), rbt=vf(2, 8, 128), mask=vf(2, 8, seq // 2), tally=vf(6, 8, 128), vt=vb(width, seq),
        rb=vf(2, 8, 128), level=vf(seq // BLK, seq), bias=vf(seq, 256), loc_sem=dma((5,)), w_sem=dma((6,)), y_sem=dma((8,)),
        z_send=dma((2, 2, 4, 2)), z_recv=dma((2, 4, 2)), x_send=dma((2, 4)), x_recv=dma((2, 4)), yw_send=dma((2, 4)),
        yw_recv=dma((2, 4)),
        c_send=dma((2, 4)), c_recv=dma((2, 4)), h_send=dma((2, 4, 2)), h_recv=dma((2, 4, 2)), o_send=dma((2, 4)), o_recv=dma((2, 4)),
        n_sem=dma((2, 3)),
        g_v=vb(4, depth, UW), act=vb(4, 256, 768),
        slope=vb(4, 256, 768), piece=vb(2, 128, depth), gone=vf(2, 128, depth), gatt=vb(4, 2, 128, width),
        do_in=vb(4, 2, 128, width), dx=vb(4, qr, UW), dy=vb(4, qr, UW), do=vb(heads, seq, HD), proj=vb(3, seq, width),
        dqt=vf(width, seq), ip=vb(2, 4, 128, depth),
        qg=vb(3, depth, width), qc=vb(4, 3, rows_f, width),
        load_sem=dma((15,)), s_sem=dma((6,)), lo_send=dma((2, 4)), lo_recv=dma((4,)), a_send=dma((4,)), a_recv=dma((4,)),
        rc_send=dma((2, 5)), rc_recv=dma((2, 5)), dx_send=dma((5,)), dx_recv=dma((5,)), dy_send=dma((5,)),
        dy_recv=dma((5,)), xg_send=dma((5, 2)), xg_recv=dma((5, 2)), yg_send=dma((5, 2)), yg_recv=dma((5, 2)),
        zw_send=dma((4,)), zw_recv_l=dma((4,)), zw_recv_r=dma((4,)), i_send=dma((2, 4)), i_recv_l=dma((2, 4)),
        i_recv_r=dma((2, 4)), ig_send=dma((2, 2, 4)), ig_recv=dma((2, 4)), q_sem=dma((8,)), ez=vf(4, 8, depth), ef=vf(8, 8, depth),
        sz=vf(4, 8, 128), sf=vf(8, 8, 128), e_sem=dma((2, 11)), f_sem=dma((2, 11)),
        free=pltpu.SemaphoreType.REGULAR((3, 5)),
    )
    return pl.pallas_call(
        functools.partial(train_kernel, (*ins, *outs, *scratch)),
        name="train",
        out_shape=[jax.ShapeDtypeStruct(s, d) for s, d, _ in outs.values()],
        in_specs=[m for _, m in ins.values()],
        out_specs=[m for _, _, m in outs.values()],
        scratch_shapes=list(scratch.values()),
        compiler_params=pltpu.CompilerParams(
            collective_id=0, has_side_effects=True, vmem_limit_bytes=62 * 2**20
        ),
    )(*(a for a, _ in ins.values()))


def update_kernel(kinds, names, *refs):
    r = types.SimpleNamespace(**dict(zip(names, refs, strict=True)))
    f = lax.axis_index("fsdp")
    copies = [pltpu.make_async_copy(getattr(r, n), getattr(r, n + "_v"), r.in_sem.at[i]) for i, n in enumerate(kinds[0])]
    ready = dict(zip(kinds[0], copies, strict=True))
    for copy in copies:
        copy.start()
    outs = {
        n: pltpu.make_async_copy(getattr(r, n + "_v"), getattr(r, n), r.out_sem.at[i]) for i, n in enumerate(kinds[1])
    }
    depth = r.sums.shape[1]
    rows_f = depth // 4
    sums = r.sums[0:4, :]
    total = r.squares[0:1, 0:1] + jnp.sum(jnp.sum(sums * sums, 1, keepdims=True), 0, keepdims=True)
    norm = jnp.sqrt(total)
    factor = jnp.minimum(1.0, clip_level / (norm + 1e-06))
    r.norm[...] = norm
    r.loss[...] = r.sums[4:5, 0:1] / (r.count[0:1, 0:1] * depth)
    steps = jnp.full((1, 1), r.steps[0]).astype(f32)
    one = 1.0 / (1.0 - jnp.exp(steps * -0.10536051565782628))
    two = 1.0 / (1.0 - jnp.exp(steps * -0.0010005003335835335))

    def move(name, grad, at, rate):
        read = [getattr(r, f"{name}_{k}_v")[at] for k in "wms"]
        write = [getattr(r, f"{name}_{k}_new_v") for k in "wms"]
        clipped = grad * factor
        new_moment = beta_one * read[1] + (1.0 - beta_one) * clipped
        new_square = beta_two * read[2] + (1.0 - beta_two) * clipped * clipped
        step = new_moment * one / (jnp.sqrt(new_square * two) + adam_eps) + decay_rate * read[0]
        write[0][at] = read[0] - rate * step
        write[1][at] = new_moment
        write[2][at] = new_square

    def begin(name):
        for k in "wms":
            ready[f"{name}_{k}"].wait()

    def end(name):
        for k in "wms":
            outs[f"{name}_{k}_new"].start()

    def by_rows(name, work):
        begin(name)

        def one_step(i, carry):
            work(pl.ds(pl.multiple_of(i * 16, 16), 16))
            return carry

        lax.fori_loop(0, rows_f // 16, one_step, 0)
        end(name)

    every = slice(None)
    ready["gsum"].wait()
    by_rows("up", lambda rows: move("up", r.gsum_v[rows, 0:768].astype(f32), (rows, every), rate_list[2]))
    by_rows("down", lambda rows: move("down", r.gsum_v[rows, 768:1536].astype(f32), (rows, every), rate_list[3]))
    ready["ig"].wait()

    def cast_step(i, carry):
        rows = pl.ds(pl.multiple_of(i * 64, 64), 64)
        for s in range(2):
            r.input_grad_v[s, rows, :] = r.ig_v[s, rows, :].astype(f32)
        return carry

    lax.fori_loop(0, r.ig_v.shape[1] // 64, cast_step, 0)
    outs["input_grad"].start()
    ready["qsum"].wait()

    def qkv_rows(rows):
        for j in range(3):
            move("qkv", r.qsum_v[j, rows, :], (j, rows, every), rate_list[0])

    by_rows("qkv", qkv_rows)
    begin("out")
    move("out", r.gsum_v[:, 1536:1728].astype(f32).T, (every, every), rate_list[1])
    end("out")
    ready["lo"].wait()
    layer_out = pltpu.make_async_copy(r.lo_v, r.layer_out, r.out_sem.at[len(kinds[1])])
    layer_out.start()
    mine = sums[:, 0:rows_f]
    for i in range(1, 4):
        mine = jnp.where(f == i, sums[:, i * rows_f : (i + 1) * rows_f], mine)
    begin("norm")
    move("norm", mine, (every, every), rate_list[4])
    end("norm")
    for copy in (*outs.values(), layer_out):
        copy.wait()


def update(steps, lo, ig, gsum, qsum, sums, squares, count, state):
    vm = pl.BlockSpec(memory_space=pltpu.VMEM)
    smem = pl.BlockSpec(memory_space=pltpu.SMEM)
    hbm = pl.BlockSpec(memory_space=pl.ANY)
    shape = jax.ShapeDtypeStruct
    ins = dict(steps=(steps, smem), sums=(sums, vm), squares=(squares, vm), count=(count, vm))
    moved = dict(gsum=gsum)
    order = ("up", "down", "qkv", "out", "norm")
    for name in order:
        if name == "qkv":
            moved.update(ig=ig, qsum=qsum)
        moved.update({f"{name}_{k}": a for k, a in zip("wms", state[name])})
    moved.update(lo=lo)
    ins.update({n: (a, hbm) for n, a in moved.items()})
    made = dict(input_grad=shape(ig.shape, f32))
    made.update({f"{n}_{k}_new": shape(a.shape, f32) for n, group in state.items() for k, a in zip("wms", group)})
    outs = dict(layer_out=(shape(lo.shape, bf16), hbm), loss=(shape((1, 1), f32), vm), norm=(shape((1, 1), f32), vm))
    outs.update({n: (a, hbm) for n, a in made.items()})
    scratch = {n + "_v": pltpu.VMEM(a.shape, a.dtype) for n, a in (*moved.items(), *made.items())}
    scratch.update(in_sem=pltpu.SemaphoreType.DMA((len(moved),)), out_sem=pltpu.SemaphoreType.DMA((len(made) + 1,)))
    results = pl.pallas_call(
        functools.partial(update_kernel, (tuple(moved), tuple(made)), (*ins, *outs, *scratch)),
        name="update",
        out_shape=[a for a, _ in outs.values()],
        in_specs=[m for _, m in ins.values()],
        out_specs=[m for _, m in outs.values()],
        scratch_shapes=list(scratch.values()),
        compiler_params=pltpu.CompilerParams(vmem_limit_bytes=62 * 2**20),
    )(*(a for a, _ in ins.values()))
    got = dict(zip(outs, results, strict=True))
    return got.pop("layer_out"), got.pop("loss"), got.pop("input_grad"), got.pop("norm"), *got.values()


def body_swapped(
    tokens,
    teacher,
    lengths,
    valid_mask,
    random_blocks,
    step_count,
    qkv_weight,
    out_weight,
    up_weight,
    down_weight,
    norm_params,
    qkv_moment,
    qkv_square,
    out_moment,
    out_square,
    up_moment,
    up_square,
    down_moment,
    down_square,
    norm_moment,
    norm_square,
):
    blocks = jnp.transpose(random_blocks, (2, 0, 1))
    lo, ig, gsum, qsum, sums, squares, count = train(
        lengths, tokens, teacher, qkv_weight, up_weight, down_weight.T, out_weight, norm_params, blocks, valid_mask
    )
    gsum = gsum.reshape(-1, UW)
    state = dict(
        qkv=(qkv_weight, qkv_moment, qkv_square),
        out=(out_weight, out_moment, out_square),
        up=(up_weight, up_moment, up_square),
        down=(down_weight.T, down_moment.T, down_square.T),
        norm=(norm_params, norm_moment, norm_square),
    )
    layer_out, loss, input_grad, grad_norm, *new = update(
        step_count, lo, ig, gsum, qsum, sums, squares, count, state
    )
    new[9:12] = [v.T for v in new[9:12]]
    return (layer_out, loss.reshape(()), input_grad, grad_norm.reshape(()), *new)


def solution(mesh):
    in_specs = (
        P("fsdp", "ctx", None),
        P("fsdp", "ctx", None),
        P("fsdp"),
        P("fsdp", "ctx"),
        P("fsdp", "ctx", None),
        P(),
        P(None, "fsdp", "tp"),
        P("tp", "fsdp"),
        P("fsdp", "tp"),
        P("tp", "fsdp"),
        P(None, "fsdp"),
        P(None, "fsdp", "tp"),
        P(None, "fsdp", "tp"),
        P("tp", "fsdp"),
        P("tp", "fsdp"),
        P("fsdp", "tp"),
        P("fsdp", "tp"),
        P("tp", "fsdp"),
        P("tp", "fsdp"),
        P(None, "fsdp"),
        P(None, "fsdp"),
    )
    out_specs = (
        P("fsdp", "ctx", None),
        P(),
        P("fsdp", "ctx", None),
        P(),
        P(None, "fsdp", "tp"),
        P(None, "fsdp", "tp"),
        P(None, "fsdp", "tp"),
        P("tp", "fsdp"),
        P("tp", "fsdp"),
        P("tp", "fsdp"),
        P("fsdp", "tp"),
        P("fsdp", "tp"),
        P("fsdp", "tp"),
        P("tp", "fsdp"),
        P("tp", "fsdp"),
        P("tp", "fsdp"),
        P(None, "fsdp"),
        P(None, "fsdp"),
        P(None, "fsdp"),
    )
    sizes = dict(mesh.shape)
    small = sizes == {"fsdp": 4, "ctx": 2, "tp": 4}
    body = body_swapped if small else body_general
    return jax.shard_map(body, mesh=mesh, in_specs=in_specs, out_specs=out_specs, check_vma=False)
```

```python
import functools
import types
from functools import partial

import jax
import jax.numpy as jnp
from jax import lax
from jax.experimental import pallas as pl
from jax.experimental.pallas import tpu as pltpu
from jax.sharding import PartitionSpec as P

HD = 64
BLK = 64
MESH = pl.DeviceIdType.MESH
f32 = jnp.float32
bf16 = jnp.bfloat16

norm_eps = 1e-06
beta_one = 0.9
beta_two = 0.999
adam_eps = 1e-08
decay_rate = 0.01
clip_level = 0.001
rate_list = (0.04, 0.4, 0.04, 0.02, 0.2)
negative = -1e30
VMEM_LIMIT = 58 * 2**20


def layer_norm(values, gain, shift):
    center = values - jnp.mean(values, -1, keepdims=True)
    inverse = lax.rsqrt(jnp.mean(center * center, -1, keepdims=True) + norm_eps)
    normed = center * inverse
    return (normed * gain + shift, normed, inverse)


def norm_backward(upstream, normed, inverse, gain):
    scaled = upstream * gain
    return inverse * (
        scaled
        - jnp.mean(scaled, -1, keepdims=True)
        - normed * jnp.mean(scaled * normed, -1, keepdims=True)
    )


def adam_update(weight, gradient, moment, square, factor, steps_done, rate):
    clipped = gradient * factor
    new_moment = beta_one * moment + (1.0 - beta_one) * clipped
    new_square = beta_two * square + (1.0 - beta_two) * clipped * clipped
    corrected = new_moment / (1.0 - beta_one**steps_done)
    scaled = new_square / (1.0 - beta_two**steps_done)
    new_weight = weight - rate * (corrected / (jnp.sqrt(scaled) + adam_eps) + decay_rate * weight)
    return (new_weight, new_moment, new_square)


def body_general(
    tokens,
    teacher,
    lengths,
    valid_mask,
    random_blocks,
    step_count,
    qkv_weight,
    out_weight,
    up_weight,
    down_weight,
    norm_params,
    qkv_moment,
    qkv_square,
    out_moment,
    out_square,
    up_moment,
    up_square,
    down_moment,
    down_square,
    norm_moment,
    norm_square,
):
    ctx_index = lax.axis_index("ctx")
    ctx_count = lax.axis_size("ctx")
    tp_index = lax.axis_index("tp")
    seqs_here, tok_count, width = tokens.shape
    local_blocks = tok_count // BLK
    block_count = local_blocks * ctx_count
    seq_len = tok_count * ctx_count
    width_local = qkv_weight.shape[2]
    heads_local = width_local // HD
    scale = HD ** (-0.5)
    full_qkv, full_out, full_up, full_down, full_norms = (
        lax.all_gather(qkv_weight.astype(bf16), "fsdp", axis=1, tiled=True),
        lax.all_gather(out_weight.astype(bf16), "fsdp", axis=1, tiled=True),
        lax.all_gather(up_weight.astype(bf16), "fsdp", axis=0, tiled=True),
        lax.all_gather(down_weight.astype(bf16), "fsdp", axis=1, tiled=True),
        lax.all_gather(norm_params.astype(bf16), "fsdp", axis=1, tiled=True),
    )
    gains = full_norms.astype(f32)
    projected = jnp.einsum("std,cde->stce", tokens, full_qkv, preferred_element_type=f32).astype(
        bf16
    )
    queries = projected[:, :, 0, :]
    kv_local = projected[:, :, 1:, :]
    gathered = lax.all_gather(kv_local, "ctx", axis=1, tiled=True)
    own_blocks = ctx_index * local_blocks + jnp.arange(local_blocks, dtype=jnp.int32)
    zero_row = own_blocks * 0
    window = jnp.stack([zero_row, zero_row + 1, own_blocks - 1, own_blocks, own_blocks + 1], -1)
    listed = jnp.concatenate(
        [jnp.broadcast_to(window[None], (seqs_here, local_blocks, 5)), random_blocks], -1
    )
    inside = (listed >= 0) & (listed < block_count)
    safe = jnp.clip(listed, 0, block_count - 1)
    key_pos = safe[..., None] * BLK + jnp.arange(BLK, dtype=jnp.int32)
    counted = (inside[..., None] & (key_pos < lengths[:, None, None, None])).reshape(
        seqs_here, local_blocks, 8 * BLK
    )
    key_live = jnp.arange(seq_len, dtype=jnp.int32)[None, :] < lengths[:, None]
    q_blocks = queries.reshape(seqs_here, local_blocks, BLK, heads_local, HD)
    head_rows = queries[:, : 2 * BLK].reshape(seqs_here, 2 * BLK, heads_local, HD)
    blocked = gathered.reshape(seqs_here, block_count, BLK, 2, width_local)
    flat = blocked.reshape(seqs_here * block_count, BLK, 2, width_local)
    offset = jnp.arange(seqs_here, dtype=jnp.int32)[:, None, None] * block_count
    picked = lax.map(
        lambda at: lax.dynamic_index_in_dim(flat, at, 0, keepdims=False), (safe + offset).reshape(-1)
    ).reshape(seqs_here, local_blocks, 8, BLK, 2, width_local)
    key_rows = picked[..., 0, :].reshape(seqs_here, local_blocks, 8 * BLK, heads_local, HD)
    value_rows = picked[..., 1, :].reshape(seqs_here, local_blocks, 8 * BLK, heads_local, HD)
    scores = (
        jnp.einsum("sbqhd,sbkhd->sbhqk", q_blocks, key_rows, preferred_element_type=f32) * scale
    )
    scores = jnp.where(counted[:, :, None, None, :], scores, negative)
    all_keys = gathered[:, :, 0, :].reshape(seqs_here, seq_len, heads_local, HD)
    all_values = gathered[:, :, 1, :].reshape(seqs_here, seq_len, heads_local, HD)
    wide_scores = (
        jnp.einsum("sqhd,skhd->shqk", head_rows, all_keys, preferred_element_type=f32) * scale
    )
    wide_scores = jnp.where(key_live[:, None, None, :], wide_scores, negative)
    top_value = jnp.max(scores, -1, keepdims=True)
    expo = jnp.exp(scores - top_value)
    summed = jnp.sum(expo, -1, keepdims=True)
    sparse_lse = top_value + jnp.log(summed)
    probs_b = (expo / summed).astype(bf16)
    sparse_out = jnp.einsum(
        "sbhqk,sbkhd->sbqhd", probs_b, value_rows, preferred_element_type=f32
    ).reshape(seqs_here, tok_count, width_local)
    wide_top = jnp.max(wide_scores, -1, keepdims=True)
    wide_expo = jnp.exp(wide_scores - wide_top)
    wide_sum = jnp.sum(wide_expo, -1, keepdims=True)
    wide_lse = wide_top + jnp.log(wide_sum)
    wide_probs = (wide_expo / wide_sum).astype(bf16)
    wide_out = jnp.einsum(
        "shqk,skhd->sqhd", wide_probs, all_values, preferred_element_type=f32
    ).reshape(seqs_here, 2 * BLK, width_local)
    is_first = ctx_index == 0
    row_ids = jnp.arange(tok_count, dtype=jnp.int32)
    global_row = (row_ids < 2 * BLK) & is_first
    rest_zeros = jnp.zeros((seqs_here, tok_count - 2 * BLK, width_local), f32)
    padded_wide = jnp.concatenate([wide_out, rest_zeros], 1)
    attended = jnp.where(global_row[None, :, None], padded_wide, sparse_out).astype(bf16)
    attn_part = jnp.einsum("ste,ed->std", attended, full_out, preferred_element_type=f32)
    positions = ctx_index * tok_count + row_ids
    live_rows = ((valid_mask == 1) & (positions[None, :] < lengths[:, None])).astype(f32)
    count_local = jnp.sum(live_rows)
    gelu_fn = partial(jax.nn.gelu, approximate=True)
    attn = lax.psum(attn_part.astype(jnp.bfloat16), "tp").astype(jnp.float32)
    hidden, normed_one, inverse_one = layer_norm(tokens.astype(f32) + attn, gains[0], gains[1])
    hidden_b = hidden.astype(bf16)
    upper = jnp.einsum("std,df->stf", hidden_b, full_up, preferred_element_type=f32)
    active_f, gelu_back = jax.vjp(gelu_fn, upper)
    active = active_f.astype(bf16)
    mixed = lax.psum(
        jnp.einsum("stf,fd->std", active, full_down, preferred_element_type=f32).astype(
            jnp.bfloat16
        ),
        "tp",
    ).astype(jnp.float32)
    result, normed_two, inverse_two = layer_norm(hidden + mixed, gains[2], gains[3])
    differ = result - teacher.astype(f32)
    error_local = jnp.sum(live_rows[..., None] * differ * differ)
    error_total, live_count = lax.psum((error_local, count_local), ("fsdp", "ctx"))
    loss_value = error_total / (live_count * width)
    grad_y = 2.0 * differ * live_rows[..., None] / (live_count * width)
    gain_two_grad = jnp.sum(grad_y * normed_two, (0, 1))
    bias_two_grad = jnp.sum(grad_y, (0, 1))
    grad_two = norm_backward(grad_y, normed_two, inverse_two, gains[2])
    grad_mixed = grad_two.astype(bf16)
    grad_active = jnp.einsum("std,fd->stf", grad_mixed, full_down, preferred_element_type=f32)
    grad_upper = gelu_back(grad_active)[0].astype(bf16)
    down_grad = jnp.einsum("stf,std->fd", active, grad_mixed, preferred_element_type=f32)
    up_grad = jnp.einsum("std,stf->df", hidden_b, grad_upper, preferred_element_type=f32)
    grad_hidden = grad_two + lax.psum(
        jnp.einsum("stf,df->std", grad_upper, full_up, preferred_element_type=f32).astype(
            jnp.bfloat16
        ),
        "tp",
    ).astype(jnp.float32)
    gain_one_grad = jnp.sum(grad_hidden * normed_one, (0, 1))
    bias_one_grad = jnp.sum(grad_hidden, (0, 1))
    grad_one = norm_backward(grad_hidden, normed_one, inverse_one, gains[0])
    norm_grad = jnp.stack([gain_one_grad, bias_one_grad, gain_two_grad, bias_two_grad], 0)
    grad_attn = grad_one.astype(bf16)
    out_grad = jnp.einsum("ste,std->ed", attended, grad_attn, preferred_element_type=f32)
    grad_attended = jnp.einsum(
        "std,ed->ste", grad_attn, full_out, preferred_element_type=f32
    ).astype(bf16)
    sparse_grad = jnp.where(global_row[None, :, None], jnp.zeros_like(grad_attended), grad_attended)
    sparse_grad = sparse_grad.reshape(seqs_here, local_blocks, BLK, heads_local, HD)
    probs = jnp.exp(scores - sparse_lse)
    grad_probs = jnp.einsum(
        "sbqhd,sbkhd->sbhqk", sparse_grad, value_rows, preferred_element_type=f32
    )
    row_dot = jnp.sum(probs * grad_probs, -1, keepdims=True)
    grad_scores = (probs * (grad_probs - row_dot)).astype(bf16)
    dq_sparse = (
        jnp.einsum("sbhqk,sbkhd->sbqhd", grad_scores, key_rows, preferred_element_type=f32) * scale
    )
    dk_rows = (
        jnp.einsum("sbhqk,sbqhd->sbkhd", grad_scores, q_blocks, preferred_element_type=f32) * scale
    )
    dv_rows = jnp.einsum(
        "sbhqk,sbqhd->sbkhd", probs.astype(bf16), sparse_grad, preferred_element_type=f32
    )
    list_grads = jnp.stack(
        [
            dk_rows.reshape(seqs_here, local_blocks, 8, BLK, width_local),
            dv_rows.reshape(seqs_here, local_blocks, 8, BLK, width_local),
        ],
        4,
    )
    seq_ids = jnp.broadcast_to(jnp.arange(seqs_here, dtype=jnp.int32)[:, None, None], safe.shape)
    kv_term = (
        jnp.zeros((block_count, seqs_here, BLK, 2, width_local), f32)
        .at[safe, seq_ids]
        .add(list_grads)
    )
    head_grad = jnp.where(
        is_first, grad_attended[:, : 2 * BLK], jnp.zeros_like(grad_attended[:, : 2 * BLK])
    )
    head_grad = head_grad.reshape(seqs_here, 2 * BLK, heads_local, HD)
    wide_probs_f = jnp.exp(wide_scores - wide_lse)
    wide_dprobs = jnp.einsum("sqhd,skhd->shqk", head_grad, all_values, preferred_element_type=f32)
    wide_dot = jnp.sum(wide_probs_f * wide_dprobs, -1, keepdims=True)
    wide_dscores = (wide_probs_f * (wide_dprobs - wide_dot)).astype(bf16)
    dq_wide = (
        jnp.einsum("shqk,skhd->sqhd", wide_dscores, all_keys, preferred_element_type=f32) * scale
    )
    split_scores = wide_dscores.reshape(seqs_here, heads_local, 2 * BLK, block_count, BLK)
    split_probs = wide_probs_f.astype(bf16).reshape(
        seqs_here, heads_local, 2 * BLK, block_count, BLK
    )
    dk_wide = (
        jnp.einsum("shqnb,sqhd->nsbhd", split_scores, head_rows, preferred_element_type=f32) * scale
    )
    dv_wide = jnp.einsum("shqnb,sqhd->nsbhd", split_probs, head_grad, preferred_element_type=f32)
    kv_term = kv_term + jnp.stack(
        [
            dk_wide.reshape(block_count, seqs_here, BLK, width_local),
            dv_wide.reshape(block_count, seqs_here, BLK, width_local),
        ],
        3,
    )
    kv_grads = lax.psum_scatter(
        kv_term.astype(jnp.bfloat16), "ctx", scatter_dimension=0, tiled=True
    ).astype(jnp.float32)
    kv_grads = jnp.transpose(kv_grads, (1, 0, 2, 3, 4)).reshape(
        seqs_here, tok_count, 2, width_local
    )
    dq_total = dq_sparse.reshape(seqs_here, tok_count, width_local) + jnp.concatenate(
        [dq_wide.reshape(seqs_here, 2 * BLK, width_local), rest_zeros], 1
    )
    grad_projected = jnp.concatenate([dq_total[:, :, None, :], kv_grads], 2).astype(bf16)
    qkv_grad = jnp.einsum("std,stce->cde", tokens, grad_projected, preferred_element_type=f32)
    input_part = jnp.einsum("stce,cde->std", grad_projected, full_qkv, preferred_element_type=f32)
    input_grad = grad_one + lax.psum(input_part.astype(jnp.bfloat16), "tp").astype(jnp.float32)
    local_grads = (qkv_grad, out_grad, up_grad, down_grad, norm_grad)
    owned = (
        lax.psum_scatter(
            local_grads[0].astype(jnp.bfloat16), "fsdp", scatter_dimension=1, tiled=True
        ).astype(jnp.float32),
        lax.psum_scatter(
            local_grads[1].astype(jnp.bfloat16), "fsdp", scatter_dimension=1, tiled=True
        ).astype(jnp.float32),
        lax.psum_scatter(
            local_grads[2].astype(jnp.bfloat16), "fsdp", scatter_dimension=0, tiled=True
        ).astype(jnp.float32),
        lax.psum_scatter(
            local_grads[3].astype(jnp.bfloat16), "fsdp", scatter_dimension=1, tiled=True
        ).astype(jnp.float32),
        lax.psum_scatter(
            local_grads[4].astype(jnp.bfloat16), "fsdp", scatter_dimension=1, tiled=True
        ).astype(jnp.float32),
    )
    shards = (
        lax.psum(owned[0].astype(jnp.bfloat16), "ctx").astype(jnp.float32),
        lax.psum(owned[1].astype(jnp.bfloat16), "ctx").astype(jnp.float32),
        lax.psum(owned[2].astype(jnp.bfloat16), "ctx").astype(jnp.float32),
        lax.psum(owned[3].astype(jnp.bfloat16), "ctx").astype(jnp.float32),
        lax.psum(owned[4].astype(jnp.bfloat16), "ctx").astype(jnp.float32),
    )
    matrix_squares = sum((jnp.sum(member * member) for member in shards[:4]))
    norm_squares = jnp.where(tp_index == 0, jnp.sum(shards[4] * shards[4]), 0.0)
    squares_total = lax.psum(matrix_squares + norm_squares, ("fsdp", "tp"))
    grad_norm = jnp.sqrt(squares_total)
    factor = jnp.minimum(1.0, clip_level / (grad_norm + 1e-06))
    steps_done = step_count[0].astype(f32)
    qkv_new = adam_update(
        qkv_weight, shards[0], qkv_moment, qkv_square, factor, steps_done, rate_list[0]
    )
    out_new = adam_update(
        out_weight, shards[1], out_moment, out_square, factor, steps_done, rate_list[1]
    )
    up_new = adam_update(
        up_weight, shards[2], up_moment, up_square, factor, steps_done, rate_list[2]
    )
    down_new = adam_update(
        down_weight, shards[3], down_moment, down_square, factor, steps_done, rate_list[3]
    )
    norm_new = adam_update(
        norm_params, shards[4], norm_moment, norm_square, factor, steps_done, rate_list[4]
    )
    return (
        result.astype(bf16),
        loss_value,
        input_grad,
        grad_norm,
        qkv_new[0],
        qkv_new[1],
        qkv_new[2],
        out_new[0],
        out_new[1],
        out_new[2],
        up_new[0],
        up_new[1],
        up_new[2],
        down_new[0],
        down_new[1],
        down_new[2],
        norm_new[0],
        norm_new[1],
        norm_new[2],
    )


def remote(src, dst, send, recv, dev):
    return pltpu.make_async_remote_copy(
        src_ref=src, dst_ref=dst, send_sem=send, recv_sem=recv, device_id=dev, device_id_type=MESH
    )


def dot_nn(a, b):
    return lax.dot_general(a, b, (((1,), (0,)), ((), ())), preferred_element_type=f32)


def dot_nt(a, b):
    return lax.dot_general(a, b, (((1,), (1,)), ((), ())), preferred_element_type=f32)


def dot_tn(a, b):
    return lax.dot_general(a, b, (((0,), (0,)), ((), ())), preferred_element_type=f32)


UW = 1792


class Peers:
    def __init__(self):
        f, c, t = lax.axis_index("fsdp"), lax.axis_index("ctx"), lax.axis_index("tp")
        x, k = f // 2, f % 2
        self.f, self.c, self.t = f, c, t
        self.f_core = x * 2 + (1 - k)
        self.f_x = (1 - x) * 2 + k
        self.f_xc = (1 - x) * 2 + (1 - k)
        self.core = (self.f_core, c, t)
        self.xdev = (self.f_x, c, t)
        self.ydev = (f, 1 - c, t)

    def z(self, t):
        return (self.f, self.c, t)

    def flipped(self, d):
        x, k = self.f // 2, self.f % 2
        x = 1 - x if d // 4 else x
        k = 1 - k if d % 2 else k
        return x * 2 + k, 1 - self.c if d // 2 % 2 else self.c

    def owners(self):
        return [(d, (*self.flipped(d), self.t)) for d in range(1, 8)]

    def barrier(self, whole=False):
        sem = pltpu.get_barrier_semaphore()
        devs = [dev for _, dev in self.owners()] if whole else [self.core, self.xdev, self.ydev]
        devs += [self.z((self.t + d) % 4) for d in (1, 2, 3)]
        for dev in devs:
            pl.semaphore_signal(sem, inc=1, device_id=dev, device_id_type=MESH)
        pl.semaphore_wait(sem, len(devs))


def column(row):
    return row.T[:, 0:1]


def add_rows(dst, a, b, step=16):
    if len(dst.shape) == 3:
        for i in range(dst.shape[0]):
            add_rows(dst.at[i], a.at[i], b.at[i], step)
        return

    def one(i, carry):
        rows = pl.ds(pl.multiple_of(i * step, step), step)
        dst[rows, :] = a[rows, :] + b[rows, :]
        return carry

    lax.fori_loop(0, dst.shape[0] // step, one, 0)


class Line:
    def __init__(self, me, go, block, send, recv):
        self.me, self.go, self.block, self.send, self.recv = me, go, block, send, recv

    def first(self, src=None):
        t = self.me.t
        mine = self.block(t)
        src = mine if src is None else src
        return [
            (remote(src, mine, self.send.at[0, t], self.recv.at[t], self.me.z(t + 1)), t < 3),
            (remote(src, mine, self.send.at[1, t], self.recv.at[t], self.me.z(t - 1)), t > 0),
        ]

    def start(self, src=None):
        for copy, pred in self.first(src):
            self.go(copy, pred)

    def step(self, d):
        t = self.me.t
        for tt, ok, on, nxt, way in ((t - d, t - d >= 0, t < 3, t + 1, 0), (t + d, t + d <= 3, t > 0, t - 1, 1)):
            piece = self.block(tt)
            pl.when(ok)(remote(piece, piece, self.send.at[way, tt], self.recv.at[tt], self.me.z(t)).wait_recv)
            if d < 3:
                self.go(remote(piece, piece, self.send.at[way, tt], self.recv.at[tt], self.me.z(nxt)), ok & on)


class Chain:
    def __init__(self, me, go, own, left, right, send, recv_l, recv_r):
        self.me, self.go, self.own, self.left, self.right = me, go, own, left, right
        self.send, self.recv_l, self.recv_r = send, recv_l, recv_r

    def arrived(self, tt, way):
        buf, recv = (self.left, self.recv_l) if way == 0 else (self.right, self.recv_r)
        remote(buf(tt), buf(tt), self.send.at[tt], recv.at[tt], self.me.z(self.me.t)).wait_recv()

    def pass_on(self, tt, way):
        t = self.me.t
        inner = (t > 0) if way == 0 else (t < 3)
        ahead = (tt > t) if way == 0 else (tt < t)
        buf, recv = (self.left, self.recv_l) if way == 0 else (self.right, self.recv_r)

        @pl.when(ahead & inner)
        def _():
            self.arrived(tt, way)
            add_rows(self.own(tt), self.own(tt), buf(tt))

        to = self.me.z(t + 1 if way == 0 else t - 1)
        self.go(remote(self.own(tt), buf(tt), self.send.at[tt], recv.at[tt], to), ahead)

    def end(self):
        t = self.me.t
        mine = self.own(t)

        @pl.when(t > 0)
        def _():
            self.arrived(t, 0)
            add_rows(mine, mine, self.left(t))

        @pl.when(t < 3)
        def _():
            self.arrived(t, 1)
            add_rows(mine, mine, self.right(t))


CHAIN_ORDER = ((3, 0), (0, 1), (2, 0), (1, 1), (1, 0), (2, 1))


TAIL = None
FF_COLS = 1536


def train_kernel(names, *refs):
    r = types.SimpleNamespace(**dict(zip(names, refs, strict=True)))
    me = Peers()
    f, c, t = me.f, me.c, me.t
    seq = r.t_v.shape[0]
    half = seq // 2
    rows_f = r.qkvb.shape[1]
    sends = []
    heads = r.q_v.shape[0]
    width = heads * HD
    depth = rows_f * 4
    hrows = rows_f // 2
    qrows = rows_f // 4
    r.qkvb[...] = r.qkv[...].astype(bf16)
    r.upack[:, 0:768] = r.up[...].astype(bf16)
    r.upack[:, 768:1536] = r.down[...].astype(bf16)
    tail = jnp.concatenate(
        [r.out[...].T, jnp.concatenate([r.norm[...], jnp.zeros((60, rows_f), f32)], 0).T], 1
    )
    r.upack[:, 1536:1792] = tail.astype(bf16)
    for s in range(2):
        r.rbt[s] = jnp.zeros((8, 128), f32)
        r.rbt[s, 0:3, 0 : r.blocks.shape[2]] = r.blocks[:, s, :].astype(f32)
        r.mask[s] = jnp.broadcast_to(r.valid[s : s + 1, :].astype(f32), (8, half))
    spot = c * half + lax.broadcasted_iota(jnp.int32, (1, half), 1)
    found = jnp.zeros((1, half), f32)
    for s in range(2):
        found += jnp.where((r.valid[s : s + 1, :] == 1) & (spot < r.lengths[s]), 1.0, 0.0)
    r.count[...] = jnp.broadcast_to(jnp.sum(found, 1, keepdims=True), (8, 128))
    me.barrier(True)

    def go(copy, pred=None):
        if pred is None:
            copy.start()
        else:
            pl.when(pred)(copy.start)
        sends.append((copy, pred))
    own_rows = pl.ds(pl.multiple_of(c * half, half), half)
    go(remote(r.tokens.at[1 - c], r.t_v.at[own_rows], r.y_sem.at[0], r.y_sem.at[1], me.ydev))
    go(remote(r.rbt.at[1 - c], r.rb.at[c], r.y_sem.at[2], r.y_sem.at[3], me.ydev))
    go(remote(r.mask.at[1 - c], r.live.at[c], r.y_sem.at[4], r.y_sem.at[5], me.ydev))
    part = pl.ds(pl.multiple_of(t * 128, 128), 128)

    def wblock(ff):
        return r.w_v.at[:, pl.ds(pl.multiple_of(ff * rows_f, rows_f), rows_f), :]

    go(remote(r.qkvb, wblock(f), r.w_sem.at[0], r.w_sem.at[1], me.xdev))
    go(remote(r.qkvb, wblock(f), r.w_sem.at[2], r.w_sem.at[3], me.core))

    def cols(u):
        return (slice(FF_COLS, UW), slice(0, FF_COLS // 2), slice(FF_COLS // 2, FF_COLS))[u]

    def shard(tt, ff, u):
        return r.u_v.at[tt, pl.ds(pl.multiple_of(ff * rows_f, rows_f), rows_f), cols(u)]

    def slab(tt, ff, h, u):
        return r.u_v.at[tt, pl.ds(pl.multiple_of(ff * rows_f + h * hrows, hrows), hrows), cols(u)]

    def own_half(h, u):
        return r.upack.at[pl.ds(pl.multiple_of(h * hrows, hrows), hrows), cols(u)]

    hs = (c, 1 - c)
    for u in (0, 1, 2):
        go(remote(own_half(c, u), slab(t, f, c, u), r.x_send.at[u, t], r.x_recv.at[u, t], me.xdev))
        for i in (0, 1):
            mine, there = own_half(hs[i], u), slab(t, f, hs[i], u)
            go(remote(mine, there, r.z_send.at[u, 0, t, i], r.z_recv.at[u, t, i], me.z(t + 1)), t < 3)
            go(remote(mine, there, r.z_send.at[u, 1, t, i], r.z_recv.at[u, t, i], me.z(t - 1)), t > 0)
        go(remote(r.upack.at[:, cols(u)], shard(t, f, u), r.c_send.at[u, t], r.c_recv.at[u, t], me.core))

    local = [
        pltpu.make_async_copy(r.tokens.at[c], r.t_v.at[own_rows], r.loc_sem.at[0]),
        pltpu.make_async_copy(r.qkvb, wblock(f), r.loc_sem.at[1]),
        pltpu.make_async_copy(r.upack, r.u_v.at[t, pl.ds(pl.multiple_of(f * rows_f, rows_f), rows_f), :], r.loc_sem.at[2]),
        pltpu.make_async_copy(r.teacher.at[c, part], r.teach.at[c], r.loc_sem.at[3]),
    ]
    for copy in local:
        copy.start()
    r.rb[c] = r.rbt[c]
    r.live[c] = r.mask[c]

    peers = (me.core, me.xdev, me.ydev)

    def tally_send(i):
        go(remote(r.count if i == 0 else r.tally.at[i + 2], r.tally.at[i], r.n_sem.at[0, i], r.n_sem.at[1, i], peers[i]))

    def tally_take(i):
        remote(r.tally.at[i], r.tally.at[i], r.n_sem.at[0, i], r.n_sem.at[1, i], peers[i]).wait_recv()
        r.tally[3 + i] = (r.count[...] if i == 0 else r.tally[i + 2]) + r.tally[i]

    tally_send(0)

    def z_step(d, u):
        for tt, ok, on, nxt, way in ((t - d, t - d >= 0, t < 3, t + 1, 0), (t + d, t + d <= 3, t > 0, t - 1, 1)):
            go_on = ok & on
            for i in (0, 1):
                piece = slab(tt, f, hs[i], u)
                send, recv = r.z_send.at[u, way, tt, i], r.z_recv.at[u, tt, i]
                pl.when(ok)(remote(piece, piece, send, recv, me.z(t)).wait_recv)
                go(remote(piece, piece, send, recv, me.z(nxt)), go_on)
                if i == 0:
                    go(remote(piece, piece, r.x_send.at[u, tt], r.x_recv.at[u, tt], me.xdev), ok)
            whole = shard(tt, f, u)
            go(remote(whole, whole, r.c_send.at[u, tt], r.c_recv.at[u, tt], me.core), ok)

    def around(d):
        return ((t, None),) if d == 0 else ((t - d, t - d >= 0), (t + d, t + d <= 3))

    def when(ok, fn):
        if ok is None:
            fn()
        else:
            pl.when(ok)(fn)

    def x_step(d, u):
        for tt, ok in around(d):
            piece = slab(tt, me.f_x, c, u)
            when(ok, remote(piece, piece, r.x_send.at[u, tt], r.x_recv.at[u, tt], me.xdev).wait_recv)
            go(remote(piece, piece, r.yw_send.at[u, tt], r.yw_recv.at[u, tt], me.ydev), ok)
            go(remote(piece, piece, r.h_send.at[u, tt, 0], r.h_recv.at[u, tt, 0], me.core), ok)

    def y_step(d, u):
        for tt, ok in around(d):
            piece = slab(tt, me.f_x, 1 - c, u)
            when(ok, remote(piece, piece, r.yw_send.at[u, tt], r.yw_recv.at[u, tt], me.ydev).wait_recv)
            go(remote(piece, piece, r.h_send.at[u, tt, 1], r.h_recv.at[u, tt, 1], me.core), ok)

    def core_wait(tt, u):
        whole = shard(tt, me.f_core, u)
        remote(whole, whole, r.c_send.at[u, tt], r.c_recv.at[u, tt], me.core).wait_recv()
        for i in (0, 1):
            piece = slab(tt, me.f_xc, hs[i], u)
            remote(piece, piece, r.h_send.at[u, tt, i], r.h_recv.at[u, tt, i], me.core).wait_recv()

    remote(wblock(me.f_x), wblock(me.f_x), r.w_sem.at[0], r.w_sem.at[1], me.xdev).wait_recv()
    go(remote(wblock(me.f_x), wblock(me.f_x), r.w_sem.at[4], r.w_sem.at[5], me.core))
    remote(wblock(me.f_core), wblock(me.f_core), r.w_sem.at[2], r.w_sem.at[3], me.core).wait_recv()
    for copy in local[:2]:
        copy.wait()
    remote(wblock(me.f_xc), wblock(me.f_xc), r.w_sem.at[4], r.w_sem.at[5], me.core).wait_recv()


    def project(base, count):
        def step(i, carry):
            rows = pl.ds(pl.multiple_of(base + i * 256, 256), 256)
            piece = r.t_v[rows, :]
            for j, ref in enumerate((r.q_v, r.k_v, r.v_v)):
                made = dot_nn(piece, r.w_v[j])
                for h in range(heads):
                    ref[h, rows, :] = made[:, h * HD : (h + 1) * HD].astype(bf16)
                if j:
                    (r.kt_v if j == 1 else r.vt)[:, rows] = made.T.astype(bf16)
            return carry

        lax.fori_loop(0, count, step, 0)
    tally_take(0)
    tally_send(1)
    project(c * half, half // 256)
    x_step(0, 0)
    z_step(1, 0)
    x_step(0, 1)
    x_step(0, 2)
    z_step(1, 1)
    z_step(1, 2)
    x_step(1, 0)
    z_step(2, 0)
    y_step(0, 0)
    tally_take(1)
    tally_send(2)
    other_rows = pl.ds(pl.multiple_of((1 - c) * half, half), half)
    remote(r.t_v.at[other_rows], r.t_v.at[other_rows], r.y_sem.at[0], r.y_sem.at[1], me.ydev).wait_recv()
    project((1 - c) * half, half // 256)
    remote(r.rb.at[1 - c], r.rb.at[1 - c], r.y_sem.at[2], r.y_sem.at[3], me.ydev).wait_recv()
    length = r.lengths[c]
    nblk = seq // BLK
    pos_block = lax.broadcasted_iota(jnp.int32, (128, seq), 1) // BLK
    row = lax.broadcasted_iota(jnp.int32, (128, seq), 0)
    picks = dot_nn(r.rb[0].astype(bf16), (pos_block == row).astype(bf16)) + dot_nn(
        r.rb[1].astype(bf16), (pos_block == row + nblk // 2).astype(bf16)
    )
    key_block = lax.broadcasted_iota(jnp.int32, (nblk, seq), 0)
    query = lax.broadcasted_iota(jnp.int32, (nblk, seq), 1)
    own = query // BLK

    def same(a, b):
        return (a == b).astype(f32)

    times = same(key_block, 0) + same(key_block, 1) + same(key_block, own - 1)
    times += same(key_block, own) + same(key_block, own + 1)
    for j in range(3):
        times += same(key_block.astype(f32), picks[j : j + 1, :])
    times = jnp.where(query < 2 * BLK, 1.0, times)
    level = jnp.where(times > 0, jnp.log2(jnp.maximum(times, 1.0)), negative)
    r.level[...] = level
    factor = HD ** (-0.5) * 1.4426950408889634
    wide = 256

    def attend(i):
        cols = slice(i * wide, (i + 1) * wide)
        for b in range(nblk):
            place = b * BLK + lax.broadcasted_iota(jnp.int32, (BLK, wide), 0)
            row = jnp.broadcast_to(r.level[b : b + 1, cols], (BLK, wide))
            r.bias[b * BLK : (b + 1) * BLK, :] = jnp.where(place < length, row, negative)

        def step(h, carry):
            scores = dot_nt(r.k_v[h], r.q_v[h, cols, :]) * factor + r.bias[...]
            top = jnp.max(scores, 0, keepdims=True)
            expo = jnp.exp2(scores - top)
            probs = (expo * (1.0 / jnp.sum(expo, 0, keepdims=True))).astype(bf16)
            r.pt_v[h, :, cols] = probs
            rows = pl.ds(pl.multiple_of(h * HD, HD), HD)
            r.dqt[rows, cols] = dot_nn(r.vt[rows, :], probs)
            return carry

        lax.fori_loop(0, heads, step, 0)
        s = i * wide // half
        for tt in range(i * wide % half // 128, i * wide % half // 128 + 2):
            at = s * half + tt * 128
            made = r.dqt[:, at : at + 128].T.astype(bf16)
            r.gatt[tt, s] = made

            @pl.when(t == tt)
            def _():
                r.att_v[tt, s] = made

            go(remote(r.gatt.at[tt, s], r.att_v.at[t, s], r.o_send.at[s, tt], r.o_recv.at[s, t], me.z(tt)), t != tt)

    attend(0)
    x_step(1, 1)
    x_step(1, 2)
    z_step(2, 1)
    z_step(2, 2)
    z_step(3, 0)
    x_step(2, 0)
    y_step(1, 0)
    attend(1)
    y_step(0, 1)
    y_step(0, 2)
    x_step(3, 0)
    y_step(2, 0)
    attend(2)
    y_step(3, 0)
    attend(3)
    go(remote(r.teacher.at[1 - c, part], r.teach.at[c], r.y_sem.at[6], r.y_sem.at[7], me.ydev))
    y_step(1, 1)
    y_step(1, 2)
    x_step(2, 1)
    x_step(2, 2)
    z_step(3, 1)
    x_step(3, 1)
    z_step(3, 2)
    x_step(3, 2)
    for s in range(2):
        r.tok[s] = r.t_v[pl.ds(pl.multiple_of(s * half + t * 128, 128), 128), :]
    for s in range(2):
        for d in (1, 2, 3):
            src = (t + d) % 4
            piece = r.att_v.at[src, s]
            remote(piece, piece, r.o_send.at[s, t], r.o_recv.at[s, src], me.z(t)).wait_recv()
    for copy in local[2:]:
        copy.wait()
    for tt in range(4):
        core_wait(tt, 0)

    x = f // 2
    k = f % 2
    att_v, u_v, g_v, act, slope = r.att_v, r.u_v, r.g_v, r.act, r.slope
    rows = 2 * 128
    inv_width = 1.0 / depth

    def both(ref):
        return ref[...].reshape(rows, depth).astype(f32)

    def mean(v):
        return jnp.sum(v, -1, keepdims=True) * inv_width

    def normalize(v):
        center = v - mean(v)
        inverse = lax.rsqrt(mean(center * center) + norm_eps)
        return center * inverse, inverse

    def back(up, normed, inverse, gain):
        scaled = up * gain
        return inverse * (scaled - mean(scaled) - normed * mean(scaled * normed))
    norms = u_v[0, :, 1728:1736].astype(f32).T
    gains = [norms[i : i + 1, :] for i in range(4)]
    att = [att_v[tt].reshape(rows, width) for tt in range(4)]
    attn = dot_nt(att[0], u_v[0, :, 1536:1728])
    for tt in range(1, 4):
        attn += dot_nt(att[tt], u_v[tt, :, 1536:1728])
    normed_one, inverse_one = normalize(both(r.tok) + attn)
    hidden = normed_one * gains[0] + gains[1]
    hidden_b = hidden.astype(bf16)
    cube = 0.044715
    root = 0.7978845608028654

    def up_step(tt, mixed):
        upper = dot_nn(hidden_b, u_v[tt, :, 0:768])
        square = upper * upper
        th = jnp.tanh(root * upper * (1.0 + cube * square))
        act_t = (0.5 * upper * (1.0 + th)).astype(bf16)
        act[tt] = act_t
        bend = 0.5 * (1.0 + th) + 0.5 * upper * (1.0 - th * th) * root * (1.0 + 3.0 * cube * square)
        slope[tt] = bend.astype(bf16)
        return mixed + dot_nt(act_t, u_v[tt, :, 768:1536])
    second = t - 1 + 2 * ((3 - t) // 3)
    fourth = 3 * (1 - t // 2)
    core_wait(t, 1)
    core_wait(t, 2)
    mixed = up_step(t, jnp.zeros((rows, depth), f32))
    y_step(2, 1)
    y_step(2, 2)
    core_wait(second, 1)
    core_wait(second, 2)
    mixed = up_step(second, mixed)
    core_wait(6 - t - second - fourth, 1)
    core_wait(6 - t - second - fourth, 2)
    mixed = up_step(6 - t - second - fourth, mixed)
    y_step(3, 1)
    y_step(3, 2)
    core_wait(fourth, 1)
    core_wait(fourth, 2)
    mixed = up_step(fourth, mixed)
    there = r.live.at[1 - c]
    remote(there, there, r.y_sem.at[4], r.y_sem.at[5], me.ydev).wait_recv()
    there = r.teach.at[1 - c]
    remote(there, there, r.y_sem.at[6], r.y_sem.at[7], me.ydev).wait_recv()
    tally_take(2)
    for copy, pred in sends:
        when(pred, copy.wait_send)
    r.count[...] = r.tally[5]
    sends.clear()
    normed_two, inverse_two = normalize(hidden + mixed)
    result = normed_two * gains[2] + gains[3]

    r.piece[...] = result.astype(bf16).reshape(2, 128, depth)
    lo = r.lo
    lo_send = remote(r.piece.at[1 - c], lo.at[c, part], r.s_sem.at[0], r.s_sem.at[1], me.ydev)
    lo_send.start()
    own_lo = pltpu.make_async_copy(r.piece.at[c], lo.at[c, part], r.load_sem.at[1])
    own_lo.start()

    def lo_block(tt):
        return lo.at[:, pl.ds(pl.multiple_of(tt * 128, 128), 128), :]

    lo_line = Line(me, go, lo_block, r.lo_send, r.lo_recv)

    alive = jnp.concatenate([column(r.live[s, :, part]) for s in range(2)], 0)
    row = lax.broadcasted_iota(jnp.int32, (rows, 1), 0)
    place = jnp.where(row < 128, row, row - 128 + half) + t * 128
    live = jnp.where((alive == 1.0) & (place < length), 1.0, 0.0)
    differ = result - both(r.teach)
    weighed = differ * live
    missed = jnp.sum(jnp.sum(weighed * differ, 1, keepdims=True), 0, keepdims=True)
    grad_y = weighed * (2.0 / (r.count[0:1, 0:1] * depth))
    sums = [None] * 4
    sums[2] = jnp.sum(grad_y * normed_two, 0, keepdims=True)
    sums[3] = jnp.sum(grad_y, 0, keepdims=True)
    grad_two = back(grad_y, normed_two, inverse_two, gains[2])
    gm = grad_two.astype(bf16)
    gm_t = grad_two.T.astype(bf16)
    hidden_t = hidden.T.astype(bf16)
    there = lo.at[1 - c, part]
    lo_there = remote(there, there, r.s_sem.at[0], r.s_sem.at[1], me.ydev)
    lo_first = lo_line.first()
    sends.extend(lo_first)

    far = 1 - x
    trio = (me.core, me.xdev, me.ydev)

    def region(ref, unit, at, n, whole=None):
        rows_at = pl.ds(pl.multiple_of(at, qrows), n)
        if whole is not None:
            return ref.at[unit, rows_at, :]
        return ref.at[:, rows_at, FF_COLS:UW] if unit is TAIL else ref.at[unit, rows_at, 0:FF_COLS]

    def g_rows(unit, ff):
        return region(g_v, unit, ff * rows_f, rows_f)

    def rc_rows(xx, unit, at=0, n=rows_f):
        return region(u_v, unit, xx * rows_f + at, n)

    def room(n):
        return lambda unit, i: region(u_v, unit, (4 + n) * hrows + i * qrows, qrows)

    xg_at, yg_at = room(0), room(1)

    def d_at(ref, unit):
        return ref.at[:, :, FF_COLS:UW] if unit is TAIL else ref.at[unit, :, 0:FF_COLS]

    def slot(unit):
        return 4 if unit is TAIL else unit

    def credit(unit):
        for j, dev in enumerate(trio):
            pl.semaphore_signal(r.free.at[j, slot(unit)], inc=1, device_id=dev, device_id_type=MESH)

    def rc_copies(unit):
        return [
            remote(g_rows(unit, xx * 2 + 1 - k), rc_rows(xx, unit), r.rc_send.at[xx, slot(unit)],
                   r.rc_recv.at[xx, slot(unit)], me.core)
            for xx in (far, x)
        ]

    def far_copies(unit):
        i = slot(unit)
        h, other = c * hrows, (1 - c) * hrows
        return [
            remote(rc_rows(far, unit, other, qrows), d_at(r.dx, unit), r.dx_send.at[i], r.dx_recv.at[i], me.xdev),
            remote(rc_rows(far, unit, other + qrows, qrows), d_at(r.dy, unit), r.dy_send.at[i], r.dy_recv.at[i], me.ydev),
            remote(rc_rows(far, unit, h, qrows), xg_at(unit, 0), r.xg_send.at[i, 0], r.xg_recv.at[i, 0], me.xdev),
        ]

    def rc_step(unit):
        pl.semaphore_wait(r.free.at[0, slot(unit)], 1)
        for copy in rc_copies(unit):
            copy.start()

    def core_step(xx, unit):
        view = rc_rows(xx, unit)
        i = slot(unit)
        remote(view, view, r.rc_send.at[xx, i], r.rc_recv.at[xx, i], me.core).wait_recv()
        add_rows(view, view, g_rows(unit, xx * 2 + k))

    def far_step(unit):
        core_step(far, unit)
        for j in (1, 2):
            pl.semaphore_wait(r.free.at[j, slot(unit)], 1)
        for copy in far_copies(unit):
            copy.start()

    def near_step(unit):
        core_step(x, unit)
        i = slot(unit)
        mine = rc_rows(x, unit, (1 - c) * hrows + qrows, qrows)
        go(remote(mine, yg_at(unit, 1), r.yg_send.at[i, 1], r.yg_recv.at[i, 1], me.ydev))

    def diag_step(unit):
        i = slot(unit)
        dx, dy = d_at(r.dx, unit), d_at(r.dy, unit)
        remote(dx, dx, r.dx_send.at[i], r.dx_recv.at[i], me.xdev).wait_recv()
        mine = rc_rows(x, unit, (1 - c) * hrows, qrows)
        add_rows(mine, mine, dx)
        go(remote(mine, yg_at(unit, 0), r.yg_send.at[i, 0], r.yg_recv.at[i, 0], me.ydev))
        remote(dy, dy, r.dy_send.at[i], r.dy_recv.at[i], me.ydev).wait_recv()
        mine = rc_rows(far, unit, c * hrows + qrows, qrows)
        add_rows(mine, mine, dy)
        go(remote(mine, xg_at(unit, 1), r.xg_send.at[i, 1], r.xg_recv.at[i, 1], me.xdev))

    def sum_step(unit):
        at = slot(unit)
        for i in (0, 1):
            xg, yg = xg_at(unit, i), yg_at(unit, i)
            mine = rc_rows(x, unit, c * hrows + i * qrows, qrows)
            remote(xg, xg, r.xg_send.at[at, i], r.xg_recv.at[at, i], me.xdev).wait_recv()
            add_rows(mine, mine, xg)
            remote(yg, yg, r.yg_send.at[at, i], r.yg_recv.at[at, i], me.ydev).wait_recv()
            add_rows(mine, mine, yg)

    def sum_rows(tt):
        return u_v.at[tt, pl.ds(pl.multiple_of(x * rows_f + c * hrows, hrows), hrows), :]

    w_chain = Chain(
        me, go, sum_rows, lambda tt: u_v.at[tt, pl.ds(6 * hrows, hrows), :],
        lambda tt: u_v.at[tt, pl.ds(7 * hrows, hrows), :], r.zw_send, r.zw_recv_l, r.zw_recv_r,
    )

    def turn(i):
        return ((i + 1) % 2) * (3 - i // 2) + (i % 2) * (i // 2)

    ORDER = (3, 0, 2, 1)

    def down_step(i, total):
        tt = turn(i)
        ga = dot_nn(gm, u_v[tt, :, 768:1536])
        gu = (ga * slope[tt].astype(f32)).astype(bf16)
        g_v[tt, :, 768:1536] = dot_nn(gm_t, act[tt]).astype(bf16)
        g_v[tt, :, 0:768] = dot_nn(hidden_t, gu).astype(bf16)
        total = total + dot_nt(gu, u_v[tt, :, 0:768])
        credit(tt)

        @pl.when(i == 1)
        def _():
            lo_there.wait_recv()
            own_lo.wait()
            for copy, pred in lo_first:
                when(pred, copy.start)

        @pl.when(i >= 1)
        def _():
            rc_step(turn(i - 1))

        @pl.when(i >= 2)
        def _():
            far_step(turn(i - 2))

        return total

    grad_hidden = lax.fori_loop(0, 4, down_step, grad_two)
    rc_step(ORDER[3])
    sums[0] = jnp.sum(grad_hidden * normed_one, 0, keepdims=True)
    sums[1] = jnp.sum(grad_hidden, 0, keepdims=True)
    grad_one = back(grad_hidden, normed_one, inverse_one, gains[0])
    r.gone[...] = grad_one.reshape(2, 128, depth)
    ga = grad_one.astype(bf16)
    gatt, do_in = r.gatt, r.do_in
    for tt in range(4):
        back_t = dot_nn(ga, u_v[tt, :, 1536:1728]).astype(bf16)
        gatt[tt] = back_t.reshape(2, 128, width)
    for d in (1, 2, 3):
        to = (t + d) % 4
        go(remote(gatt.at[to], do_in.at[t], r.a_send.at[d], r.a_recv.at[d], me.z(to)))
    do_in[t] = gatt[t]
    credit(TAIL)
    far_step(ORDER[2])
    ga_t = grad_one.T.astype(bf16)
    ez, ef = r.ez, r.ef
    mine_at = f * 2 + c
    ez[t] = jnp.concatenate(sums + [jnp.broadcast_to(missed, (4, depth))], 0)
    for d in (1, 2, 3):
        go(remote(ez.at[t], ez.at[t], r.e_sem.at[0, d], r.e_sem.at[1, d], me.z((t + d) % 4)))

    def sums_on():
        for d in (1, 2, 3):
            src = ez.at[(t + 4 - d) % 4]
            remote(src, src, r.e_sem.at[0, d], r.e_sem.at[1, d], me.z(t)).wait_recv()
        ef[mine_at] = (ez[0] + ez[1]) + (ez[2] + ez[3])
        for d, dev in me.owners():
            go(remote(ef.at[mine_at], ef.at[mine_at], r.e_sem.at[0, 3 + d], r.e_sem.at[1, 3 + d], dev))

    def sums_end():
        for d, dev in me.owners():
            ff, cc = me.flipped(d)
            src = ef.at[ff * 2 + cc]
            remote(src, src, r.e_sem.at[0, 3 + d], r.e_sem.at[1, 3 + d], dev).wait_recv()
        total = ef[0]
        for i in range(1, 8):
            total += ef[i]
        r.sums[...] = total

    for tt in range(4):
        g_v[tt, :, 1536:1728] = dot_nn(ga_t, att[tt]).astype(bf16)
        g_v[tt, :, 1728:1792] = jnp.zeros((depth, UW - 1728), bf16)
    rc_step(TAIL)
    near_step(ORDER[0])
    far_step(ORDER[3])
    near_step(ORDER[1])
    lo_line.step(1)
    far_step(TAIL)
    near_step(ORDER[2])
    near_step(ORDER[3])
    near_step(TAIL)
    for unit in (*ORDER, TAIL):
        sends.extend((copy, None) for copy in rc_copies(unit) + far_copies(unit))

    do, proj, dqt = r.do, r.proj, r.dqt
    dk, dv = r.bias.at[:, 0:HD], r.bias.at[:, 128 : 128 + HD]
    for d in (1, 2, 3):
        src = (t + 4 - d) % 4
        remote(do_in.at[src], do_in.at[src], r.a_send.at[d], r.a_recv.at[d], me.z(src)).wait_recv()
    for s in range(2):
        for tt in range(4):
            at = s * half + tt * 128
            for h in range(heads):
                do[h, at : at + 128, :] = do_in[tt, s, :, h * HD : (h + 1) * HD]
    q_v, k_v, v_v, kt_v, pt_v, t_v, w_v = (r.q_v, r.k_v, r.v_v, r.kt_v, r.pt_v, r.t_v, r.w_v)
    scale = HD ** (-0.5)

    def attend_back(h):
        dk[...] = jnp.zeros((seq, HD), f32)
        dv[...] = jnp.zeros((seq, HD), f32)

        def step(i, carry):
            cols = pl.ds(pl.multiple_of(i * wide, wide), wide)
            mine = do[h, cols, :]
            probs = pt_v[h, :, cols]
            gp = dot_nt(v_v[h], mine)
            pf = probs.astype(f32)
            mix = jnp.sum(pf * gp, 0, keepdims=True)
            gs = (pf * (gp - mix)).astype(bf16)
            dk[...] += dot_nn(gs, q_v[h, cols, :])
            dv[...] += dot_nn(probs, mine)
            dqt[h * HD : (h + 1) * HD, cols] = dot_nn(kt_v[h * HD : (h + 1) * HD, :], gs)
            return carry

        lax.fori_loop(0, seq // wide, step, 0)
        proj[1, :, h * HD : (h + 1) * HD] = (dk[...] * scale).astype(bf16)
        proj[2, :, h * HD : (h + 1) * HD] = dv[...].astype(bf16)
    attend_back(0)
    diag_step(ORDER[0])
    lo_line.step(2)
    diag_step(ORDER[1])
    attend_back(1)
    diag_step(TAIL)
    diag_step(ORDER[2])
    attend_back(2)
    lo_send.wait_send()
    proj[0] = (dqt[...].T * scale).astype(bf16)
    ip = r.ip

    def input_part(s):
        def rows_step(i, carry):
            at = pl.ds(pl.multiple_of(s * half + i * 128, 128), 128)
            total = dot_nt(proj[0, at, :], w_v[0])
            for j in (1, 2):
                total += dot_nt(proj[j, at, :], w_v[j])
            ip[s, i] = total.astype(bf16)
            return carry

        lax.fori_loop(0, half // 128, rows_step, 0)

    def ip_chain(j, s):
        return Chain(
            me, go, lambda tt: ip.at[s, tt], lambda tt: act.at[tt, pl.ds(j * 128, 128), :], lambda tt: slope.at[tt, pl.ds(j * 128, 128), :],
            r.i_send.at[j], r.i_recv_l.at[j], r.i_recv_r.at[j],
        )

    chains = [ip_chain(0, 1 - c), ip_chain(1, c)]
    ig, igp, qg, qc, qs = r.ig, r.piece, r.qg, r.qc, r.q_sem

    def q_rows(ff):
        return qg.at[:, pl.ds(pl.multiple_of(ff * rows_f, rows_f), rows_f), :]

    def finish(j, s):
        chains[j].end()
        igp[j] = (ip[s, t].astype(f32) + r.gone[s]).astype(bf16)

    def ig_line(j, s):
        def block(tt):
            return ig.at[s, pl.ds(pl.multiple_of(tt * 128, 128), 128), :]

        return Line(me, go, block, r.ig_send.at[j], r.ig_recv.at[j])

    lines = [ig_line(0, c), ig_line(1, 1 - c)]

    def sum_pass(tt, passes):
        sum_step(tt)
        for at, way in passes:
            w_chain.pass_on(at, way)

    def q_take(i, j, dev):
        remote(qc.at[i], qc.at[i], qs.at[j], qs.at[j + 1], dev).wait_recv()

    def q_add(i, ff):
        qc[i] = qc[i] + qg[:, pl.ds(pl.multiple_of(ff * rows_f, rows_f), rows_f), :]

    def chain_pass(j, lo_at, hi_at):
        for tt, way in CHAIN_ORDER[lo_at:hi_at]:
            chains[j].pass_on(tt, way)

    input_part(1 - c)
    chain_pass(0, 0, 2)
    input_part(c)
    chain_pass(0, 2, 4)
    chain_pass(1, 0, 2)
    sum_step(TAIL)
    sum_pass(3, CHAIN_ORDER[:1])
    sum_pass(0, CHAIN_ORDER[1:2])
    chain_pass(0, 4, 6)
    finish(0, 1 - c)
    go(remote(igp.at[0], ig.at[c, part], r.s_sem.at[2], r.s_sem.at[3], me.ydev))
    diag_step(ORDER[3])
    sums_on()
    chain_pass(1, 2, 4)
    for j in range(3):
        qg[j] = dot_tn(t_v[...], proj[j]).astype(bf16)
    go(remote(q_rows(far * 2 + 1 - k), qc.at[0], qs.at[0], qs.at[1], me.core))
    go(remote(q_rows(x * 2 + 1 - k), qc.at[1], qs.at[2], qs.at[3], me.core))
    chain_pass(1, 4, 6)
    there = ig.at[1 - c, part]
    remote(there, there, r.s_sem.at[2], r.s_sem.at[3], me.ydev).wait_recv()
    lines[1].start()
    finish(1, c)
    own_ig = pltpu.make_async_copy(igp.at[1], ig.at[c, part], r.load_sem.at[2])
    own_ig.start()
    lines[0].start(igp.at[1])
    q_take(0, 0, me.core)
    q_add(0, far * 2 + k)
    go(remote(qc.at[0], qc.at[2], qs.at[4], qs.at[5], me.xdev))
    q_take(1, 2, me.core)
    q_add(1, x * 2 + k)
    lo_line.step(3)
    sum_pass(2, ((2, 0),))
    sum_pass(1, ((1, 1), (1, 0), (2, 1)))
    lines[1].step(1)
    q_take(2, 4, me.xdev)
    qc[1] = qc[1] + qc[2]
    go(remote(qc.at[1], qc.at[3], qs.at[6], qs.at[7], me.ydev))
    lines[0].step(1)
    w_chain.end()
    fin = r.dx

    def fin_half(h):
        return fin.at[pl.ds(h * 2, 2)]

    for i in (0, 1):
        fin[c * 2 + i] = region(u_v, t, x * rows_f + c * hrows + i * qrows, qrows, 0)[...]
    go(remote(fin_half(c), fin_half(c), r.s_sem.at[4], r.s_sem.at[5], me.ydev))
    q_take(3, 6, me.ydev)
    qsum = r.qsum
    total = jnp.zeros((1, width), f32)
    for j in range(3):
        qsum[j] = qc[1, j].astype(f32) + qc[3, j].astype(f32)
        total += jnp.sum(qsum[j] * qsum[j], 0, keepdims=True)
    total = 0.5 * jnp.sum(total, 1, keepdims=True)

    def square_step(i, carry):
        for j in (0, 1):
            row = fin[c * 2 + j, pl.ds(pl.multiple_of(i * 16, 16), 16), :].astype(f32)
            carry += jnp.sum(row * row, 0, keepdims=True)
        return carry

    wide_total = lax.fori_loop(0, qrows // 16, square_step, jnp.zeros((1, UW), f32))
    total += jnp.sum(wide_total, 1, keepdims=True)
    sz, sf = r.sz, r.sf
    sz[t] = jnp.broadcast_to(total, (8, 128))
    for d in (1, 2, 3):
        go(remote(sz.at[t], sz.at[t], r.f_sem.at[0, d], r.f_sem.at[1, d], me.z((t + d) % 4)))
    lines[0].step(2)
    lines[1].step(2)
    for d in (1, 2, 3):
        src = sz.at[(t + 4 - d) % 4]
        remote(src, src, r.f_sem.at[0, d], r.f_sem.at[1, d], me.z(t)).wait_recv()
    mine = f * 2 + c
    sf[mine] = (sz[0] + sz[1]) + (sz[2] + sz[3])
    for d, dev in me.owners():
        go(remote(sf.at[mine], sf.at[mine], r.f_sem.at[0, 3 + d], r.f_sem.at[1, 3 + d], dev))
    lines[0].step(3)
    lines[1].step(3)
    remote(fin_half(1 - c), fin_half(1 - c), r.s_sem.at[4], r.s_sem.at[5], me.ydev).wait_recv()
    out_copy = pltpu.make_async_copy(fin, r.gsum, r.load_sem.at[0])
    out_copy.start()
    sums_end()
    for d, dev in me.owners():
        ff, cc = me.flipped(d)
        src = sf.at[ff * 2 + cc]
        remote(src, src, r.f_sem.at[0, 3 + d], r.f_sem.at[1, 3 + d], dev).wait_recv()
    all_sq = sf[0]
    for i in range(1, 8):
        all_sq += sf[i]
    r.squares[...] = all_sq
    for copy, pred in sends:
        when(pred, copy.wait_send)
    out_copy.wait()
    own_ig.wait()


def train(lengths, tokens, teacher, qkv, up, down, out, norm, blocks, valid):
    seq = tokens.shape[1] * 2
    width = qkv.shape[2]
    heads = width // HD
    rows_f = qkv.shape[1]
    depth = rows_f * 4
    vm = pl.BlockSpec(memory_space=pltpu.VMEM)
    smem = pl.BlockSpec(memory_space=pltpu.SMEM)
    hbm = pl.BlockSpec(memory_space=pl.ANY)
    dma = pltpu.SemaphoreType.DMA

    def vb(*shape):
        return pltpu.VMEM(shape, bf16)

    def vf(*shape):
        return pltpu.VMEM(shape, f32)

    ins = dict(
        lengths=(lengths, smem), tokens=(tokens, hbm), teacher=(teacher, hbm), qkv=(qkv, vm), up=(up, vm), down=(down, vm),
        out=(out, vm), norm=(norm, vm), blocks=(blocks, vm), valid=(valid, vm),
    )
    qr = rows_f // 4
    outs = dict(
        lo=((2, seq // 2, depth), bf16, hbm),
        ig=((2, seq // 2, depth), bf16, hbm),
        gsum=((4, qr, UW), bf16, hbm),
        qsum=((3, rows_f, width), f32, vm),
        sums=((8, depth), f32, vm),
        squares=((8, 128), f32, vm),
        count=((8, 128), f32, vm),
    )
    scratch = dict(
        att_v=vb(4, 2, 128, width), u_v=vb(4, depth, UW), pt_v=vb(heads, seq, seq), q_v=vb(heads, seq, HD),
        k_v=vb(heads, seq, HD), v_v=vb(heads, seq, HD), kt_v=vb(width, seq), w_v=vb(3, depth, width), t_v=vb(seq, depth),
        tok=vb(2, 128, depth), teach=vb(2, 128, depth), live=vf(2, 8, seq // 2), upack=vb(rows_f, UW),
        qkvb=vb(3, rows_f, width), rbt=vf(2, 8, 128), mask=vf(2, 8, seq // 2), tally=vf(6, 8, 128), vt=vb(width, seq),
        rb=vf(2, 8, 128), level=vf(seq // BLK, seq), bias=vf(seq, 256), loc_sem=dma((5,)), w_sem=dma((6,)), y_sem=dma((8,)),
        z_send=dma((3, 2, 4, 2)), z_recv=dma((3, 4, 2)), x_send=dma((3, 4)), x_recv=dma((3, 4)), yw_send=dma((3, 4)),
        yw_recv=dma((3, 4)),
        c_send=dma((3, 4)), c_recv=dma((3, 4)), h_send=dma((3, 4, 2)), h_recv=dma((3, 4, 2)), o_send=dma((2, 4)), o_recv=dma((2, 4)),
        n_sem=dma((2, 3)),
        g_v=vb(4, depth, UW), act=vb(4, 256, 768),
        slope=vb(4, 256, 768), piece=vb(2, 128, depth), gone=vf(2, 128, depth), gatt=vb(4, 2, 128, width),
        do_in=vb(4, 2, 128, width), dx=vb(4, qr, UW), dy=vb(4, qr, UW), do=vb(heads, seq, HD), proj=vb(3, seq, width),
        dqt=vf(width, seq), ip=vb(2, 4, 128, depth),
        qg=vb(3, depth, width), qc=vb(4, 3, rows_f, width),
        load_sem=dma((15,)), s_sem=dma((6,)), lo_send=dma((2, 4)), lo_recv=dma((4,)), a_send=dma((4,)), a_recv=dma((4,)),
        rc_send=dma((2, 5)), rc_recv=dma((2, 5)), dx_send=dma((5,)), dx_recv=dma((5,)), dy_send=dma((5,)),
        dy_recv=dma((5,)), xg_send=dma((5, 2)), xg_recv=dma((5, 2)), yg_send=dma((5, 2)), yg_recv=dma((5, 2)),
        zw_send=dma((4,)), zw_recv_l=dma((4,)), zw_recv_r=dma((4,)), i_send=dma((2, 4)), i_recv_l=dma((2, 4)),
        i_recv_r=dma((2, 4)), ig_send=dma((2, 2, 4)), ig_recv=dma((2, 4)), q_sem=dma((8,)), ez=vf(4, 8, depth), ef=vf(8, 8, depth),
        sz=vf(4, 8, 128), sf=vf(8, 8, 128), e_sem=dma((2, 11)), f_sem=dma((2, 11)),
        free=pltpu.SemaphoreType.REGULAR((3, 5)),
    )
    return pl.pallas_call(
        functools.partial(train_kernel, (*ins, *outs, *scratch)),
        name="train",
        out_shape=[jax.ShapeDtypeStruct(s, d) for s, d, _ in outs.values()],
        in_specs=[m for _, m in ins.values()],
        out_specs=[m for _, _, m in outs.values()],
        scratch_shapes=list(scratch.values()),
        compiler_params=pltpu.CompilerParams(
            collective_id=0, has_side_effects=True, vmem_limit_bytes=62 * 2**20
        ),
    )(*(a for a, _ in ins.values()))


def update_kernel(kinds, names, *refs):
    r = types.SimpleNamespace(**dict(zip(names, refs, strict=True)))
    f = lax.axis_index("fsdp")
    copies = [pltpu.make_async_copy(getattr(r, n), getattr(r, n + "_v"), r.in_sem.at[i]) for i, n in enumerate(kinds[0])]
    ready = dict(zip(kinds[0], copies, strict=True))
    for copy in copies:
        copy.start()
    outs = {
        n: pltpu.make_async_copy(getattr(r, n + "_v"), getattr(r, n), r.out_sem.at[i]) for i, n in enumerate(kinds[1])
    }
    depth = r.sums.shape[1]
    rows_f = depth // 4
    sums = r.sums[0:4, :]
    total = r.squares[0:1, 0:1] + jnp.sum(jnp.sum(sums * sums, 1, keepdims=True), 0, keepdims=True)
    norm = jnp.sqrt(total)
    factor = jnp.minimum(1.0, clip_level / (norm + 1e-06))
    r.norm[...] = norm
    r.loss[...] = r.sums[4:5, 0:1] / (r.count[0:1, 0:1] * depth)
    steps = jnp.full((1, 1), r.steps[0]).astype(f32)
    one = 1.0 / (1.0 - jnp.exp(steps * -0.10536051565782628))
    two = 1.0 / (1.0 - jnp.exp(steps * -0.0010005003335835335))

    def move(name, grad, at, rate):
        read = [getattr(r, f"{name}_{k}_v")[at] for k in "wms"]
        write = [getattr(r, f"{name}_{k}_new_v") for k in "wms"]
        clipped = grad * factor
        new_moment = beta_one * read[1] + (1.0 - beta_one) * clipped
        new_square = beta_two * read[2] + (1.0 - beta_two) * clipped * clipped
        step = new_moment * one / (jnp.sqrt(new_square * two) + adam_eps) + decay_rate * read[0]
        write[0][at] = read[0] - rate * step
        write[1][at] = new_moment
        write[2][at] = new_square

    def begin(name):
        for k in "wms":
            ready[f"{name}_{k}"].wait()

    def end(name):
        for k in "wms":
            outs[f"{name}_{k}_new"].start()

    def by_rows(name, work):
        begin(name)

        def one_step(i, carry):
            work(pl.ds(pl.multiple_of(i * 16, 16), 16))
            return carry

        lax.fori_loop(0, rows_f // 16, one_step, 0)
        end(name)

    every = slice(None)
    ready["gsum"].wait()
    by_rows("up", lambda rows: move("up", r.gsum_v[rows, 0:768].astype(f32), (rows, every), rate_list[2]))
    by_rows("down", lambda rows: move("down", r.gsum_v[rows, 768:1536].astype(f32), (rows, every), rate_list[3]))
    ready["ig"].wait()

    def cast_step(i, carry):
        rows = pl.ds(pl.multiple_of(i * 64, 64), 64)
        for s in range(2):
            r.input_grad_v[s, rows, :] = r.ig_v[s, rows, :].astype(f32)
        return carry

    lax.fori_loop(0, r.ig_v.shape[1] // 64, cast_step, 0)
    outs["input_grad"].start()
    ready["qsum"].wait()

    def qkv_rows(rows):
        for j in range(3):
            move("qkv", r.qsum_v[j, rows, :], (j, rows, every), rate_list[0])

    by_rows("qkv", qkv_rows)
    begin("out")
    move("out", r.gsum_v[:, 1536:1728].astype(f32).T, (every, every), rate_list[1])
    end("out")
    ready["lo"].wait()
    layer_out = pltpu.make_async_copy(r.lo_v, r.layer_out, r.out_sem.at[len(kinds[1])])
    layer_out.start()
    mine = sums[:, 0:rows_f]
    for i in range(1, 4):
        mine = jnp.where(f == i, sums[:, i * rows_f : (i + 1) * rows_f], mine)
    begin("norm")
    move("norm", mine, (every, every), rate_list[4])
    end("norm")
    for copy in (*outs.values(), layer_out):
        copy.wait()


def update(steps, lo, ig, gsum, qsum, sums, squares, count, state):
    vm = pl.BlockSpec(memory_space=pltpu.VMEM)
    smem = pl.BlockSpec(memory_space=pltpu.SMEM)
    hbm = pl.BlockSpec(memory_space=pl.ANY)
    shape = jax.ShapeDtypeStruct
    ins = dict(steps=(steps, smem), sums=(sums, vm), squares=(squares, vm), count=(count, vm))
    moved = dict(gsum=gsum)
    order = ("up", "down", "qkv", "out", "norm")
    for name in order:
        if name == "qkv":
            moved.update(ig=ig, qsum=qsum)
        moved.update({f"{name}_{k}": a for k, a in zip("wms", state[name])})
    moved.update(lo=lo)
    ins.update({n: (a, hbm) for n, a in moved.items()})
    made = dict(input_grad=shape(ig.shape, f32))
    made.update({f"{n}_{k}_new": shape(a.shape, f32) for n, group in state.items() for k, a in zip("wms", group)})
    outs = dict(layer_out=(shape(lo.shape, bf16), hbm), loss=(shape((1, 1), f32), vm), norm=(shape((1, 1), f32), vm))
    outs.update({n: (a, hbm) for n, a in made.items()})
    scratch = {n + "_v": pltpu.VMEM(a.shape, a.dtype) for n, a in (*moved.items(), *made.items())}
    scratch.update(in_sem=pltpu.SemaphoreType.DMA((len(moved),)), out_sem=pltpu.SemaphoreType.DMA((len(made) + 1,)))
    results = pl.pallas_call(
        functools.partial(update_kernel, (tuple(moved), tuple(made)), (*ins, *outs, *scratch)),
        name="update",
        out_shape=[a for a, _ in outs.values()],
        in_specs=[m for _, m in ins.values()],
        out_specs=[m for _, m in outs.values()],
        scratch_shapes=list(scratch.values()),
        compiler_params=pltpu.CompilerParams(vmem_limit_bytes=62 * 2**20),
    )(*(a for a, _ in ins.values()))
    got = dict(zip(outs, results, strict=True))
    return got.pop("layer_out"), got.pop("loss"), got.pop("input_grad"), got.pop("norm"), *got.values()


def body_swapped(
    tokens,
    teacher,
    lengths,
    valid_mask,
    random_blocks,
    step_count,
    qkv_weight,
    out_weight,
    up_weight,
    down_weight,
    norm_params,
    qkv_moment,
    qkv_square,
    out_moment,
    out_square,
    up_moment,
    up_square,
    down_moment,
    down_square,
    norm_moment,
    norm_square,
):
    blocks = jnp.transpose(random_blocks, (2, 0, 1))
    lo, ig, gsum, qsum, sums, squares, count = train(
        lengths, tokens, teacher, qkv_weight, up_weight, down_weight.T, out_weight, norm_params, blocks, valid_mask
    )
    gsum = gsum.reshape(-1, UW)
    state = dict(
        qkv=(qkv_weight, qkv_moment, qkv_square),
        out=(out_weight, out_moment, out_square),
        up=(up_weight, up_moment, up_square),
        down=(down_weight.T, down_moment.T, down_square.T),
        norm=(norm_params, norm_moment, norm_square),
    )
    layer_out, loss, input_grad, grad_norm, *new = update(
        step_count, lo, ig, gsum, qsum, sums, squares, count, state
    )
    new[9:12] = [v.T for v in new[9:12]]
    return (layer_out, loss.reshape(()), input_grad, grad_norm.reshape(()), *new)


def solution(mesh):
    in_specs = (
        P("fsdp", "ctx", None),
        P("fsdp", "ctx", None),
        P("fsdp"),
        P("fsdp", "ctx"),
        P("fsdp", "ctx", None),
        P(),
        P(None, "fsdp", "tp"),
        P("tp", "fsdp"),
        P("fsdp", "tp"),
        P("tp", "fsdp"),
        P(None, "fsdp"),
        P(None, "fsdp", "tp"),
        P(None, "fsdp", "tp"),
        P("tp", "fsdp"),
        P("tp", "fsdp"),
        P("fsdp", "tp"),
        P("fsdp", "tp"),
        P("tp", "fsdp"),
        P("tp", "fsdp"),
        P(None, "fsdp"),
        P(None, "fsdp"),
    )
    out_specs = (
        P("fsdp", "ctx", None),
        P(),
        P("fsdp", "ctx", None),
        P(),
        P(None, "fsdp", "tp"),
        P(None, "fsdp", "tp"),
        P(None, "fsdp", "tp"),
        P("tp", "fsdp"),
        P("tp", "fsdp"),
        P("tp", "fsdp"),
        P("fsdp", "tp"),
        P("fsdp", "tp"),
        P("fsdp", "tp"),
        P("tp", "fsdp"),
        P("tp", "fsdp"),
        P("tp", "fsdp"),
        P(None, "fsdp"),
        P(None, "fsdp"),
        P(None, "fsdp"),
    )
    sizes = dict(mesh.shape)
    small = sizes == {"fsdp": 4, "ctx": 2, "tp": 4}
    body = body_swapped if small else body_general
    return jax.shard_map(body, mesh=mesh, in_specs=in_specs, out_specs=out_specs, check_vma=False)
```
